32 devices in a mesh: groups: 2 (over x), seq: 8 (over z, y), dp: 2 (over core).
Axes of the slice: x: 2, y: 2, z: 4, core: 2. Of those that a mesh axis runs over, the one named last changes fastest.
Arguments:
- tower_input: bfloat16 [4, 2048, 384], P(('groups', 'dp'), 'seq'), parts along dimension 0, may hold values from -8 to 8
- conv_weight: bfloat16 [5, 384, 768], replicated, may hold values from -0.125 to 0.125
- norm_gain: float32 [768], replicated, may hold values from 0.25 to 1.75
- query_weight: bfloat16 [768, 1024], replicated, may hold values from -0.25 to 0.25
- key_weight: bfloat16 [768, 128], replicated, may hold values from -8 to 8
- value_weight: bfloat16 [768, 192], replicated, may hold values from -0.21875 to 0.21875
- cotangent: bfloat16 [4, 1024, 1536], P(('groups', 'dp'), 'seq'), parts along dimension 0, may hold values from -6 to 6
Outputs:
- attended: bfloat16 [4, 1024, 1536], P(('groups', 'dp'), 'seq'), parts along dimension 0
- input_grad: bfloat16 [4, 2048, 384], P(('groups', 'dp'), 'seq'), parts along dimension 0
- conv_grad: float32 [3840, 768], P(('groups', 'seq', 'dp')), parts along dimension 0
- query_grad: float32 [1536, 1024], P(('groups', 'seq', 'dp')), parts along dimension 0
- key_grad: float32 [1536, 128], P(('groups', 'seq', 'dp')), parts along dimension 0
- value_grad: float32 [1536, 192], P(('groups', 'seq', 'dp')), parts along dimension 0
- gain_grad: float32 [1536], P(('groups', 'seq', 'dp')), parts along dimension 0
The draws below stay inside these ranges and needn't reach their ends.
There are 2 independent parts, one for each index of `groups`. The reference program is written for one: setup_inputs(seed, part) draws one part's arguments, and reference() takes and returns one part's arrays. A program takes and returns all parts, laid end to end along the dimension named above; an argument that names none is the same for every part. Nothing has to cross between parts.
All inputs are finite; a program needn't handle non-finite values.
Results may differ from the reference program's by a relative error of at most 0.038.
The reference program's roundings to bfloat16 on the way (of `activated`, `normed`, `queries`, `weights`, `score_cot`, `query_cot` and `conv_cot`) count: a program that leaves them out, or rounds other values in their place, can miss the bound.
Values may be sent and summed in bfloat16 or wider, within the bound.
No kernel may reach another device: no remote copies, remote signals or barrier semaphores. Data moves between devices by JAX's collectives and lax.ppermute only.
A program may use at most 128 MiB of HBM per device.

```python
import math
import jax
import jax.numpy as jnp
from jax import lax

C_IN = 384
D = 768
KW = 5
H = 8
DK = 128
DV = 192
SEQS = 2
LENGTH = 1024
POSITIONS = 2048


def shared_matrix(key):
    return jnp.clip(jax.random.normal(key, (D, H * DK), jnp.float32), -4.5, 4.5)


def draw_tower_input(key, part):
    key = jax.random.fold_in(key, 21)
    first = jax.random.fold_in(key, 0)
    base = jax.random.normal(first, (SEQS, POSITIONS, C_IN), jnp.float32)
    return jnp.clip(base, -8.0, 8.0).astype(jnp.bfloat16)


def draw_query_weight(key, part):
    base = shared_matrix(key)
    scaled = jnp.clip(base * D ** (-0.5), -0.25, 0.25)
    scaled = scaled.at[0, 0].set(0.25).at[1, 0].set(-0.25)
    return scaled.astype(jnp.bfloat16)


def draw_key_weight(key, part):
    key = jax.random.fold_in(key, 32)
    fresh = jnp.clip(jax.random.normal(key, (D, DK), jnp.float32), -4.5, 4.5)
    scaled = fresh * D ** (-0.5)
    scaled = jnp.clip(scaled, -8.0, 8.0)
    scaled = scaled.at[0, 1].set(8.0).at[1, 1].set(-8.0)
    return scaled.astype(jnp.bfloat16)


def block_levels(rng, dims, shards, low, high):
    factor_of, own = 1.0, jax.random.fold_in(rng, 6)
    for axis_at, blocks in shards:
        steps = jnp.exp(jax.random.uniform(jax.random.fold_in(own, axis_at), (blocks,), jnp.float32, low / len(shards), high / len(shards)))
        factor_of = factor_of * jnp.repeat(steps, dims[axis_at] // blocks).reshape([-1 if axis == axis_at else 1 for axis in range(len(dims))])
    return factor_of


def gaussian(key, extent, deviation, bound, cuts=(), kind=jnp.bfloat16):
    gain = block_levels(key, extent, cuts, -0.22, 0.18) if cuts else 1.0
    result = jax.random.normal(key, extent, jnp.float32) * deviation * gain
    return jnp.minimum(jnp.maximum(result, -bound), bound).astype(kind)


def setup_inputs(seed: int = 0, part: int = 0) -> dict:
    key_of = jax.random.split(jax.random.key(seed), 8)
    part_keys = jax.random.split(jax.random.fold_in(key_of[7], part), 8)
    return {
        "tower_input": draw_tower_input(jax.random.fold_in(jax.random.fold_in(key_of[7], part), 71), part),
        "conv_weight": gaussian(key_of[1], (KW, C_IN, D), (KW * C_IN) ** -0.5, 0.125),
        "norm_gain": jnp.clip(1.0 + 0.15 * jax.random.normal(key_of[2], (D,), jnp.float32), 0.25, 1.75),
        "query_weight": draw_query_weight(jax.random.fold_in(key_of[7], 71), part),
        "key_weight": draw_key_weight(jax.random.fold_in(key_of[7], 71), part),
        "value_weight": gaussian(key_of[5], (D, DV), D ** -0.5, 0.21875),
        "cotangent": gaussian(part_keys[6], (SEQS, LENGTH, H * DV), 1.0, 6.0, ((0, 2), (1, 8))),
    }


def gelu_slope(values_in):
    root_ratio = math.sqrt(2.0 / math.pi)
    inner = root_ratio * (values_in + 0.044715 * values_in * values_in * values_in)
    tangent = jnp.tanh(inner)
    return 0.5 * (1.0 + tangent) + 0.5 * values_in * (1.0 - tangent * tangent) * root_ratio * (1.0 + 3.0 * 0.044715 * values_in * values_in)

def attend_sequence(queries, keys, values, cotangent):
    block_len = math.gcd(LENGTH, 256)
    block_count = LENGTH // block_len
    query_blocks = queries.reshape(block_count, block_len, H, DK)
    cot_blocks = cotangent.reshape(block_count, block_len, H, DV)
    keys_wide = keys.astype(jnp.float32)
    values_wide = values.astype(jnp.float32)

    def step(state_now, pieces):
        key_sum, value_sum = state_now
        query_piece, cot_piece = pieces
        query_wide = query_piece.astype(jnp.float32)
        cot_wide = cot_piece.astype(jnp.float32)
        scores = jnp.einsum('thd,kd->thk', query_wide, keys_wide)
        row_max = lax.optimization_barrier(jnp.max(scores, axis=-1, keepdims=True))
        log_total = row_max + jnp.log(lax.optimization_barrier(jnp.sum(jnp.exp(scores - row_max), axis=-1, keepdims=True)))
        probabilities = jnp.exp(scores - log_total)
        weights = probabilities.astype(jnp.bfloat16)
        output = jnp.einsum('thk,kc->thc', weights.astype(jnp.float32), values_wide).astype(jnp.bfloat16)
        row_delta = lax.optimization_barrier(jnp.sum(cot_wide * output.astype(jnp.float32), axis=-1, keepdims=True))
        prob_cot = jnp.einsum('thc,kc->thk', cot_wide, values_wide)
        score_cot = (probabilities * (prob_cot - row_delta)).astype(jnp.bfloat16)
        score_wide = score_cot.astype(jnp.float32)
        query_cot = (jnp.einsum('thk,kd->thd', score_wide, keys_wide) * DK ** (-0.5)).astype(jnp.bfloat16)
        key_sum = key_sum + jnp.einsum('thk,thd->kd', score_wide, query_wide)
        value_sum = value_sum + jnp.einsum('thk,thc->kc', weights.astype(jnp.float32), cot_wide)
        return ((key_sum, value_sum), (output, query_cot))
    start_state = (jnp.zeros((LENGTH, DK), jnp.float32), jnp.zeros((LENGTH, DV), jnp.float32))
    final_state, outputs = lax.scan(step, start_state, (query_blocks, cot_blocks))
    attended = outputs[0].reshape(LENGTH, H * DV)
    query_cot = outputs[1].reshape(LENGTH, H * DK)
    return (attended, query_cot, final_state[0].astype(jnp.bfloat16), final_state[1].astype(jnp.bfloat16))

def reference(tower_input, conv_weight, norm_gain, query_weight, key_weight, value_weight, cotangent):
    input_wide = tower_input.astype(jnp.float32)
    activated = jax.nn.gelu(input_wide, approximate=True).astype(jnp.bfloat16)
    padded = jnp.pad(activated, ((0, 0), (2, 2), (0, 0)))
    conv_out = jnp.zeros((SEQS, POSITIONS, D), jnp.float32)
    for offset in range(KW):
        conv_out = conv_out + jnp.einsum('spc,cd->spd', padded[:, offset:offset + POSITIONS].astype(jnp.float32), conv_weight[offset].astype(jnp.float32))
    paired = conv_out.reshape(SEQS, LENGTH, 2, D)
    pooled = 0.5 * (paired[:, :, 0] + paired[:, :, 1])
    inv_rms = lax.rsqrt(lax.optimization_barrier(jnp.mean(pooled * pooled, axis=-1, keepdims=True)) + 1e-06)
    normed = (pooled * inv_rms * norm_gain).astype(jnp.bfloat16)
    normed_flat = normed.reshape(SEQS * LENGTH, D)
    queries = (jnp.dot(normed_flat, query_weight, preferred_element_type=jnp.float32) * DK ** (-0.5)).astype(jnp.bfloat16).reshape(SEQS, LENGTH, H, DK)
    keys = jnp.dot(normed_flat, key_weight, preferred_element_type=jnp.float32).astype(jnp.bfloat16).reshape(SEQS, LENGTH, DK)
    values = jnp.dot(normed_flat, value_weight, preferred_element_type=jnp.float32).astype(jnp.bfloat16).reshape(SEQS, LENGTH, DV)
    cot_heads = cotangent.reshape(SEQS, LENGTH, H, DV)
    results = [attend_sequence(queries[index], keys[index], values[index], cot_heads[index]) for index in range(SEQS)]
    attended = jnp.stack([item[0] for item in results])
    query_cot = jnp.stack([item[1] for item in results]).reshape(SEQS * LENGTH, H * DK)
    key_cot = jnp.stack([item[2] for item in results]).reshape(SEQS * LENGTH, DK)
    value_cot = jnp.stack([item[3] for item in results]).reshape(SEQS * LENGTH, DV)
    query_grad = jnp.dot(normed_flat.T, query_cot, preferred_element_type=jnp.float32)
    key_grad = jnp.dot(normed_flat.T, key_cot, preferred_element_type=jnp.float32)
    value_grad = jnp.dot(normed_flat.T, value_cot, preferred_element_type=jnp.float32)
    normed_cot = jnp.dot(query_cot, query_weight.T, preferred_element_type=jnp.float32)
    normed_cot = normed_cot + jnp.dot(key_cot, key_weight.T, preferred_element_type=jnp.float32)
    normed_cot = normed_cot + jnp.dot(value_cot, value_weight.T, preferred_element_type=jnp.float32)
    normed_cot = normed_cot.reshape(SEQS, LENGTH, D)
    gain_grad = lax.optimization_barrier(jnp.sum(normed_cot * pooled * inv_rms, axis=(0, 1)))
    gained = norm_gain * normed_cot
    pooled_cot = inv_rms * gained - pooled * inv_rms * inv_rms * inv_rms * lax.optimization_barrier(jnp.sum(gained * pooled, axis=-1, keepdims=True)) / D
    conv_cot = jnp.repeat(0.5 * pooled_cot, 2, axis=1).astype(jnp.bfloat16)
    conv_cot_wide = conv_cot.astype(jnp.float32)
    conv_grad = jnp.concatenate([jnp.einsum('spc,spd->cd', padded[:, offset:offset + POSITIONS].astype(jnp.float32), conv_cot_wide) for offset in range(KW)], axis=0)
    padded_cot = jnp.pad(conv_cot_wide, ((0, 0), (2, 2), (0, 0)))
    active_cot = jnp.zeros((SEQS, POSITIONS, C_IN), jnp.float32)
    for offset in range(KW):
        active_cot = active_cot + jnp.einsum('spd,cd->spc', padded_cot[:, 4 - offset:4 - offset + POSITIONS], conv_weight[offset].astype(jnp.float32))
    input_grad = (active_cot * gelu_slope(input_wide)).astype(jnp.bfloat16)
    return (attended, input_grad, conv_grad, query_grad, key_grad, value_grad, gain_grad)
```

```python
import math

import jax
import jax.numpy as jnp
from jax import lax
from jax.experimental import pallas as pl
from jax.experimental.pallas import tpu as pltpu
from jax.sharding import PartitionSpec as P

BF = jnp.bfloat16
F32 = jnp.float32
ROOT = math.sqrt(2.0 / math.pi)
EPS = 1e-06
LANES = 128
VMEM_BYTES = 40 * 2**20


def dot(a, b):
    return lax.dot_general(a, b, (((1,), (0,)), ((), ())), preferred_element_type=F32)


def dot_t(a, b):
    return lax.dot_general(a, b, (((1,), (1,)), ((), ())), preferred_element_type=F32)


def run(body, outs, args, scratch=(), flops=0, name=None):
    size = sum(math.prod(a.shape) * a.dtype.itemsize for a in args)
    size += sum(math.prod(s) * jnp.dtype(t).itemsize for s, t in outs)
    vmem = pl.BlockSpec(memory_space=pltpu.VMEM)
    return pl.pallas_call(
        body,
        out_shape=[jax.ShapeDtypeStruct(s, t) for s, t in outs],
        in_specs=[vmem] * len(args),
        out_specs=[vmem] * len(outs),
        scratch_shapes=list(scratch),
        compiler_params=pltpu.CompilerParams(vmem_limit_bytes=VMEM_BYTES),
        cost_estimate=pl.CostEstimate(flops=flops, bytes_accessed=size, transcendentals=0),
        name=name,
    )(*args)


def gelu(v):
    return v * (0.5 * (1.0 + jnp.tanh(ROOT * (v + 0.044715 * (v * v * v)))))


def gelu_slope(v):
    tangent = jnp.tanh(ROOT * (v + 0.044715 * v * v * v))
    return 0.5 * (1.0 + tangent) + 0.5 * v * (1.0 - tangent * tangent) * ROOT * (
        1.0 + 3.0 * 0.044715 * v * v
    )


def round_up(value, step):
    return -(-value // step) * step


def pack_kv(keys, values):
    tokens, size = keys.shape
    rest = values[:, size:]
    half = tokens // 2
    tail = jnp.concatenate([rest[:half], rest[half:]], axis=1)
    return jnp.concatenate([keys, values[:, :size], tail], axis=0)


def unpack_values(packed, tokens, size):
    tail = packed[2 * tokens :]
    width = tail.shape[1] // 2
    rest = jnp.concatenate([tail[:, :width], tail[:, width:]], axis=0)
    return jnp.concatenate([packed[tokens : 2 * tokens], rest], axis=1)


def put(ref, start, rows):
    for c in range(ref.shape[0]):
        ref[c, start : start + rows.shape[0]] = rows[:, c * LANES : (c + 1) * LANES]


def every_second(ref, start, count):
    parts = [ref[c, pl.ds(start, count, stride=2)] for c in range(ref.shape[0])]
    return jnp.concatenate(parts, axis=1)


def front_kernel(x, before, after, weight, gain, wk, wv, kv_out, early, pooled_out, pad):
    positions, channels = x.shape
    tokens = positions // 2
    ext = early.shape[0] // 2 - tokens
    put(pad, 6, gelu(before[...].astype(F32)).astype(BF).astype(F32))
    put(pad, 8, gelu(x[...].astype(F32)).astype(BF).astype(F32))
    put(pad, 8 + positions, jnp.zeros((pad.shape[1] - 8 - positions, channels), F32))
    put(pad, 8 + positions, gelu(after[...].astype(F32)).astype(BF).astype(F32))
    pieces = [every_second(pad, 6 + u, tokens).astype(BF) for u in range(6)]
    total = None
    for tap in range(5):
        rows = jnp.concatenate([pieces[tap], pieces[tap + 1]], axis=0)
        term = dot(rows, weight[tap])
        total = term if total is None else total + term
    pooled = 0.5 * (total[:tokens] + total[tokens:])
    inv = lax.rsqrt(jnp.mean(pooled * pooled, axis=-1, keepdims=True) + EPS)
    normed = (pooled * inv * gain[...]).astype(BF)
    pooled_out[...] = pooled
    kv_out[...] = pack_kv(dot(normed, wk[...]), dot(normed, wv[...])).astype(BF)
    early[0:ext] = every_second(pad, 6, ext).astype(BF)
    early[ext : 2 * ext] = every_second(pad, 7, ext).astype(BF)
    early[2 * ext : 2 * ext + tokens] = normed[:, :channels]
    early[2 * ext + tokens :] = normed[:, channels:]


def query_kernel(early, wq, out, *, ext, scale):
    tokens = out.shape[0]
    normed = jnp.concatenate(
        [early[2 * ext : 2 * ext + tokens], early[2 * ext + tokens :]], axis=1
    )
    out[...] = (dot(normed, wq[...]) * scale).astype(BF)


def attend_kernel(*refs, blocks, heads, key_size, value_size, scale):
    q, cot = refs[:2]
    parts = refs[2 : 2 + blocks]
    att, dq, near, far, ks, vs, kt, vt, dk, dv = refs[2 + blocks :]
    tokens = q.shape[0]
    half = tokens // 2
    wide = value_size - key_size
    for i, part in enumerate(parts):
        at = i * tokens
        ks[at : at + tokens] = part[:tokens]
        vs[at : at + tokens, :key_size] = part[tokens : 2 * tokens]
        vs[at : at + half, key_size:] = part[2 * tokens :, :wide]
        vs[at + half : at + tokens, key_size:] = part[2 * tokens :, wide:]
        kt[:, at : at + tokens] = ks[at : at + tokens].astype(F32).T.astype(BF)
        vt[:, at : at + tokens] = vs[at : at + tokens].astype(F32).T.astype(BF)
    for pair in range(heads // 2):
        ql, cl, al = 2 * pair * key_size, 2 * pair * value_size, 2 * pair * value_size
        qs = jnp.concatenate(
            [q[:, ql : ql + key_size], q[:, ql + key_size : ql + 2 * key_size]], axis=0
        )
        both = cot[:, cl : cl + 2 * value_size]
        cs = jnp.concatenate([both[:, :value_size], both[:, value_size:]], axis=0)
        scores = dot_t(ks[...], qs)
        raised = jnp.exp(scores - jnp.max(scores, axis=0, keepdims=True))
        probs = raised * (1.0 / jnp.sum(raised, axis=0, keepdims=True))
        weights = probs.astype(BF)
        out_t = dot(vt[...], weights).astype(BF).astype(F32)
        delta = jnp.sum(cs.astype(F32).T * out_t, axis=0, keepdims=True)
        prob_cot = dot_t(vs[...], cs)
        score_cot = (probs * (prob_cot - delta)).astype(BF)
        dq_t = dot(kt[...], score_cot) * scale
        dk_term = dot(score_cot, qs)
        dv_term = dot(weights, cs)
        if pair == 0:
            dk[...] = dk_term
            dv[...] = dv_term
        else:
            dk[...] += dk_term
            dv[...] += dv_term
        out_rows = jnp.concatenate([out_t[:, :tokens].T, out_t[:, tokens:].T], axis=1)
        att[:, al : al + 2 * value_size] = out_rows.astype(BF)
        dq_rows = jnp.concatenate([dq_t[:, :tokens].T, dq_t[:, tokens:].T], axis=1)
        dq[:, ql : ql + 2 * key_size] = dq_rows.astype(BF)
    count = blocks // 2
    for i in range(blocks):
        at = slice(i * tokens, (i + 1) * tokens)
        packed = pack_kv(dk[at], dv[at])
        if i < count:
            near[i] = packed
        else:
            far[i - count] = packed.astype(BF)


def add_kernel(near, far, own, *others):
    own[...] = near[0] + far[0].astype(F32)
    for k, other in enumerate(others):
        other[...] = (near[k + 1] + far[k + 1].astype(F32)).astype(BF)


def query_cot_kernel(dq, wq, out):
    out[...] = dot_t(dq[...], wq[...])


def make_middle(count):
    def middle(*refs):
        own, others = refs[0], refs[1:count]
        part, pooled_in, gain_in, wk, wv, message, edge = refs[count:]
        size = own.shape[1]
        tokens, width = pooled_in.shape
        total = own[...]
        for other in others:
            total = total + other[...].astype(F32)
        total = total.astype(BF).astype(F32)
        key_cot = total[:tokens]
        value_cot = unpack_values(total, tokens, size)
        normed_cot = part[...] + dot_t(key_cot.astype(BF), wk[...])
        normed_cot = normed_cot + dot_t(value_cot.astype(BF), wv[...])
        pooled, gain = pooled_in[...], gain_in[...]
        inv = lax.rsqrt(jnp.mean(pooled * pooled, axis=-1, keepdims=True) + EPS)
        gain_term = jnp.sum(normed_cot * pooled * inv, axis=0, keepdims=True)
        gained = gain * normed_cot
        pooled_cot = inv * gained - pooled * (inv * inv * inv) * (
            jnp.sum(gained * pooled, axis=-1, keepdims=True) / width
        )
        conv_cot = 0.5 * pooled_cot
        high = gain_term.astype(BF).astype(F32)
        low = gain_term - high
        row = lax.broadcasted_iota(jnp.int32, (16, width), 0)
        gains = jnp.where(row == 0, high, jnp.where(row == 1, low, 0.0))
        both = jnp.concatenate([key_cot, value_cot], axis=1)
        fill = width // 2 - both.shape[1]
        both = jnp.concatenate([both, jnp.zeros((tokens, fill), F32)], axis=1)
        side = jnp.concatenate([both[: tokens // 2], both[tokens // 2 :]], axis=1)
        message[:tokens] = conv_cot.astype(BF)
        message[tokens : tokens + 16] = gains.astype(BF)
        message[tokens + 16 :] = side.astype(BF)
        ends = jnp.where(row == 0, conv_cot[:1], jnp.where(row == 1, conv_cot[tokens - 1 :], 0.0))
        edge[...] = ends.astype(BF)

    return middle


def place():
    seq, dp = lax.axis_index("seq"), lax.axis_index("dp")
    high, low = seq // 2, seq % 2
    return lambda k: ((high ^ k) * 2 + low) * 2 + dp


def chosen(rows, padded, columns, block):
    row = lax.broadcasted_iota(jnp.int32, (padded, columns), 0)
    column = lax.broadcasted_iota(jnp.int32, (padded, columns), 1)
    hit = (column == row + block * rows) & (row < rows)
    return jnp.where(hit, 1.0, 0.0).astype(BF)


def select_kernel(*refs, groups, conv_rows, conv_pad, norm_rows, norm_pad):
    blocks = refs[:4]
    conv_out, norm_out, even, odd = refs[4:]
    ext, channels = even.shape
    tokens = (blocks[0].shape[0] - 2 * ext) // 2
    block_of = place()
    conv_pick = jnp.concatenate(
        [chosen(conv_rows, conv_pad, 5 * channels, block_of(k)) for k in range(groups)], axis=0
    )
    norm_pick = jnp.concatenate(
        [chosen(norm_rows, norm_pad, 2 * channels, block_of(k)) for k in range(groups)], axis=0
    )
    for i, block in enumerate(blocks):
        even[...] = block[:ext].astype(F32)
        odd[...] = block[ext : 2 * ext].astype(F32)
        pieces = []
        for shift in range(3):
            pieces += [even[shift : shift + tokens].astype(BF), odd[shift : shift + tokens].astype(BF)]
        rows = jnp.concatenate(
            [jnp.concatenate(pieces[:5], axis=1), jnp.concatenate(pieces[1:], axis=1)], axis=0
        )
        conv_out[:, 2 * i * tokens : 2 * (i + 1) * tokens] = dot_t(conv_pick, rows).astype(BF)
        normed = jnp.concatenate(
            [block[2 * ext : 2 * ext + tokens], block[2 * ext + tokens :]], axis=1
        )
        norm_out[:, i * tokens : (i + 1) * tokens] = dot_t(norm_pick, normed).astype(BF)


def query_grad_kernel(*refs, pad):
    pick, blocks = refs[0], refs[1:5]
    outs, right = refs[5:-1], refs[-1]
    tokens = blocks[0].shape[0]
    for i, block in enumerate(blocks):
        right[i * tokens : (i + 1) * tokens] = block[...]
    for k, out in enumerate(outs):
        out[...] = dot(pick[k * pad : (k + 1) * pad], right[...]).astype(out.dtype)


def query_sum_kernel(*refs):
    parts, out = refs[:-1], refs[-1]
    total = parts[0][...]
    for part in parts[1:]:
        total = total + part[...].astype(F32)
    out[...] = total[: out.shape[0]]


def conv_grad_kernel(*refs, conv_rows, conv_pad, norm_pad):
    pick, norm_pick, blocks = refs[0], refs[1], refs[2:6]
    outs, right, side = refs[6:-2], refs[-2], refs[-1]
    width = right.shape[1]
    tokens = side.shape[0] // 4
    half = tokens // 2
    gain = None
    for i, block in enumerate(blocks):
        piece = block[:tokens]
        right[2 * i * tokens : (2 * i + 1) * tokens] = piece
        right[(2 * i + 1) * tokens : (2 * i + 2) * tokens] = piece
        side[i * tokens : i * tokens + half] = block[tokens + 16 :, : width // 2]
        side[i * tokens + half : (i + 1) * tokens] = block[tokens + 16 :, width // 2 :]
        two = block[tokens : tokens + 16].astype(F32)
        term = two[0:1] + two[1:2]
        gain = term if gain is None else gain + term
    high = gain.astype(BF).astype(F32)
    low = gain - high
    row = lax.broadcasted_iota(jnp.int32, (conv_pad, width), 0)
    split = norm_pad // 2
    for k, out in enumerate(outs):
        conv = dot(pick[k * conv_pad : (k + 1) * conv_pad], right[...])
        conv = jnp.where(row == conv_rows, high, jnp.where(row == conv_rows + 1, low, conv))
        both = dot(norm_pick[k * norm_pad : (k + 1) * norm_pad], side[...])
        out[:conv_pad] = conv.astype(out.dtype)
        packed = jnp.concatenate([both[:split], both[split:]], axis=1)
        fill = out.shape[0] - conv_pad - split
        if fill:
            packed = jnp.concatenate([packed, jnp.zeros((fill, width), F32)], axis=0)
        out[conv_pad:] = packed.astype(out.dtype)


def final_kernel(*refs, conv_pad, norm_pad):
    parts = refs[:-4]
    conv, key, value, gain = refs[-4:]
    total = parts[0][...]
    for part in parts[1:]:
        total = total + part[...].astype(F32)
    rows, width = conv.shape
    count = key.shape[0]
    split = norm_pad // 2
    conv[...] = total[:rows]
    packed = total[conv_pad : conv_pad + split]
    both = jnp.concatenate([packed[:, : width // 2], packed[:, width // 2 :]], axis=0)
    size = key.shape[1]
    key[...] = both[:count, :size]
    value[...] = both[:count, size : size + value.shape[1]]
    line = jnp.broadcast_to(total[rows : rows + 1] + total[rows + 1 : rows + 2], (8, width))
    start = place()(0) * count
    gain[...] = pltpu.roll(line, lax.rem(width - start, width), 1)[:1, :count]


def input_kernel(x, cc, pair_cc, edge, weight, out, ext, mixed):
    tokens = x.shape[0] // 2
    low = lax.axis_index("seq") % 2
    ext[8 : 8 + tokens] = cc[:tokens].astype(F32)
    pair_first = pair_cc[0:16].astype(F32)[0:1]
    pair_last = pair_cc[tokens - 16 : tokens].astype(F32)[15:16]
    ends = edge[...].astype(F32)
    ext[7:8] = jnp.where(low == 0, ends[1:2], pair_last)
    ext[8 + tokens : 9 + tokens] = jnp.where(low == 0, pair_first, ends[0:1])
    back = ext[7 : 7 + tokens].astype(BF)
    here = ext[8 : 8 + tokens].astype(BF)
    ahead = ext[9 : 9 + tokens].astype(BF)
    evens = (ahead, here, here, back, back)
    odds = (ahead, ahead, here, here, back)
    total = None
    for tap in range(5):
        term = dot_t(jnp.concatenate([evens[tap], odds[tap]], axis=0), weight[tap])
        total = term if total is None else total + term
    for c in range(mixed.shape[0]):
        lanes = slice(c * LANES, (c + 1) * LANES)
        mixed[c, pl.ds(0, tokens, stride=2)] = total[:tokens, lanes]
        mixed[c, pl.ds(1, tokens, stride=2)] = total[tokens:, lanes]
        out[:, lanes] = (mixed[c] * gelu_slope(x[:, lanes].astype(F32))).astype(BF)


def on_device(x, conv_weight, norm_gain, wq, wk, wv, cotangent):
    devices = lax.axis_size("seq")
    both_axes = ("seq", "dp")
    x, cotangent = x[0], cotangent[0]
    positions, channels = x.shape
    tokens = positions // 2
    taps, _, width = conv_weight.shape
    key_size, value_size = wk.shape[1], wv.shape[1]
    heads = cotangent.shape[1] // value_size
    scale = key_size ** (-0.5)
    groups = devices // 2
    owners = devices * 2
    conv_rows, norm_rows = taps * channels // owners, width // owners
    conv_pad, norm_pad = round_up(conv_rows + 2, 16), round_up(norm_rows, 16)
    ext = tokens + 16
    gain = norm_gain.reshape(1, width)

    def swap(value, seq_bits, dp_bit=0):
        mask = 2 * seq_bits + dp_bit
        return lax.ppermute(value, both_axes, [(i, i ^ mask) for i in range(owners)])

    def quad(value):
        core = swap(value, 0, 1)
        near = swap(value, 1)
        return [value, core, near, swap(near, 0, 1)]

    up = [(i, i + 1) for i in range(devices - 1)]
    down = [(j, i) for i, j in up]
    before = lax.ppermute(x[positions - 2 :], "seq", up)
    after = lax.ppermute(x[:2], "seq", down)
    kv, early, pooled = run(
        front_kernel,
        [
            ((5 * tokens // 2, key_size), BF),
            ((2 * ext + 2 * tokens, channels), BF),
            ((tokens, width), F32),
        ],
        [x, before, after, conv_weight, gain, wk, wv],
        [pltpu.VMEM((channels // LANES, 8 + 2 * ext + 8, LANES), F32)],
        flops=2 * positions * taps * channels * width,
        name="front",
    )
    near_kv = [kv] + [swap(kv, 2 * k) for k in range(1, groups)]
    far_kv = [swap(block, 1) for block in near_kv]
    (queries,) = run(
        lambda e, w, o: query_kernel(e, w, o, ext=ext, scale=scale),
        [((tokens, heads * key_size), BF)],
        [early, wq],
        flops=2 * tokens * width * heads * key_size,
        name="queries",
    )
    length = devices * tokens
    attended, query_cot, near_cot, far_cot = run(
        lambda *refs: attend_kernel(
            *refs,
            blocks=devices,
            heads=heads,
            key_size=key_size,
            value_size=value_size,
            scale=scale,
        ),
        [
            ((tokens, heads * value_size), BF),
            ((tokens, heads * key_size), BF),
            ((groups, 5 * tokens // 2, key_size), F32),
            ((groups, 5 * tokens // 2, key_size), BF),
        ],
        [queries, cotangent] + near_kv + far_kv,
        [
            pltpu.VMEM((length, key_size), BF),
            pltpu.VMEM((length, value_size), BF),
            pltpu.VMEM((key_size, length), BF),
            pltpu.VMEM((value_size, length), BF),
            pltpu.VMEM((length, key_size), F32),
            pltpu.VMEM((length, value_size), F32),
        ],
        flops=6 * tokens * heads * length * (key_size + value_size),
        name="attend",
    )
    early_blocks = quad(early)
    conv_pick, norm_pick = run(
        lambda *refs: select_kernel(
            *refs,
            groups=groups,
            conv_rows=conv_rows,
            conv_pad=conv_pad,
            norm_rows=norm_rows,
            norm_pad=norm_pad,
        ),
        [((groups * conv_pad, 8 * tokens), BF), ((groups * norm_pad, 4 * tokens), BF)],
        early_blocks,
        [pltpu.VMEM((ext, channels), F32), pltpu.VMEM((ext, channels), F32)],
        flops=2 * groups * conv_pad * taps * channels * 8 * tokens,
        name="select",
    )
    far_sum = swap(far_cot, 1)
    block_shape = (5 * tokens // 2, key_size)
    own, *others = run(
        add_kernel,
        [(block_shape, F32)] + [(block_shape, BF)] * (groups - 1),
        [near_cot, far_sum],
        name="kv_cot_sum",
    )
    arrived = [swap(other, 2 * (k + 1)) for k, other in enumerate(others)]
    (normed_cot,) = run(
        query_cot_kernel,
        [((tokens, width), F32)],
        [query_cot, wq],
        flops=2 * tokens * width * heads * key_size,
        name="query_part",
    )
    query_blocks = quad(query_cot)
    query_parts = run(
        lambda *refs: query_grad_kernel(*refs, pad=norm_pad),
        [((norm_pad, heads * key_size), F32 if k == 0 else BF) for k in range(groups)],
        [norm_pick] + query_blocks,
        [pltpu.VMEM((4 * tokens, heads * key_size), BF)],
        flops=2 * groups * norm_pad * 4 * tokens * heads * key_size,
        name="query_grad",
    )
    message, edge = run(
        make_middle(groups),
        [((tokens + 16 + tokens // 2, width), BF), ((16, width), BF)],
        [own] + arrived + [normed_cot, pooled, gain, wk, wv],
        flops=2 * tokens * width * (key_size + value_size),
        name="conv_cot",
    )
    blocks = quad(message)
    crossing = [(i, i + 1) for i in range(1, devices - 1, 2)]
    crossing = crossing + [(j, i) for i, j in crossing]
    edge_in = lax.ppermute(edge, "seq", crossing)
    chunk_rows = round_up(conv_pad + norm_pad // 2, 16)
    conv_parts = run(
        lambda *refs: conv_grad_kernel(
            *refs, conv_rows=conv_rows, conv_pad=conv_pad, norm_pad=norm_pad
        ),
        [((chunk_rows, width), F32 if k == 0 else BF) for k in range(groups)],
        [conv_pick, norm_pick] + blocks,
        [pltpu.VMEM((8 * tokens, width), BF), pltpu.VMEM((4 * tokens, width // 2), BF)],
        flops=2 * groups * conv_pad * 8 * tokens * width,
        name="conv_grad",
    )
    conv_in = [swap(part, 2 * (k + 1)) for k, part in enumerate(conv_parts[1:])]
    query_in = [swap(part, 2 * (k + 1)) for k, part in enumerate(query_parts[1:])]
    (input_grad,) = run(
        input_kernel,
        [((positions, channels), BF)],
        [x, message, blocks[2], edge_in, conv_weight],
        [pltpu.VMEM((tokens + 16, width), F32), pltpu.VMEM((channels // LANES, positions, LANES), F32)],
        flops=2 * positions * taps * channels * width,
        name="input_grad",
    )
    (query_grad,) = run(
        query_sum_kernel,
        [((norm_rows, heads * key_size), F32)],
        [query_parts[0]] + query_in,
        name="query_sum",
    )
    conv_grad, key_grad, value_grad, gain_grad = run(
        lambda *refs: final_kernel(*refs, conv_pad=conv_pad, norm_pad=norm_pad),
        [
            ((conv_rows, width), F32),
            ((norm_rows, key_size), F32),
            ((norm_rows, value_size), F32),
            ((1, norm_rows), F32),
        ],
        [conv_parts[0]] + conv_in,
        name="conv_sum",
    )
    return (
        attended[None],
        input_grad[None],
        conv_grad,
        query_grad,
        key_grad,
        value_grad,
        gain_grad.reshape(norm_rows),
    )


def solution(mesh):
    placed = (
        P(("groups", "dp"), "seq", None),
        P(),
        P(),
        P(),
        P(),
        P(),
        P(("groups", "dp"), "seq", None),
    )
    return jax.shard_map(
        on_device,
        mesh=mesh,
        in_specs=placed,
        out_specs=(
            P(("groups", "dp"), "seq", None),
            P(("groups", "dp"), "seq", None),
            P(("groups", "seq", "dp"), None),
            P(("groups", "seq", "dp"), None),
            P(("groups", "seq", "dp"), None),
            P(("groups", "seq", "dp"), None),
            P(("groups", "seq", "dp")),
        ),
        check_vma=False,
    )
```

```python
import math

import jax
import jax.numpy as jnp
from jax import lax
from jax.experimental import pallas as pl
from jax.experimental.pallas import tpu as pltpu
from jax.sharding import PartitionSpec as P

BF = jnp.bfloat16
F32 = jnp.float32
ROOT = math.sqrt(2.0 / math.pi)
EPS = 1e-06
LANES = 128
VMEM_BYTES = 40 * 2**20


def dot(a, b):
    return lax.dot_general(a, b, (((1,), (0,)), ((), ())), preferred_element_type=F32)


def dot_t(a, b):
    return lax.dot_general(a, b, (((1,), (1,)), ((), ())), preferred_element_type=F32)


def run(body, outs, args, scratch=(), flops=0, name=None, after=()):
    size = sum(math.prod(a.shape) * a.dtype.itemsize for a in args)
    size += sum(math.prod(s) * jnp.dtype(t).itemsize for s, t in outs)
    vmem = pl.BlockSpec(memory_space=pltpu.VMEM)
    rest = pl.BlockSpec(memory_space=pl.ANY)
    count, skip = len(args), len(args) + len(after)

    def whole(*refs):
        body(*refs[:count], *refs[skip:])

    return pl.pallas_call(
        whole,
        out_shape=[jax.ShapeDtypeStruct(s, t) for s, t in outs],
        in_specs=[vmem] * count + [rest] * len(after),
        out_specs=[vmem] * len(outs),
        scratch_shapes=list(scratch),
        compiler_params=pltpu.CompilerParams(vmem_limit_bytes=VMEM_BYTES),
        cost_estimate=pl.CostEstimate(flops=flops, bytes_accessed=size, transcendentals=0),
        name=name,
    )(*args, *after)


def gelu(v):
    return v * (0.5 * (1.0 + jnp.tanh(ROOT * (v + 0.044715 * (v * v * v)))))


def gelu_slope(v):
    tangent = jnp.tanh(ROOT * (v + 0.044715 * v * v * v))
    return 0.5 * (1.0 + tangent) + 0.5 * v * (1.0 - tangent * tangent) * ROOT * (
        1.0 + 3.0 * 0.044715 * v * v
    )


def round_up(value, step):
    return -(-value // step) * step


def pack_kv(keys, values):
    tokens, size = keys.shape
    rest = values[:, size:]
    half = tokens // 2
    tail = jnp.concatenate([rest[:half], rest[half:]], axis=1)
    return jnp.concatenate([keys, values[:, :size], tail], axis=0)


def unpack_values(packed, tokens, size):
    tail = packed[2 * tokens :]
    width = tail.shape[1] // 2
    rest = jnp.concatenate([tail[:, :width], tail[:, width:]], axis=0)
    return jnp.concatenate([packed[tokens : 2 * tokens], rest], axis=1)


def put(ref, start, rows):
    for c in range(ref.shape[0]):
        ref[c, start : start + rows.shape[0]] = rows[:, c * LANES : (c + 1) * LANES]


def every_second(ref, start, count):
    parts = [ref[c, pl.ds(start, count, stride=2)] for c in range(ref.shape[0])]
    return jnp.concatenate(parts, axis=1)


def prepare_kernel(x, pad):
    positions, channels = x.shape
    put(pad, 0, jnp.zeros((8, channels), F32))
    put(pad, 8, gelu(x[...].astype(F32)).astype(BF).astype(F32))
    put(pad, 8 + positions, jnp.zeros((pad.shape[1] - 8 - positions, channels), F32))


def front_kernel(ready, before, after, weight, gain, wk, wv, kv_out, early, normed_out, pooled_out, pad):
    channels = before.shape[1]
    tokens = pooled_out.shape[0]
    ext = early.shape[0] // 2
    pad[...] = ready[...]
    put(pad, 6, gelu(before[...].astype(F32)).astype(BF).astype(F32))
    put(pad, 8 + 2 * tokens, gelu(after[...].astype(F32)).astype(BF).astype(F32))
    pieces = [every_second(pad, 6 + u, tokens).astype(BF) for u in range(6)]
    total = None
    for tap in range(5):
        rows = jnp.concatenate([pieces[tap], pieces[tap + 1]], axis=0)
        term = dot(rows, weight[tap])
        total = term if total is None else total + term
    pooled = 0.5 * (total[:tokens] + total[tokens:])
    inv = lax.rsqrt(jnp.mean(pooled * pooled, axis=-1, keepdims=True) + EPS)
    normed = (pooled * inv * gain[...]).astype(BF)
    pooled_out[...] = pooled
    normed_out[...] = normed
    kv_out[...] = pack_kv(dot(normed, wk[...]), dot_t(normed, wv[...])).astype(BF)
    early[0:ext] = every_second(pad, 6, ext).astype(BF)
    early[ext : 2 * ext] = every_second(pad, 7, ext).astype(BF)


def query_kernel(normed, wq, early, out, early_out, *picks, groups, rows, padded, scale):
    width = normed.shape[1]
    value = normed[...]
    out[...] = (dot(value, wq[...]) * scale).astype(BF)
    for i in range(4):
        block_of = place(i)
        pick = [chosen(rows, padded, width, block_of(k)) for k in range(groups)]
        picks[i][...] = dot_t(jnp.concatenate(pick, axis=0), value).astype(BF)
    early_out[...] = early[...]


def attend_pair(index, q, cot, ks, vs, kt, vt, dk, dv, att, dq, key_size, value_size, scale, first):
    tokens = q.shape[0]
    ql, cl = 2 * index * key_size, 2 * index * value_size
    qs = jnp.concatenate(
        [q[:, ql : ql + key_size], q[:, ql + key_size : ql + 2 * key_size]], axis=0
    )
    both = cot[:, cl : cl + 2 * value_size]
    cs = jnp.concatenate([both[:, :value_size], both[:, value_size:]], axis=0)
    scores = dot_t(ks[...], qs)
    raised = jnp.exp(scores - jnp.max(scores, axis=0, keepdims=True))
    probs = raised * (1.0 / jnp.sum(raised, axis=0, keepdims=True))
    weights = probs.astype(BF)
    out_t = dot(vt[...], weights).astype(BF).astype(F32)
    delta = jnp.sum(cs.astype(F32).T * out_t, axis=0, keepdims=True)
    prob_cot = dot_t(vs[...], cs)
    score_cot = (probs * (prob_cot - delta)).astype(BF)
    dq_t = dot(kt[...], score_cot) * scale
    dk_term = dot(score_cot, qs)
    dv_term = dot(weights, cs)
    if first:
        dk[...] = dk_term
        dv[...] = dv_term
    else:
        dk[...] += dk_term
        dv[...] += dv_term
    out_rows = jnp.concatenate([out_t[:, :tokens].T, out_t[:, tokens:].T], axis=1)
    att[:, cl : cl + 2 * value_size] = out_rows.astype(BF)
    dq_rows = jnp.concatenate([dq_t[:, :tokens].T, dq_t[:, tokens:].T], axis=1)
    dq[:, ql % dq.shape[1] : ql % dq.shape[1] + 2 * key_size] = dq_rows.astype(BF)


def attend_first_kernel(*refs, blocks, heads, key_size, value_size, scale):
    q, cot = refs[:2]
    parts = refs[2 : 2 + blocks]
    att, dq, ks, vs, kt, vt, dk, dv = refs[2 + blocks :]
    tokens = q.shape[0]
    half = tokens // 2
    wide = value_size - key_size
    for i, part in enumerate(parts):
        at = i * tokens
        ks[at : at + tokens] = part[:tokens]
        vs[at : at + tokens, :key_size] = part[tokens : 2 * tokens]
        vs[at : at + half, key_size:] = part[2 * tokens :, :wide]
        vs[at + half : at + tokens, key_size:] = part[2 * tokens :, wide:]
        kt[:, at : at + tokens] = ks[at : at + tokens].astype(F32).T.astype(BF)
        vt[:, at : at + tokens] = vs[at : at + tokens].astype(F32).T.astype(BF)
    for pair in range(heads // 4):
        attend_pair(
            pair, q, cot, ks, vs, kt, vt, dk, dv, att, dq, key_size, value_size, scale, pair == 0
        )


def attend_second_kernel(*refs, blocks, heads, key_size, value_size, scale):
    q, cot, att_in, ks, vs, kt, vt, dk_in, dv_in = refs[:9]
    att, dq, near, far_first, far_last, dk, dv = refs[9:]
    tokens = q.shape[0]
    att[:, : att_in.shape[1]] = att_in[...]
    for pair in range(heads // 4, heads // 2):
        if pair == heads // 4:
            dk[...] = dk_in[...]
            dv[...] = dv_in[...]
        attend_pair(
            pair, q, cot, ks, vs, kt, vt, dk, dv, att, dq, key_size, value_size, scale, False
        )
    count = blocks // 2
    half = count // 2
    for i in range(blocks):
        at = slice(i * tokens, (i + 1) * tokens)
        packed = pack_kv(dk[at], dv[at])
        k = i - count
        if k < 0:
            near[i] = packed
        elif k < half:
            far_last[k] = packed.astype(BF)
        else:
            far_first[k - half] = packed.astype(BF)


def add_kernel(near, far, *outs, start):
    for k, out in enumerate(outs):
        out[...] = (near[start + k] + far[k].astype(F32)).astype(out.dtype)


def add_near_kernel(near, far, left, right, both, *outs):
    both[:, : left.shape[1]] = left[...]
    both[:, left.shape[1] :] = right[...]
    add_kernel(near, far, *outs, start=0)


def query_cot_kernel(dq, wq, out):
    out[...] = dot_t(dq[...], wq[...])


def make_middle(count):
    def middle(*refs):
        own, others = refs[0], refs[1:count]
        part, pooled_in, gain_in, wk, wv, message, edge = refs[count:]
        size = own.shape[1]
        tokens, width = pooled_in.shape
        total = own[...]
        for other in others:
            total = total + other[...].astype(F32)
        total = total.astype(BF).astype(F32)
        key_cot = total[:tokens]
        value_cot = unpack_values(total, tokens, size)
        normed_cot = part[...] + dot_t(key_cot.astype(BF), wk[...])
        normed_cot = normed_cot + dot(value_cot.astype(BF), wv[...])
        pooled, gain = pooled_in[...], gain_in[...]
        inv = lax.rsqrt(jnp.mean(pooled * pooled, axis=-1, keepdims=True) + EPS)
        gain_term = jnp.sum(normed_cot * pooled * inv, axis=0, keepdims=True)
        gained = gain * normed_cot
        pooled_cot = inv * gained - pooled * (inv * inv * inv) * (
            jnp.sum(gained * pooled, axis=-1, keepdims=True) / width
        )
        conv_cot = 0.5 * pooled_cot
        high = gain_term.astype(BF).astype(F32)
        low = gain_term - high
        row = lax.broadcasted_iota(jnp.int32, (16, width), 0)
        gains = jnp.where(row == 0, high, jnp.where(row == 1, low, 0.0))
        both = jnp.concatenate([key_cot, value_cot], axis=1)
        fill = width // 2 - both.shape[1]
        both = jnp.concatenate([both, jnp.zeros((tokens, fill), F32)], axis=1)
        side = jnp.concatenate([both[: tokens // 2], both[tokens // 2 :]], axis=1)
        message[:tokens] = conv_cot.astype(BF)
        message[tokens : tokens + 16] = gains.astype(BF)
        message[tokens + 16 :] = side.astype(BF)
        ends = jnp.where(row == 0, conv_cot[:1], jnp.where(row == 1, conv_cot[tokens - 1 :], 0.0))
        edge[...] = ends.astype(BF)

    return middle


def place(other=0):
    seq, dp = lax.axis_index("seq"), lax.axis_index("dp") ^ (other % 2)
    high, low = seq // 2, (seq % 2) ^ (other // 2)
    return lambda k: ((high ^ k) * 2 + low) * 2 + dp


def chosen(rows, padded, columns, block):
    row = lax.broadcasted_iota(jnp.int32, (padded, columns), 0)
    column = lax.broadcasted_iota(jnp.int32, (padded, columns), 1)
    hit = (column == row + block * rows) & (row < rows)
    return jnp.where(hit, 1.0, 0.0).astype(BF)


def relay_kernel(value, out):
    out[...] = value[...]


def select_kernel(*refs, groups, rows, padded):
    blocks = refs[:4]
    out, even, odd = refs[4:]
    ext, channels = even.shape
    tokens = out.shape[1] // 8
    block_of = place()
    pick = jnp.concatenate(
        [chosen(rows, padded, 5 * channels, block_of(k)) for k in range(groups)], axis=0
    )
    for i, block in enumerate(blocks):
        even[...] = block[:ext].astype(F32)
        odd[...] = block[ext : 2 * ext].astype(F32)
        pieces = []
        for shift in range(3):
            pieces += [even[shift : shift + tokens].astype(BF), odd[shift : shift + tokens].astype(BF)]
        shifted = jnp.concatenate(
            [jnp.concatenate(pieces[:5], axis=1), jnp.concatenate(pieces[1:], axis=1)], axis=0
        )
        out[:, 2 * i * tokens : 2 * (i + 1) * tokens] = dot_t(pick, shifted).astype(BF)


def query_grad_kernel(*refs, pad):
    picks, blocks = refs[:4], refs[4:8]
    outs, right = refs[8:-1], refs[-1]
    tokens = blocks[0].shape[0]
    for i, block in enumerate(blocks):
        right[i * tokens : (i + 1) * tokens] = block[...]
    pick = jnp.concatenate([part[...] for part in picks], axis=1)
    for k, out in enumerate(outs):
        out[...] = dot(pick[k * pad : (k + 1) * pad], right[...]).astype(out.dtype)


def query_sum_kernel(*refs):
    parts, out = refs[:-1], refs[-1]
    total = parts[0][...]
    for part in parts[1:]:
        total = total + part[...].astype(F32)
    out[...] = total[: out.shape[0]]


def chunk_layout(conv_rows, norm_rows, width, key_size, value_size):
    key_rows = norm_rows * key_size // width
    value_rows = norm_rows * value_size // width
    return conv_rows, conv_rows + key_rows, conv_rows + key_rows + value_rows


def conv_grad_kernel(*refs, conv_rows, conv_pad, norm_rows, norm_pad, key_size, value_size):
    pick, picks, blocks = refs[0], refs[1:5], refs[5:9]
    outs, right, side, stage = refs[9:-3], refs[-3], refs[-2], refs[-1]
    norm_pick = jnp.concatenate([part[...] for part in picks], axis=1)
    width = right.shape[1]
    tokens = side.shape[0] // 4
    half = tokens // 2
    gain = None
    for i, block in enumerate(blocks):
        piece = block[:tokens]
        right[2 * i * tokens : (2 * i + 1) * tokens] = piece
        right[(2 * i + 1) * tokens : (2 * i + 2) * tokens] = piece
        side[i * tokens : i * tokens + half] = block[tokens + 16 :, : width // 2]
        side[i * tokens + half : (i + 1) * tokens] = block[tokens + 16 :, width // 2 :]
        two = block[tokens : tokens + 16].astype(F32)
        term = two[0:1] + two[1:2]
        gain = term if gain is None else gain + term
    high = gain.astype(BF).astype(F32)
    key_at, value_at, gain_at = chunk_layout(conv_rows, norm_rows, width, key_size, value_size)
    stage[...] = jnp.zeros(stage.shape, F32)
    stage[gain_at : gain_at + 1] = high
    stage[gain_at + 1 : gain_at + 2] = gain - high
    for k, out in enumerate(outs):
        conv = dot(pick[k * conv_pad : (k + 1) * conv_pad], right[...])
        stage[:conv_rows] = conv[:conv_rows]
        both = dot(norm_pick[k * norm_pad : (k + 1) * norm_pad], side[...])
        key, value = both[:, :key_size], both[:, key_size : key_size + value_size]
        for part, at, end in ((key, key_at, value_at), (value, value_at, gain_at)):
            count = end - at
            pieces = [part[i : i + count] for i in range(0, norm_rows, count)]
            stage[at:end] = jnp.concatenate(pieces, axis=1)
        out[...] = stage[...].astype(out.dtype)


def final_kernel(*refs):
    parts = refs[:-5]
    conv, key, value, gain, stage = refs[-5:]
    total = parts[0][...]
    for part in parts[1:]:
        total = total + part[...].astype(F32)
    rows, width = conv.shape
    count = key.shape[0]
    stage[...] = total
    conv[...] = stage[:rows]
    key_at, value_at, gain_at = chunk_layout(
        rows, count, width, key.shape[1], value.shape[1]
    )
    for part, at, end in ((key, key_at, value_at), (value, value_at, gain_at)):
        size, step = part.shape[1], end - at
        packed = stage[at:end]
        for i in range(count // step):
            part[i * step : (i + 1) * step] = packed[:, i * size : (i + 1) * size]
    line = stage[gain_at : gain_at + 1] + stage[gain_at + 1 : gain_at + 2]
    line = jnp.broadcast_to(line, (8, width))
    start = place()(0) * count
    gain[...] = pltpu.roll(line, lax.rem(width - start, width), 1)[:1, :count]


def input_kernel(x, cc, pair_cc, edge, weight, out, ext, mixed):
    tokens = x.shape[0] // 2
    low = lax.axis_index("seq") % 2
    ext[8 : 8 + tokens] = cc[:tokens].astype(F32)
    pair_first = pair_cc[0:16].astype(F32)[0:1]
    pair_last = pair_cc[tokens - 16 : tokens].astype(F32)[15:16]
    ends = edge[...].astype(F32)
    ext[7:8] = jnp.where(low == 0, ends[1:2], pair_last)
    ext[8 + tokens : 9 + tokens] = jnp.where(low == 0, pair_first, ends[0:1])
    back = ext[7 : 7 + tokens].astype(BF)
    here = ext[8 : 8 + tokens].astype(BF)
    ahead = ext[9 : 9 + tokens].astype(BF)
    evens = (ahead, here, here, back, back)
    odds = (ahead, ahead, here, here, back)
    total = None
    for tap in range(5):
        term = dot_t(jnp.concatenate([evens[tap], odds[tap]], axis=0), weight[tap])
        total = term if total is None else total + term
    for c in range(mixed.shape[0]):
        lanes = slice(c * LANES, (c + 1) * LANES)
        mixed[c, pl.ds(0, tokens, stride=2)] = total[:tokens, lanes]
        mixed[c, pl.ds(1, tokens, stride=2)] = total[tokens:, lanes]
        out[:, lanes] = (mixed[c] * gelu_slope(x[:, lanes].astype(F32))).astype(BF)


def on_device(x, conv_weight, norm_gain, wq, wk, wv, cotangent):
    devices = lax.axis_size("seq")
    both_axes = ("seq", "dp")
    x, cotangent = x[0], cotangent[0]
    positions, channels = x.shape
    tokens = positions // 2
    taps, _, width = conv_weight.shape
    key_size, value_size = wk.shape[1], wv.shape[1]
    heads = cotangent.shape[1] // value_size
    scale = key_size ** (-0.5)
    groups = devices // 2
    owners = devices * 2
    conv_rows, norm_rows = taps * channels // owners, width // owners
    conv_pad, norm_pad = round_up(conv_rows, 16), round_up(norm_rows, 16)
    ext = tokens + 16
    gain = norm_gain.reshape(1, width)

    def swap(value, seq_bits, dp_bit=0):
        mask = 2 * seq_bits + dp_bit
        return lax.ppermute(value, both_axes, [(i, i ^ mask) for i in range(owners)])

    def quad(value):
        core = swap(value, 0, 1)
        near = swap(value, 1)
        return [value, core, near, swap(near, 0, 1)]

    up = [(i, i + 1) for i in range(devices - 1)]
    down = [(j, i) for i, j in up]
    before = lax.ppermute(x[positions - 2 :], "seq", up)
    after = lax.ppermute(x[:2], "seq", down)
    pad_shape = (channels // LANES, 8 + 2 * ext + 8, LANES)
    wv = wv.T
    (ready,) = run(prepare_kernel, [(pad_shape, F32)], [x], flops=4 * 10**9, name="gelu")
    kv, early, normed, pooled = run(
        front_kernel,
        [
            ((5 * tokens // 2, key_size), BF),
            ((2 * ext, channels), BF),
            ((tokens, width), BF),
            ((tokens, width), F32),
        ],
        [ready, before, after, conv_weight, gain, wk, wv],
        [pltpu.VMEM(pad_shape, F32)],
        flops=2 * positions * taps * channels * width,
        name="front",
    )
    near_kv = [kv] + [swap(kv, 2 * k) for k in range(1, groups)]
    far_kv = [swap(block, 1) for block in near_kv]
    queries, early, *picks = run(
        lambda *refs: query_kernel(
            *refs, groups=groups, rows=norm_rows, padded=norm_pad, scale=scale
        ),
        [
            ((tokens, heads * key_size), BF),
            (early.shape, BF),
        ]
        + [((groups * norm_pad, tokens), BF)] * 4,
        [normed, wq, early],
        flops=4 * tokens * width * heads * key_size,
        name="queries",
    )
    length = devices * tokens
    sizes = dict(
        blocks=devices, heads=heads, key_size=key_size, value_size=value_size, scale=scale
    )
    attend_flops = 3 * tokens * heads * length * (key_size + value_size)
    half_att = heads // 2 * value_size
    half_query = heads // 2 * key_size
    totals = [((length, key_size), F32), ((length, value_size), F32)]
    att_first, dq_first, *held = run(
        lambda *refs: attend_first_kernel(*refs, **sizes),
        [
            ((tokens, half_att), BF),
            ((tokens, half_query), BF),
            ((length, key_size), BF),
            ((length, value_size), BF),
            ((key_size, length), BF),
            ((value_size, length), BF),
        ]
        + totals,
        [queries, cotangent] + near_kv + far_kv,
        flops=attend_flops,
        name="attend_first",
    )
    early_near, early_core = swap(early, 1), swap(early, 0, 1)
    norm_picks = [picks[0], swap(picks[1], 0, 1), swap(picks[2], 1), swap(picks[3], 1, 1)]
    block_shape = (5 * tokens // 2, key_size)
    split = groups // 2
    attended, dq_second, near_cot, far_first, far_last = run(
        lambda *refs: attend_second_kernel(*refs, **sizes),
        [
            ((tokens, heads * value_size), BF),
            ((tokens, half_query), BF),
            ((groups,) + block_shape, F32),
            ((groups - split,) + block_shape, BF),
            ((split,) + block_shape, BF),
        ],
        [queries, cotangent, att_first] + held,
        [pltpu.VMEM(s, t) for s, t in totals],
        flops=attend_flops,
        name="attend_second",
        after=[early_near, early_core] + norm_picks[1:],
    )
    far_first = swap(far_first, 1)
    far_last = swap(far_last, 1)
    early_blocks = [early, early_core, early_near, swap(early_near, 0, 1)]
    (conv_pick,) = run(
        lambda *refs: select_kernel(*refs, groups=groups, rows=conv_rows, padded=conv_pad),
        [((groups * conv_pad, 8 * tokens), BF)],
        early_blocks,
        [pltpu.VMEM((ext, channels), F32), pltpu.VMEM((ext, channels), F32)],
        flops=2 * groups * conv_pad * taps * channels * 8 * tokens,
        name="select",
    )
    last = run(
        lambda *refs: add_kernel(*refs, start=split),
        [(block_shape, BF)] * (groups - split),
        [near_cot, far_first],
        name="kv_cot_far",
        after=[conv_pick],
    )
    query_cot, own, *others = run(
        add_near_kernel,
        [((tokens, heads * key_size), BF), (block_shape, F32)] + [(block_shape, BF)] * (split - 1),
        [near_cot, far_last, dq_first, dq_second],
        name="kv_cot_near",
        after=[last[0]],
    )
    others = others + list(last)
    arrived = [swap(other, 2 * (k + 1)) for k, other in enumerate(others)]
    (normed_cot,) = run(
        query_cot_kernel,
        [((tokens, width), F32)],
        [query_cot, wq],
        flops=2 * tokens * width * heads * key_size,
        name="query_part",
    )
    query_blocks = quad(query_cot)
    query_parts = run(
        lambda *refs: query_grad_kernel(*refs, pad=norm_pad),
        [((norm_pad, heads * key_size), F32 if k == 0 else BF) for k in range(groups)],
        norm_picks + query_blocks,
        [pltpu.VMEM((4 * tokens, heads * key_size), BF)],
        flops=2 * groups * norm_pad * 4 * tokens * heads * key_size,
        name="query_grad",
    )
    message, edge = run(
        make_middle(groups),
        [((tokens + 16 + tokens // 2, width), BF), ((16, width), BF)],
        [own] + arrived + [normed_cot, pooled, gain, wk, wv],
        flops=2 * tokens * width * (key_size + value_size),
        name="conv_cot",
        after=[query_blocks[2]],
    )
    near_message = swap(message, 1)
    (relay,) = run(
        relay_kernel,
        [(message.shape, BF)],
        [near_message],
        name="relay",
        after=[query_parts[0]],
    )
    blocks = [message, swap(message, 0, 1), near_message, swap(relay, 0, 1)]
    crossing = [(i, i + 1) for i in range(1, devices - 1, 2)]
    crossing = crossing + [(j, i) for i, j in crossing]
    edge_in = lax.ppermute(edge, "seq", crossing)
    query_in = [swap(part, 2 * (k + 1)) for k, part in enumerate(query_parts[1:])]
    _, _, gain_at = chunk_layout(conv_rows, norm_rows, width, key_size, value_size)
    chunk = (round_up(gain_at + 2, 16), width)
    conv_parts = run(
        lambda *refs: conv_grad_kernel(
            *refs,
            conv_rows=conv_rows,
            conv_pad=conv_pad,
            norm_rows=norm_rows,
            norm_pad=norm_pad,
            key_size=key_size,
            value_size=value_size,
        ),
        [(chunk, F32 if k == 0 else BF) for k in range(groups)],
        [conv_pick] + norm_picks + blocks,
        [
            pltpu.VMEM((8 * tokens, width), BF),
            pltpu.VMEM((4 * tokens, width // 2), BF),
            pltpu.VMEM(chunk, F32),
        ],
        flops=2 * groups * conv_pad * 8 * tokens * width,
        name="conv_grad",
        after=[edge_in] + query_in,
    )
    conv_in = [swap(part, 2 * (k + 1)) for k, part in enumerate(conv_parts[1:])]
    (input_grad,) = run(
        input_kernel,
        [((positions, channels), BF)],
        [x, message, blocks[2], edge_in, conv_weight],
        [
            pltpu.VMEM((tokens + 16, width), F32),
            pltpu.VMEM((channels // LANES, positions, LANES), F32),
        ],
        flops=2 * positions * taps * channels * width,
        name="input_grad",
        after=[conv_parts[0]],
    )
    (query_grad,) = run(
        query_sum_kernel,
        [((norm_rows, heads * key_size), F32)],
        [query_parts[0]] + query_in,
        name="query_sum",
        after=[conv_parts[0]],
    )
    conv_grad, key_grad, value_grad, gain_grad = run(
        final_kernel,
        [
            ((conv_rows, width), F32),
            ((norm_rows, key_size), F32),
            ((norm_rows, value_size), F32),
            ((1, norm_rows), F32),
        ],
        [conv_parts[0]] + conv_in,
        [pltpu.VMEM(chunk, F32)],
        name="conv_sum",
    )
    return (
        attended[None],
        input_grad[None],
        conv_grad,
        query_grad,
        key_grad,
        value_grad,
        gain_grad.reshape(norm_rows),
    )


def solution(mesh):
    placed = (
        P(("groups", "dp"), "seq", None),
        P(),
        P(),
        P(),
        P(),
        P(),
        P(("groups", "dp"), "seq", None),
    )
    return jax.shard_map(
        on_device,
        mesh=mesh,
        in_specs=placed,
        out_specs=(
            P(("groups", "dp"), "seq", None),
            P(("groups", "dp"), "seq", None),
            P(("groups", "seq", "dp"), None),
            P(("groups", "seq", "dp"), None),
            P(("groups", "seq", "dp"), None),
            P(("groups", "seq", "dp"), None),
            P(("groups", "seq", "dp")),
        ),
        check_vma=False,
    )
```

```python
import math

import jax
import jax.numpy as jnp
from jax import lax
from jax.experimental import pallas as pl
from jax.experimental.pallas import tpu as pltpu
from jax.sharding import PartitionSpec as P

BF = jnp.bfloat16
F32 = jnp.float32
ROOT = math.sqrt(2.0 / math.pi)
EPS = 1e-06
LANES = 128
VMEM_BYTES = 40 * 2**20


def dot(a, b):
    return lax.dot_general(a, b, (((1,), (0,)), ((), ())), preferred_element_type=F32)


def dot_t(a, b):
    return lax.dot_general(a, b, (((1,), (1,)), ((), ())), preferred_element_type=F32)


def run(body, outs, args, scratch=(), flops=0, name=None, after=()):
    size = sum(math.prod(a.shape) * a.dtype.itemsize for a in args)
    size += sum(math.prod(s) * jnp.dtype(t).itemsize for s, t in outs)
    vmem = pl.BlockSpec(memory_space=pltpu.VMEM)
    rest = pl.BlockSpec(memory_space=pl.ANY)
    count, skip = len(args), len(args) + len(after)

    def whole(*refs):
        body(*refs[:count], *refs[skip:])

    return pl.pallas_call(
        whole,
        out_shape=[jax.ShapeDtypeStruct(s, t) for s, t in outs],
        in_specs=[vmem] * count + [rest] * len(after),
        out_specs=[vmem] * len(outs),
        scratch_shapes=list(scratch),
        compiler_params=pltpu.CompilerParams(vmem_limit_bytes=VMEM_BYTES),
        cost_estimate=pl.CostEstimate(flops=flops, bytes_accessed=size, transcendentals=0),
        name=name,
    )(*args, *after)


def gelu(v):
    return v * (0.5 * (1.0 + jnp.tanh(ROOT * (v + 0.044715 * (v * v * v)))))


def gelu_slope(v):
    tangent = jnp.tanh(ROOT * (v + 0.044715 * v * v * v))
    return 0.5 * (1.0 + tangent) + 0.5 * v * (1.0 - tangent * tangent) * ROOT * (
        1.0 + 3.0 * 0.044715 * v * v
    )


def round_up(value, step):
    return -(-value // step) * step


def pack_kv(keys, values):
    tokens, size = keys.shape
    rest = values[:, size:]
    half = tokens // 2
    tail = jnp.concatenate([rest[:half], rest[half:]], axis=1)
    return jnp.concatenate([keys, values[:, :size], tail], axis=0)


def unpack_values(packed, tokens, size):
    tail = packed[2 * tokens :]
    width = tail.shape[1] // 2
    rest = jnp.concatenate([tail[:, :width], tail[:, width:]], axis=0)
    return jnp.concatenate([packed[tokens : 2 * tokens], rest], axis=1)


def put(ref, start, rows):
    for c in range(ref.shape[0]):
        ref[c, start : start + rows.shape[0]] = rows[:, c * LANES : (c + 1) * LANES]


def every_second(ref, start, count):
    parts = [ref[c, pl.ds(start, count, stride=2)] for c in range(ref.shape[0])]
    return jnp.concatenate(parts, axis=1)


def prepare_kernel(x, pad):
    positions, channels = x.shape
    put(pad, 0, jnp.zeros((8, channels), F32))
    put(pad, 8, gelu(x[...].astype(F32)).astype(BF).astype(F32))
    put(pad, 8 + positions, jnp.zeros((pad.shape[1] - 8 - positions, channels), F32))


def front_kernel(ready, before, after, weight, gain, wk, wv, kv_out, early, normed_out, pooled_out, pad):
    channels = before.shape[1]
    tokens = pooled_out.shape[0]
    ext = early.shape[0] // 2
    pad[...] = ready[...]
    put(pad, 6, gelu(before[...].astype(F32)).astype(BF).astype(F32))
    put(pad, 8 + 2 * tokens, gelu(after[...].astype(F32)).astype(BF).astype(F32))
    pieces = [every_second(pad, 6 + u, tokens).astype(BF) for u in range(6)]
    total = None
    for tap in range(5):
        rows = jnp.concatenate([pieces[tap], pieces[tap + 1]], axis=0)
        term = dot(rows, weight[tap])
        total = term if total is None else total + term
    pooled = 0.5 * (total[:tokens] + total[tokens:])
    inv = lax.rsqrt(jnp.mean(pooled * pooled, axis=-1, keepdims=True) + EPS)
    normed = (pooled * inv * gain[...]).astype(BF)
    pooled_out[...] = pooled
    normed_out[...] = normed
    packed = pack_kv(dot(normed, wk[...]), dot_t(normed, wv[...])).astype(BF)
    for i in range(kv_out.shape[0]):
        kv_out[i] = packed
    early[0:ext] = every_second(pad, 6, ext).astype(BF)
    early[ext : 2 * ext] = every_second(pad, 7, ext).astype(BF)


def query_kernel(normed, wq, early, out, early_out, *picks, groups, rows, padded, scale):
    width = normed.shape[1]
    value = normed[...]
    out[...] = (dot(value, wq[...]) * scale).astype(BF)
    for i in range(4):
        block_of = place(i)
        pick = [chosen(rows, padded, width, block_of(k)) for k in range(groups)]
        picks[i][...] = dot_t(jnp.concatenate(pick, axis=0), value).astype(BF)
    early_out[...] = early[...]


def attend_pair(index, q, cot, ks, vs, kt, vt, dk, dv, att, dq, key_size, value_size, scale, first):
    tokens = q.shape[0]
    ql, cl = 2 * index * key_size, 2 * index * value_size
    qs = jnp.concatenate(
        [q[:, ql : ql + key_size], q[:, ql + key_size : ql + 2 * key_size]], axis=0
    )
    both = cot[:, cl : cl + 2 * value_size]
    cs = jnp.concatenate([both[:, :value_size], both[:, value_size:]], axis=0)
    scores = dot_t(ks[...], qs)
    raised = jnp.exp(scores - jnp.max(scores, axis=0, keepdims=True))
    probs = raised * (1.0 / jnp.sum(raised, axis=0, keepdims=True))
    weights = probs.astype(BF)
    out_t = dot(vt[...], weights).astype(BF).astype(F32)
    delta = jnp.sum(cs.astype(F32).T * out_t, axis=0, keepdims=True)
    prob_cot = dot_t(vs[...], cs)
    score_cot = (probs * (prob_cot - delta)).astype(BF)
    dq_t = dot(kt[...], score_cot) * scale
    dk_term = dot(score_cot, qs)
    dv_term = dot(weights, cs)
    if first:
        dk[...] = dk_term
        dv[...] = dv_term
    else:
        dk[...] += dk_term
        dv[...] += dv_term
    out_rows = jnp.concatenate([out_t[:, :tokens].T, out_t[:, tokens:].T], axis=1)
    att[:, cl : cl + 2 * value_size] = out_rows.astype(BF)
    dq_rows = jnp.concatenate([dq_t[:, :tokens].T, dq_t[:, tokens:].T], axis=1)
    dq[:, ql % dq.shape[1] : ql % dq.shape[1] + 2 * key_size] = dq_rows.astype(BF)


def attend_first_kernel(*refs, blocks, heads, key_size, value_size, scale):
    q, cot, parts, att, dq, ks, vs, kt, vt, dk, dv = refs
    tokens = q.shape[0]
    half = tokens // 2
    wide = value_size - key_size
    for i in range(blocks):
        part = parts[i]
        at = i * tokens
        ks[at : at + tokens] = part[:tokens]
        vs[at : at + tokens, :key_size] = part[tokens : 2 * tokens]
        vs[at : at + half, key_size:] = part[2 * tokens :, :wide]
        vs[at + half : at + tokens, key_size:] = part[2 * tokens :, wide:]
        kt[:, at : at + tokens] = ks[at : at + tokens].astype(F32).T.astype(BF)
        vt[:, at : at + tokens] = vs[at : at + tokens].astype(F32).T.astype(BF)
    for pair in range(heads // 4):
        attend_pair(
            pair, q, cot, ks, vs, kt, vt, dk, dv, att, dq, key_size, value_size, scale, pair == 0
        )


def attend_second_kernel(*refs, blocks, heads, key_size, value_size, scale):
    q, cot, att_in, ks, vs, kt, vt, dk_in, dv_in = refs[:9]
    att, dq, terms, dk, dv = refs[9:]
    tokens = q.shape[0]
    att[:, : att_in.shape[1]] = att_in[...]
    for pair in range(heads // 4, heads // 2):
        if pair == heads // 4:
            dk[...] = dk_in[...]
            dv[...] = dv_in[...]
        attend_pair(
            pair, q, cot, ks, vs, kt, vt, dk, dv, att, dq, key_size, value_size, scale, False
        )
    for i in range(blocks):
        at = slice(i * tokens, (i + 1) * tokens)
        terms[i] = pack_kv(dk[at], dv[at]).astype(BF)


def query_cot_kernel(left, right, wq, both, out):
    both[:, : left.shape[1]] = left[...]
    both[:, left.shape[1] :] = right[...]
    out[...] = dot_t(both[...], wq[...])


def middle_kernel(terms, part, pooled_in, gain_in, wk, wv, near, message, edge, near_out):
    near_out[...] = near[...]
    size = terms.shape[2]
    tokens, width = pooled_in.shape
    total = terms[0].astype(F32)
    for i in range(1, terms.shape[0]):
        total = total + terms[i].astype(F32)
    total = total.astype(BF).astype(F32)
    key_cot = total[:tokens]
    value_cot = unpack_values(total, tokens, size)
    normed_cot = part[...] + dot_t(key_cot.astype(BF), wk[...])
    normed_cot = normed_cot + dot(value_cot.astype(BF), wv[...])
    pooled, gain = pooled_in[...], gain_in[...]
    inv = lax.rsqrt(jnp.mean(pooled * pooled, axis=-1, keepdims=True) + EPS)
    gain_term = jnp.sum(normed_cot * pooled * inv, axis=0, keepdims=True)
    gained = gain * normed_cot
    pooled_cot = inv * gained - pooled * (inv * inv * inv) * (
        jnp.sum(gained * pooled, axis=-1, keepdims=True) / width
    )
    conv_cot = 0.5 * pooled_cot
    high = gain_term.astype(BF).astype(F32)
    low = gain_term - high
    row = lax.broadcasted_iota(jnp.int32, (16, width), 0)
    gains = jnp.where(row == 0, high, jnp.where(row == 1, low, 0.0))
    both = jnp.concatenate([key_cot, value_cot], axis=1)
    fill = width // 2 - both.shape[1]
    both = jnp.concatenate([both, jnp.zeros((tokens, fill), F32)], axis=1)
    side = jnp.concatenate([both[: tokens // 2], both[tokens // 2 :]], axis=1)
    message[:tokens] = conv_cot.astype(BF)
    message[tokens : tokens + 16] = gains.astype(BF)
    message[tokens + 16 :] = side.astype(BF)
    ends = jnp.where(row == 0, conv_cot[:1], jnp.where(row == 1, conv_cot[tokens - 1 :], 0.0))
    edge[...] = ends.astype(BF)


def place(other=0):
    seq, dp = lax.axis_index("seq"), lax.axis_index("dp") ^ (other % 2)
    high, low = seq // 2, (seq % 2) ^ (other // 2)
    return lambda k: ((high ^ k) * 2 + low) * 2 + dp


def chosen(rows, padded, columns, block):
    row = lax.broadcasted_iota(jnp.int32, (padded, columns), 0)
    column = lax.broadcasted_iota(jnp.int32, (padded, columns), 1)
    hit = (column == row + block * rows) & (row < rows)
    return jnp.where(hit, 1.0, 0.0).astype(BF)


def relay_kernel(value, out):
    out[...] = value[...]


def select_kernel(*refs, groups, rows, padded):
    blocks = refs[:4]
    out, even, odd = refs[4:]
    ext, channels = even.shape
    tokens = out.shape[1] // 8
    block_of = place()
    pick = jnp.concatenate(
        [chosen(rows, padded, 5 * channels, block_of(k)) for k in range(groups)], axis=0
    )
    for i, block in enumerate(blocks):
        even[...] = block[:ext].astype(F32)
        odd[...] = block[ext : 2 * ext].astype(F32)
        pieces = []
        for shift in range(3):
            pieces += [even[shift : shift + tokens].astype(BF), odd[shift : shift + tokens].astype(BF)]
        shifted = jnp.concatenate(
            [jnp.concatenate(pieces[:5], axis=1), jnp.concatenate(pieces[1:], axis=1)], axis=0
        )
        out[:, 2 * i * tokens : 2 * (i + 1) * tokens] = dot_t(pick, shifted).astype(BF)


def query_grad_kernel(*refs, pad):
    picks, blocks = refs[:4], refs[4:8]
    outs, right = refs[8:-1], refs[-1]
    tokens = blocks[0].shape[0]
    for i, block in enumerate(blocks):
        right[i * tokens : (i + 1) * tokens] = block[...]
    pick = jnp.concatenate([part[...] for part in picks], axis=1)
    for k, out in enumerate(outs):
        out[...] = dot(pick[k * pad : (k + 1) * pad], right[...]).astype(out.dtype)


def chunk_layout(conv_rows, norm_rows, width, key_size, value_size):
    key_rows = norm_rows * key_size // width
    value_rows = norm_rows * value_size // width
    return conv_rows, conv_rows + key_rows, conv_rows + key_rows + value_rows


def conv_grad_kernel(*refs, conv_rows, conv_pad, norm_rows, norm_pad, key_size, value_size):
    pick, picks, blocks = refs[0], refs[1:5], refs[5:9]
    outs, right, side, stage = refs[9:-3], refs[-3], refs[-2], refs[-1]
    norm_pick = jnp.concatenate([part[...] for part in picks], axis=1)
    width = right.shape[1]
    tokens = side.shape[0] // 4
    half = tokens // 2
    gain = None
    for i, block in enumerate(blocks):
        piece = block[:tokens]
        right[2 * i * tokens : (2 * i + 1) * tokens] = piece
        right[(2 * i + 1) * tokens : (2 * i + 2) * tokens] = piece
        side[i * tokens : i * tokens + half] = block[tokens + 16 :, : width // 2]
        side[i * tokens + half : (i + 1) * tokens] = block[tokens + 16 :, width // 2 :]
        two = block[tokens : tokens + 16].astype(F32)
        term = two[0:1] + two[1:2]
        gain = term if gain is None else gain + term
    high = gain.astype(BF).astype(F32)
    key_at, value_at, gain_at = chunk_layout(conv_rows, norm_rows, width, key_size, value_size)
    stage[...] = jnp.zeros(stage.shape, F32)
    stage[gain_at : gain_at + 1] = high
    stage[gain_at + 1 : gain_at + 2] = gain - high
    for k, out in enumerate(outs):
        conv = dot(pick[k * conv_pad : (k + 1) * conv_pad], right[...])
        stage[:conv_rows] = conv[:conv_rows]
        both = dot(norm_pick[k * norm_pad : (k + 1) * norm_pad], side[...])
        key, value = both[:, :key_size], both[:, key_size : key_size + value_size]
        for part, at, end in ((key, key_at, value_at), (value, value_at, gain_at)):
            count = end - at
            pieces = [part[i : i + count] for i in range(0, norm_rows, count)]
            stage[at:end] = jnp.concatenate(pieces, axis=1)
        out[...] = stage[...].astype(out.dtype)


def summed(parts):
    total = parts[0][...]
    for part in parts[1:]:
        total = total + part[...].astype(F32)
    return total


def final_kernel(*refs):
    conv, query, key, value, gain, stage = refs[-6:]
    count = len(refs[:-6]) // 2
    total = summed(refs[:count])
    query[...] = summed(refs[count : 2 * count])[: query.shape[0]]
    rows, width = conv.shape
    count = key.shape[0]
    stage[...] = total
    conv[...] = stage[:rows]
    key_at, value_at, gain_at = chunk_layout(
        rows, count, width, key.shape[1], value.shape[1]
    )
    for part, at, end in ((key, key_at, value_at), (value, value_at, gain_at)):
        size, step = part.shape[1], end - at
        packed = stage[at:end]
        for i in range(count // step):
            part[i * step : (i + 1) * step] = packed[:, i * size : (i + 1) * size]
    line = stage[gain_at : gain_at + 1] + stage[gain_at + 1 : gain_at + 2]
    line = jnp.broadcast_to(line, (8, width))
    start = place()(0) * count
    gain[...] = pltpu.roll(line, lax.rem(width - start, width), 1)[:1, :count]


def input_kernel(x, cc, pair_cc, edge, weight, out, ext, mixed):
    tokens = x.shape[0] // 2
    low = lax.axis_index("seq") % 2
    ext[8 : 8 + tokens] = cc[:tokens].astype(F32)
    pair_first = pair_cc[0:16].astype(F32)[0:1]
    pair_last = pair_cc[tokens - 16 : tokens].astype(F32)[15:16]
    ends = edge[...].astype(F32)
    ext[7:8] = jnp.where(low == 0, ends[1:2], pair_last)
    ext[8 + tokens : 9 + tokens] = jnp.where(low == 0, pair_first, ends[0:1])
    back = ext[7 : 7 + tokens].astype(BF)
    here = ext[8 : 8 + tokens].astype(BF)
    ahead = ext[9 : 9 + tokens].astype(BF)
    evens = (ahead, here, here, back, back)
    odds = (ahead, ahead, here, here, back)
    total = None
    for tap in range(5):
        term = dot_t(jnp.concatenate([evens[tap], odds[tap]], axis=0), weight[tap])
        total = term if total is None else total + term
    for c in range(mixed.shape[0]):
        lanes = slice(c * LANES, (c + 1) * LANES)
        mixed[c, pl.ds(0, tokens, stride=2)] = total[:tokens, lanes]
        mixed[c, pl.ds(1, tokens, stride=2)] = total[tokens:, lanes]
        out[:, lanes] = (mixed[c] * gelu_slope(x[:, lanes].astype(F32))).astype(BF)


def on_device(x, conv_weight, norm_gain, wq, wk, wv, cotangent):
    devices = lax.axis_size("seq")
    both_axes = ("seq", "dp")
    x, cotangent = x[0], cotangent[0]
    positions, channels = x.shape
    tokens = positions // 2
    taps, _, width = conv_weight.shape
    key_size, value_size = wk.shape[1], wv.shape[1]
    heads = cotangent.shape[1] // value_size
    scale = key_size ** (-0.5)
    groups = devices // 2
    owners = devices * 2
    conv_rows, norm_rows = taps * channels // owners, width // owners
    conv_pad, norm_pad = round_up(conv_rows, 16), round_up(norm_rows, 16)
    ext = tokens + 16
    gain = norm_gain.reshape(1, width)

    def swap(value, seq_bits, dp_bit=0):
        mask = 2 * seq_bits + dp_bit
        return lax.ppermute(value, both_axes, [(i, i ^ mask) for i in range(owners)])

    def quad(value):
        core = swap(value, 0, 1)
        near = swap(value, 1)
        return [value, core, near, swap(near, 0, 1)]

    up = [(i, i + 1) for i in range(devices - 1)]
    down = [(j, i) for i, j in up]
    before = lax.ppermute(x[positions - 2 :], "seq", up)
    after = lax.ppermute(x[:2], "seq", down)
    pad_shape = (channels // LANES, 8 + 2 * ext + 8, LANES)
    wv = wv.T
    (ready,) = run(prepare_kernel, [(pad_shape, F32)], [x], flops=4 * 10**9, name="gelu")
    kv, early, normed, pooled = run(
        front_kernel,
        [
            ((devices, 5 * tokens // 2, key_size), BF),
            ((2 * ext, channels), BF),
            ((tokens, width), BF),
            ((tokens, width), F32),
        ],
        [ready, before, after, conv_weight, gain, wk, wv],
        [pltpu.VMEM(pad_shape, F32)],
        flops=2 * positions * taps * channels * width,
        name="front",
    )
    kv = lax.all_to_all(kv, "seq", 0, 0, tiled=True)
    queries, early, *picks = run(
        lambda *refs: query_kernel(
            *refs, groups=groups, rows=norm_rows, padded=norm_pad, scale=scale
        ),
        [
            ((tokens, heads * key_size), BF),
            (early.shape, BF),
        ]
        + [((groups * norm_pad, tokens), BF)] * 4,
        [normed, wq, early],
        flops=4 * tokens * width * heads * key_size,
        name="queries",
    )
    length = devices * tokens
    sizes = dict(
        blocks=devices, heads=heads, key_size=key_size, value_size=value_size, scale=scale
    )
    attend_flops = 3 * tokens * heads * length * (key_size + value_size)
    half_att = heads // 2 * value_size
    half_query = heads // 2 * key_size
    totals = [((length, key_size), F32), ((length, value_size), F32)]
    att_first, dq_first, *held = run(
        lambda *refs: attend_first_kernel(*refs, **sizes),
        [
            ((tokens, half_att), BF),
            ((tokens, half_query), BF),
            ((length, key_size), BF),
            ((length, value_size), BF),
            ((key_size, length), BF),
            ((value_size, length), BF),
        ]
        + totals,
        [queries, cotangent, kv],
        flops=attend_flops,
        name="attend_first",
    )
    early_near, early_core = swap(early, 1), swap(early, 0, 1)
    norm_picks = [picks[0], swap(picks[1], 0, 1), swap(picks[2], 1), swap(picks[3], 1, 1)]
    attended, dq_second, terms = run(
        lambda *refs: attend_second_kernel(*refs, **sizes),
        [
            ((tokens, heads * value_size), BF),
            ((tokens, half_query), BF),
            (kv.shape, BF),
        ],
        [queries, cotangent, att_first] + held,
        [pltpu.VMEM(s, t) for s, t in totals],
        flops=attend_flops,
        name="attend_second",
        after=[early_near, early_core] + norm_picks[1:],
    )
    early_blocks = [early, early_core, early_near, swap(early_near, 0, 1)]
    (conv_pick,) = run(
        lambda *refs: select_kernel(*refs, groups=groups, rows=conv_rows, padded=conv_pad),
        [((groups * conv_pad, 8 * tokens), BF)],
        early_blocks,
        [pltpu.VMEM((ext, channels), F32), pltpu.VMEM((ext, channels), F32)],
        flops=2 * groups * conv_pad * taps * channels * 8 * tokens,
        name="select",
    )
    query_cot, normed_cot = run(
        query_cot_kernel,
        [((tokens, heads * key_size), BF), ((tokens, width), F32)],
        [dq_first, dq_second, wq],
        flops=2 * tokens * width * heads * key_size,
        name="query_part",
    )
    terms = lax.all_to_all(terms, "seq", 0, 0, tiled=True)
    query_near = swap(query_cot, 1)
    message, edge, query_relay = run(
        middle_kernel,
        [
            ((tokens + 16 + tokens // 2, width), BF),
            ((16, width), BF),
            (query_near.shape, BF),
        ],
        [terms, normed_cot, pooled, gain, wk, wv, query_near],
        flops=2 * tokens * width * (key_size + value_size),
        name="conv_cot",
    )
    query_blocks = [query_cot, swap(query_cot, 0, 1), query_near, swap(query_relay, 0, 1)]
    query_parts = run(
        lambda *refs: query_grad_kernel(*refs, pad=norm_pad),
        [((norm_pad, heads * key_size), F32 if k == 0 else BF) for k in range(groups)],
        norm_picks + query_blocks,
        [pltpu.VMEM((4 * tokens, heads * key_size), BF)],
        flops=2 * groups * norm_pad * 4 * tokens * heads * key_size,
        name="query_grad",
    )
    query_in = [swap(part, 2 * (k + 1)) for k, part in enumerate(query_parts[1:])]
    near_message = swap(message, 1)
    (relay,) = run(
        relay_kernel,
        [(message.shape, BF)],
        [near_message],
        name="relay",
        after=[query_in[1], conv_pick],
    )
    blocks = [message, swap(message, 0, 1), near_message, swap(relay, 0, 1)]
    crossing = [(i, i + 1) for i in range(1, devices - 1, 2)]
    crossing = crossing + [(j, i) for i, j in crossing]
    edge_in = lax.ppermute(edge, "seq", crossing)
    _, _, gain_at = chunk_layout(conv_rows, norm_rows, width, key_size, value_size)
    chunk = (round_up(gain_at + 2, 16), width)
    conv_parts = run(
        lambda *refs: conv_grad_kernel(
            *refs,
            conv_rows=conv_rows,
            conv_pad=conv_pad,
            norm_rows=norm_rows,
            norm_pad=norm_pad,
            key_size=key_size,
            value_size=value_size,
        ),
        [(chunk, F32 if k == 0 else BF) for k in range(groups)],
        [conv_pick] + norm_picks + blocks,
        [
            pltpu.VMEM((8 * tokens, width), BF),
            pltpu.VMEM((4 * tokens, width // 2), BF),
            pltpu.VMEM(chunk, F32),
        ],
        flops=2 * groups * conv_pad * 8 * tokens * width,
        name="conv_grad",
        after=[edge_in, query_in[0]],
    )
    conv_in = [swap(part, 2 * (k + 1)) for k, part in enumerate(conv_parts[1:])]
    (input_grad,) = run(
        input_kernel,
        [((positions, channels), BF)],
        [x, message, blocks[2], edge_in, conv_weight],
        [
            pltpu.VMEM((tokens + 16, width), F32),
            pltpu.VMEM((channels // LANES, positions, LANES), F32),
        ],
        flops=2 * positions * taps * channels * width,
        name="input_grad",
        after=[conv_parts[0]],
    )
    conv_grad, query_grad, key_grad, value_grad, gain_grad = run(
        final_kernel,
        [
            ((conv_rows, width), F32),
            ((norm_rows, heads * key_size), F32),
            ((norm_rows, key_size), F32),
            ((norm_rows, value_size), F32),
            ((1, norm_rows), F32),
        ],
        [conv_parts[0]] + conv_in + [query_parts[0]] + query_in,
        [pltpu.VMEM(chunk, F32)],
        name="final_sum",
    )
    return (
        attended[None],
        input_grad[None],
        conv_grad,
        query_grad,
        key_grad,
        value_grad,
        gain_grad.reshape(norm_rows),
    )


def solution(mesh):
    placed = (
        P(("groups", "dp"), "seq", None),
        P(),
        P(),
        P(),
        P(),
        P(),
        P(("groups", "dp"), "seq", None),
    )
    return jax.shard_map(
        on_device,
        mesh=mesh,
        in_specs=placed,
        out_specs=(
            P(("groups", "dp"), "seq", None),
            P(("groups", "dp"), "seq", None),
            P(("groups", "seq", "dp"), None),
            P(("groups", "seq", "dp"), None),
            P(("groups", "seq", "dp"), None),
            P(("groups", "seq", "dp"), None),
            P(("groups", "seq", "dp")),
        ),
        check_vma=False,
    )
```

```python
import math

import jax
import jax.numpy as jnp
from jax import lax
from jax.experimental import pallas as pl
from jax.experimental.pallas import tpu as pltpu
from jax.sharding import PartitionSpec as P

BF = jnp.bfloat16
F32 = jnp.float32
ROOT = math.sqrt(2.0 / math.pi)
EPS = 1e-06
LANES = 128
VMEM_BYTES = 40 * 2**20


def dot(a, b):
    return lax.dot_general(a, b, (((1,), (0,)), ((), ())), preferred_element_type=F32)


def dot_t(a, b):
    return lax.dot_general(a, b, (((1,), (1,)), ((), ())), preferred_element_type=F32)


def run(body, outs, args, scratch=(), flops=0, name=None, after=()):
    size = sum(math.prod(a.shape) * a.dtype.itemsize for a in args)
    size += sum(math.prod(s) * jnp.dtype(t).itemsize for s, t in outs)
    vmem = pl.BlockSpec(memory_space=pltpu.VMEM)
    rest = pl.BlockSpec(memory_space=pl.ANY)
    count, skip = len(args), len(args) + len(after)

    def whole(*refs):
        body(*refs[:count], *refs[skip:])

    return pl.pallas_call(
        whole,
        out_shape=[jax.ShapeDtypeStruct(s, t) for s, t in outs],
        in_specs=[vmem] * count + [rest] * len(after),
        out_specs=[vmem] * len(outs),
        scratch_shapes=list(scratch),
        compiler_params=pltpu.CompilerParams(vmem_limit_bytes=VMEM_BYTES),
        cost_estimate=pl.CostEstimate(flops=flops, bytes_accessed=size, transcendentals=0),
        name=name,
    )(*args, *after)


def gelu(v):
    return v * (0.5 * (1.0 + jnp.tanh(ROOT * (v + 0.044715 * (v * v * v)))))


def gelu_slope(v):
    tangent = jnp.tanh(ROOT * (v + 0.044715 * v * v * v))
    return 0.5 * (1.0 + tangent) + 0.5 * v * (1.0 - tangent * tangent) * ROOT * (
        1.0 + 3.0 * 0.044715 * v * v
    )


def round_up(value, step):
    return -(-value // step) * step


def pack_kv(keys, values):
    tokens, size = keys.shape
    rest = values[:, size:]
    half = tokens // 2
    tail = jnp.concatenate([rest[:half], rest[half:]], axis=1)
    return jnp.concatenate([keys, values[:, :size], tail], axis=0)


def unpack_values(packed, tokens, size):
    tail = packed[2 * tokens :]
    width = tail.shape[1] // 2
    rest = jnp.concatenate([tail[:, :width], tail[:, width:]], axis=0)
    return jnp.concatenate([packed[tokens : 2 * tokens], rest], axis=1)


def put(ref, start, rows):
    for c in range(ref.shape[0]):
        ref[c, start : start + rows.shape[0]] = rows[:, c * LANES : (c + 1) * LANES]


def every_second(ref, start, count):
    parts = [ref[c, pl.ds(start, count, stride=2)] for c in range(ref.shape[0])]
    return jnp.concatenate(parts, axis=1)


def open_kernel(x, pad, first, last):
    positions, channels = x.shape
    first[...] = x[:16][:2]
    last[...] = x[positions - 16 :][14:]
    put(pad, 0, jnp.zeros((8, channels), F32))
    put(pad, 8, gelu(x[...].astype(F32)).astype(BF).astype(F32))
    put(pad, 8 + positions, jnp.zeros((pad.shape[1] - 8 - positions, channels), F32))


def front_kernel(ready, before, after, weight, gain, wk, wv, kv_out, early, normed_out, pooled_out, pad):
    channels = before.shape[1]
    tokens = pooled_out.shape[0]
    ext = early.shape[0] // 2
    pad[...] = ready[...]
    put(pad, 6, gelu(before[...].astype(F32)).astype(BF).astype(F32))
    put(pad, 8 + 2 * tokens, gelu(after[...].astype(F32)).astype(BF).astype(F32))
    pieces = [every_second(pad, 6 + u, tokens).astype(BF) for u in range(6)]
    total = None
    for tap in range(5):
        rows = jnp.concatenate([pieces[tap], pieces[tap + 1]], axis=0)
        term = dot(rows, weight[tap])
        total = term if total is None else total + term
    pooled = 0.5 * (total[:tokens] + total[tokens:])
    inv = lax.rsqrt(jnp.mean(pooled * pooled, axis=-1, keepdims=True) + EPS)
    normed = (pooled * inv * gain[...]).astype(BF)
    pooled_out[...] = pooled
    normed_out[...] = normed
    kv_out[...] = pack_kv(dot(normed, wk[...]), dot_t(normed, wv[...])).astype(BF)
    early[0:ext] = every_second(pad, 6, ext).astype(BF)
    early[ext : 2 * ext] = every_second(pad, 7, ext).astype(BF)


def ordered(bits):
    masks = [0]
    for bit in reversed(bits):
        masks = masks + [mask | (1 << bit) for mask in masks]
    return masks


def split_rows(rows, columns):
    return round_up(-(-rows * LANES // columns), 16)


def query_kernel(normed, wq, early, out, message, own, *, order, rows, padded, scale):
    width = normed.shape[1]
    value = normed[...]
    out[...] = (dot(value, wq[...]) * scale).astype(BF)
    at, channels = early.shape
    message[:at] = early[...]
    count = len(order) * padded
    step = split_rows(count, channels)
    for i in range(4):
        block_of = place(i)
        pick = [chosen(rows, padded, width, block_of(k)) for k in order]
        part = dot_t(jnp.concatenate(pick, axis=0), value).astype(BF)
        if i == 0:
            own[...] = part
            continue
        for c in range(channels // LANES):
            piece = part[c * step : min((c + 1) * step, count)]
            message[at : at + piece.shape[0], c * LANES : (c + 1) * LANES] = piece
        at += step


def attend_kernel(*refs, blocks, masks, heads, key_size, value_size, scale):
    q, cot = refs[:2]
    parts = refs[2 : 2 + blocks]
    att, dq, keep_a, send_a, keep_b, send_b = refs[2 + blocks : 8 + blocks]
    ks, vs, kt, vt, qs, cs, weights, score_cots = refs[8 + blocks :]
    tokens = q.shape[0]
    half = tokens // 2
    wide = value_size - key_size
    for i, part in enumerate(parts):
        at = i * tokens
        ks[at : at + tokens] = part[:tokens]
        vs[at : at + tokens, :key_size] = part[tokens : 2 * tokens]
        vs[at : at + half, key_size:] = part[2 * tokens :, :wide]
        vs[at + half : at + tokens, key_size:] = part[2 * tokens :, wide:]
        kt[:, at : at + tokens] = ks[at : at + tokens].astype(F32).T.astype(BF)
        vt[:, at : at + tokens] = vs[at : at + tokens].astype(F32).T.astype(BF)
    for pair in range(heads // 2):
        ql, cl = 2 * pair * key_size, 2 * pair * value_size
        rows = slice(2 * pair * tokens, 2 * (pair + 1) * tokens)
        both = cot[:, cl : cl + 2 * value_size]
        qs[rows] = jnp.concatenate(
            [q[:, ql : ql + key_size], q[:, ql + key_size : ql + 2 * key_size]], axis=0
        )
        cs[rows] = jnp.concatenate([both[:, :value_size], both[:, value_size:]], axis=0)
        scores = dot_t(ks[...], qs[rows])
        raised = jnp.exp(scores - jnp.max(scores, axis=0, keepdims=True))
        probs = raised * (1.0 / jnp.sum(raised, axis=0, keepdims=True))
        weights[:, rows] = probs.astype(BF)
        out_t = dot(vt[...], weights[:, rows]).astype(BF).astype(F32)
        delta = jnp.sum(cs[rows].astype(F32).T * out_t, axis=0, keepdims=True)
        score_cots[:, rows] = (probs * (dot_t(vs[...], cs[rows]) - delta)).astype(BF)
        dq_t = dot(kt[...], score_cots[:, rows]) * scale
        out_rows = jnp.concatenate([out_t[:, :tokens].T, out_t[:, tokens:].T], axis=1)
        att[:, cl : cl + 2 * value_size] = out_rows.astype(BF)
        dq_rows = jnp.concatenate([dq_t[:, :tokens].T, dq_t[:, tokens:].T], axis=1)
        dq[:, ql : ql + 2 * key_size] = dq_rows.astype(BF)
    edge = keep_a.shape[1]
    count = blocks // 2
    for i in range(blocks):
        at = slice(i * tokens, (i + 1) * tokens)
        packed = pack_kv(dot(score_cots[at], qs[...]), dot(weights[at], cs[...]))
        for order, keep, send, part in (
            (masks[0], keep_a, send_a, packed[:edge]),
            (masks[1], keep_b, send_b, packed[edge:]),
        ):
            k = order.index(i)
            if k < count:
                keep[k] = part
            else:
                send[k - count] = part.astype(BF)


def total_of(parts):
    total = parts[0][...]
    for part in parts[1:]:
        total = total + part[...].astype(F32)
    return total


def fold_kernel(*refs):
    keep, send = refs[-2:]
    total = total_of(refs[:-2])
    keep[...] = total[: keep.shape[0]]
    send[...] = total[keep.shape[0] :].astype(BF)


def fold_two_kernel(*refs):
    fold_kernel(refs[0], refs[1], refs[4], refs[5])
    fold_kernel(refs[2], refs[3], refs[6], refs[7])


def merge_kernel(keep_a, in_a, keep_b, in_b, keep, send):
    total = jnp.concatenate([total_of((keep_a, in_a)), total_of((keep_b, in_b))], axis=1)
    keep[...] = total[: keep.shape[0]]
    send[...] = total[keep.shape[0] :].astype(BF)


def send_on_kernel(keep, came, out):
    out[...] = (keep[...] + came[...].astype(F32)).astype(BF)


def query_cot_kernel(dq, wq, out):
    out[...] = dot_t(dq[...], wq[...])


def middle_kernel(own, came, part, pooled_in, gain_in, wk, wv, message, edge):
    size = own.shape[2]
    tokens, width = pooled_in.shape
    total = (own[0] + came[0].astype(F32)).astype(BF).astype(F32)
    key_cot = total[:tokens]
    value_cot = unpack_values(total, tokens, size)
    normed_cot = part[...] + dot_t(key_cot.astype(BF), wk[...])
    normed_cot = normed_cot + dot(value_cot.astype(BF), wv[...])
    pooled, gain = pooled_in[...], gain_in[...]
    inv = lax.rsqrt(jnp.mean(pooled * pooled, axis=-1, keepdims=True) + EPS)
    gain_term = jnp.sum(normed_cot * pooled * inv, axis=0, keepdims=True)
    gained = gain * normed_cot
    pooled_cot = inv * gained - pooled * (inv * inv * inv) * (
        jnp.sum(gained * pooled, axis=-1, keepdims=True) / width
    )
    conv_cot = 0.5 * pooled_cot
    high = gain_term.astype(BF).astype(F32)
    low = gain_term - high
    row = lax.broadcasted_iota(jnp.int32, (16, width), 0)
    gains = jnp.where(row == 0, high, jnp.where(row == 1, low, 0.0))
    both = jnp.concatenate([key_cot, value_cot], axis=1)
    fill = width // 2 - both.shape[1]
    both = jnp.concatenate([both, jnp.zeros((tokens, fill), F32)], axis=1)
    side = jnp.concatenate([both[: tokens // 2], both[tokens // 2 :]], axis=1)
    message[:tokens] = conv_cot.astype(BF)
    message[tokens : tokens + 16] = gains.astype(BF)
    message[tokens + 16 :] = side.astype(BF)
    ends = jnp.where(row == 0, conv_cot[:1], jnp.where(row == 1, conv_cot[tokens - 1 :], 0.0))
    edge[...] = ends.astype(BF)


def place(other=0):
    seq, dp = lax.axis_index("seq"), lax.axis_index("dp") ^ (other % 2)
    high, low = seq // 2, (seq % 2) ^ (other // 2)
    return lambda k: ((high ^ k) * 2 + low) * 2 + dp


def chosen(rows, padded, columns, block):
    row = lax.broadcasted_iota(jnp.int32, (padded, columns), 0)
    column = lax.broadcasted_iota(jnp.int32, (padded, columns), 1)
    hit = (column == row + block * rows) & (row < rows)
    return jnp.where(hit, 1.0, 0.0).astype(BF)


def relay_kernel(value, keep_in, came, out, keep, send):
    out[...] = value[...]
    fold_kernel(keep_in, came, keep, send)


def select_kernel(*refs, order, rows, padded):
    own, blocks = refs[0], refs[1:5]
    out, norm_out, even, odd = refs[5:]
    ext, channels = even.shape
    tokens = own.shape[1]
    count = own.shape[0]
    step = split_rows(count, channels)
    norm_out[:, :tokens] = own[...]
    for i in range(1, 4):
        at = 2 * ext + (i - 1) * step
        for c in range(channels // LANES):
            end = min((c + 1) * step, count)
            piece = blocks[i][at : at + end - c * step, c * LANES : (c + 1) * LANES]
            norm_out[c * step : end, i * tokens : (i + 1) * tokens] = piece
    block_of = place()
    pick = jnp.concatenate(
        [chosen(rows, padded, 5 * channels, block_of(k)) for k in order], axis=0
    )
    for i, block in enumerate(blocks):
        even[...] = block[:ext].astype(F32)
        odd[...] = block[ext : 2 * ext].astype(F32)
        pieces = []
        for shift in range(3):
            pieces += [even[shift : shift + tokens].astype(BF), odd[shift : shift + tokens].astype(BF)]
        shifted = jnp.concatenate(
            [jnp.concatenate(pieces[:5], axis=1), jnp.concatenate(pieces[1:], axis=1)], axis=0
        )
        out[:, 2 * i * tokens : 2 * (i + 1) * tokens] = dot_t(pick, shifted).astype(BF)


def query_grad_kernel(pick, first, second, third, fourth, keep, send, right):
    tokens = first.shape[0]
    for i, block in enumerate((first, second, third, fourth)):
        right[i * tokens : (i + 1) * tokens] = block[...]
    count, pad = keep.shape[:2]
    for k in range(2 * count):
        term = dot(pick[k * pad : (k + 1) * pad], right[...])
        if k < count:
            keep[k] = term
        else:
            send[k - count] = term.astype(BF)


def chunk_layout(conv_rows, norm_rows, width, key_size, value_size):
    key_rows = norm_rows * key_size // width
    value_rows = norm_rows * value_size // width
    return conv_rows, conv_rows + key_rows, conv_rows + key_rows + value_rows


def conv_grad_kernel(*refs, conv_rows, conv_pad, norm_rows, norm_pad, key_size, value_size):
    pick, norm_pick, blocks = refs[0], refs[1], refs[2:6]
    outs, right, side, stage = refs[6:-3], refs[-3], refs[-2], refs[-1]
    width = right.shape[1]
    tokens = side.shape[0] // 4
    half = tokens // 2
    gain = None
    for i, block in enumerate(blocks):
        piece = block[:tokens]
        right[2 * i * tokens : (2 * i + 1) * tokens] = piece
        right[(2 * i + 1) * tokens : (2 * i + 2) * tokens] = piece
        side[i * tokens : i * tokens + half] = block[tokens + 16 :, : width // 2]
        side[i * tokens + half : (i + 1) * tokens] = block[tokens + 16 :, width // 2 :]
        two = block[tokens : tokens + 16].astype(F32)
        term = two[0:1] + two[1:2]
        gain = term if gain is None else gain + term
    high = gain.astype(BF).astype(F32)
    key_at, value_at, gain_at = chunk_layout(conv_rows, norm_rows, width, key_size, value_size)
    stage[...] = jnp.zeros(stage.shape, F32)
    stage[gain_at : gain_at + 1] = high
    stage[gain_at + 1 : gain_at + 2] = gain - high
    count = outs[0].shape[0]
    for k in range(4 * count):
        out = outs[k // count]
        conv = dot(pick[k * conv_pad : (k + 1) * conv_pad], right[...])
        stage[:conv_rows] = conv[:conv_rows]
        both = dot(norm_pick[k * norm_pad : (k + 1) * norm_pad], side[...])
        key, value = both[:, :key_size], both[:, key_size : key_size + value_size]
        for part, at, end in ((key, key_at, value_at), (value, value_at, gain_at)):
            step = end - at
            pieces = [part[i : i + step] for i in range(0, norm_rows, step)]
            stage[at:end] = jnp.concatenate(pieces, axis=1)
        out[k % count] = stage[...].astype(out.dtype)


def final_kernel(*refs, conv_parts):
    conv, query, key, value, gain, stage = refs[-6:]
    total = total_of(refs[:conv_parts])[0]
    query[...] = total_of(refs[conv_parts:-6])[0, : query.shape[0]]
    rows, width = conv.shape
    count = key.shape[0]
    stage[...] = total
    conv[...] = stage[:rows]
    key_at, value_at, gain_at = chunk_layout(
        rows, count, width, key.shape[1], value.shape[1]
    )
    for part, at, end in ((key, key_at, value_at), (value, value_at, gain_at)):
        size, step = part.shape[1], end - at
        packed = stage[at:end]
        for i in range(count // step):
            part[i * step : (i + 1) * step] = packed[:, i * size : (i + 1) * size]
    line = stage[gain_at : gain_at + 1] + stage[gain_at + 1 : gain_at + 2]
    line = jnp.broadcast_to(line, (8, width))
    start = place()(0) * count
    gain[...] = pltpu.roll(line, lax.rem(width - start, width), 1)[:1, :count]


def input_kernel(x, cc, pair_cc, edge, weight, out, ext, mixed):
    tokens = x.shape[0] // 2
    low = lax.axis_index("seq") % 2
    ext[8 : 8 + tokens] = cc[:tokens].astype(F32)
    pair_first = pair_cc[0:16].astype(F32)[0:1]
    pair_last = pair_cc[tokens - 16 : tokens].astype(F32)[15:16]
    ends = edge[...].astype(F32)
    ext[7:8] = jnp.where(low == 0, ends[1:2], pair_last)
    ext[8 + tokens : 9 + tokens] = jnp.where(low == 0, pair_first, ends[0:1])
    back = ext[7 : 7 + tokens].astype(BF)
    here = ext[8 : 8 + tokens].astype(BF)
    ahead = ext[9 : 9 + tokens].astype(BF)
    evens = (ahead, here, here, back, back)
    odds = (ahead, ahead, here, here, back)
    total = None
    for tap in range(5):
        term = dot_t(jnp.concatenate([evens[tap], odds[tap]], axis=0), weight[tap])
        total = term if total is None else total + term
    for c in range(mixed.shape[0]):
        lanes = slice(c * LANES, (c + 1) * LANES)
        mixed[c, pl.ds(0, tokens, stride=2)] = total[:tokens, lanes]
        mixed[c, pl.ds(1, tokens, stride=2)] = total[tokens:, lanes]
        out[:, lanes] = (mixed[c] * gelu_slope(x[:, lanes].astype(F32))).astype(BF)


def on_device(x, conv_weight, norm_gain, wq, wk, wv, cotangent):
    devices = lax.axis_size("seq")
    both_axes = ("seq", "dp")
    x, cotangent = x[0], cotangent[0]
    positions, channels = x.shape
    tokens = positions // 2
    taps, _, width = conv_weight.shape
    key_size, value_size = wk.shape[1], wv.shape[1]
    heads = cotangent.shape[1] // value_size
    scale = key_size ** (-0.5)
    groups = devices // 2
    owners = devices * 2
    conv_rows, norm_rows = taps * channels // owners, width // owners
    conv_pad, norm_pad = round_up(conv_rows, 16), round_up(norm_rows, 16)
    ext = tokens + 16
    gain = norm_gain.reshape(1, width)

    def swap(value, seq_bits, dp_bit=0):
        mask = 2 * seq_bits + dp_bit
        return lax.ppermute(value, both_axes, [(i, i ^ mask) for i in range(owners)])

    def held(value, *until):
        return lax.optimization_barrier((value,) + until)[0]

    def quad(value, *until):
        core = swap(value, 0, 1)
        near = swap(value, 1)
        return [value, core, near, swap(held(near, *until), 0, 1)]

    def fold(parts, name):
        shape = (parts[0].shape[0] // 2,) + parts[0].shape[1:]
        return run(fold_kernel, [(shape, F32), (shape, BF)], parts, name=name)

    def halved(keep, send, bits, name):
        for bit in bits[:-1]:
            keep, send = fold([keep, swap(send, 1 << bit)], name)
        return [keep, swap(send, 1 << bits[-1])]

    bits = list(range(devices.bit_length() - 1))
    order = [mask // 2 for mask in ordered(bits[1:])]
    up = [(i, i + 1) for i in range(devices - 1)]
    down = [(j, i) for i, j in up]
    pad_shape = (channels // LANES, 8 + 2 * ext + 8, LANES)
    ready, first, last = run(
        open_kernel,
        [(pad_shape, F32), ((2, channels), BF), ((2, channels), BF)],
        [x],
        flops=4 * 10**9,
        name="gelu",
    )
    before = lax.ppermute(last, "seq", up)
    after = lax.ppermute(first, "seq", down)
    wv = wv.T
    kv, early, normed, pooled = run(
        front_kernel,
        [
            ((5 * tokens // 2, key_size), BF),
            ((2 * ext, channels), BF),
            ((tokens, width), BF),
            ((tokens, width), F32),
        ],
        [ready, before, after, conv_weight, gain, wk, wv],
        [pltpu.VMEM(pad_shape, F32)],
        flops=2 * positions * taps * channels * width,
        name="front",
    )
    near_kv = [kv] + [swap(kv, 2 * k) for k in range(1, groups)]
    far_kv = [swap(block, 1) for block in near_kv]
    picked = (groups * norm_pad, tokens)
    rows = 2 * ext + 3 * split_rows(picked[0], channels)
    queries, early, pick_own = run(
        lambda *refs: query_kernel(
            *refs, order=order, rows=norm_rows, padded=norm_pad, scale=scale
        ),
        [((tokens, heads * key_size), BF), ((rows, channels), BF), (picked, BF)],
        [normed, wq, early],
        flops=4 * tokens * width * heads * key_size,
        name="queries",
        after=near_kv[1:],
    )
    early = held(early, *far_kv)
    length = devices * tokens
    masks = [2 * k for k in range(groups)] + [2 * k + 1 for k in range(groups)]
    half_block = (groups, 5 * tokens // 4, key_size)
    attended, query_cot, keep_a, send_a, keep_b, send_b = run(
        lambda *refs: attend_kernel(
            *refs,
            blocks=devices,
            masks=[
                [masks.index(m) for m in ordered(way)] for way in (bits, [1, 0] + bits[2:])
            ],
            heads=heads,
            key_size=key_size,
            value_size=value_size,
            scale=scale,
        ),
        [((tokens, heads * value_size), BF), ((tokens, heads * key_size), BF)]
        + [(half_block, F32), (half_block, BF)] * 2,
        [queries, cotangent] + near_kv + far_kv,
        [
            pltpu.VMEM((length, key_size), BF),
            pltpu.VMEM((length, value_size), BF),
            pltpu.VMEM((key_size, length), BF),
            pltpu.VMEM((value_size, length), BF),
            pltpu.VMEM((heads * tokens, key_size), BF),
            pltpu.VMEM((heads * tokens, value_size), BF),
            pltpu.VMEM((length, heads * tokens), BF),
            pltpu.VMEM((length, heads * tokens), BF),
        ],
        flops=6 * tokens * heads * length * (key_size + value_size),
        name="attend",
    )
    early_blocks = quad(early, send_a)
    in_a, in_b = swap(send_a, 1), swap(send_b, 2)
    conv_pick, norm_pick = run(
        lambda *refs: select_kernel(*refs, order=order, rows=conv_rows, padded=conv_pad),
        [((groups * conv_pad, 8 * tokens), BF), ((groups * norm_pad, 4 * tokens), BF)],
        [pick_own] + early_blocks,
        [pltpu.VMEM((ext, channels), F32), pltpu.VMEM((ext, channels), F32)],
        flops=2 * groups * conv_pad * taps * channels * 8 * tokens,
        name="select",
    )
    fourth = (groups // 2,) + half_block[1:]
    keep_a, send_a, keep_b, send_b = run(
        fold_two_kernel,
        [(fourth, F32), (fourth, BF)] * 2,
        [keep_a, in_a, keep_b, in_b],
        name="kv_cot_fold",
        after=[conv_pick],
    )
    in_a, in_b = swap(send_a, 2), swap(send_b, 1)
    block = (groups // 4, 5 * tokens // 2, key_size)
    keep, send = run(
        merge_kernel,
        [(block, F32), (block, BF)],
        [keep_a, in_a, keep_b, in_b],
        name="kv_cot_merge",
    )
    query_cot = held(query_cot, keep)
    query_near, query_core = swap(query_cot, 1), swap(query_cot, 0, 1)
    pooled = held(pooled, query_near, query_core)
    kv_cot = halved(keep, send, bits[2:], "kv_cot_fold")
    (normed_cot,) = run(
        query_cot_kernel,
        [((tokens, width), F32)],
        [query_cot, wq],
        flops=2 * tokens * width * heads * key_size,
        name="query_part",
    )
    message, edge = run(
        middle_kernel,
        [((tokens + 16 + tokens // 2, width), BF), ((16, width), BF)],
        kv_cot + [normed_cot, pooled, gain, wk, wv],
        flops=2 * tokens * width * (key_size + value_size),
        name="conv_cot",
    )
    near_message, core_message = swap(message, 1), swap(message, 0, 1)
    crossing = [(i, i + 1) for i in range(1, devices - 1, 2)]
    crossing = crossing + [(j, i) for i, j in crossing]
    edge_in = lax.ppermute(edge, "seq", crossing)
    query_half = (groups // 2, norm_pad, heads * key_size)
    keep, send = run(
        query_grad_kernel,
        [(query_half, F32), (query_half, BF)],
        [norm_pick, query_cot, query_core, query_near, swap(held(query_near, message), 0, 1)],
        [pltpu.VMEM((4 * tokens, heads * key_size), BF)],
        flops=2 * groups * norm_pad * 4 * tokens * heads * key_size,
        name="query_grad",
    )
    query_fourth = (groups // 4,) + query_half[1:]
    relay, keep, send = run(
        relay_kernel,
        [(message.shape, BF), (query_fourth, F32), (query_fourth, BF)],
        [near_message, keep, swap(send, 2)],
        name="relay",
        after=[edge_in],
    )
    query_parts = halved(keep, send, bits[2:], "query_fold")
    blocks = [message, core_message, near_message, swap(relay, 0, 1)]
    _, _, gain_at = chunk_layout(conv_rows, norm_rows, width, key_size, value_size)
    chunk = (round_up(gain_at + 2, 16), width)
    chunks = (groups // 4,) + chunk
    near_keep, far_keep, near_send, far_send = run(
        lambda *refs: conv_grad_kernel(
            *refs,
            conv_rows=conv_rows,
            conv_pad=conv_pad,
            norm_rows=norm_rows,
            norm_pad=norm_pad,
            key_size=key_size,
            value_size=value_size,
        ),
        [(chunks, F32), (chunks, F32), (chunks, BF), (chunks, BF)],
        [conv_pick, norm_pick] + blocks,
        [
            pltpu.VMEM((8 * tokens, width), BF),
            pltpu.VMEM((4 * tokens, width // 2), BF),
            pltpu.VMEM(chunk, F32),
        ],
        flops=2 * groups * conv_pad * 8 * tokens * width,
        name="conv_grad",
    )
    far_in = swap(far_send, 2)
    near_in = swap(near_send, 2)
    (far_sum,) = run(send_on_kernel, [(chunks, BF)], [far_keep, far_in], name="conv_send_on")
    conv_parts = [near_keep, near_in, swap(far_sum, 4)]
    if len(bits) > 3:
        keep, send = fold(conv_parts, "conv_fold")
        conv_parts = halved(keep, send, bits[3:], "conv_fold")
    (input_grad,) = run(
        input_kernel,
        [((positions, channels), BF)],
        [x, message, near_message, edge_in, conv_weight],
        [
            pltpu.VMEM((tokens + 16, width), F32),
            pltpu.VMEM((channels // LANES, positions, LANES), F32),
        ],
        flops=2 * positions * taps * channels * width,
        name="input_grad",
        after=[far_sum],
    )
    conv_grad, query_grad, key_grad, value_grad, gain_grad = run(
        lambda *refs: final_kernel(*refs, conv_parts=len(conv_parts)),
        [
            ((conv_rows, width), F32),
            ((norm_rows, heads * key_size), F32),
            ((norm_rows, key_size), F32),
            ((norm_rows, value_size), F32),
            ((1, norm_rows), F32),
        ],
        conv_parts + query_parts,
        [pltpu.VMEM(chunk, F32)],
        name="final_sum",
    )
    return (
        attended[None],
        input_grad[None],
        conv_grad,
        query_grad,
        key_grad,
        value_grad,
        gain_grad.reshape(norm_rows),
    )


def solution(mesh):
    placed = (
        P(("groups", "dp"), "seq", None),
        P(),
        P(),
        P(),
        P(),
        P(),
        P(("groups", "dp"), "seq", None),
    )
    return jax.shard_map(
        on_device,
        mesh=mesh,
        in_specs=placed,
        out_specs=(
            P(("groups", "dp"), "seq", None),
            P(("groups", "dp"), "seq", None),
            P(("groups", "seq", "dp"), None),
            P(("groups", "seq", "dp"), None),
            P(("groups", "seq", "dp"), None),
            P(("groups", "seq", "dp"), None),
            P(("groups", "seq", "dp")),
        ),
        check_vma=False,
    )
```

```python
import math

import jax
import jax.numpy as jnp
from jax import lax
from jax.experimental import pallas as pl
from jax.experimental.pallas import tpu as pltpu
from jax.sharding import PartitionSpec as P

BF = jnp.bfloat16
F32 = jnp.float32
ROOT = math.sqrt(2.0 / math.pi)
EPS = 1e-06
LANES = 128
VMEM_BYTES = 40 * 2**20


def dot(a, b):
    return lax.dot_general(a, b, (((1,), (0,)), ((), ())), preferred_element_type=F32)


def dot_t(a, b):
    return lax.dot_general(a, b, (((1,), (1,)), ((), ())), preferred_element_type=F32)


def run(body, outs, args, scratch=(), flops=0, name=None, after=()):
    size = sum(math.prod(a.shape) * a.dtype.itemsize for a in args)
    size += sum(math.prod(s) * jnp.dtype(t).itemsize for s, t in outs)
    vmem = pl.BlockSpec(memory_space=pltpu.VMEM)
    rest = pl.BlockSpec(memory_space=pl.ANY)
    count, skip = len(args), len(args) + len(after)

    def whole(*refs):
        body(*refs[:count], *refs[skip:])

    return pl.pallas_call(
        whole,
        out_shape=[jax.ShapeDtypeStruct(s, t) for s, t in outs],
        in_specs=[vmem] * count + [rest] * len(after),
        out_specs=[vmem] * len(outs),
        scratch_shapes=list(scratch),
        compiler_params=pltpu.CompilerParams(vmem_limit_bytes=VMEM_BYTES),
        cost_estimate=pl.CostEstimate(flops=flops, bytes_accessed=size, transcendentals=0),
        name=name,
    )(*args, *after)


def gelu(v):
    return v * (0.5 * (1.0 + jnp.tanh(ROOT * (v + 0.044715 * (v * v * v)))))


def gelu_slope(v):
    tangent = jnp.tanh(ROOT * (v + 0.044715 * v * v * v))
    return 0.5 * (1.0 + tangent) + 0.5 * v * (1.0 - tangent * tangent) * ROOT * (
        1.0 + 3.0 * 0.044715 * v * v
    )


def round_up(value, step):
    return -(-value // step) * step


def pack_kv(keys, values):
    tokens, size = keys.shape
    rest = values[:, size:]
    half = tokens // 2
    tail = jnp.concatenate([rest[:half], rest[half:]], axis=1)
    return jnp.concatenate([keys, values[:, :size], tail], axis=0)


def unpack_values(packed, tokens, size):
    tail = packed[2 * tokens :]
    width = tail.shape[1] // 2
    rest = jnp.concatenate([tail[:, :width], tail[:, width:]], axis=0)
    return jnp.concatenate([packed[tokens : 2 * tokens], rest], axis=1)


def put(ref, start, rows):
    for c in range(ref.shape[0]):
        ref[c, start : start + rows.shape[0]] = rows[:, c * LANES : (c + 1) * LANES]


def every_second(ref, start, count):
    parts = [ref[c, pl.ds(start, count, stride=2)] for c in range(ref.shape[0])]
    return jnp.concatenate(parts, axis=1)


def open_kernel(x, pad, ends):
    positions, channels = x.shape
    ends[:16] = x[:16]
    ends[16:] = x[positions - 16 :]
    put(pad, 0, jnp.zeros((8, channels), F32))
    put(pad, 8, gelu(x[...].astype(F32)).astype(BF).astype(F32))
    put(pad, 8 + positions, jnp.zeros((pad.shape[1] - 8 - positions, channels), F32))


def front_kernel(ready, pair, across, weight, gain, wk, wv, kv_out, early, normed_out, pooled_out, pad):
    tokens = pooled_out.shape[0]
    ext = early.shape[0] // 2
    even = lax.axis_index("seq") % 2 == 0
    pair_wide, across_wide = pair[...].astype(F32), across[...].astype(F32)
    before = jnp.where(even, across_wide[16:], pair_wide[16:])[14:]
    after = jnp.where(even, pair_wide[:16], across_wide[:16])[:2]
    pad[...] = ready[...]
    put(pad, 6, gelu(before).astype(BF).astype(F32))
    put(pad, 8 + 2 * tokens, gelu(after).astype(BF).astype(F32))
    pieces = [every_second(pad, 6 + u, tokens).astype(BF) for u in range(6)]
    total = None
    for tap in range(5):
        rows = jnp.concatenate([pieces[tap], pieces[tap + 1]], axis=0)
        term = dot(rows, weight[tap])
        total = term if total is None else total + term
    pooled = 0.5 * (total[:tokens] + total[tokens:])
    inv = lax.rsqrt(jnp.mean(pooled * pooled, axis=-1, keepdims=True) + EPS)
    normed = (pooled * inv * gain[...]).astype(BF)
    pooled_out[...] = pooled
    normed_out[...] = normed
    kv_out[...] = pack_kv(dot(normed, wk[...]), dot_t(normed, wv[...])).astype(BF)
    early[0:ext] = every_second(pad, 6, ext).astype(BF)
    early[ext : 2 * ext] = every_second(pad, 7, ext).astype(BF)


def ordered(bits):
    masks = [0]
    for bit in reversed(bits):
        masks = masks + [mask | (1 << bit) for mask in masks]
    return masks


def split_rows(rows, columns):
    return round_up(-(-rows * LANES // columns), 16)


def query_kernel(normed, wq, early, out, message, own, *, order, rows, padded, scale):
    width = normed.shape[1]
    value = normed[...]
    out[...] = (dot(value, wq[...]) * scale).astype(BF)
    at, channels = early.shape
    message[:at] = early[...]
    count = len(order) * padded
    step = split_rows(count, channels)
    for i in range(4):
        block_of = place(i)
        pick = [chosen(rows, padded, width, block_of(k)) for k in order]
        part = dot_t(jnp.concatenate(pick, axis=0), value).astype(BF)
        if i == 0:
            own[...] = part
            continue
        for c in range(channels // LANES):
            piece = part[c * step : min((c + 1) * step, count)]
            message[at : at + piece.shape[0], c * LANES : (c + 1) * LANES] = piece
        at += step


def attend_kernel(*refs, blocks, masks, heads, key_size, value_size, scale):
    q, cot = refs[:2]
    parts = refs[2 : 2 + blocks]
    att, dq, keep_a, send_a, keep_b, send_b = refs[2 + blocks : 8 + blocks]
    ks, vs, kt, vt, qs, cs, weights, score_cots = refs[8 + blocks :]
    tokens = q.shape[0]
    half = tokens // 2
    wide = value_size - key_size
    for i, part in enumerate(parts):
        at = i * tokens
        ks[at : at + tokens] = part[:tokens]
        vs[at : at + tokens, :key_size] = part[tokens : 2 * tokens]
        vs[at : at + half, key_size:] = part[2 * tokens :, :wide]
        vs[at + half : at + tokens, key_size:] = part[2 * tokens :, wide:]
        kt[:, at : at + tokens] = ks[at : at + tokens].astype(F32).T.astype(BF)
        vt[:, at : at + tokens] = vs[at : at + tokens].astype(F32).T.astype(BF)
    for pair in range(heads // 2):
        ql, cl = 2 * pair * key_size, 2 * pair * value_size
        rows = slice(2 * pair * tokens, 2 * (pair + 1) * tokens)
        both = cot[:, cl : cl + 2 * value_size]
        qs[rows] = jnp.concatenate(
            [q[:, ql : ql + key_size], q[:, ql + key_size : ql + 2 * key_size]], axis=0
        )
        cs[rows] = jnp.concatenate([both[:, :value_size], both[:, value_size:]], axis=0)
        scores = dot_t(ks[...], qs[rows])
        raised = jnp.exp(scores - jnp.max(scores, axis=0, keepdims=True))
        probs = raised * (1.0 / jnp.sum(raised, axis=0, keepdims=True))
        weights[:, rows] = probs.astype(BF)
        out_t = dot(vt[...], weights[:, rows]).astype(BF).astype(F32)
        delta = jnp.sum(cs[rows].astype(F32).T * out_t, axis=0, keepdims=True)
        score_cots[:, rows] = (probs * (dot_t(vs[...], cs[rows]) - delta)).astype(BF)
        dq_t = dot(kt[...], score_cots[:, rows]) * scale
        out_rows = jnp.concatenate([out_t[:, :tokens].T, out_t[:, tokens:].T], axis=1)
        att[:, cl : cl + 2 * value_size] = out_rows.astype(BF)
        dq_rows = jnp.concatenate([dq_t[:, :tokens].T, dq_t[:, tokens:].T], axis=1)
        dq[:, ql : ql + 2 * key_size] = dq_rows.astype(BF)
    edge = keep_a.shape[1]
    count = blocks // 2
    for i in range(blocks):
        at = slice(i * tokens, (i + 1) * tokens)
        packed = pack_kv(dot(score_cots[at], qs[...]), dot(weights[at], cs[...]))
        for order, keep, send, part in (
            (masks[0], keep_a, send_a, packed[:edge]),
            (masks[1], keep_b, send_b, packed[edge:]),
        ):
            k = order.index(i)
            if k < count:
                keep[k] = part
            else:
                send[k - count] = part.astype(BF)


def total_of(parts):
    total = parts[0][...]
    for part in parts[1:]:
        total = total + part[...].astype(F32)
    return total


def fold_kernel(*refs):
    keep, send = refs[-2:]
    total = total_of(refs[:-2])
    keep[...] = total[: keep.shape[0]]
    send[...] = total[keep.shape[0] :].astype(BF)


def fold_two_kernel(*refs):
    fold_kernel(refs[0], refs[1], refs[4], refs[5])
    fold_kernel(refs[2], refs[3], refs[6], refs[7])


def merge_kernel(keep_a, in_a, keep_b, in_b, keep, send):
    total = jnp.concatenate([total_of((keep_a, in_a)), total_of((keep_b, in_b))], axis=1)
    keep[...] = total[: keep.shape[0]]
    send[...] = total[keep.shape[0] :].astype(BF)


def send_on_kernel(keep, came, out):
    out[...] = (keep[...] + came[...].astype(F32)).astype(BF)


def query_cot_kernel(dq, wq, out):
    out[...] = dot_t(dq[...], wq[...])


def middle_kernel(own, came, part, pooled_in, gain_in, wk, wv, message, edge):
    size = own.shape[2]
    tokens, width = pooled_in.shape
    total = (own[0] + came[0].astype(F32)).astype(BF).astype(F32)
    key_cot = total[:tokens]
    value_cot = unpack_values(total, tokens, size)
    normed_cot = part[...] + dot_t(key_cot.astype(BF), wk[...])
    normed_cot = normed_cot + dot(value_cot.astype(BF), wv[...])
    pooled, gain = pooled_in[...], gain_in[...]
    inv = lax.rsqrt(jnp.mean(pooled * pooled, axis=-1, keepdims=True) + EPS)
    gain_term = jnp.sum(normed_cot * pooled * inv, axis=0, keepdims=True)
    gained = gain * normed_cot
    pooled_cot = inv * gained - pooled * (inv * inv * inv) * (
        jnp.sum(gained * pooled, axis=-1, keepdims=True) / width
    )
    conv_cot = 0.5 * pooled_cot
    high = gain_term.astype(BF).astype(F32)
    low = gain_term - high
    row = lax.broadcasted_iota(jnp.int32, (16, width), 0)
    gains = jnp.where(row == 0, high, jnp.where(row == 1, low, 0.0))
    both = jnp.concatenate([key_cot, value_cot], axis=1)
    fill = width // 2 - both.shape[1]
    both = jnp.concatenate([both, jnp.zeros((tokens, fill), F32)], axis=1)
    side = jnp.concatenate([both[: tokens // 2], both[tokens // 2 :]], axis=1)
    message[:tokens] = conv_cot.astype(BF)
    message[tokens : tokens + 16] = gains.astype(BF)
    message[tokens + 16 :] = side.astype(BF)
    ends = jnp.where(row == 0, conv_cot[:1], jnp.where(row == 1, conv_cot[tokens - 1 :], 0.0))
    edge[...] = ends.astype(BF)


def place(other=0):
    seq, dp = lax.axis_index("seq"), lax.axis_index("dp") ^ (other % 2)
    high, low = seq // 2, (seq % 2) ^ (other // 2)
    return lambda k: ((high ^ k) * 2 + low) * 2 + dp


def chosen(rows, padded, columns, block):
    row = lax.broadcasted_iota(jnp.int32, (padded, columns), 0)
    column = lax.broadcasted_iota(jnp.int32, (padded, columns), 1)
    hit = (column == row + block * rows) & (row < rows)
    return jnp.where(hit, 1.0, 0.0).astype(BF)


def relay_kernel(value, keep_in, came, out, keep, send):
    out[...] = value[...]
    fold_kernel(keep_in, came, keep, send)


def select_kernel(*refs, order, rows, padded):
    own, blocks = refs[0], refs[1:5]
    out, norm_out, even, odd = refs[5:]
    ext, channels = even.shape
    tokens = own.shape[1]
    count = own.shape[0]
    step = split_rows(count, channels)
    norm_out[:, :tokens] = own[...]
    for i in range(1, 4):
        at = 2 * ext + (i - 1) * step
        for c in range(channels // LANES):
            end = min((c + 1) * step, count)
            piece = blocks[i][at : at + end - c * step, c * LANES : (c + 1) * LANES]
            norm_out[c * step : end, i * tokens : (i + 1) * tokens] = piece
    block_of = place()
    pick = jnp.concatenate(
        [chosen(rows, padded, 5 * channels, block_of(k)) for k in order], axis=0
    )
    for i, block in enumerate(blocks):
        even[...] = block[:ext].astype(F32)
        odd[...] = block[ext : 2 * ext].astype(F32)
        pieces = []
        for shift in range(3):
            pieces += [even[shift : shift + tokens].astype(BF), odd[shift : shift + tokens].astype(BF)]
        shifted = jnp.concatenate(
            [jnp.concatenate(pieces[:5], axis=1), jnp.concatenate(pieces[1:], axis=1)], axis=0
        )
        out[:, 2 * i * tokens : 2 * (i + 1) * tokens] = dot_t(pick, shifted).astype(BF)


def query_grad_kernel(pick, first, second, third, fourth, keep, send, right):
    tokens = first.shape[0]
    for i, block in enumerate((first, second, third, fourth)):
        right[i * tokens : (i + 1) * tokens] = block[...]
    count, pad = keep.shape[:2]
    for k in range(2 * count):
        term = dot(pick[k * pad : (k + 1) * pad], right[...])
        if k < count:
            keep[k] = term
        else:
            send[k - count] = term.astype(BF)


def chunk_layout(conv_rows, norm_rows, width, key_size, value_size):
    key_rows = norm_rows * key_size // width
    value_rows = norm_rows * value_size // width
    return conv_rows, conv_rows + key_rows, conv_rows + key_rows + value_rows


def conv_grad_kernel(*refs, conv_rows, conv_pad, norm_rows, norm_pad, key_size, value_size):
    pick, norm_pick, blocks = refs[0], refs[1], refs[2:6]
    outs, right, side, stage = refs[6:-3], refs[-3], refs[-2], refs[-1]
    width = right.shape[1]
    tokens = side.shape[0] // 4
    half = tokens // 2
    gain = None
    for i, block in enumerate(blocks):
        piece = block[:tokens]
        right[2 * i * tokens : (2 * i + 1) * tokens] = piece
        right[(2 * i + 1) * tokens : (2 * i + 2) * tokens] = piece
        side[i * tokens : i * tokens + half] = block[tokens + 16 :, : width // 2]
        side[i * tokens + half : (i + 1) * tokens] = block[tokens + 16 :, width // 2 :]
        two = block[tokens : tokens + 16].astype(F32)
        term = two[0:1] + two[1:2]
        gain = term if gain is None else gain + term
    high = gain.astype(BF).astype(F32)
    key_at, value_at, gain_at = chunk_layout(conv_rows, norm_rows, width, key_size, value_size)
    stage[...] = jnp.zeros(stage.shape, F32)
    stage[gain_at : gain_at + 1] = high
    stage[gain_at + 1 : gain_at + 2] = gain - high
    count = outs[0].shape[0]
    for k in range(4 * count):
        out = outs[k // count]
        conv = dot(pick[k * conv_pad : (k + 1) * conv_pad], right[...])
        stage[:conv_rows] = conv[:conv_rows]
        both = dot(norm_pick[k * norm_pad : (k + 1) * norm_pad], side[...])
        key, value = both[:, :key_size], both[:, key_size : key_size + value_size]
        for part, at, end in ((key, key_at, value_at), (value, value_at, gain_at)):
            step = end - at
            pieces = [part[i : i + step] for i in range(0, norm_rows, step)]
            stage[at:end] = jnp.concatenate(pieces, axis=1)
        out[k % count] = stage[...].astype(out.dtype)


def final_kernel(*refs, conv_parts):
    conv, query, key, value, gain, stage = refs[-6:]
    total = total_of(refs[:conv_parts])[0]
    query[...] = total_of(refs[conv_parts:-6])[0, : query.shape[0]]
    rows, width = conv.shape
    count = key.shape[0]
    stage[...] = total
    conv[...] = stage[:rows]
    key_at, value_at, gain_at = chunk_layout(
        rows, count, width, key.shape[1], value.shape[1]
    )
    for part, at, end in ((key, key_at, value_at), (value, value_at, gain_at)):
        size, step = part.shape[1], end - at
        packed = stage[at:end]
        for i in range(count // step):
            part[i * step : (i + 1) * step] = packed[:, i * size : (i + 1) * size]
    line = stage[gain_at : gain_at + 1] + stage[gain_at + 1 : gain_at + 2]
    line = jnp.broadcast_to(line, (8, width))
    start = place()(0) * count
    gain[...] = pltpu.roll(line, lax.rem(width - start, width), 1)[:1, :count]


def input_kernel(x, cc, pair_cc, edge, weight, out, ext, mixed):
    tokens = x.shape[0] // 2
    low = lax.axis_index("seq") % 2
    ext[8 : 8 + tokens] = cc[:tokens].astype(F32)
    pair_first = pair_cc[0:16].astype(F32)[0:1]
    pair_last = pair_cc[tokens - 16 : tokens].astype(F32)[15:16]
    ends = edge[...].astype(F32)
    ext[7:8] = jnp.where(low == 0, ends[1:2], pair_last)
    ext[8 + tokens : 9 + tokens] = jnp.where(low == 0, pair_first, ends[0:1])
    back = ext[7 : 7 + tokens].astype(BF)
    here = ext[8 : 8 + tokens].astype(BF)
    ahead = ext[9 : 9 + tokens].astype(BF)
    evens = (ahead, here, here, back, back)
    odds = (ahead, ahead, here, here, back)
    total = None
    for tap in range(5):
        term = dot_t(jnp.concatenate([evens[tap], odds[tap]], axis=0), weight[tap])
        total = term if total is None else total + term
    for c in range(mixed.shape[0]):
        lanes = slice(c * LANES, (c + 1) * LANES)
        mixed[c, pl.ds(0, tokens, stride=2)] = total[:tokens, lanes]
        mixed[c, pl.ds(1, tokens, stride=2)] = total[tokens:, lanes]
        out[:, lanes] = (mixed[c] * gelu_slope(x[:, lanes].astype(F32))).astype(BF)


def on_device(x, conv_weight, norm_gain, wq, wk, wv, cotangent):
    devices = lax.axis_size("seq")
    both_axes = ("seq", "dp")
    x, cotangent = x[0], cotangent[0]
    positions, channels = x.shape
    tokens = positions // 2
    taps, _, width = conv_weight.shape
    key_size, value_size = wk.shape[1], wv.shape[1]
    heads = cotangent.shape[1] // value_size
    scale = key_size ** (-0.5)
    groups = devices // 2
    owners = devices * 2
    conv_rows, norm_rows = taps * channels // owners, width // owners
    conv_pad, norm_pad = round_up(conv_rows, 16), round_up(norm_rows, 16)
    ext = tokens + 16
    gain = norm_gain.reshape(1, width)

    def swap(value, seq_bits, dp_bit=0):
        mask = 2 * seq_bits + dp_bit
        return lax.ppermute(value, both_axes, [(i, i ^ mask) for i in range(owners)])

    def held(value, *until):
        return lax.optimization_barrier((value,) + until)[0]

    def quad(value, *until):
        core = swap(value, 0, 1)
        near = swap(value, 1)
        return [value, core, near, swap(held(near, *until), 0, 1)]

    def fold(parts, name):
        shape = (parts[0].shape[0] // 2,) + parts[0].shape[1:]
        return run(fold_kernel, [(shape, F32), (shape, BF)], parts, name=name)

    def halved(keep, send, bits, name):
        for bit in bits[:-1]:
            keep, send = fold([keep, swap(send, 1 << bit)], name)
        return [keep, swap(send, 1 << bits[-1])]

    bits = list(range(devices.bit_length() - 1))
    order = [mask // 2 for mask in ordered(bits[1:])]
    crossing = [(i, i + 1) for i in range(1, devices - 1, 2)]
    crossing = crossing + [(j, i) for i, j in crossing]
    pad_shape = (channels // LANES, 8 + 2 * ext + 8, LANES)
    ready, ends = run(
        open_kernel,
        [(pad_shape, F32), ((32, channels), BF)],
        [x],
        flops=4 * 10**9,
        name="gelu",
    )
    pair, across = swap(ends, 1), lax.ppermute(ends, "seq", crossing)
    wv = wv.T
    kv, early, normed, pooled = run(
        front_kernel,
        [
            ((5 * tokens // 2, key_size), BF),
            ((2 * ext, channels), BF),
            ((tokens, width), BF),
            ((tokens, width), F32),
        ],
        [ready, pair, across, conv_weight, gain, wk, wv],
        [pltpu.VMEM(pad_shape, F32)],
        flops=2 * positions * taps * channels * width,
        name="front",
    )
    near_kv = [kv] + [swap(kv, 2 * k) for k in range(1, groups)]
    far_kv = [swap(block, 1) for block in near_kv]
    picked = (groups * norm_pad, tokens)
    rows = 2 * ext + 3 * split_rows(picked[0], channels)
    queries, early, pick_own = run(
        lambda *refs: query_kernel(
            *refs, order=order, rows=norm_rows, padded=norm_pad, scale=scale
        ),
        [((tokens, heads * key_size), BF), ((rows, channels), BF), (picked, BF)],
        [normed, wq, early],
        flops=4 * tokens * width * heads * key_size,
        name="queries",
        after=near_kv[1:],
    )
    early = held(early, *far_kv)
    length = devices * tokens
    masks = [2 * k for k in range(groups)] + [2 * k + 1 for k in range(groups)]
    half_block = (groups, 5 * tokens // 4, key_size)
    attended, query_cot, keep_a, send_a, keep_b, send_b = run(
        lambda *refs: attend_kernel(
            *refs,
            blocks=devices,
            masks=[
                [masks.index(m) for m in ordered(way)] for way in (bits, [1, 0] + bits[2:])
            ],
            heads=heads,
            key_size=key_size,
            value_size=value_size,
            scale=scale,
        ),
        [((tokens, heads * value_size), BF), ((tokens, heads * key_size), BF)]
        + [(half_block, F32), (half_block, BF)] * 2,
        [queries, cotangent] + near_kv + far_kv,
        [
            pltpu.VMEM((length, key_size), BF),
            pltpu.VMEM((length, value_size), BF),
            pltpu.VMEM((key_size, length), BF),
            pltpu.VMEM((value_size, length), BF),
            pltpu.VMEM((heads * tokens, key_size), BF),
            pltpu.VMEM((heads * tokens, value_size), BF),
            pltpu.VMEM((length, heads * tokens), BF),
            pltpu.VMEM((length, heads * tokens), BF),
        ],
        flops=6 * tokens * heads * length * (key_size + value_size),
        name="attend",
    )
    early_blocks = quad(early, send_a)
    in_a, in_b = swap(send_a, 1), swap(send_b, 2)
    conv_pick, norm_pick = run(
        lambda *refs: select_kernel(*refs, order=order, rows=conv_rows, padded=conv_pad),
        [((groups * conv_pad, 8 * tokens), BF), ((groups * norm_pad, 4 * tokens), BF)],
        [pick_own] + early_blocks,
        [pltpu.VMEM((ext, channels), F32), pltpu.VMEM((ext, channels), F32)],
        flops=2 * groups * conv_pad * taps * channels * 8 * tokens,
        name="select",
    )
    fourth = (groups // 2,) + half_block[1:]
    keep_a, send_a, keep_b, send_b = run(
        fold_two_kernel,
        [(fourth, F32), (fourth, BF)] * 2,
        [keep_a, in_a, keep_b, in_b],
        name="kv_cot_fold",
        after=[conv_pick],
    )
    in_a, in_b = swap(send_a, 2), swap(send_b, 1)
    block = (groups // 4, 5 * tokens // 2, key_size)
    keep, send = run(
        merge_kernel,
        [(block, F32), (block, BF)],
        [keep_a, in_a, keep_b, in_b],
        name="kv_cot_merge",
    )
    (normed_cot,) = run(
        query_cot_kernel,
        [((tokens, width), F32)],
        [query_cot, wq],
        flops=2 * tokens * width * heads * key_size,
        name="query_part",
    )
    query_cot = held(query_cot, keep)
    query_near, query_core = swap(query_cot, 1), swap(query_cot, 0, 1)
    kv_cot = halved(keep, send, bits[2:], "kv_cot_fold")
    message, edge = run(
        middle_kernel,
        [((tokens + 16 + tokens // 2, width), BF), ((16, width), BF)],
        kv_cot + [normed_cot, pooled, gain, wk, wv],
        flops=2 * tokens * width * (key_size + value_size),
        name="conv_cot",
    )
    near_message, core_message = swap(message, 1), swap(message, 0, 1)
    edge_in = lax.ppermute(edge, "seq", crossing)
    query_half = (groups // 2, norm_pad, heads * key_size)
    keep, send = run(
        query_grad_kernel,
        [(query_half, F32), (query_half, BF)],
        [norm_pick, query_cot, query_core, query_near, swap(held(query_near, message), 0, 1)],
        [pltpu.VMEM((4 * tokens, heads * key_size), BF)],
        flops=2 * groups * norm_pad * 4 * tokens * heads * key_size,
        name="query_grad",
    )
    query_fourth = (groups // 4,) + query_half[1:]
    relay, keep, send = run(
        relay_kernel,
        [(message.shape, BF), (query_fourth, F32), (query_fourth, BF)],
        [near_message, keep, swap(send, 2)],
        name="relay",
        after=[edge_in],
    )
    query_parts = halved(keep, send, bits[2:], "query_fold")
    blocks = [message, core_message, near_message, swap(relay, 0, 1)]
    _, _, gain_at = chunk_layout(conv_rows, norm_rows, width, key_size, value_size)
    chunk = (round_up(gain_at + 2, 16), width)
    chunks = (groups // 4,) + chunk
    near_keep, far_keep, near_send, far_send = run(
        lambda *refs: conv_grad_kernel(
            *refs,
            conv_rows=conv_rows,
            conv_pad=conv_pad,
            norm_rows=norm_rows,
            norm_pad=norm_pad,
            key_size=key_size,
            value_size=value_size,
        ),
        [(chunks, F32), (chunks, F32), (chunks, BF), (chunks, BF)],
        [conv_pick, norm_pick] + blocks,
        [
            pltpu.VMEM((8 * tokens, width), BF),
            pltpu.VMEM((4 * tokens, width // 2), BF),
            pltpu.VMEM(chunk, F32),
        ],
        flops=2 * groups * conv_pad * 8 * tokens * width,
        name="conv_grad",
    )
    far_in = swap(far_send, 2)
    near_in = swap(near_send, 2)
    (far_sum,) = run(send_on_kernel, [(chunks, BF)], [held(far_keep, query_parts[1]), far_in], name="conv_send_on")
    conv_parts = [near_keep, near_in, swap(far_sum, 4)]
    if len(bits) > 3:
        keep, send = fold(conv_parts, "conv_fold")
        conv_parts = halved(keep, send, bits[3:], "conv_fold")
    (input_grad,) = run(
        input_kernel,
        [((positions, channels), BF)],
        [x, message, near_message, edge_in, conv_weight],
        [
            pltpu.VMEM((tokens + 16, width), F32),
            pltpu.VMEM((channels // LANES, positions, LANES), F32),
        ],
        flops=2 * positions * taps * channels * width,
        name="input_grad",
        after=[far_sum],
    )
    conv_grad, query_grad, key_grad, value_grad, gain_grad = run(
        lambda *refs: final_kernel(*refs, conv_parts=len(conv_parts)),
        [
            ((conv_rows, width), F32),
            ((norm_rows, heads * key_size), F32),
            ((norm_rows, key_size), F32),
            ((norm_rows, value_size), F32),
            ((1, norm_rows), F32),
        ],
        conv_parts + query_parts,
        [pltpu.VMEM(chunk, F32)],
        name="final_sum",
    )
    return (
        attended[None],
        input_grad[None],
        conv_grad,
        query_grad,
        key_grad,
        value_grad,
        gain_grad.reshape(norm_rows),
    )


def solution(mesh):
    placed = (
        P(("groups", "dp"), "seq", None),
        P(),
        P(),
        P(),
        P(),
        P(),
        P(("groups", "dp"), "seq", None),
    )
    return jax.shard_map(
        on_device,
        mesh=mesh,
        in_specs=placed,
        out_specs=(
            P(("groups", "dp"), "seq", None),
            P(("groups", "dp"), "seq", None),
            P(("groups", "seq", "dp"), None),
            P(("groups", "seq", "dp"), None),
            P(("groups", "seq", "dp"), None),
            P(("groups", "seq", "dp"), None),
            P(("groups", "seq", "dp")),
        ),
        check_vma=False,
    )
```

```python
import math

import jax
import jax.numpy as jnp
from jax import lax
from jax.experimental import pallas as pl
from jax.experimental.pallas import tpu as pltpu
from jax.sharding import PartitionSpec as P

BF = jnp.bfloat16
F32 = jnp.float32
ROOT = math.sqrt(2.0 / math.pi)
EPS = 1e-06
LANES = 128
VMEM_BYTES = 40 * 2**20


def dot(a, b):
    return lax.dot_general(a, b, (((1,), (0,)), ((), ())), preferred_element_type=F32)


def dot_t(a, b):
    return lax.dot_general(a, b, (((1,), (1,)), ((), ())), preferred_element_type=F32)


def run(body, outs, args, scratch=(), flops=0, name=None, after=()):
    size = sum(math.prod(a.shape) * a.dtype.itemsize for a in args)
    size += sum(math.prod(s) * jnp.dtype(t).itemsize for s, t in outs)
    vmem = pl.BlockSpec(memory_space=pltpu.VMEM)
    rest = pl.BlockSpec(memory_space=pl.ANY)
    count, skip = len(args), len(args) + len(after)

    def whole(*refs):
        body(*refs[:count], *refs[skip:])

    return pl.pallas_call(
        whole,
        out_shape=[jax.ShapeDtypeStruct(s, t) for s, t in outs],
        in_specs=[vmem] * count + [rest] * len(after),
        out_specs=[vmem] * len(outs),
        scratch_shapes=list(scratch),
        compiler_params=pltpu.CompilerParams(vmem_limit_bytes=VMEM_BYTES),
        cost_estimate=pl.CostEstimate(flops=flops, bytes_accessed=size, transcendentals=0),
        name=name,
    )(*args, *after)


def gelu(v):
    return v * (0.5 * (1.0 + jnp.tanh(ROOT * (v + 0.044715 * (v * v * v)))))


def gelu_slope(v):
    tangent = jnp.tanh(ROOT * (v + 0.044715 * v * v * v))
    return 0.5 * (1.0 + tangent) + 0.5 * v * (1.0 - tangent * tangent) * ROOT * (
        1.0 + 3.0 * 0.044715 * v * v
    )


def round_up(value, step):
    return -(-value // step) * step


def pack_kv(keys, values):
    tokens, size = keys.shape
    rest = values[:, size:]
    half = tokens // 2
    tail = jnp.concatenate([rest[:half], rest[half:]], axis=1)
    return jnp.concatenate([keys, values[:, :size], tail], axis=0)


def unpack_values(packed, tokens, size):
    tail = packed[2 * tokens :]
    width = tail.shape[1] // 2
    rest = jnp.concatenate([tail[:, :width], tail[:, width:]], axis=0)
    return jnp.concatenate([packed[tokens : 2 * tokens], rest], axis=1)


def put(ref, start, rows):
    for c in range(ref.shape[0]):
        ref[c, start : start + rows.shape[0]] = rows[:, c * LANES : (c + 1) * LANES]


def every_second(ref, start, count):
    parts = [ref[c, pl.ds(start, count, stride=2)] for c in range(ref.shape[0])]
    return jnp.concatenate(parts, axis=1)


def open_kernel(x, pad, ends):
    positions, channels = x.shape
    ends[:16] = x[:16]
    ends[16:] = x[positions - 16 :]
    put(pad, 0, jnp.zeros((8, channels), F32))
    put(pad, 8, gelu(x[...].astype(F32)).astype(BF).astype(F32))
    put(pad, 8 + positions, jnp.zeros((pad.shape[1] - 8 - positions, channels), F32))


def front_kernel(ready, pair, across, weight, gain, wk, wv, kv_out, early, normed_out, pooled_out, pad):
    tokens = pooled_out.shape[0]
    ext = early.shape[0] // 2
    even = lax.axis_index("seq") % 2 == 0
    pair_wide, across_wide = pair[...].astype(F32), across[...].astype(F32)
    before = jnp.where(even, across_wide[16:], pair_wide[16:])[14:]
    after = jnp.where(even, pair_wide[:16], across_wide[:16])[:2]
    pad[...] = ready[...]
    put(pad, 6, gelu(before).astype(BF).astype(F32))
    put(pad, 8 + 2 * tokens, gelu(after).astype(BF).astype(F32))
    pieces = [every_second(pad, 6 + u, tokens).astype(BF) for u in range(6)]
    total = None
    for tap in range(5):
        rows = jnp.concatenate([pieces[tap], pieces[tap + 1]], axis=0)
        term = dot(rows, weight[tap])
        total = term if total is None else total + term
    pooled = 0.5 * (total[:tokens] + total[tokens:])
    inv = lax.rsqrt(jnp.mean(pooled * pooled, axis=-1, keepdims=True) + EPS)
    normed = (pooled * inv * gain[...]).astype(BF)
    pooled_out[...] = pooled
    normed_out[...] = normed
    kv_out[...] = pack_kv(dot(normed, wk[...]), dot_t(normed, wv[...])).astype(BF)
    early[0:ext] = every_second(pad, 6, ext).astype(BF)
    early[ext : 2 * ext] = every_second(pad, 7, ext).astype(BF)


def ordered(bits):
    masks = [0]
    for bit in reversed(bits):
        masks = masks + [mask | (1 << bit) for mask in masks]
    return masks


def split_rows(rows, columns):
    return round_up(-(-rows * LANES // columns), 16)


def query_kernel(normed, wq, early, out, message, own, *, order, rows, padded, scale):
    width = normed.shape[1]
    value = normed[...]
    out[...] = (dot(value, wq[...]) * scale).astype(BF)
    at, channels = early.shape
    message[:at] = early[...]
    count = len(order) * padded
    step = split_rows(count, channels)
    for i in range(4):
        block_of = place(i)
        pick = [chosen(rows, padded, width, block_of(k)) for k in order]
        part = dot_t(jnp.concatenate(pick, axis=0), value).astype(BF)
        if i == 0:
            own[...] = part
            continue
        for c in range(channels // LANES):
            piece = part[c * step : min((c + 1) * step, count)]
            message[at : at + piece.shape[0], c * LANES : (c + 1) * LANES] = piece
        at += step


def attend_kernel(*refs, blocks, masks, heads, key_size, value_size, scale):
    q, cot = refs[:2]
    parts = refs[2 : 2 + blocks]
    att, dq, keep_a, send_a, keep_b, send_b = refs[2 + blocks : 8 + blocks]
    ks, vs, kt, vt, qs, cs, weights, score_cots = refs[8 + blocks :]
    tokens = q.shape[0]
    half = tokens // 2
    wide = value_size - key_size
    for i, part in enumerate(parts):
        at = i * tokens
        ks[at : at + tokens] = part[:tokens]
        vs[at : at + tokens, :key_size] = part[tokens : 2 * tokens]
        vs[at : at + half, key_size:] = part[2 * tokens :, :wide]
        vs[at + half : at + tokens, key_size:] = part[2 * tokens :, wide:]
        kt[:, at : at + tokens] = ks[at : at + tokens].astype(F32).T.astype(BF)
        vt[:, at : at + tokens] = vs[at : at + tokens].astype(F32).T.astype(BF)
    for pair in range(heads // 2):
        ql, cl = 2 * pair * key_size, 2 * pair * value_size
        rows = slice(2 * pair * tokens, 2 * (pair + 1) * tokens)
        both = cot[:, cl : cl + 2 * value_size]
        qs[rows] = jnp.concatenate(
            [q[:, ql : ql + key_size], q[:, ql + key_size : ql + 2 * key_size]], axis=0
        )
        cs[rows] = jnp.concatenate([both[:, :value_size], both[:, value_size:]], axis=0)
        scores = dot_t(ks[...], qs[rows])
        raised = jnp.exp(scores - jnp.max(scores, axis=0, keepdims=True))
        probs = raised * (1.0 / jnp.sum(raised, axis=0, keepdims=True))
        weights[:, rows] = probs.astype(BF)
        out_t = dot(vt[...], weights[:, rows]).astype(BF).astype(F32)
        delta = jnp.sum(cs[rows].astype(F32).T * out_t, axis=0, keepdims=True)
        score_cots[:, rows] = (probs * (dot_t(vs[...], cs[rows]) - delta)).astype(BF)
        dq_t = dot(kt[...], score_cots[:, rows]) * scale
        out_rows = jnp.concatenate([out_t[:, :tokens].T, out_t[:, tokens:].T], axis=1)
        att[:, cl : cl + 2 * value_size] = out_rows.astype(BF)
        dq_rows = jnp.concatenate([dq_t[:, :tokens].T, dq_t[:, tokens:].T], axis=1)
        dq[:, ql : ql + 2 * key_size] = dq_rows.astype(BF)
    edge = keep_a.shape[1]
    count = blocks // 2
    for i in range(blocks):
        at = slice(i * tokens, (i + 1) * tokens)
        packed = pack_kv(dot(score_cots[at], qs[...]), dot(weights[at], cs[...]))
        for order, keep, send, part in (
            (masks[0], keep_a, send_a, packed[:edge]),
            (masks[1], keep_b, send_b, packed[edge:]),
        ):
            k = order.index(i)
            if k < count:
                keep[k] = part
            else:
                send[k - count] = part.astype(BF)


def total_of(parts):
    total = parts[0][...]
    for part in parts[1:]:
        total = total + part[...].astype(F32)
    return total


def fold_kernel(*refs):
    keep, send = refs[-2:]
    total = total_of(refs[:-2])
    keep[...] = total[: keep.shape[0]]
    send[...] = total[keep.shape[0] :].astype(BF)


def fold_two_kernel(*refs):
    fold_kernel(refs[0], refs[1], refs[4], refs[5])
    fold_kernel(refs[2], refs[3], refs[6], refs[7])


def merge_kernel(keep_a, in_a, keep_b, in_b, keep, send):
    total = jnp.concatenate([total_of((keep_a, in_a)), total_of((keep_b, in_b))], axis=1)
    keep[...] = total[: keep.shape[0]]
    send[...] = total[keep.shape[0] :].astype(BF)


def send_on_kernel(keep, came, out):
    out[...] = (keep[...] + came[...].astype(F32)).astype(BF)


def query_cot_kernel(dq, wq, out):
    out[...] = dot_t(dq[...], wq[...])


def middle_kernel(own, came, part, pooled_in, gain_in, wk, wv, first, second, edge):
    size = own.shape[2]
    tokens, width = pooled_in.shape
    total = (own[0] + came[0].astype(F32)).astype(BF).astype(F32)
    key_cot = total[:tokens]
    value_cot = unpack_values(total, tokens, size)
    normed_cot = part[...] + dot_t(key_cot.astype(BF), wk[...])
    normed_cot = normed_cot + dot(value_cot.astype(BF), wv[...])
    pooled, gain = pooled_in[...], gain_in[...]
    inv = lax.rsqrt(jnp.mean(pooled * pooled, axis=-1, keepdims=True) + EPS)
    gain_term = jnp.sum(normed_cot * pooled * inv, axis=0, keepdims=True)
    gained = gain * normed_cot
    pooled_cot = inv * gained - pooled * (inv * inv * inv) * (
        jnp.sum(gained * pooled, axis=-1, keepdims=True) / width
    )
    conv_cot = 0.5 * pooled_cot
    high = gain_term.astype(BF).astype(F32)
    low = gain_term - high
    row = lax.broadcasted_iota(jnp.int32, (16, width), 0)
    split = width // 2
    lines = (high[:, :split], low[:, :split], high[:, split:], low[:, split:])
    gains = jnp.zeros((16, split), F32)
    for i, line in enumerate(lines):
        gains = jnp.where(row[:, :split] == i, line, gains)
    fill = split - size - value_cot.shape[1]
    side = jnp.concatenate([key_cot, value_cot, jnp.zeros((tokens, fill), F32)], axis=1)
    first[:tokens] = conv_cot[:, :split].astype(BF)
    first[tokens:] = gains.astype(BF)
    second[:tokens] = conv_cot[:, split:].astype(BF)
    second[tokens:] = side.astype(BF)
    ends = jnp.where(row == 0, conv_cot[:1], jnp.where(row == 1, conv_cot[tokens - 1 :], 0.0))
    edge[...] = ends.astype(BF)


def place(other=0):
    seq, dp = lax.axis_index("seq"), lax.axis_index("dp") ^ (other % 2)
    high, low = seq // 2, (seq % 2) ^ (other // 2)
    return lambda k: ((high ^ k) * 2 + low) * 2 + dp


def chosen(rows, padded, columns, block):
    row = lax.broadcasted_iota(jnp.int32, (padded, columns), 0)
    column = lax.broadcasted_iota(jnp.int32, (padded, columns), 1)
    hit = (column == row + block * rows) & (row < rows)
    return jnp.where(hit, 1.0, 0.0).astype(BF)


def select_kernel(*refs, order, rows, padded):
    own, blocks = refs[0], refs[1:5]
    out, norm_out, even, odd = refs[5:]
    ext, channels = even.shape
    tokens = own.shape[1]
    count = own.shape[0]
    step = split_rows(count, channels)
    norm_out[:, :tokens] = own[...]
    for i in range(1, 4):
        at = 2 * ext + (i - 1) * step
        for c in range(channels // LANES):
            end = min((c + 1) * step, count)
            piece = blocks[i][at : at + end - c * step, c * LANES : (c + 1) * LANES]
            norm_out[c * step : end, i * tokens : (i + 1) * tokens] = piece
    block_of = place()
    pick = jnp.concatenate(
        [chosen(rows, padded, 5 * channels, block_of(k)) for k in order], axis=0
    )
    for i, block in enumerate(blocks):
        even[...] = block[:ext].astype(F32)
        odd[...] = block[ext : 2 * ext].astype(F32)
        pieces = []
        for shift in range(3):
            pieces += [even[shift : shift + tokens].astype(BF), odd[shift : shift + tokens].astype(BF)]
        shifted = jnp.concatenate(
            [jnp.concatenate(pieces[:5], axis=1), jnp.concatenate(pieces[1:], axis=1)], axis=0
        )
        out[:, 2 * i * tokens : 2 * (i + 1) * tokens] = dot_t(pick, shifted).astype(BF)


def query_grad_kernel(pick, first, second, third, fourth, keep, send, right):
    tokens = first.shape[0]
    for i, block in enumerate((first, second, third, fourth)):
        right[i * tokens : (i + 1) * tokens] = block[...]
    count, pad = keep.shape[:2]
    for k in range(2 * count):
        term = dot(pick[k * pad : (k + 1) * pad], right[...])
        if k < count:
            keep[k] = term
        else:
            send[k - count] = term.astype(BF)


def side_rows(norm_rows, size, width):
    return norm_rows * size // width


def put_side(stage, at, part, rows):
    pieces = [part[i : i + rows] for i in range(0, part.shape[0], rows)]
    stage[at : at + rows] = jnp.concatenate(pieces, axis=1)


def get_side(packed, part, rows):
    size = part.shape[1]
    for i in range(part.shape[0] // rows):
        part[i * rows : (i + 1) * rows] = packed[:, i * size : (i + 1) * size]


def stack_cots(blocks, right, tokens):
    for i, block in enumerate(blocks):
        piece = block[:tokens]
        right[2 * i * tokens : (2 * i + 1) * tokens] = piece
        right[(2 * i + 1) * tokens : (2 * i + 2) * tokens] = piece


def conv_first_kernel(*refs, conv_rows, conv_pad):
    pick, blocks, outs, right, stage = refs[0], refs[1:5], refs[5:9], refs[9], refs[10]
    tokens = right.shape[0] // 8
    stack_cots(blocks, right, tokens)
    stage[...] = jnp.zeros(stage.shape, F32)
    for half in range(2):
        gain = None
        for block in blocks:
            lines = block[tokens : tokens + 16].astype(F32)[2 * half : 2 * half + 2]
            term = lines[0:1] + lines[1:2]
            gain = term if gain is None else gain + term
        high = gain.astype(BF).astype(F32)
        at = conv_rows + 2 * half
        stage[at : at + 1] = high
        stage[at + 1 : at + 2] = gain - high
    count = outs[0].shape[0]
    for k in range(4 * count):
        conv = dot(pick[k * conv_pad : (k + 1) * conv_pad], right[...])
        stage[:conv_rows] = conv[:conv_rows]
        out = outs[k // count]
        out[k % count] = stage[...].astype(out.dtype)


def conv_second_kernel(*refs, conv_rows, conv_pad, norm_rows, norm_pad, key_size, value_size):
    pick, norm_pick, blocks, first_send = refs[0], refs[1], refs[2:6], refs[6]
    near_keep, far_keep, near_send, far_send, right, side, stage = refs[7:]
    tokens, width = right.shape[0] // 8, right.shape[1]
    stack_cots(blocks, right, tokens)
    for i, block in enumerate(blocks):
        side[i * tokens : (i + 1) * tokens] = block[tokens:]
    key_rows = side_rows(norm_rows, key_size, width)
    value_rows = side_rows(norm_rows, value_size, width)
    stage[...] = jnp.zeros(stage.shape, F32)
    count, above = first_send.shape[:2]
    near_send[:, :above] = first_send[...]
    for k in range(4 * count):
        conv = dot(pick[k * conv_pad : (k + 1) * conv_pad], right[...])
        stage[:conv_rows] = conv[:conv_rows]
        both = dot(norm_pick[k * norm_pad : (k + 1) * norm_pad], side[...])
        put_side(stage, conv_rows, both[:norm_rows, :key_size], key_rows)
        value = both[:norm_rows, key_size : key_size + value_size]
        put_side(stage, conv_rows + key_rows, value, value_rows)
        if k < 2 * count:
            (near_keep, far_keep)[k // count][k % count] = stage[...]
        elif k < 3 * count:
            near_send[k % count, above:] = stage[...].astype(BF)
        else:
            far_send[k % count] = stage[...].astype(BF)


def first_sum_kernel(keep, near, far, out):
    above = keep.shape[1]
    out[...] = keep[...] + near[:, :above].astype(F32) + far[...].astype(F32)


def combine_kernel(first, second, near, far, out):
    above = first.shape[1]
    out[:, :above] = first[...]
    out[:, above:] = second[...] + near[:, above:].astype(F32) + far[...].astype(F32)


def final_kernel(*refs, conv_parts, above):
    conv, query, key, value, gain, stage = refs[-6:]
    rows, width = conv.shape
    split = width // 2
    count = key.shape[0]
    if conv_parts == 4:
        combine_kernel(*refs[:4], stage)
    else:
        stage[...] = total_of(refs[:conv_parts])
    query[...] = total_of(refs[conv_parts:-6])[0, : query.shape[0]]
    conv[:, :split] = stage[0, :rows]
    conv[:, split:] = stage[0, above : above + rows]
    at = above + rows
    for part in (key, value):
        step = side_rows(count, part.shape[1], split)
        get_side(stage[0, at : at + step], part, step)
        at += step
    lines = stage[0, rows : rows + 4]
    line = jnp.concatenate([lines[0:1] + lines[1:2], lines[2:3] + lines[3:4]], axis=1)
    line = jnp.broadcast_to(line, (8, width))
    start = place()(0) * count
    gain[...] = pltpu.roll(line, lax.rem(width - start, width), 1)[:1, :count]


def input_kernel(x, first, second, pair_first, pair_second, edge, weight, out, ext, mixed):
    tokens = x.shape[0] // 2
    low = lax.axis_index("seq") % 2
    split = first.shape[1]
    for half, own, pair in ((0, first, pair_first), (1, second, pair_second)):
        lanes = slice(half * split, (half + 1) * split)
        ends = edge[:, lanes].astype(F32)
        top = pair[0:16].astype(F32)[0:1]
        bottom = pair[tokens - 16 : tokens].astype(F32)[15:16]
        ext[8 : 8 + tokens, lanes] = own[:tokens].astype(F32)
        ext[7:8, lanes] = jnp.where(low == 0, ends[1:2], bottom)
        ext[8 + tokens : 9 + tokens, lanes] = jnp.where(low == 0, top, ends[0:1])
    back = ext[7 : 7 + tokens].astype(BF)
    here = ext[8 : 8 + tokens].astype(BF)
    ahead = ext[9 : 9 + tokens].astype(BF)
    evens = (ahead, here, here, back, back)
    odds = (ahead, ahead, here, here, back)
    total = None
    for tap in range(5):
        term = dot_t(jnp.concatenate([evens[tap], odds[tap]], axis=0), weight[tap])
        total = term if total is None else total + term
    for c in range(mixed.shape[0]):
        lanes = slice(c * LANES, (c + 1) * LANES)
        mixed[c, pl.ds(0, tokens, stride=2)] = total[:tokens, lanes]
        mixed[c, pl.ds(1, tokens, stride=2)] = total[tokens:, lanes]
        out[:, lanes] = (mixed[c] * gelu_slope(x[:, lanes].astype(F32))).astype(BF)


def on_device(x, conv_weight, norm_gain, wq, wk, wv, cotangent):
    devices = lax.axis_size("seq")
    both_axes = ("seq", "dp")
    x, cotangent = x[0], cotangent[0]
    positions, channels = x.shape
    tokens = positions // 2
    taps, _, width = conv_weight.shape
    key_size, value_size = wk.shape[1], wv.shape[1]
    heads = cotangent.shape[1] // value_size
    scale = key_size ** (-0.5)
    groups = devices // 2
    owners = devices * 2
    conv_rows, norm_rows = taps * channels // owners, width // owners
    conv_pad, norm_pad = round_up(conv_rows, 16), round_up(norm_rows, 16)
    ext = tokens + 16
    gain = norm_gain.reshape(1, width)

    def swap(value, seq_bits, dp_bit=0):
        mask = 2 * seq_bits + dp_bit
        return lax.ppermute(value, both_axes, [(i, i ^ mask) for i in range(owners)])

    def held(value, *until):
        return lax.optimization_barrier((value,) + until)[0]

    def quad(value, *until):
        core = swap(value, 0, 1)
        near = swap(value, 1)
        return [value, core, near, swap(held(near, *until), 0, 1)]

    def fold(parts, name):
        shape = (parts[0].shape[0] // 2,) + parts[0].shape[1:]
        return run(fold_kernel, [(shape, F32), (shape, BF)], parts, name=name)

    def halved(keep, send, bits, name):
        for bit in bits[:-1]:
            keep, send = fold([keep, swap(send, 1 << bit)], name)
        return [keep, swap(send, 1 << bits[-1])]

    bits = list(range(devices.bit_length() - 1))
    order = [mask // 2 for mask in ordered(bits[1:])]
    crossing = [(i, i + 1) for i in range(1, devices - 1, 2)]
    crossing = crossing + [(j, i) for i, j in crossing]
    pad_shape = (channels // LANES, 8 + 2 * ext + 8, LANES)
    ready, ends = run(
        open_kernel,
        [(pad_shape, F32), ((32, channels), BF)],
        [x],
        flops=4 * 10**9,
        name="gelu",
    )
    pair, across = swap(ends, 1), lax.ppermute(ends, "seq", crossing)
    wv = wv.T
    kv, early, normed, pooled = run(
        front_kernel,
        [
            ((5 * tokens // 2, key_size), BF),
            ((2 * ext, channels), BF),
            ((tokens, width), BF),
            ((tokens, width), F32),
        ],
        [ready, pair, across, conv_weight, gain, wk, wv],
        [pltpu.VMEM(pad_shape, F32)],
        flops=2 * positions * taps * channels * width,
        name="front",
    )
    near_kv = [kv] + [swap(kv, 2 * k) for k in range(1, groups)]
    far_kv = [swap(block, 1) for block in near_kv]
    picked = (groups * norm_pad, tokens)
    rows = 2 * ext + 3 * split_rows(picked[0], channels)
    queries, early, pick_own = run(
        lambda *refs: query_kernel(
            *refs, order=order, rows=norm_rows, padded=norm_pad, scale=scale
        ),
        [((tokens, heads * key_size), BF), ((rows, channels), BF), (picked, BF)],
        [normed, wq, early],
        flops=4 * tokens * width * heads * key_size,
        name="queries",
        after=near_kv[1:],
    )
    early = held(early, *far_kv)
    length = devices * tokens
    masks = [2 * k for k in range(groups)] + [2 * k + 1 for k in range(groups)]
    half_block = (groups, 5 * tokens // 4, key_size)
    attended, query_cot, keep_a, send_a, keep_b, send_b = run(
        lambda *refs: attend_kernel(
            *refs,
            blocks=devices,
            masks=[
                [masks.index(m) for m in ordered(way)] for way in (bits, [1, 0] + bits[2:])
            ],
            heads=heads,
            key_size=key_size,
            value_size=value_size,
            scale=scale,
        ),
        [((tokens, heads * value_size), BF), ((tokens, heads * key_size), BF)]
        + [(half_block, F32), (half_block, BF)] * 2,
        [queries, cotangent] + near_kv + far_kv,
        [
            pltpu.VMEM((length, key_size), BF),
            pltpu.VMEM((length, value_size), BF),
            pltpu.VMEM((key_size, length), BF),
            pltpu.VMEM((value_size, length), BF),
            pltpu.VMEM((heads * tokens, key_size), BF),
            pltpu.VMEM((heads * tokens, value_size), BF),
            pltpu.VMEM((length, heads * tokens), BF),
            pltpu.VMEM((length, heads * tokens), BF),
        ],
        flops=6 * tokens * heads * length * (key_size + value_size),
        name="attend",
    )
    early_blocks = quad(early, send_a)
    in_a, in_b = swap(send_a, 1), swap(send_b, 2)
    conv_pick, norm_pick = run(
        lambda *refs: select_kernel(*refs, order=order, rows=conv_rows, padded=conv_pad),
        [((groups * conv_pad, 8 * tokens), BF), ((groups * norm_pad, 4 * tokens), BF)],
        [pick_own] + early_blocks,
        [pltpu.VMEM((ext, channels), F32), pltpu.VMEM((ext, channels), F32)],
        flops=2 * groups * conv_pad * taps * channels * 8 * tokens,
        name="select",
    )
    fourth = (groups // 2,) + half_block[1:]
    keep_a, send_a, keep_b, send_b = run(
        fold_two_kernel,
        [(fourth, F32), (fourth, BF)] * 2,
        [keep_a, in_a, keep_b, in_b],
        name="kv_cot_fold",
        after=[conv_pick],
    )
    in_a, in_b = swap(send_a, 2), swap(send_b, 1)
    query_cot = held(query_cot, early_blocks[3])
    query_near, query_core = swap(query_cot, 1), swap(query_cot, 0, 1)
    query_last = swap(held(query_near, in_a, in_b), 0, 1)
    keep_a = held(keep_a, query_near)
    block = (groups // 4, 5 * tokens // 2, key_size)
    keep, send = run(
        merge_kernel,
        [(block, F32), (block, BF)],
        [keep_a, in_a, keep_b, in_b],
        name="kv_cot_merge",
    )
    (normed_cot,) = run(
        query_cot_kernel,
        [((tokens, width), F32)],
        [query_cot, wq],
        flops=2 * tokens * width * heads * key_size,
        name="query_part",
    )
    kv_cot = halved(keep, send, bits[2:], "kv_cot_fold")
    query_half = (groups // 2, norm_pad, heads * key_size)
    query_keep, query_send = run(
        query_grad_kernel,
        [(query_half, F32), (query_half, BF)],
        [norm_pick, query_cot, query_core, query_near, query_last],
        [pltpu.VMEM((4 * tokens, heads * key_size), BF)],
        flops=2 * groups * norm_pad * 4 * tokens * heads * key_size,
        name="query_grad",
    )
    query_parts = halved(query_keep, query_send, bits[1:], "query_fold")
    first, second, edge = run(
        middle_kernel,
        [
            ((tokens + 16, width // 2), BF),
            ((2 * tokens, width // 2), BF),
            ((16, width), BF),
        ],
        kv_cot + [normed_cot, held(pooled, query_keep), gain, wk, wv],
        flops=2 * tokens * width * (key_size + value_size),
        name="conv_cot",
    )
    near_first, near_second = swap(first, 1), swap(second, 1)
    core_first, core_second = swap(first, 0, 1), swap(second, 0, 1)
    split = width // 2
    side = side_rows(norm_rows, key_size, split) + side_rows(norm_rows, value_size, split)
    above, below = round_up(conv_rows + 4, 16), round_up(conv_rows + side, 16)
    count = groups // 4
    near_keep, far_keep, near_send, far_send = run(
        lambda *refs: conv_first_kernel(*refs, conv_rows=conv_rows, conv_pad=conv_pad),
        [((count, above, split), t) for t in (F32, F32, BF, BF)],
        [conv_pick, first, core_first, near_first, swap(near_first, 0, 1)],
        [pltpu.VMEM((8 * tokens, split), BF), pltpu.VMEM((above, split), F32)],
        flops=groups * conv_pad * 8 * tokens * width,
        name="conv_grad_first",
    )
    far_in = swap(far_send, 2)
    last_second = swap(held(near_second, near_keep), 0, 1)
    near_keep_second, far_keep_second, near_send, far_send = run(
        lambda *refs: conv_second_kernel(
            *refs,
            conv_rows=conv_rows,
            conv_pad=conv_pad,
            norm_rows=norm_rows,
            norm_pad=norm_pad,
            key_size=key_size,
            value_size=value_size,
        ),
        [
            ((count, below, split), F32),
            ((count, below, split), F32),
            ((count, above + below, split), BF),
            ((count, below, split), BF),
        ],
        [conv_pick, norm_pick, second, core_second, near_second, last_second, near_send],
        [
            pltpu.VMEM((8 * tokens, split), BF),
            pltpu.VMEM((4 * tokens, split), BF),
            pltpu.VMEM((below, split), F32),
        ],
        flops=groups * conv_pad * 8 * tokens * width,
        name="conv_grad_second",
    )
    edge_in = lax.ppermute(held(edge, near_keep), "seq", crossing)
    far_in_second = swap(far_send, 2)
    near_in = swap(near_send, 2)
    (far_sum,) = run(
        send_on_kernel,
        [((count, above, split), BF)],
        [far_keep, far_in],
        name="conv_send_on",
    )
    far_last = swap(far_sum, 4)
    (input_grad,) = run(
        input_kernel,
        [((positions, channels), BF)],
        [x, first, second, near_first, near_second, edge_in, conv_weight],
        [
            pltpu.VMEM((tokens + 16, width), F32),
            pltpu.VMEM((channels // LANES, positions, LANES), F32),
        ],
        flops=20 * positions * taps * channels * width,
        name="input_grad",
        after=[far_sum],
    )
    (far_sum,) = run(
        send_on_kernel,
        [((count, below, split), BF)],
        [held(far_keep_second, input_grad), far_in_second],
        name="conv_send_on",
    )
    (first_sum,) = run(
        first_sum_kernel,
        [((count, above, split), F32)],
        [near_keep, near_in, far_last],
        flops=5 * 10**9,
        name="conv_first_sum",
    )
    conv_parts = [first_sum, near_keep_second, near_in, swap(far_sum, 4)]
    chunk = (count, above + below, split)
    if len(bits) > 3:
        keep = run(combine_kernel, [(chunk, F32)], conv_parts, name="conv_combine")[0]
        half = (count // 2,) + chunk[1:]
        keep, send = run(fold_kernel, [(half, F32), (half, BF)], [keep], name="conv_fold")
        conv_parts = halved(keep, send, bits[3:], "conv_fold")
    conv_grad, query_grad, key_grad, value_grad, gain_grad = run(
        lambda *refs: final_kernel(*refs, conv_parts=len(conv_parts), above=above),
        [
            ((conv_rows, width), F32),
            ((norm_rows, heads * key_size), F32),
            ((norm_rows, key_size), F32),
            ((norm_rows, value_size), F32),
            ((1, norm_rows), F32),
        ],
        conv_parts + query_parts,
        [pltpu.VMEM((1,) + chunk[1:], F32)],
        name="final_sum",
    )
    return (
        attended[None],
        input_grad[None],
        conv_grad,
        query_grad,
        key_grad,
        value_grad,
        gain_grad.reshape(norm_rows),
    )


def solution(mesh):
    placed = (
        P(("groups", "dp"), "seq", None),
        P(),
        P(),
        P(),
        P(),
        P(),
        P(("groups", "dp"), "seq", None),
    )
    return jax.shard_map(
        on_device,
        mesh=mesh,
        in_specs=placed,
        out_specs=(
            P(("groups", "dp"), "seq", None),
            P(("groups", "dp"), "seq", None),
            P(("groups", "seq", "dp"), None),
            P(("groups", "seq", "dp"), None),
            P(("groups", "seq", "dp"), None),
            P(("groups", "seq", "dp"), None),
            P(("groups", "seq", "dp")),
        ),
        check_vma=False,
    )
```

```python
import math

import jax
import jax.numpy as jnp
from jax import lax
from jax.experimental import pallas as pl
from jax.experimental.pallas import tpu as pltpu
from jax.sharding import PartitionSpec as P

BF = jnp.bfloat16
F32 = jnp.float32
ROOT = math.sqrt(2.0 / math.pi)
EPS = 1e-06
LANES = 128
VMEM_BYTES = 40 * 2**20


def dot(a, b):
    return lax.dot_general(a, b, (((1,), (0,)), ((), ())), preferred_element_type=F32)


def dot_t(a, b):
    return lax.dot_general(a, b, (((1,), (1,)), ((), ())), preferred_element_type=F32)


def run(body, outs, args, scratch=(), flops=0, name=None, after=()):
    size = sum(math.prod(a.shape) * a.dtype.itemsize for a in args)
    size += sum(math.prod(s) * jnp.dtype(t).itemsize for s, t in outs)
    vmem = pl.BlockSpec(memory_space=pltpu.VMEM)
    rest = pl.BlockSpec(memory_space=pl.ANY)
    count, skip = len(args), len(args) + len(after)

    def whole(*refs):
        body(*refs[:count], *refs[skip:])

    return pl.pallas_call(
        whole,
        out_shape=[jax.ShapeDtypeStruct(s, t) for s, t in outs],
        in_specs=[vmem] * count + [rest] * len(after),
        out_specs=[vmem] * len(outs),
        scratch_shapes=list(scratch),
        compiler_params=pltpu.CompilerParams(vmem_limit_bytes=VMEM_BYTES),
        cost_estimate=pl.CostEstimate(flops=flops, bytes_accessed=size, transcendentals=0),
        name=name,
    )(*args, *after)


def gelu(v):
    return v * (0.5 * (1.0 + jnp.tanh(ROOT * (v + 0.044715 * (v * v * v)))))


def gelu_slope(v):
    tangent = jnp.tanh(ROOT * (v + 0.044715 * v * v * v))
    return 0.5 * (1.0 + tangent) + 0.5 * v * (1.0 - tangent * tangent) * ROOT * (
        1.0 + 3.0 * 0.044715 * v * v
    )


def round_up(value, step):
    return -(-value // step) * step


def pack_kv(keys, values):
    tokens, size = keys.shape
    rest = values[:, size:]
    half = tokens // 2
    tail = jnp.concatenate([rest[:half], rest[half:]], axis=1)
    return jnp.concatenate([keys, values[:, :size], tail], axis=0)


def unpack_values(packed, tokens, size):
    tail = packed[2 * tokens :]
    width = tail.shape[1] // 2
    rest = jnp.concatenate([tail[:, :width], tail[:, width:]], axis=0)
    return jnp.concatenate([packed[tokens : 2 * tokens], rest], axis=1)


def put(ref, start, rows):
    for c in range(ref.shape[0]):
        ref[c, start : start + rows.shape[0]] = rows[:, c * LANES : (c + 1) * LANES]


def every_second(ref, start, count):
    parts = [ref[c, pl.ds(start, count, stride=2)] for c in range(ref.shape[0])]
    return jnp.concatenate(parts, axis=1)


def open_kernel(x, pad, ends):
    positions, channels = x.shape
    ends[:16] = x[:16]
    ends[16:] = x[positions - 16 :]
    put(pad, 0, jnp.zeros((8, channels), F32))
    put(pad, 8, gelu(x[...].astype(F32)).astype(BF).astype(F32))
    put(pad, 8 + positions, jnp.zeros((pad.shape[1] - 8 - positions, channels), F32))


def front_kernel(ready, pair, across, weight, gain, wk, wv, kv_out, early, normed_out, pooled_out, pad):
    tokens = pooled_out.shape[0]
    ext = early.shape[0] // 2
    even = lax.axis_index("seq") % 2 == 0
    pair_wide, across_wide = pair[...].astype(F32), across[...].astype(F32)
    before = jnp.where(even, across_wide[16:], pair_wide[16:])[14:]
    after = jnp.where(even, pair_wide[:16], across_wide[:16])[:2]
    pad[...] = ready[...]
    put(pad, 6, gelu(before).astype(BF).astype(F32))
    put(pad, 8 + 2 * tokens, gelu(after).astype(BF).astype(F32))
    pieces = [every_second(pad, 6 + u, tokens).astype(BF) for u in range(6)]
    total = None
    for tap in range(5):
        rows = jnp.concatenate([pieces[tap], pieces[tap + 1]], axis=0)
        term = dot(rows, weight[tap])
        total = term if total is None else total + term
    pooled = 0.5 * (total[:tokens] + total[tokens:])
    inv = lax.rsqrt(jnp.mean(pooled * pooled, axis=-1, keepdims=True) + EPS)
    normed = (pooled * inv * gain[...]).astype(BF)
    pooled_out[...] = pooled
    normed_out[...] = normed
    kv_out[...] = pack_kv(dot(normed, wk[...]), dot_t(normed, wv[...])).astype(BF)
    early[0:ext] = every_second(pad, 6, ext).astype(BF)
    early[ext : 2 * ext] = every_second(pad, 7, ext).astype(BF)


def ordered(bits):
    masks = [0]
    for bit in reversed(bits):
        masks = masks + [mask | (1 << bit) for mask in masks]
    return masks


def split_rows(rows, columns):
    return round_up(-(-rows * LANES // columns), 16)


def query_kernel(normed, wq, early, out, message, own, *, order, rows, padded, scale):
    width = normed.shape[1]
    value = normed[...]
    out[...] = (dot(value, wq[...]) * scale).astype(BF)
    at, channels = early.shape
    message[:at] = early[...]
    count = len(order) * padded
    step = split_rows(count, channels)
    for i in range(4):
        block_of = place(i)
        pick = [chosen(rows, padded, width, block_of(k)) for k in order]
        part = dot_t(jnp.concatenate(pick, axis=0), value).astype(BF)
        if i == 0:
            own[...] = part
            continue
        for c in range(channels // LANES):
            piece = part[c * step : min((c + 1) * step, count)]
            message[at : at + piece.shape[0], c * LANES : (c + 1) * LANES] = piece
        at += step


def attend_kernel(*refs, blocks, masks, heads, key_size, value_size, scale):
    q, cot = refs[:2]
    parts = refs[2 : 2 + blocks]
    att, dq, keep_a, send_a, keep_b, send_b = refs[2 + blocks : 8 + blocks]
    ks, vs, kt, vt, qs, cs, weights, score_cots = refs[8 + blocks :]
    tokens = q.shape[0]
    half = tokens // 2
    wide = value_size - key_size
    for i, part in enumerate(parts):
        at = i * tokens
        ks[at : at + tokens] = part[:tokens]
        vs[at : at + tokens, :key_size] = part[tokens : 2 * tokens]
        vs[at : at + half, key_size:] = part[2 * tokens :, :wide]
        vs[at + half : at + tokens, key_size:] = part[2 * tokens :, wide:]
        kt[:, at : at + tokens] = ks[at : at + tokens].astype(F32).T.astype(BF)
        vt[:, at : at + tokens] = vs[at : at + tokens].astype(F32).T.astype(BF)
    for pair in range(heads // 2):
        ql, cl = 2 * pair * key_size, 2 * pair * value_size
        rows = slice(2 * pair * tokens, 2 * (pair + 1) * tokens)
        both = cot[:, cl : cl + 2 * value_size]
        qs[rows] = jnp.concatenate(
            [q[:, ql : ql + key_size], q[:, ql + key_size : ql + 2 * key_size]], axis=0
        )
        cs[rows] = jnp.concatenate([both[:, :value_size], both[:, value_size:]], axis=0)
        scores = dot_t(ks[...], qs[rows])
        raised = jnp.exp(scores - jnp.max(scores, axis=0, keepdims=True))
        probs = raised * (1.0 / jnp.sum(raised, axis=0, keepdims=True))
        weights[:, rows] = probs.astype(BF)
        out_t = dot(vt[...], weights[:, rows]).astype(BF).astype(F32)
        delta = jnp.sum(cs[rows].astype(F32).T * out_t, axis=0, keepdims=True)
        score_cots[:, rows] = (probs * (dot_t(vs[...], cs[rows]) - delta)).astype(BF)
        dq_t = dot(kt[...], score_cots[:, rows]) * scale
        out_rows = jnp.concatenate([out_t[:, :tokens].T, out_t[:, tokens:].T], axis=1)
        att[:, cl : cl + 2 * value_size] = out_rows.astype(BF)
        dq_rows = jnp.concatenate([dq_t[:, :tokens].T, dq_t[:, tokens:].T], axis=1)
        dq[:, ql : ql + 2 * key_size] = dq_rows.astype(BF)
    edge = keep_a.shape[1]
    count = blocks // 2
    for i in range(blocks):
        at = slice(i * tokens, (i + 1) * tokens)
        packed = pack_kv(dot(score_cots[at], qs[...]), dot(weights[at], cs[...]))
        for order, keep, send, part in (
            (masks[0], keep_a, send_a, packed[:edge]),
            (masks[1], keep_b, send_b, packed[edge:]),
        ):
            k = order.index(i)
            if k < count:
                keep[k] = part
            else:
                send[k - count] = part.astype(BF)


def total_of(parts):
    total = parts[0][...]
    for part in parts[1:]:
        total = total + part[...].astype(F32)
    return total


def fold_kernel(*refs):
    keep, send = refs[-2:]
    total = total_of(refs[:-2])
    keep[...] = total[: keep.shape[0]]
    send[...] = total[keep.shape[0] :].astype(BF)


def fold_two_kernel(*refs):
    fold_kernel(refs[0], refs[1], refs[4], refs[5])
    fold_kernel(refs[2], refs[3], refs[6], refs[7])


def merge_kernel(keep_a, in_a, keep_b, in_b, keep, send):
    total = jnp.concatenate([total_of((keep_a, in_a)), total_of((keep_b, in_b))], axis=1)
    keep[...] = total[: keep.shape[0]]
    send[...] = total[keep.shape[0] :].astype(BF)


def send_on_kernel(keep, came, out):
    out[...] = (keep[...] + came[...].astype(F32)).astype(BF)


def query_cot_kernel(dq, wq, out):
    out[...] = dot_t(dq[...], wq[...])


def middle_kernel(own, came, part, pooled_in, gain_in, wk, wv, first, second, edge):
    size = own.shape[2]
    tokens, width = pooled_in.shape
    total = (own[0] + came[0].astype(F32)).astype(BF).astype(F32)
    key_cot = total[:tokens]
    value_cot = unpack_values(total, tokens, size)
    normed_cot = part[...] + dot_t(key_cot.astype(BF), wk[...])
    normed_cot = normed_cot + dot(value_cot.astype(BF), wv[...])
    pooled, gain = pooled_in[...], gain_in[...]
    inv = lax.rsqrt(jnp.mean(pooled * pooled, axis=-1, keepdims=True) + EPS)
    gain_term = jnp.sum(normed_cot * pooled * inv, axis=0, keepdims=True)
    gained = gain * normed_cot
    pooled_cot = inv * gained - pooled * (inv * inv * inv) * (
        jnp.sum(gained * pooled, axis=-1, keepdims=True) / width
    )
    conv_cot = 0.5 * pooled_cot
    high = gain_term.astype(BF).astype(F32)
    low = gain_term - high
    row = lax.broadcasted_iota(jnp.int32, (16, width), 0)
    split = width // 2
    lines = (high[:, :split], low[:, :split], high[:, split:], low[:, split:])
    lines += (conv_cot[:1, split:], conv_cot[tokens - 1 :, split:])
    gains = jnp.zeros((16, split), F32)
    for i, line in enumerate(lines):
        gains = jnp.where(row[:, :split] == i, line, gains)
    fill = split - size - value_cot.shape[1]
    side = jnp.concatenate([key_cot, value_cot, jnp.zeros((tokens, fill), F32)], axis=1)
    first[:tokens] = conv_cot[:, :split].astype(BF)
    first[tokens:] = gains.astype(BF)
    second[:tokens] = conv_cot[:, split:].astype(BF)
    second[tokens:] = side.astype(BF)
    ends = jnp.where(row == 0, conv_cot[:1], jnp.where(row == 1, conv_cot[tokens - 1 :], 0.0))
    edge[...] = ends.astype(BF)


def place(other=0):
    seq, dp = lax.axis_index("seq"), lax.axis_index("dp") ^ (other % 2)
    high, low = seq // 2, (seq % 2) ^ (other // 2)
    return lambda k: ((high ^ k) * 2 + low) * 2 + dp


def chosen(rows, padded, columns, block):
    row = lax.broadcasted_iota(jnp.int32, (padded, columns), 0)
    column = lax.broadcasted_iota(jnp.int32, (padded, columns), 1)
    hit = (column == row + block * rows) & (row < rows)
    return jnp.where(hit, 1.0, 0.0).astype(BF)


def select_kernel(*refs, order, rows, padded):
    own, blocks = refs[0], refs[1:5]
    out, norm_out, even, odd = refs[5:]
    ext, channels = even.shape
    tokens = own.shape[1]
    count = own.shape[0]
    step = split_rows(count, channels)
    norm_out[:, :tokens] = own[...]
    for i in range(1, 4):
        at = 2 * ext + (i - 1) * step
        for c in range(channels // LANES):
            end = min((c + 1) * step, count)
            piece = blocks[i][at : at + end - c * step, c * LANES : (c + 1) * LANES]
            norm_out[c * step : end, i * tokens : (i + 1) * tokens] = piece
    block_of = place()
    pick = jnp.concatenate(
        [chosen(rows, padded, 5 * channels, block_of(k)) for k in order], axis=0
    )
    for i, block in enumerate(blocks):
        even[...] = block[:ext].astype(F32)
        odd[...] = block[ext : 2 * ext].astype(F32)
        pieces = []
        for shift in range(3):
            pieces += [even[shift : shift + tokens].astype(BF), odd[shift : shift + tokens].astype(BF)]
        shifted = jnp.concatenate(
            [jnp.concatenate(pieces[:5], axis=1), jnp.concatenate(pieces[1:], axis=1)], axis=0
        )
        out[:, 2 * i * tokens : 2 * (i + 1) * tokens] = dot_t(pick, shifted).astype(BF)


def query_grad_kernel(pick, first, second, third, fourth, keep, send, right):
    tokens = first.shape[0]
    for i, block in enumerate((first, second, third, fourth)):
        right[i * tokens : (i + 1) * tokens] = block[...]
    count, pad = keep.shape[:2]
    for k in range(2 * count):
        term = dot(pick[k * pad : (k + 1) * pad], right[...])
        if k < count:
            keep[k] = term
        else:
            send[k - count] = term.astype(BF)


def side_rows(norm_rows, size, width):
    return norm_rows * size // width


def put_side(stage, at, part, rows):
    pieces = [part[i : i + rows] for i in range(0, part.shape[0], rows)]
    stage[at : at + rows] = jnp.concatenate(pieces, axis=1)


def get_side(packed, part, rows):
    size = part.shape[1]
    for i in range(part.shape[0] // rows):
        part[i * rows : (i + 1) * rows] = packed[:, i * size : (i + 1) * size]


def stack_cots(blocks, right, tokens):
    for i, block in enumerate(blocks):
        piece = block[:tokens]
        right[2 * i * tokens : (2 * i + 1) * tokens] = piece
        right[(2 * i + 1) * tokens : (2 * i + 2) * tokens] = piece


def conv_first_kernel(*refs, conv_rows, conv_pad):
    pick, blocks, outs, right, stage = refs[0], refs[1:5], refs[5:9], refs[9], refs[10]
    tokens = right.shape[0] // 8
    stack_cots(blocks, right, tokens)
    stage[...] = jnp.zeros(stage.shape, F32)
    for half in range(2):
        gain = None
        for block in blocks:
            lines = block[tokens : tokens + 16].astype(F32)[2 * half : 2 * half + 2]
            term = lines[0:1] + lines[1:2]
            gain = term if gain is None else gain + term
        high = gain.astype(BF).astype(F32)
        at = conv_rows + 2 * half
        stage[at : at + 1] = high
        stage[at + 1 : at + 2] = gain - high
    count, above = outs[0].shape[:2]
    even = lax.axis_index("seq") % 2 == 0
    own, pair = blocks[0], blocks[2]
    tops = [b[0:16].astype(F32)[0:1] for b in (own, pair)]
    bottoms = [b[tokens - 16 : tokens].astype(F32)[15:16] for b in (own, pair)]
    rests = [b[tokens : tokens + 16].astype(F32)[4:6] for b in (own, pair)]
    for k in range(4 * count):
        conv = dot(pick[k * conv_pad : (k + 1) * conv_pad], right[...])
        stage[:conv_rows] = conv[:conv_rows]
        if k == 3 * count:
            stage[above - 4 : above - 3] = jnp.where(even, tops[0], tops[1])
            stage[above - 3 : above - 2] = jnp.where(even, rests[0][0:1], rests[1][0:1])
            stage[above - 2 : above - 1] = jnp.where(even, bottoms[1], bottoms[0])
            stage[above - 1 : above] = jnp.where(even, rests[1][1:2], rests[0][1:2])
        out = outs[k // count]
        out[k % count] = stage[...].astype(out.dtype)


def conv_second_kernel(*refs, conv_rows, conv_pad, norm_rows, norm_pad, key_size, value_size):
    pick, norm_pick, blocks, first_send = refs[0], refs[1], refs[2:6], refs[6]
    near_keep, far_keep, near_send, far_send, right, side, stage = refs[7:]
    tokens, width = right.shape[0] // 8, right.shape[1]
    stack_cots(blocks, right, tokens)
    for i, block in enumerate(blocks):
        side[i * tokens : (i + 1) * tokens] = block[tokens:]
    key_rows = side_rows(norm_rows, key_size, width)
    value_rows = side_rows(norm_rows, value_size, width)
    stage[...] = jnp.zeros(stage.shape, F32)
    count, above = first_send.shape[:2]
    near_send[:, :above] = first_send[...]
    for k in range(4 * count):
        conv = dot(pick[k * conv_pad : (k + 1) * conv_pad], right[...])
        stage[:conv_rows] = conv[:conv_rows]
        both = dot(norm_pick[k * norm_pad : (k + 1) * norm_pad], side[...])
        put_side(stage, conv_rows, both[:norm_rows, :key_size], key_rows)
        value = both[:norm_rows, key_size : key_size + value_size]
        put_side(stage, conv_rows + key_rows, value, value_rows)
        if k < 2 * count:
            (near_keep, far_keep)[k // count][k % count] = stage[...]
        elif k < 3 * count:
            near_send[k % count, above:] = stage[...].astype(BF)
        else:
            far_send[k % count] = stage[...].astype(BF)


def first_sum_kernel(keep, near, far, out):
    above = keep.shape[1]
    out[...] = keep[...] + near[:, :above].astype(F32) + far[...].astype(F32)


def combine_kernel(first, second, near, far, out):
    above = first.shape[1]
    out[:, :above] = first[...]
    out[:, above:] = second[...] + near[:, above:].astype(F32) + far[...].astype(F32)


def final_kernel(*refs, conv_parts, above):
    conv, query, key, value, gain, stage = refs[-6:]
    rows, width = conv.shape
    split = width // 2
    count = key.shape[0]
    if conv_parts == 4:
        combine_kernel(*refs[:4], stage)
    else:
        stage[...] = total_of(refs[:conv_parts])
    query[...] = total_of(refs[conv_parts:-6])[0, : query.shape[0]]
    conv[:, :split] = stage[0, :rows]
    conv[:, split:] = stage[0, above : above + rows]
    at = above + rows
    for part in (key, value):
        step = side_rows(count, part.shape[1], split)
        get_side(stage[0, at : at + step], part, step)
        at += step
    lines = stage[0, rows : rows + 4]
    line = jnp.concatenate([lines[0:1] + lines[1:2], lines[2:3] + lines[3:4]], axis=1)
    line = jnp.broadcast_to(line, (8, width))
    start = place()(0) * count
    gain[...] = pltpu.roll(line, lax.rem(width - start, width), 1)[:1, :count]


def input_kernel(*refs):
    x, first, second, pair_first, pair_second, one, three, weight, out, ext, mixed = refs
    tokens = x.shape[0] // 2
    seq, devices = lax.axis_index("seq"), lax.axis_size("seq")
    low, high = seq % 2, seq // 2
    split = first.shape[1]
    above = one.shape[1]
    one_rows = one[0, above - 16 :].astype(F32)[12:]
    three_rows = three[0, above - 16 :].astype(F32)[12:]
    heads = jnp.where(high % 2 == 0, one_rows[:2], three_rows[:2])
    tails = jnp.where(high % 2 == 0, three_rows[2:], one_rows[2:])
    heads = jnp.where(seq == devices - 1, 0.0, heads)
    tails = jnp.where(seq == 0, 0.0, tails)
    for half, own, pair in ((0, first, pair_first), (1, second, pair_second)):
        lanes = slice(half * split, (half + 1) * split)
        top = pair[0:16].astype(F32)[0:1]
        bottom = pair[tokens - 16 : tokens].astype(F32)[15:16]
        ext[8 : 8 + tokens, lanes] = own[:tokens].astype(F32)
        ext[7:8, lanes] = jnp.where(low == 0, tails[half : half + 1], bottom)
        ext[8 + tokens : 9 + tokens, lanes] = jnp.where(low == 0, top, heads[half : half + 1])
    back = ext[7 : 7 + tokens].astype(BF)
    here = ext[8 : 8 + tokens].astype(BF)
    ahead = ext[9 : 9 + tokens].astype(BF)
    evens = (ahead, here, here, back, back)
    odds = (ahead, ahead, here, here, back)
    total = None
    for tap in range(5):
        term = dot_t(jnp.concatenate([evens[tap], odds[tap]], axis=0), weight[tap])
        total = term if total is None else total + term
    for c in range(mixed.shape[0]):
        lanes = slice(c * LANES, (c + 1) * LANES)
        mixed[c, pl.ds(0, tokens, stride=2)] = total[:tokens, lanes]
        mixed[c, pl.ds(1, tokens, stride=2)] = total[tokens:, lanes]
        out[:, lanes] = (mixed[c] * gelu_slope(x[:, lanes].astype(F32))).astype(BF)


def on_device(x, conv_weight, norm_gain, wq, wk, wv, cotangent):
    devices = lax.axis_size("seq")
    both_axes = ("seq", "dp")
    x, cotangent = x[0], cotangent[0]
    positions, channels = x.shape
    tokens = positions // 2
    taps, _, width = conv_weight.shape
    key_size, value_size = wk.shape[1], wv.shape[1]
    heads = cotangent.shape[1] // value_size
    scale = key_size ** (-0.5)
    groups = devices // 2
    owners = devices * 2
    conv_rows, norm_rows = taps * channels // owners, width // owners
    conv_pad, norm_pad = round_up(conv_rows, 16), round_up(norm_rows, 16)
    ext = tokens + 16
    gain = norm_gain.reshape(1, width)

    def swap(value, seq_bits, dp_bit=0):
        mask = 2 * seq_bits + dp_bit
        return lax.ppermute(value, both_axes, [(i, i ^ mask) for i in range(owners)])

    def held(value, *until):
        return lax.optimization_barrier((value,) + until)[0]

    def quad(value, *until):
        core = swap(value, 0, 1)
        near = swap(value, 1)
        return [value, core, near, swap(held(near, *until), 0, 1)]

    def fold(parts, name):
        shape = (parts[0].shape[0] // 2,) + parts[0].shape[1:]
        return run(fold_kernel, [(shape, F32), (shape, BF)], parts, name=name)

    def halved(keep, send, bits, name):
        for bit in bits[:-1]:
            keep, send = fold([keep, swap(send, 1 << bit)], name)
        return [keep, swap(send, 1 << bits[-1])]

    bits = list(range(devices.bit_length() - 1))
    order = [mask // 2 for mask in ordered(bits[1:])]
    crossing = [(i, i + 1) for i in range(1, devices - 1, 2)]
    crossing = crossing + [(j, i) for i, j in crossing]
    pad_shape = (channels // LANES, 8 + 2 * ext + 8, LANES)
    ready, ends = run(
        open_kernel,
        [(pad_shape, F32), ((32, channels), BF)],
        [x],
        flops=4 * 10**9,
        name="gelu",
    )
    pair, across = swap(ends, 1), lax.ppermute(ends, "seq", crossing)
    wv = wv.T
    kv, early, normed, pooled = run(
        front_kernel,
        [
            ((5 * tokens // 2, key_size), BF),
            ((2 * ext, channels), BF),
            ((tokens, width), BF),
            ((tokens, width), F32),
        ],
        [ready, pair, across, conv_weight, gain, wk, wv],
        [pltpu.VMEM(pad_shape, F32)],
        flops=2 * positions * taps * channels * width,
        name="front",
    )
    near_kv = [kv] + [swap(kv, 2 * k) for k in range(1, groups)]
    far_kv = [swap(block, 1) for block in near_kv]
    picked = (groups * norm_pad, tokens)
    rows = 2 * ext + 3 * split_rows(picked[0], channels)
    queries, early, pick_own = run(
        lambda *refs: query_kernel(
            *refs, order=order, rows=norm_rows, padded=norm_pad, scale=scale
        ),
        [((tokens, heads * key_size), BF), ((rows, channels), BF), (picked, BF)],
        [normed, wq, early],
        flops=4 * tokens * width * heads * key_size,
        name="queries",
        after=near_kv[1:],
    )
    early = held(early, *far_kv)
    length = devices * tokens
    masks = [2 * k for k in range(groups)] + [2 * k + 1 for k in range(groups)]
    half_block = (groups, 5 * tokens // 4, key_size)
    attended, query_cot, keep_a, send_a, keep_b, send_b = run(
        lambda *refs: attend_kernel(
            *refs,
            blocks=devices,
            masks=[
                [masks.index(m) for m in ordered(way)] for way in (bits, [1, 0] + bits[2:])
            ],
            heads=heads,
            key_size=key_size,
            value_size=value_size,
            scale=scale,
        ),
        [((tokens, heads * value_size), BF), ((tokens, heads * key_size), BF)]
        + [(half_block, F32), (half_block, BF)] * 2,
        [queries, cotangent] + near_kv + far_kv,
        [
            pltpu.VMEM((length, key_size), BF),
            pltpu.VMEM((length, value_size), BF),
            pltpu.VMEM((key_size, length), BF),
            pltpu.VMEM((value_size, length), BF),
            pltpu.VMEM((heads * tokens, key_size), BF),
            pltpu.VMEM((heads * tokens, value_size), BF),
            pltpu.VMEM((length, heads * tokens), BF),
            pltpu.VMEM((length, heads * tokens), BF),
        ],
        flops=6 * tokens * heads * length * (key_size + value_size),
        name="attend",
    )
    in_a, in_b = swap(send_a, 1), swap(send_b, 2)
    early_blocks = quad(early, send_a)
    conv_pick, norm_pick = run(
        lambda *refs: select_kernel(*refs, order=order, rows=conv_rows, padded=conv_pad),
        [((groups * conv_pad, 8 * tokens), BF), ((groups * norm_pad, 4 * tokens), BF)],
        [pick_own] + early_blocks,
        [pltpu.VMEM((ext, channels), F32), pltpu.VMEM((ext, channels), F32)],
        flops=2 * groups * conv_pad * taps * channels * 8 * tokens,
        name="select",
    )
    fourth = (groups // 2,) + half_block[1:]
    keep_a, send_a, keep_b, send_b = run(
        fold_two_kernel,
        [(fourth, F32), (fourth, BF)] * 2,
        [keep_a, in_a, keep_b, in_b],
        name="kv_cot_fold",
        after=[conv_pick],
    )
    in_a, in_b = swap(send_a, 2), swap(send_b, 1)
    block = (groups // 4, 5 * tokens // 2, key_size)
    keep, send = run(
        merge_kernel,
        [(block, F32), (block, BF)],
        [keep_a, in_a, keep_b, in_b],
        name="kv_cot_merge",
    )
    (normed_cot,) = run(
        query_cot_kernel,
        [((tokens, width), F32)],
        [query_cot, wq],
        flops=2 * tokens * width * heads * key_size,
        name="query_part",
    )
    query_cot = held(query_cot, keep)
    query_near, query_core = swap(query_cot, 1), swap(query_cot, 0, 1)
    kv_cot = halved(keep, send, bits[2:], "kv_cot_fold")
    first, second, edge = run(
        middle_kernel,
        [
            ((tokens + 16, width // 2), BF),
            ((2 * tokens, width // 2), BF),
            ((16, width), BF),
        ],
        kv_cot + [normed_cot, pooled, gain, wk, wv],
        flops=2 * tokens * width * (key_size + value_size),
        name="conv_cot",
    )
    near_first, near_second = swap(first, 1), swap(second, 1)
    query_last = swap(held(query_near, first), 0, 1)
    query_half = (groups // 2, norm_pad, heads * key_size)
    query_keep, query_send = run(
        query_grad_kernel,
        [(query_half, F32), (query_half, BF)],
        [norm_pick, query_cot, query_core, query_near, query_last],
        [pltpu.VMEM((4 * tokens, heads * key_size), BF)],
        flops=2 * groups * norm_pad * 4 * tokens * heads * key_size,
        name="query_grad",
    )
    query_parts = halved(query_keep, query_send, bits[1:], "query_fold")
    core_first, core_second = swap(first, 0, 1), swap(second, 0, 1)
    split = width // 2
    side = side_rows(norm_rows, key_size, split) + side_rows(norm_rows, value_size, split)
    above, below = round_up(conv_rows + 8, 16), round_up(conv_rows + side, 16)
    count = groups // 4
    last_first = swap(held(near_first, query_keep), 0, 1)
    near_keep, far_keep, near_send, far_send = run(
        lambda *refs: conv_first_kernel(*refs, conv_rows=conv_rows, conv_pad=conv_pad),
        [((count, above, split), t) for t in (F32, F32, BF, BF)],
        [conv_pick, first, core_first, near_first, last_first],
        [pltpu.VMEM((8 * tokens, split), BF), pltpu.VMEM((above, split), F32)],
        flops=groups * conv_pad * 8 * tokens * width,
        name="conv_grad_first",
    )
    far_in = swap(far_send, 2)
    last_second = swap(held(near_second, near_keep), 0, 1)
    near_keep_second, far_keep_second, near_send, far_send = run(
        lambda *refs: conv_second_kernel(
            *refs,
            conv_rows=conv_rows,
            conv_pad=conv_pad,
            norm_rows=norm_rows,
            norm_pad=norm_pad,
            key_size=key_size,
            value_size=value_size,
        ),
        [
            ((count, below, split), F32),
            ((count, below, split), F32),
            ((count, above + below, split), BF),
            ((count, below, split), BF),
        ],
        [held(conv_pick, query_parts[0]), norm_pick, second, core_second, near_second, last_second, near_send],
        [
            pltpu.VMEM((8 * tokens, split), BF),
            pltpu.VMEM((4 * tokens, split), BF),
            pltpu.VMEM((below, split), F32),
        ],
        flops=groups * conv_pad * 8 * tokens * width,
        name="conv_grad_second",
    )
    far_in_second = swap(far_send, 2)
    near_in = swap(near_send, 2)
    (far_sum,) = run(
        send_on_kernel,
        [((count, above, split), BF)],
        [far_keep, far_in],
        name="conv_send_on",
    )
    far_last = swap(far_sum, 4)
    edges = [far_in, far_last]
    if len(bits) > 3:
        came = lax.ppermute(edge, "seq", crossing)
        rows = jnp.concatenate([came[:1, :split], came[:1, split:], came[1:2, :split], came[1:2, split:]])
        edges = [jnp.pad(rows, ((above - 4, 0), (0, 0)))[None]] * 2
    (input_grad,) = run(
        input_kernel,
        [((positions, channels), BF)],
        [x, first, second, near_first, near_second] + edges + [conv_weight],
        [
            pltpu.VMEM((tokens + 16, width), F32),
            pltpu.VMEM((channels // LANES, positions, LANES), F32),
        ],
        flops=20 * positions * taps * channels * width,
        name="input_grad",
    )
    (far_sum,) = run(
        send_on_kernel,
        [((count, below, split), BF)],
        [far_keep_second, far_in_second],
        name="conv_send_on",
    )
    (first_sum,) = run(
        first_sum_kernel,
        [((count, above, split), F32)],
        [near_keep, near_in, far_last],
        flops=5 * 10**9,
        name="conv_first_sum",
    )
    conv_parts = [first_sum, near_keep_second, near_in, swap(far_sum, 4)]
    chunk = (count, above + below, split)
    if len(bits) > 3:
        keep = run(combine_kernel, [(chunk, F32)], conv_parts, name="conv_combine")[0]
        half = (count // 2,) + chunk[1:]
        keep, send = run(fold_kernel, [(half, F32), (half, BF)], [keep], name="conv_fold")
        conv_parts = halved(keep, send, bits[3:], "conv_fold")
    conv_grad, query_grad, key_grad, value_grad, gain_grad = run(
        lambda *refs: final_kernel(*refs, conv_parts=len(conv_parts), above=above),
        [
            ((conv_rows, width), F32),
            ((norm_rows, heads * key_size), F32),
            ((norm_rows, key_size), F32),
            ((norm_rows, value_size), F32),
            ((1, norm_rows), F32),
        ],
        conv_parts + query_parts,
        [pltpu.VMEM((1,) + chunk[1:], F32)],
        name="final_sum",
    )
    return (
        attended[None],
        input_grad[None],
        conv_grad,
        query_grad,
        key_grad,
        value_grad,
        gain_grad.reshape(norm_rows),
    )


def solution(mesh):
    placed = (
        P(("groups", "dp"), "seq", None),
        P(),
        P(),
        P(),
        P(),
        P(),
        P(("groups", "dp"), "seq", None),
    )
    return jax.shard_map(
        on_device,
        mesh=mesh,
        in_specs=placed,
        out_specs=(
            P(("groups", "dp"), "seq", None),
            P(("groups", "dp"), "seq", None),
            P(("groups", "seq", "dp"), None),
            P(("groups", "seq", "dp"), None),
            P(("groups", "seq", "dp"), None),
            P(("groups", "seq", "dp"), None),
            P(("groups", "seq", "dp")),
        ),
        check_vma=False,
    )
```

```python
import math

import jax
import jax.numpy as jnp
from jax import lax
from jax.experimental import pallas as pl
from jax.experimental.pallas import tpu as pltpu
from jax.sharding import PartitionSpec as P

BF = jnp.bfloat16
F32 = jnp.float32
ROOT = math.sqrt(2.0 / math.pi)
EPS = 1e-06
LANES = 128
VMEM_BYTES = 40 * 2**20


def dot(a, b):
    return lax.dot_general(a, b, (((1,), (0,)), ((), ())), preferred_element_type=F32)


def dot_t(a, b):
    return lax.dot_general(a, b, (((1,), (1,)), ((), ())), preferred_element_type=F32)


def run(body, outs, args, scratch=(), flops=0, name=None, after=()):
    size = sum(math.prod(a.shape) * a.dtype.itemsize for a in args)
    size += sum(math.prod(s) * jnp.dtype(t).itemsize for s, t in outs)
    vmem = pl.BlockSpec(memory_space=pltpu.VMEM)
    rest = pl.BlockSpec(memory_space=pl.ANY)
    count, skip = len(args), len(args) + len(after)

    def whole(*refs):
        body(*refs[:count], *refs[skip:])

    return pl.pallas_call(
        whole,
        out_shape=[jax.ShapeDtypeStruct(s, t) for s, t in outs],
        in_specs=[vmem] * count + [rest] * len(after),
        out_specs=[vmem] * len(outs),
        scratch_shapes=list(scratch),
        compiler_params=pltpu.CompilerParams(vmem_limit_bytes=VMEM_BYTES),
        cost_estimate=pl.CostEstimate(flops=flops, bytes_accessed=size, transcendentals=0),
        name=name,
    )(*args, *after)


def gelu(v):
    return v * (0.5 * (1.0 + jnp.tanh(ROOT * (v + 0.044715 * (v * v * v)))))


def gelu_slope(v):
    tangent = jnp.tanh(ROOT * (v + 0.044715 * v * v * v))
    return 0.5 * (1.0 + tangent) + 0.5 * v * (1.0 - tangent * tangent) * ROOT * (
        1.0 + 3.0 * 0.044715 * v * v
    )


def round_up(value, step):
    return -(-value // step) * step


def pack_kv(keys, values):
    tokens, size = keys.shape
    rest = values[:, size:]
    half = tokens // 2
    tail = jnp.concatenate([rest[:half], rest[half:]], axis=1)
    return jnp.concatenate([keys, values[:, :size], tail], axis=0)


def unpack_values(packed, tokens, size):
    tail = packed[2 * tokens :]
    width = tail.shape[1] // 2
    rest = jnp.concatenate([tail[:, :width], tail[:, width:]], axis=0)
    return jnp.concatenate([packed[tokens : 2 * tokens], rest], axis=1)


def put(ref, start, rows):
    for c in range(ref.shape[0]):
        ref[c, start : start + rows.shape[0]] = rows[:, c * LANES : (c + 1) * LANES]


def every_second(ref, start, count):
    parts = [ref[c, pl.ds(start, count, stride=2)] for c in range(ref.shape[0])]
    return jnp.concatenate(parts, axis=1)


def open_kernel(x, pad, ends):
    positions, channels = x.shape
    ends[:16] = x[:16]
    ends[16:] = x[positions - 16 :]
    put(pad, 0, jnp.zeros((8, channels), F32))
    put(pad, 8, gelu(x[...].astype(F32)).astype(BF).astype(F32))
    put(pad, 8 + positions, jnp.zeros((pad.shape[1] - 8 - positions, channels), F32))


def front_kernel(ready, pair, across, weight, gain, wk, wv, kv_out, early, normed_out, pooled_out, pad):
    tokens = pooled_out.shape[0]
    ext = early.shape[0] // 2
    even = lax.axis_index("seq") % 2 == 0
    pair_wide, across_wide = pair[...].astype(F32), across[...].astype(F32)
    before = jnp.where(even, across_wide[16:], pair_wide[16:])[14:]
    after = jnp.where(even, pair_wide[:16], across_wide[:16])[:2]
    pad[...] = ready[...]
    put(pad, 6, gelu(before).astype(BF).astype(F32))
    put(pad, 8 + 2 * tokens, gelu(after).astype(BF).astype(F32))
    pieces = [every_second(pad, 6 + u, tokens).astype(BF) for u in range(6)]
    total = None
    for tap in range(5):
        rows = jnp.concatenate([pieces[tap], pieces[tap + 1]], axis=0)
        term = dot(rows, weight[tap])
        total = term if total is None else total + term
    pooled = 0.5 * (total[:tokens] + total[tokens:])
    inv = lax.rsqrt(jnp.mean(pooled * pooled, axis=-1, keepdims=True) + EPS)
    normed = (pooled * inv * gain[...]).astype(BF)
    pooled_out[...] = pooled
    normed_out[...] = normed
    kv_out[...] = pack_kv(dot(normed, wk[...]), dot_t(normed, wv[...])).astype(BF)
    early[0:ext] = every_second(pad, 6, ext).astype(BF)
    early[ext : 2 * ext] = every_second(pad, 7, ext).astype(BF)


def ordered(bits):
    masks = [0]
    for bit in reversed(bits):
        masks = masks + [mask | (1 << bit) for mask in masks]
    return masks


def split_rows(rows, columns):
    return round_up(-(-rows * LANES // columns), 16)


def query_kernel(normed, wq, early, out, message, own, *, order, rows, padded, scale):
    width = normed.shape[1]
    value = normed[...]
    out[...] = (dot(value, wq[...]) * scale).astype(BF)
    at, channels = early.shape
    message[:at] = early[...]
    count = len(order) * padded
    step = split_rows(count, channels)
    for i in range(4):
        block_of = place(i)
        pick = [chosen(rows, padded, width, block_of(k)) for k in order]
        part = dot_t(jnp.concatenate(pick, axis=0), value).astype(BF)
        if i == 0:
            own[...] = part
            continue
        for c in range(channels // LANES):
            piece = part[c * step : min((c + 1) * step, count)]
            message[at : at + piece.shape[0], c * LANES : (c + 1) * LANES] = piece
        at += step


def attend_kernel(*refs, blocks, masks, heads, key_size, value_size, scale):
    q, cot = refs[:2]
    parts = refs[2 : 2 + blocks]
    att, dq, keep_a, send_a, keep_b, send_b = refs[2 + blocks : 8 + blocks]
    ks, vs, kt, vt, qs, cs, weights, score_cots = refs[8 + blocks :]
    tokens = q.shape[0]
    half = tokens // 2
    wide = value_size - key_size
    for i, part in enumerate(parts):
        at = i * tokens
        ks[at : at + tokens] = part[:tokens]
        vs[at : at + tokens, :key_size] = part[tokens : 2 * tokens]
        vs[at : at + half, key_size:] = part[2 * tokens :, :wide]
        vs[at + half : at + tokens, key_size:] = part[2 * tokens :, wide:]
        kt[:, at : at + tokens] = ks[at : at + tokens].astype(F32).T.astype(BF)
        vt[:, at : at + tokens] = vs[at : at + tokens].astype(F32).T.astype(BF)
    for pair in range(heads // 2):
        ql, cl = 2 * pair * key_size, 2 * pair * value_size
        rows = slice(2 * pair * tokens, 2 * (pair + 1) * tokens)
        both = cot[:, cl : cl + 2 * value_size]
        qs[rows] = jnp.concatenate(
            [q[:, ql : ql + key_size], q[:, ql + key_size : ql + 2 * key_size]], axis=0
        )
        cs[rows] = jnp.concatenate([both[:, :value_size], both[:, value_size:]], axis=0)
        scores = dot_t(ks[...], qs[rows])
        raised = jnp.exp(scores - jnp.max(scores, axis=0, keepdims=True))
        probs = raised * (1.0 / jnp.sum(raised, axis=0, keepdims=True))
        weights[:, rows] = probs.astype(BF)
        out_t = dot(vt[...], weights[:, rows]).astype(BF).astype(F32)
        delta = jnp.sum(cs[rows].astype(F32).T * out_t, axis=0, keepdims=True)
        score_cots[:, rows] = (probs * (dot_t(vs[...], cs[rows]) - delta)).astype(BF)
        dq_t = dot(kt[...], score_cots[:, rows]) * scale
        out_rows = jnp.concatenate([out_t[:, :tokens].T, out_t[:, tokens:].T], axis=1)
        att[:, cl : cl + 2 * value_size] = out_rows.astype(BF)
        dq_rows = jnp.concatenate([dq_t[:, :tokens].T, dq_t[:, tokens:].T], axis=1)
        dq[:, ql : ql + 2 * key_size] = dq_rows.astype(BF)
    edge = keep_a.shape[1]
    count = blocks // 2
    for i in range(blocks):
        at = slice(i * tokens, (i + 1) * tokens)
        packed = pack_kv(dot(score_cots[at], qs[...]), dot(weights[at], cs[...]))
        for order, keep, send, part in (
            (masks[0], keep_a, send_a, packed[:edge]),
            (masks[1], keep_b, send_b, packed[edge:]),
        ):
            k = order.index(i)
            if k < count:
                keep[k] = part
            else:
                send[k - count] = part.astype(BF)


def total_of(parts):
    total = parts[0][...]
    for part in parts[1:]:
        total = total + part[...].astype(F32)
    return total


def fold_kernel(*refs):
    keep, send = refs[-2:]
    total = total_of(refs[:-2])
    keep[...] = total[: keep.shape[0]]
    send[...] = total[keep.shape[0] :].astype(BF)


def fold_two_kernel(*refs):
    fold_kernel(refs[0], refs[1], refs[4], refs[5])
    fold_kernel(refs[2], refs[3], refs[6], refs[7])


def merge_kernel(keep_a, in_a, keep_b, in_b, keep, send):
    total = jnp.concatenate([total_of((keep_a, in_a)), total_of((keep_b, in_b))], axis=1)
    keep[...] = total[: keep.shape[0]]
    send[...] = total[keep.shape[0] :].astype(BF)


def send_on_kernel(keep, came, out):
    out[...] = (keep[...] + came[...].astype(F32)).astype(BF)


def query_cot_kernel(dq, wq, out):
    out[...] = dot_t(dq[...], wq[...])


def middle_kernel(own, came, part, pooled_in, gain_in, wk, wv, first, second, *edges):
    size = own.shape[2]
    tokens, width = pooled_in.shape
    total = (own[0] + came[0].astype(F32)).astype(BF).astype(F32)
    key_cot = total[:tokens]
    value_cot = unpack_values(total, tokens, size)
    normed_cot = part[...] + dot_t(key_cot.astype(BF), wk[...])
    normed_cot = normed_cot + dot(value_cot.astype(BF), wv[...])
    pooled, gain = pooled_in[...], gain_in[...]
    inv = lax.rsqrt(jnp.mean(pooled * pooled, axis=-1, keepdims=True) + EPS)
    gain_term = jnp.sum(normed_cot * pooled * inv, axis=0, keepdims=True)
    gained = gain * normed_cot
    pooled_cot = inv * gained - pooled * (inv * inv * inv) * (
        jnp.sum(gained * pooled, axis=-1, keepdims=True) / width
    )
    conv_cot = 0.5 * pooled_cot
    high = gain_term.astype(BF).astype(F32)
    low = gain_term - high
    row = lax.broadcasted_iota(jnp.int32, (16, width), 0)
    split = width // 2
    lines = (high[:, :split], low[:, :split], high[:, split:], low[:, split:])
    lines += (conv_cot[:1, split:], conv_cot[tokens - 1 :, split:])
    gains = jnp.zeros((16, split), F32)
    for i, line in enumerate(lines):
        gains = jnp.where(row[:, :split] == i, line, gains)
    fill = split - size - value_cot.shape[1]
    side = jnp.concatenate([key_cot, value_cot, jnp.zeros((tokens, fill), F32)], axis=1)
    first[:tokens] = conv_cot[:, :split].astype(BF)
    first[tokens:] = gains.astype(BF)
    second[:tokens] = conv_cot[:, split:].astype(BF)
    second[tokens:] = side.astype(BF)
    for edge in edges:
        ends = jnp.where(row == 0, conv_cot[:1], jnp.where(row == 1, conv_cot[tokens - 1 :], 0.0))
        edge[...] = ends.astype(BF)


def place(other=0):
    seq, dp = lax.axis_index("seq"), lax.axis_index("dp") ^ (other % 2)
    high, low = seq // 2, (seq % 2) ^ (other // 2)
    return lambda k: ((high ^ k) * 2 + low) * 2 + dp


def chosen(rows, padded, columns, block):
    row = lax.broadcasted_iota(jnp.int32, (padded, columns), 0)
    column = lax.broadcasted_iota(jnp.int32, (padded, columns), 1)
    hit = (column == row + block * rows) & (row < rows)
    return jnp.where(hit, 1.0, 0.0).astype(BF)


def select_kernel(*refs, order, rows, padded):
    own, blocks = refs[0], refs[1:5]
    out, norm_out, even, odd = refs[5:]
    ext, channels = even.shape
    tokens = own.shape[1]
    count = own.shape[0]
    step = split_rows(count, channels)
    norm_out[:, :tokens] = own[...]
    for i in range(1, 4):
        at = 2 * ext + (i - 1) * step
        for c in range(channels // LANES):
            end = min((c + 1) * step, count)
            piece = blocks[i][at : at + end - c * step, c * LANES : (c + 1) * LANES]
            norm_out[c * step : end, i * tokens : (i + 1) * tokens] = piece
    block_of = place()
    pick = jnp.concatenate(
        [chosen(rows, padded, 5 * channels, block_of(k)) for k in order], axis=0
    )
    for i, block in enumerate(blocks):
        even[...] = block[:ext].astype(F32)
        odd[...] = block[ext : 2 * ext].astype(F32)
        pieces = []
        for shift in range(3):
            pieces += [even[shift : shift + tokens].astype(BF), odd[shift : shift + tokens].astype(BF)]
        shifted = jnp.concatenate(
            [jnp.concatenate(pieces[:5], axis=1), jnp.concatenate(pieces[1:], axis=1)], axis=0
        )
        out[:, 2 * i * tokens : 2 * (i + 1) * tokens] = dot_t(pick, shifted).astype(BF)


def query_grad_kernel(pick, first, second, third, fourth, keep, send, right):
    tokens = first.shape[0]
    for i, block in enumerate((first, second, third, fourth)):
        right[i * tokens : (i + 1) * tokens] = block[...]
    count, pad = keep.shape[:2]
    for k in range(2 * count):
        term = dot(pick[k * pad : (k + 1) * pad], right[...])
        if k < count:
            keep[k] = term
        else:
            send[k - count] = term.astype(BF)


def side_rows(norm_rows, size, width):
    return norm_rows * size // width


def put_side(stage, at, part, rows):
    pieces = [part[i : i + rows] for i in range(0, part.shape[0], rows)]
    stage[at : at + rows] = jnp.concatenate(pieces, axis=1)


def get_side(packed, part, rows):
    size = part.shape[1]
    for i in range(part.shape[0] // rows):
        part[i * rows : (i + 1) * rows] = packed[:, i * size : (i + 1) * size]


def stack_cots(blocks, right, tokens):
    for i, block in enumerate(blocks):
        piece = block[:tokens]
        right[2 * i * tokens : (2 * i + 1) * tokens] = piece
        right[(2 * i + 1) * tokens : (2 * i + 2) * tokens] = piece


def conv_first_kernel(*refs, conv_rows, conv_pad):
    pick, blocks, outs, right, stage = refs[0], refs[1:5], refs[5:9], refs[9], refs[10]
    tokens = right.shape[0] // 8
    stack_cots(blocks, right, tokens)
    stage[...] = jnp.zeros(stage.shape, F32)
    for half in range(2):
        gain = None
        for block in blocks:
            lines = block[tokens : tokens + 16].astype(F32)[2 * half : 2 * half + 2]
            term = lines[0:1] + lines[1:2]
            gain = term if gain is None else gain + term
        high = gain.astype(BF).astype(F32)
        at = conv_rows + 2 * half
        stage[at : at + 1] = high
        stage[at + 1 : at + 2] = gain - high
    count, above = outs[0].shape[:2]
    even = lax.axis_index("seq") % 2 == 0
    own, pair = blocks[0], blocks[2]
    tops = [b[0:16].astype(F32)[0:1] for b in (own, pair)]
    bottoms = [b[tokens - 16 : tokens].astype(F32)[15:16] for b in (own, pair)]
    rests = [b[tokens : tokens + 16].astype(F32)[4:6] for b in (own, pair)]
    for k in range(4 * count):
        conv = dot(pick[k * conv_pad : (k + 1) * conv_pad], right[...])
        stage[:conv_rows] = conv[:conv_rows]
        if k == 3 * count:
            stage[above - 4 : above - 3] = jnp.where(even, tops[0], tops[1])
            stage[above - 3 : above - 2] = jnp.where(even, rests[0][0:1], rests[1][0:1])
            stage[above - 2 : above - 1] = jnp.where(even, bottoms[1], bottoms[0])
            stage[above - 1 : above] = jnp.where(even, rests[1][1:2], rests[0][1:2])
        out = outs[k // count]
        out[k % count] = stage[...].astype(out.dtype)


def conv_second_kernel(*refs, conv_rows, conv_pad, norm_rows, norm_pad, key_size, value_size):
    pick, norm_pick, blocks, first_send = refs[0], refs[1], refs[2:6], refs[6]
    near_keep, far_keep, near_send, far_send, right, side, stage = refs[7:]
    tokens, width = right.shape[0] // 8, right.shape[1]
    stack_cots(blocks, right, tokens)
    for i, block in enumerate(blocks):
        side[i * tokens : (i + 1) * tokens] = block[tokens:]
    key_rows = side_rows(norm_rows, key_size, width)
    value_rows = side_rows(norm_rows, value_size, width)
    stage[...] = jnp.zeros(stage.shape, F32)
    count, above = first_send.shape[:2]
    near_send[:, :above] = first_send[...]
    for k in range(4 * count):
        conv = dot(pick[k * conv_pad : (k + 1) * conv_pad], right[...])
        stage[:conv_rows] = conv[:conv_rows]
        both = dot(norm_pick[k * norm_pad : (k + 1) * norm_pad], side[...])
        put_side(stage, conv_rows, both[:norm_rows, :key_size], key_rows)
        value = both[:norm_rows, key_size : key_size + value_size]
        put_side(stage, conv_rows + key_rows, value, value_rows)
        if k < 2 * count:
            (near_keep, far_keep)[k // count][k % count] = stage[...]
        elif k < 3 * count:
            near_send[k % count, above:] = stage[...].astype(BF)
        else:
            far_send[k % count] = stage[...].astype(BF)


def first_sum_kernel(keep, near, far, out):
    above = keep.shape[1]
    out[...] = keep[...] + near[:, :above].astype(F32) + far[...].astype(F32)


def combine_kernel(first, second, near, far, out):
    above = first.shape[1]
    out[:, :above] = first[...]
    out[:, above:] = second[...] + near[:, above:].astype(F32) + far[...].astype(F32)


def final_kernel(*refs, conv_parts, above):
    conv, query, key, value, gain, stage = refs[-6:]
    rows, width = conv.shape
    split = width // 2
    count = key.shape[0]
    if conv_parts == 4:
        combine_kernel(*refs[:4], stage)
    else:
        stage[...] = total_of(refs[:conv_parts])
    query[...] = total_of(refs[conv_parts:-6])[0, : query.shape[0]]
    conv[:, :split] = stage[0, :rows]
    conv[:, split:] = stage[0, above : above + rows]
    at = above + rows
    for part in (key, value):
        step = side_rows(count, part.shape[1], split)
        get_side(stage[0, at : at + step], part, step)
        at += step
    lines = stage[0, rows : rows + 4]
    line = jnp.concatenate([lines[0:1] + lines[1:2], lines[2:3] + lines[3:4]], axis=1)
    line = jnp.broadcast_to(line, (8, width))
    start = place()(0) * count
    gain[...] = pltpu.roll(line, lax.rem(width - start, width), 1)[:1, :count]


def input_kernel(*refs):
    x, first, second, pair_first, pair_second, one, three, weight, out, ext, mixed = refs
    tokens = x.shape[0] // 2
    seq, devices = lax.axis_index("seq"), lax.axis_size("seq")
    low, high = seq % 2, seq // 2
    split = first.shape[1]
    above = one.shape[1]
    one_rows = one[0, above - 16 :].astype(F32)[12:]
    three_rows = three[0, above - 16 :].astype(F32)[12:]
    heads = jnp.where(high % 2 == 0, one_rows[:2], three_rows[:2])
    tails = jnp.where(high % 2 == 0, three_rows[2:], one_rows[2:])
    heads = jnp.where(seq == devices - 1, 0.0, heads)
    tails = jnp.where(seq == 0, 0.0, tails)
    for half, own, pair in ((0, first, pair_first), (1, second, pair_second)):
        lanes = slice(half * split, (half + 1) * split)
        top = pair[0:16].astype(F32)[0:1]
        bottom = pair[tokens - 16 : tokens].astype(F32)[15:16]
        ext[8 : 8 + tokens, lanes] = own[:tokens].astype(F32)
        ext[7:8, lanes] = jnp.where(low == 0, tails[half : half + 1], bottom)
        ext[8 + tokens : 9 + tokens, lanes] = jnp.where(low == 0, top, heads[half : half + 1])
    back = ext[7 : 7 + tokens].astype(BF)
    here = ext[8 : 8 + tokens].astype(BF)
    ahead = ext[9 : 9 + tokens].astype(BF)
    evens = (ahead, here, here, back, back)
    odds = (ahead, ahead, here, here, back)
    total = None
    for tap in range(5):
        term = dot_t(jnp.concatenate([evens[tap], odds[tap]], axis=0), weight[tap])
        total = term if total is None else total + term
    for c in range(mixed.shape[0]):
        lanes = slice(c * LANES, (c + 1) * LANES)
        mixed[c, pl.ds(0, tokens, stride=2)] = total[:tokens, lanes]
        mixed[c, pl.ds(1, tokens, stride=2)] = total[tokens:, lanes]
        out[:, lanes] = (mixed[c] * gelu_slope(x[:, lanes].astype(F32))).astype(BF)


def on_device(x, conv_weight, norm_gain, wq, wk, wv, cotangent):
    devices = lax.axis_size("seq")
    both_axes = ("seq", "dp")
    x, cotangent = x[0], cotangent[0]
    positions, channels = x.shape
    tokens = positions // 2
    taps, _, width = conv_weight.shape
    key_size, value_size = wk.shape[1], wv.shape[1]
    heads = cotangent.shape[1] // value_size
    scale = key_size ** (-0.5)
    groups = devices // 2
    owners = devices * 2
    conv_rows, norm_rows = taps * channels // owners, width // owners
    conv_pad, norm_pad = round_up(conv_rows, 16), round_up(norm_rows, 16)
    ext = tokens + 16
    gain = norm_gain.reshape(1, width)

    def swap(value, seq_bits, dp_bit=0):
        mask = 2 * seq_bits + dp_bit
        return lax.ppermute(value, both_axes, [(i, i ^ mask) for i in range(owners)])

    def held(value, *until):
        return lax.optimization_barrier((value,) + until)[0]

    def quad(value, *until):
        core = swap(value, 0, 1)
        near = swap(value, 1)
        return [value, core, near, swap(held(near, *until), 0, 1)]

    def fold(parts, name):
        shape = (parts[0].shape[0] // 2,) + parts[0].shape[1:]
        return run(fold_kernel, [(shape, F32), (shape, BF)], parts, name=name)

    def halved(keep, send, bits, name):
        for bit in bits[:-1]:
            keep, send = fold([keep, swap(send, 1 << bit)], name)
        return [keep, swap(send, 1 << bits[-1])]

    bits = list(range(devices.bit_length() - 1))
    order = [mask // 2 for mask in ordered(bits[1:])]
    crossing = [(i, i + 1) for i in range(1, devices - 1, 2)]
    crossing = crossing + [(j, i) for i, j in crossing]
    pad_shape = (channels // LANES, 8 + 2 * ext + 8, LANES)
    ready, ends = run(
        open_kernel,
        [(pad_shape, F32), ((32, channels), BF)],
        [x],
        flops=4 * 10**9,
        name="gelu",
    )
    pair, across = swap(ends, 1), lax.ppermute(ends, "seq", crossing)
    wv = wv.T
    kv, early, normed, pooled = run(
        front_kernel,
        [
            ((5 * tokens // 2, key_size), BF),
            ((2 * ext, channels), BF),
            ((tokens, width), BF),
            ((tokens, width), F32),
        ],
        [ready, pair, across, conv_weight, gain, wk, wv],
        [pltpu.VMEM(pad_shape, F32)],
        flops=2 * positions * taps * channels * width,
        name="front",
    )
    near_kv = [kv] + [swap(kv, 2 * k) for k in range(1, groups)]
    far_kv = [swap(block, 1) for block in near_kv]
    picked = (groups * norm_pad, tokens)
    rows = 2 * ext + 3 * split_rows(picked[0], channels)
    queries, early, pick_own = run(
        lambda *refs: query_kernel(
            *refs, order=order, rows=norm_rows, padded=norm_pad, scale=scale
        ),
        [((tokens, heads * key_size), BF), ((rows, channels), BF), (picked, BF)],
        [normed, wq, early],
        flops=4 * tokens * width * heads * key_size,
        name="queries",
        after=near_kv[1:],
    )
    early = held(early, *far_kv)
    length = devices * tokens
    masks = [2 * k for k in range(groups)] + [2 * k + 1 for k in range(groups)]
    half_block = (groups, 5 * tokens // 4, key_size)
    attended, query_cot, keep_a, send_a, keep_b, send_b = run(
        lambda *refs: attend_kernel(
            *refs,
            blocks=devices,
            masks=[
                [masks.index(m) for m in ordered(way)] for way in (bits, [1, 0] + bits[2:])
            ],
            heads=heads,
            key_size=key_size,
            value_size=value_size,
            scale=scale,
        ),
        [((tokens, heads * value_size), BF), ((tokens, heads * key_size), BF)]
        + [(half_block, F32), (half_block, BF)] * 2,
        [queries, cotangent] + near_kv + far_kv,
        [
            pltpu.VMEM((length, key_size), BF),
            pltpu.VMEM((length, value_size), BF),
            pltpu.VMEM((key_size, length), BF),
            pltpu.VMEM((value_size, length), BF),
            pltpu.VMEM((heads * tokens, key_size), BF),
            pltpu.VMEM((heads * tokens, value_size), BF),
            pltpu.VMEM((length, heads * tokens), BF),
            pltpu.VMEM((length, heads * tokens), BF),
        ],
        flops=6 * tokens * heads * length * (key_size + value_size),
        name="attend",
    )
    in_a, in_b = swap(send_a, 1), swap(send_b, 2)
    early_blocks = quad(early, send_a)
    conv_pick, norm_pick = run(
        lambda *refs: select_kernel(*refs, order=order, rows=conv_rows, padded=conv_pad),
        [((groups * conv_pad, 8 * tokens), BF), ((groups * norm_pad, 4 * tokens), BF)],
        [pick_own] + early_blocks,
        [pltpu.VMEM((ext, channels), F32), pltpu.VMEM((ext, channels), F32)],
        flops=2 * groups * conv_pad * taps * channels * 8 * tokens,
        name="select",
    )
    fourth = (groups // 2,) + half_block[1:]
    keep_a, send_a, keep_b, send_b = run(
        fold_two_kernel,
        [(fourth, F32), (fourth, BF)] * 2,
        [keep_a, in_a, keep_b, in_b],
        name="kv_cot_fold",
        after=[conv_pick],
    )
    in_a, in_b = swap(send_a, 2), swap(send_b, 1)
    block = (groups // 4, 5 * tokens // 2, key_size)
    keep, send = run(
        merge_kernel,
        [(block, F32), (block, BF)],
        [keep_a, in_a, keep_b, in_b],
        name="kv_cot_merge",
    )
    (normed_cot,) = run(
        query_cot_kernel,
        [((tokens, width), F32)],
        [query_cot, wq],
        flops=2 * tokens * width * heads * key_size,
        name="query_part",
    )
    query_cot = held(query_cot, keep)
    query_near, query_core = swap(query_cot, 1), swap(query_cot, 0, 1)
    kv_cot = halved(keep, send, bits[2:], "kv_cot_fold")
    first, second, *edge = run(
        middle_kernel,
        [
            ((tokens + 16, width // 2), BF),
            ((2 * tokens, width // 2), BF),
        ]
        + [((16, width), BF)] * (len(bits) > 3),
        kv_cot + [normed_cot, pooled, gain, wk, wv],
        flops=2 * tokens * width * (key_size + value_size),
        name="conv_cot",
    )
    near_first, near_second = swap(first, 1), swap(second, 1)
    query_last = swap(held(query_near, first), 0, 1)
    query_half = (groups // 2, norm_pad, heads * key_size)
    query_keep, query_send = run(
        query_grad_kernel,
        [(query_half, F32), (query_half, BF)],
        [norm_pick, query_cot, query_core, query_near, query_last],
        [pltpu.VMEM((4 * tokens, heads * key_size), BF)],
        flops=2 * groups * norm_pad * 4 * tokens * heads * key_size,
        name="query_grad",
    )
    query_parts = halved(query_keep, query_send, bits[1:], "query_fold")
    core_first, core_second = swap(first, 0, 1), swap(second, 0, 1)
    split = width // 2
    side = side_rows(norm_rows, key_size, split) + side_rows(norm_rows, value_size, split)
    above, below = round_up(conv_rows + 8, 16), round_up(conv_rows + side, 16)
    count = groups // 4
    last_first = swap(held(near_first, query_keep), 0, 1)
    near_keep, far_keep, near_send, far_send = run(
        lambda *refs: conv_first_kernel(*refs, conv_rows=conv_rows, conv_pad=conv_pad),
        [((count, above, split), t) for t in (F32, F32, BF, BF)],
        [conv_pick, first, core_first, near_first, last_first],
        [pltpu.VMEM((8 * tokens, split), BF), pltpu.VMEM((above, split), F32)],
        flops=groups * conv_pad * 8 * tokens * width,
        name="conv_grad_first",
    )
    far_in = swap(far_send, 2)
    last_second = swap(held(near_second, near_keep), 0, 1)
    near_keep_second, far_keep_second, near_send, far_send = run(
        lambda *refs: conv_second_kernel(
            *refs,
            conv_rows=conv_rows,
            conv_pad=conv_pad,
            norm_rows=norm_rows,
            norm_pad=norm_pad,
            key_size=key_size,
            value_size=value_size,
        ),
        [
            ((count, below, split), F32),
            ((count, below, split), F32),
            ((count, above + below, split), BF),
            ((count, below, split), BF),
        ],
        [held(conv_pick, query_parts[0]), norm_pick, second, core_second, near_second, last_second, near_send],
        [
            pltpu.VMEM((8 * tokens, split), BF),
            pltpu.VMEM((4 * tokens, split), BF),
            pltpu.VMEM((below, split), F32),
        ],
        flops=groups * conv_pad * 8 * tokens * width,
        name="conv_grad_second",
    )
    far_in_second = swap(far_send, 2)
    near_in = swap(near_send, 2)
    (far_sum,) = run(
        send_on_kernel,
        [((count, above, split), BF)],
        [far_keep, far_in],
        name="conv_send_on",
    )
    far_last = swap(far_sum, 4)
    (far_sum,) = run(
        send_on_kernel,
        [((count, below, split), BF)],
        [far_keep_second, far_in_second],
        name="conv_send_on",
    )
    edges = [far_in, far_last]
    if len(bits) > 3:
        came = lax.ppermute(edge[0], "seq", crossing)
        rows = jnp.concatenate([came[:1, :split], came[:1, split:], came[1:2, :split], came[1:2, split:]])
        edges = [jnp.pad(rows, ((above - 4, 0), (0, 0)))[None]] * 2
    (input_grad,) = run(
        input_kernel,
        [((positions, channels), BF)],
        [held(x, far_sum), first, second, near_first, near_second] + edges + [conv_weight],
        [
            pltpu.VMEM((tokens + 16, width), F32),
            pltpu.VMEM((channels // LANES, positions, LANES), F32),
        ],
        flops=20 * positions * taps * channels * width,
        name="input_grad",
    )
    (first_sum,) = run(
        first_sum_kernel,
        [((count, above, split), F32)],
        [near_keep, near_in, far_last],
        flops=5 * 10**9,
        name="conv_first_sum",
    )
    conv_parts = [first_sum, near_keep_second, near_in, swap(far_sum, 4)]
    chunk = (count, above + below, split)
    if len(bits) > 3:
        keep = run(combine_kernel, [(chunk, F32)], conv_parts, name="conv_combine")[0]
        half = (count // 2,) + chunk[1:]
        keep, send = run(fold_kernel, [(half, F32), (half, BF)], [keep], name="conv_fold")
        conv_parts = halved(keep, send, bits[3:], "conv_fold")
    conv_grad, query_grad, key_grad, value_grad, gain_grad = run(
        lambda *refs: final_kernel(*refs, conv_parts=len(conv_parts), above=above),
        [
            ((conv_rows, width), F32),
            ((norm_rows, heads * key_size), F32),
            ((norm_rows, key_size), F32),
            ((norm_rows, value_size), F32),
            ((1, norm_rows), F32),
        ],
        conv_parts + query_parts,
        [pltpu.VMEM((1,) + chunk[1:], F32)],
        name="final_sum",
    )
    return (
        attended[None],
        input_grad[None],
        conv_grad,
        query_grad,
        key_grad,
        value_grad,
        gain_grad.reshape(norm_rows),
    )


def solution(mesh):
    placed = (
        P(("groups", "dp"), "seq", None),
        P(),
        P(),
        P(),
        P(),
        P(),
        P(("groups", "dp"), "seq", None),
    )
    return jax.shard_map(
        on_device,
        mesh=mesh,
        in_specs=placed,
        out_specs=(
            P(("groups", "dp"), "seq", None),
            P(("groups", "dp"), "seq", None),
            P(("groups", "seq", "dp"), None),
            P(("groups", "seq", "dp"), None),
            P(("groups", "seq", "dp"), None),
            P(("groups", "seq", "dp"), None),
            P(("groups", "seq", "dp")),
        ),
        check_vma=False,
    )
```

```python
import functools
import math

import jax
import jax.numpy as jnp
from jax import lax
from jax.experimental import pallas as pl
from jax.experimental.pallas import tpu as pltpu
from jax.sharding import PartitionSpec as P

BF = jnp.bfloat16
F32 = jnp.float32
ROOT = math.sqrt(2.0 / math.pi)
EPS = 1e-06
LANES = 128
VMEM_BYTES = 40 * 2**20


def dot(a, b):
    return lax.dot_general(a, b, (((1,), (0,)), ((), ())), preferred_element_type=F32)


def dot_t(a, b):
    return lax.dot_general(a, b, (((1,), (1,)), ((), ())), preferred_element_type=F32)


def run(body, outs, args, scratch=(), flops=0, name=None, after=()):
    size = sum(math.prod(a.shape) * a.dtype.itemsize for a in args)
    size += sum(math.prod(s) * jnp.dtype(t).itemsize for s, t in outs)
    vmem = pl.BlockSpec(memory_space=pltpu.VMEM)
    rest = pl.BlockSpec(memory_space=pl.ANY)
    count, skip = len(args), len(args) + len(after)

    def whole(*refs):
        body(*refs[:count], *refs[skip:])

    return pl.pallas_call(
        whole,
        out_shape=[jax.ShapeDtypeStruct(s, t) for s, t in outs],
        in_specs=[vmem] * count + [rest] * len(after),
        out_specs=[vmem] * len(outs),
        scratch_shapes=list(scratch),
        compiler_params=pltpu.CompilerParams(vmem_limit_bytes=VMEM_BYTES),
        cost_estimate=pl.CostEstimate(flops=flops, bytes_accessed=size, transcendentals=0),
        name=name,
    )(*args, *after)


def gelu(v):
    return v * (0.5 * (1.0 + jnp.tanh(ROOT * (v + 0.044715 * (v * v * v)))))


def gelu_slope(v):
    tangent = jnp.tanh(ROOT * (v + 0.044715 * v * v * v))
    return 0.5 * (1.0 + tangent) + 0.5 * v * (1.0 - tangent * tangent) * ROOT * (
        1.0 + 3.0 * 0.044715 * v * v
    )


def round_up(value, step):
    return -(-value // step) * step


def pack_kv(keys, values):
    tokens, size = keys.shape
    rest = values[:, size:]
    half = tokens // 2
    tail = jnp.concatenate([rest[:half], rest[half:]], axis=1)
    return jnp.concatenate([keys, values[:, :size], tail], axis=0)


def unpack_values(packed, tokens, size):
    tail = packed[2 * tokens :]
    width = tail.shape[1] // 2
    rest = jnp.concatenate([tail[:, :width], tail[:, width:]], axis=0)
    return jnp.concatenate([packed[tokens : 2 * tokens], rest], axis=1)


def put(ref, start, rows):
    for c in range(ref.shape[0]):
        ref[c, start : start + rows.shape[0]] = rows[:, c * LANES : (c + 1) * LANES]


def every_second(ref, start, count):
    parts = [ref[c, pl.ds(start, count, stride=2)] for c in range(ref.shape[0])]
    return jnp.concatenate(parts, axis=1)


def open_kernel(x, pad, ends):
    positions, channels = x.shape
    ends[:16] = x[:16]
    ends[16:] = x[positions - 16 :]
    put(pad, 0, jnp.zeros((8, channels), F32))
    put(pad, 8, gelu(x[...].astype(F32)).astype(BF).astype(F32))
    put(pad, 8 + positions, jnp.zeros((pad.shape[1] - 8 - positions, channels), F32))


def front_kernel(ready, pair, across, weight, gain, wk, wv, kv_out, early, normed_out, pooled_out, pad):
    tokens = pooled_out.shape[0]
    ext = early.shape[0] // 2
    even = lax.axis_index("seq") % 2 == 0
    pair_wide, across_wide = pair[...].astype(F32), across[...].astype(F32)
    before = jnp.where(even, across_wide[16:], pair_wide[16:])[14:]
    after = jnp.where(even, pair_wide[:16], across_wide[:16])[:2]
    pad[...] = ready[...]
    put(pad, 6, gelu(before).astype(BF).astype(F32))
    put(pad, 8 + 2 * tokens, gelu(after).astype(BF).astype(F32))
    pieces = [every_second(pad, 6 + u, tokens).astype(BF) for u in range(6)]
    total = None
    for tap in range(5):
        rows = jnp.concatenate([pieces[tap], pieces[tap + 1]], axis=0)
        term = dot(rows, weight[tap])
        total = term if total is None else total + term
    pooled = 0.5 * (total[:tokens] + total[tokens:])
    inv = lax.rsqrt(jnp.mean(pooled * pooled, axis=-1, keepdims=True) + EPS)
    normed = (pooled * inv * gain[...]).astype(BF)
    pooled_out[...] = pooled
    normed_out[...] = normed
    kv_out[...] = pack_kv(dot(normed, wk[...]), dot_t(normed, wv[...])).astype(BF)
    early[0:ext] = every_second(pad, 6, ext).astype(BF)
    early[ext : 2 * ext] = every_second(pad, 7, ext).astype(BF)


def ordered(bits):
    masks = [0]
    for bit in reversed(bits):
        masks = masks + [mask | (1 << bit) for mask in masks]
    return masks


def split_rows(rows, columns):
    return round_up(-(-rows * LANES // columns), 16)


def query_kernel(normed, wq, early, out, message, own, *, order, rows, padded, scale):
    width = normed.shape[1]
    value = normed[...]
    out[...] = (dot(value, wq[...]) * scale).astype(BF)
    at, channels = early.shape
    message[:at] = early[...]
    count = len(order) * padded
    step = split_rows(count, channels)
    for i in range(4):
        block_of = place(i)
        pick = [chosen(rows, padded, width, block_of(k)) for k in order]
        part = dot_t(jnp.concatenate(pick, axis=0), value).astype(BF)
        if i == 0:
            own[...] = part
            continue
        for c in range(channels // LANES):
            piece = part[c * step : min((c + 1) * step, count)]
            message[at : at + piece.shape[0], c * LANES : (c + 1) * LANES] = piece
        at += step


def by_eight(rows):
    return rows.reshape(rows.shape[0] // 8, 8, rows.shape[1])


def attend_kernel(*refs, blocks, masks, heads, key_size, value_size, scale):
    q, cot = refs[:2]
    parts = refs[2 : 2 + blocks]
    att, dq, keep_a, send_a, keep_b, send_b = refs[2 + blocks : 8 + blocks]
    ks, vs, kt, vt, qs, cs, weights, score_cots, scores, prob_cots = refs[8 + blocks :]
    tokens = q.shape[0]
    half = tokens // 2
    wide = value_size - key_size
    for i, part in enumerate(parts):
        at = i * tokens
        ks[at : at + tokens] = part[:tokens]
        vs[at : at + tokens, :key_size] = part[tokens : 2 * tokens]
        vs[at : at + half, key_size:] = part[2 * tokens :, :wide]
        vs[at + half : at + tokens, key_size:] = part[2 * tokens :, wide:]
        kt[:, at : at + tokens] = ks[at : at + tokens].astype(F32).T.astype(BF)
        vt[:, at : at + tokens] = vs[at : at + tokens].astype(F32).T.astype(BF)
    for pair in range(heads // 2):
        ql, cl = 2 * pair * key_size, 2 * pair * value_size
        rows = slice(2 * pair * tokens, 2 * (pair + 1) * tokens)
        both = cot[:, cl : cl + 2 * value_size]
        qs[rows] = jnp.concatenate(
            [q[:, ql : ql + key_size], q[:, ql + key_size : ql + 2 * key_size]], axis=0
        )
        cs[rows] = jnp.concatenate([both[:, :value_size], both[:, value_size:]], axis=0)
        slot = pair % scores.shape[0]
        parts_of = [slice(i * tokens, (i + 1) * tokens) for i in range(blocks)]
        scores[slot] = dot_t(ks[...], qs[rows])
        prob_cots[slot] = dot_t(vs[...], cs[rows])
        top = functools.reduce(jnp.maximum, [by_eight(scores[slot, at]).max(0) for at in parts_of])
        top = jnp.max(top, axis=0, keepdims=True)
        sums = 0.0
        for at in parts_of:
            raised = jnp.exp(scores[slot, at] - top)
            sums = sums + by_eight(raised).sum(0)
            scores[slot, at] = raised
        inverse = 1.0 / jnp.sum(sums, axis=0, keepdims=True)
        for at in parts_of:
            weights[at, rows] = (scores[slot, at] * inverse).astype(BF)
        out_t = dot(vt[...], weights[:, rows]).astype(BF).astype(F32)
        delta = jnp.sum(cs[rows].astype(F32).T * out_t, axis=0, keepdims=True)
        for at in parts_of:
            probs = scores[slot, at] * inverse
            score_cots[at, rows] = (probs * (prob_cots[slot, at] - delta)).astype(BF)
        dq_t = dot(kt[...], score_cots[:, rows]) * scale
        out_rows = jnp.concatenate([out_t[:, :tokens].T, out_t[:, tokens:].T], axis=1)
        att[:, cl : cl + 2 * value_size] = out_rows.astype(BF)
        dq_rows = jnp.concatenate([dq_t[:, :tokens].T, dq_t[:, tokens:].T], axis=1)
        dq[:, ql : ql + 2 * key_size] = dq_rows.astype(BF)
    key_cots, value_cots = dot(score_cots[...], qs[...]), dot(weights[...], cs[...])
    edge = keep_a.shape[1]
    count = blocks // 2
    for i in range(blocks):
        at = slice(i * tokens, (i + 1) * tokens)
        packed = pack_kv(key_cots[at], value_cots[at])
        for order, keep, send, part in (
            (masks[0], keep_a, send_a, packed[:edge]),
            (masks[1], keep_b, send_b, packed[edge:]),
        ):
            k = order.index(i)
            if k < count:
                keep[k] = part
            else:
                send[k - count] = part.astype(BF)


def total_of(parts):
    total = parts[0][...]
    for part in parts[1:]:
        total = total + part[...].astype(F32)
    return total


def fold_kernel(*refs):
    keep, send = refs[-2:]
    total = total_of(refs[:-2])
    keep[...] = total[: keep.shape[0]]
    send[...] = total[keep.shape[0] :].astype(BF)


def fold_two_kernel(*refs):
    fold_kernel(refs[0], refs[1], refs[4], refs[5])
    fold_kernel(refs[2], refs[3], refs[6], refs[7])


def merge_kernel(keep_a, in_a, keep_b, in_b, keep, send):
    total = jnp.concatenate([total_of((keep_a, in_a)), total_of((keep_b, in_b))], axis=1)
    keep[...] = total[: keep.shape[0]]
    send[...] = total[keep.shape[0] :].astype(BF)


def send_on_kernel(keep, came, out):
    out[...] = (keep[...] + came[...].astype(F32)).astype(BF)


def query_cot_kernel(dq, wq, out):
    out[...] = dot_t(dq[...], wq[...])


def middle_kernel(own, came, part, pooled_in, gain_in, wk, wv, first, second, *edges):
    size = own.shape[2]
    tokens, width = pooled_in.shape
    total = (own[0] + came[0].astype(F32)).astype(BF).astype(F32)
    key_cot = total[:tokens]
    value_cot = unpack_values(total, tokens, size)
    normed_cot = part[...] + dot_t(key_cot.astype(BF), wk[...])
    normed_cot = normed_cot + dot(value_cot.astype(BF), wv[...])
    pooled, gain = pooled_in[...], gain_in[...]
    inv = lax.rsqrt(jnp.mean(pooled * pooled, axis=-1, keepdims=True) + EPS)
    gain_term = jnp.sum(normed_cot * pooled * inv, axis=0, keepdims=True)
    gained = gain * normed_cot
    pooled_cot = inv * gained - pooled * (inv * inv * inv) * (
        jnp.sum(gained * pooled, axis=-1, keepdims=True) / width
    )
    conv_cot = 0.5 * pooled_cot
    high = gain_term.astype(BF).astype(F32)
    low = gain_term - high
    row = lax.broadcasted_iota(jnp.int32, (16, width), 0)
    split = width // 2
    lines = (high[:, :split], low[:, :split], high[:, split:], low[:, split:])
    lines += (conv_cot[:1, split:], conv_cot[tokens - 1 :, split:])
    gains = jnp.zeros((16, split), F32)
    for i, line in enumerate(lines):
        gains = jnp.where(row[:, :split] == i, line, gains)
    fill = split - size - value_cot.shape[1]
    side = jnp.concatenate([key_cot, value_cot, jnp.zeros((tokens, fill), F32)], axis=1)
    first[:tokens] = conv_cot[:, :split].astype(BF)
    first[tokens:] = gains.astype(BF)
    second[:tokens] = conv_cot[:, split:].astype(BF)
    second[tokens:] = side.astype(BF)
    for edge in edges:
        ends = jnp.where(row == 0, conv_cot[:1], jnp.where(row == 1, conv_cot[tokens - 1 :], 0.0))
        edge[...] = ends.astype(BF)


def place(other=0):
    seq, dp = lax.axis_index("seq"), lax.axis_index("dp") ^ (other % 2)
    high, low = seq // 2, (seq % 2) ^ (other // 2)
    return lambda k: ((high ^ k) * 2 + low) * 2 + dp


def chosen(rows, padded, columns, block):
    row = lax.broadcasted_iota(jnp.int32, (padded, columns), 0)
    column = lax.broadcasted_iota(jnp.int32, (padded, columns), 1)
    hit = (column == row + block * rows) & (row < rows)
    return jnp.where(hit, 1.0, 0.0).astype(BF)


def select_kernel(*refs, order, rows, padded):
    own, blocks = refs[0], refs[1:5]
    out, norm_out, even, odd = refs[5:]
    ext, channels = even.shape
    tokens = own.shape[1]
    count = own.shape[0]
    step = split_rows(count, channels)
    norm_out[:, :tokens] = own[...]
    for i in range(1, 4):
        at = 2 * ext + (i - 1) * step
        for c in range(channels // LANES):
            end = min((c + 1) * step, count)
            piece = blocks[i][at : at + end - c * step, c * LANES : (c + 1) * LANES]
            norm_out[c * step : end, i * tokens : (i + 1) * tokens] = piece
    block_of = place()
    pick = jnp.concatenate(
        [chosen(rows, padded, 5 * channels, block_of(k)) for k in order], axis=0
    )
    for i, block in enumerate(blocks):
        even[...] = block[:ext].astype(F32)
        odd[...] = block[ext : 2 * ext].astype(F32)
        pieces = []
        for shift in range(3):
            pieces += [even[shift : shift + tokens].astype(BF), odd[shift : shift + tokens].astype(BF)]
        shifted = jnp.concatenate(
            [jnp.concatenate(pieces[:5], axis=1), jnp.concatenate(pieces[1:], axis=1)], axis=0
        )
        out[:, 2 * i * tokens : 2 * (i + 1) * tokens] = dot_t(pick, shifted).astype(BF)


def query_grad_kernel(pick, first, second, third, fourth, keep, send, right):
    tokens = first.shape[0]
    for i, block in enumerate((first, second, third, fourth)):
        right[i * tokens : (i + 1) * tokens] = block[...]
    count, pad = keep.shape[:2]
    for k in range(2 * count):
        term = dot(pick[k * pad : (k + 1) * pad], right[...])
        if k < count:
            keep[k] = term
        else:
            send[k - count] = term.astype(BF)


def side_rows(norm_rows, size, width):
    return norm_rows * size // width


def put_side(stage, at, part, rows):
    pieces = [part[i : i + rows] for i in range(0, part.shape[0], rows)]
    stage[at : at + rows] = jnp.concatenate(pieces, axis=1)


def get_side(packed, part, rows):
    size = part.shape[1]
    for i in range(part.shape[0] // rows):
        part[i * rows : (i + 1) * rows] = packed[:, i * size : (i + 1) * size]


def stack_cots(blocks, right, tokens):
    for i, block in enumerate(blocks):
        piece = block[:tokens]
        right[2 * i * tokens : (2 * i + 1) * tokens] = piece
        right[(2 * i + 1) * tokens : (2 * i + 2) * tokens] = piece


def conv_first_kernel(*refs, conv_rows, conv_pad):
    pick, blocks, outs, right, stage = refs[0], refs[1:5], refs[5:9], refs[9], refs[10]
    tokens = right.shape[0] // 8
    stack_cots(blocks, right, tokens)
    stage[...] = jnp.zeros(stage.shape, F32)
    for half in range(2):
        gain = None
        for block in blocks:
            lines = block[tokens : tokens + 16].astype(F32)[2 * half : 2 * half + 2]
            term = lines[0:1] + lines[1:2]
            gain = term if gain is None else gain + term
        high = gain.astype(BF).astype(F32)
        at = conv_rows + 2 * half
        stage[at : at + 1] = high
        stage[at + 1 : at + 2] = gain - high
    count, above = outs[0].shape[:2]
    even = lax.axis_index("seq") % 2 == 0
    own, pair = blocks[0], blocks[2]
    tops = [b[0:16].astype(F32)[0:1] for b in (own, pair)]
    bottoms = [b[tokens - 16 : tokens].astype(F32)[15:16] for b in (own, pair)]
    rests = [b[tokens : tokens + 16].astype(F32)[4:6] for b in (own, pair)]
    for k in range(4 * count):
        conv = dot(pick[k * conv_pad : (k + 1) * conv_pad], right[...])
        stage[:conv_rows] = conv[:conv_rows]
        if k == 3 * count:
            stage[above - 4 : above - 3] = jnp.where(even, tops[0], tops[1])
            stage[above - 3 : above - 2] = jnp.where(even, rests[0][0:1], rests[1][0:1])
            stage[above - 2 : above - 1] = jnp.where(even, bottoms[1], bottoms[0])
            stage[above - 1 : above] = jnp.where(even, rests[1][1:2], rests[0][1:2])
        out = outs[k // count]
        out[k % count] = stage[...].astype(out.dtype)


def conv_second_kernel(*refs, conv_rows, conv_pad, norm_rows, norm_pad, key_size, value_size):
    pick, norm_pick, blocks, outs = refs[0], refs[1], refs[2:6], refs[6:10]
    right, side, stage = refs[10:]
    tokens, width = right.shape[0] // 8, right.shape[1]
    stack_cots(blocks, right, tokens)
    for i, block in enumerate(blocks):
        side[i * tokens : (i + 1) * tokens] = block[tokens:]
    key_rows = side_rows(norm_rows, key_size, width)
    value_rows = side_rows(norm_rows, value_size, width)
    stage[...] = jnp.zeros(stage.shape, F32)
    count = outs[0].shape[0]
    for k in range(4 * count):
        conv = dot(pick[k * conv_pad : (k + 1) * conv_pad], right[...])
        stage[:conv_rows] = conv[:conv_rows]
        both = dot(norm_pick[k * norm_pad : (k + 1) * norm_pad], side[...])
        put_side(stage, conv_rows, both[:norm_rows, :key_size], key_rows)
        value = both[:norm_rows, key_size : key_size + value_size]
        put_side(stage, conv_rows + key_rows, value, value_rows)
        out = outs[k // count]
        out[k % count] = stage[...].astype(out.dtype)


def first_sum_kernel(keep, near, far, out):
    out[...] = total_of((keep, near, far))


def combine_kernel(first, second, near, far, out):
    above = first.shape[1]
    out[:, :above] = first[...]
    out[:, above:] = total_of((second, near, far))


def final_kernel(*refs, conv_parts, above):
    conv, query, key, value, gain, stage = refs[-6:]
    rows, width = conv.shape
    split = width // 2
    count = key.shape[0]
    if conv_parts == 4:
        combine_kernel(*refs[:4], stage)
    else:
        stage[...] = total_of(refs[:conv_parts])
    query[...] = total_of(refs[conv_parts:-6])[0, : query.shape[0]]
    conv[:, :split] = stage[0, :rows]
    conv[:, split:] = stage[0, above : above + rows]
    at = above + rows
    for part in (key, value):
        step = side_rows(count, part.shape[1], split)
        get_side(stage[0, at : at + step], part, step)
        at += step
    lines = stage[0, rows : rows + 4]
    line = jnp.concatenate([lines[0:1] + lines[1:2], lines[2:3] + lines[3:4]], axis=1)
    line = jnp.broadcast_to(line, (8, width))
    start = place()(0) * count
    gain[...] = pltpu.roll(line, lax.rem(width - start, width), 1)[:1, :count]


def input_kernel(*refs):
    x, first, second, pair_first, pair_second, one, three, weight, out, ext, mixed = refs
    tokens = x.shape[0] // 2
    seq, devices = lax.axis_index("seq"), lax.axis_size("seq")
    low, high = seq % 2, seq // 2
    split = first.shape[1]
    above = one.shape[1]
    one_rows = one[0, above - 16 :].astype(F32)[12:]
    three_rows = three[0, above - 16 :].astype(F32)[12:]
    heads = jnp.where(high % 2 == 0, one_rows[:2], three_rows[:2])
    tails = jnp.where(high % 2 == 0, three_rows[2:], one_rows[2:])
    heads = jnp.where(seq == devices - 1, 0.0, heads)
    tails = jnp.where(seq == 0, 0.0, tails)
    for half, own, pair in ((0, first, pair_first), (1, second, pair_second)):
        lanes = slice(half * split, (half + 1) * split)
        top = pair[0:16].astype(F32)[0:1]
        bottom = pair[tokens - 16 : tokens].astype(F32)[15:16]
        ext[8 : 8 + tokens, lanes] = own[:tokens].astype(F32)
        ext[7:8, lanes] = jnp.where(low == 0, tails[half : half + 1], bottom)
        ext[8 + tokens : 9 + tokens, lanes] = jnp.where(low == 0, top, heads[half : half + 1])
    back = ext[7 : 7 + tokens].astype(BF)
    here = ext[8 : 8 + tokens].astype(BF)
    ahead = ext[9 : 9 + tokens].astype(BF)
    evens = (ahead, here, here, back, back)
    odds = (ahead, ahead, here, here, back)
    total = None
    for tap in range(5):
        term = dot_t(jnp.concatenate([evens[tap], odds[tap]], axis=0), weight[tap])
        total = term if total is None else total + term
    for c in range(mixed.shape[0]):
        lanes = slice(c * LANES, (c + 1) * LANES)
        mixed[c, pl.ds(0, tokens, stride=2)] = total[:tokens, lanes]
        mixed[c, pl.ds(1, tokens, stride=2)] = total[tokens:, lanes]
        out[:, lanes] = (mixed[c] * gelu_slope(x[:, lanes].astype(F32))).astype(BF)


def on_device(x, conv_weight, norm_gain, wq, wk, wv, cotangent):
    devices = lax.axis_size("seq")
    both_axes = ("seq", "dp")
    x, cotangent = x[0], cotangent[0]
    positions, channels = x.shape
    tokens = positions // 2
    taps, _, width = conv_weight.shape
    key_size, value_size = wk.shape[1], wv.shape[1]
    heads = cotangent.shape[1] // value_size
    scale = key_size ** (-0.5)
    groups = devices // 2
    owners = devices * 2
    conv_rows, norm_rows = taps * channels // owners, width // owners
    conv_pad, norm_pad = round_up(conv_rows, 16), round_up(norm_rows, 16)
    ext = tokens + 16
    gain = norm_gain.reshape(1, width)

    def swap(value, seq_bits, dp_bit=0):
        mask = 2 * seq_bits + dp_bit
        return lax.ppermute(value, both_axes, [(i, i ^ mask) for i in range(owners)])

    def held(value, *until):
        return lax.optimization_barrier((value,) + until)[0]

    def quad(value, *until):
        core = swap(value, 0, 1)
        near = swap(value, 1)
        return [value, core, near, swap(held(near, *until), 0, 1)]

    def fold(parts, name):
        shape = (parts[0].shape[0] // 2,) + parts[0].shape[1:]
        return run(fold_kernel, [(shape, F32), (shape, BF)], parts, name=name)

    def halved(keep, send, bits, name):
        for bit in bits[:-1]:
            keep, send = fold([keep, swap(send, 1 << bit)], name)
        return [keep, swap(send, 1 << bits[-1])]

    bits = list(range(devices.bit_length() - 1))
    order = [mask // 2 for mask in ordered(bits[1:])]
    crossing = [(i, i + 1) for i in range(1, devices - 1, 2)]
    crossing = crossing + [(j, i) for i, j in crossing]
    pad_shape = (channels // LANES, 8 + 2 * ext + 8, LANES)
    ready, ends = run(
        open_kernel,
        [(pad_shape, F32), ((32, channels), BF)],
        [x],
        flops=4 * 10**9,
        name="gelu",
    )
    pair, across = swap(ends, 1), lax.ppermute(ends, "seq", crossing)
    wv = wv.T
    kv, early, normed, pooled = run(
        front_kernel,
        [
            ((5 * tokens // 2, key_size), BF),
            ((2 * ext, channels), BF),
            ((tokens, width), BF),
            ((tokens, width), F32),
        ],
        [ready, pair, across, conv_weight, gain, wk, wv],
        [pltpu.VMEM(pad_shape, F32)],
        flops=2 * positions * taps * channels * width,
        name="front",
    )
    near_kv = [kv] + [swap(kv, 2 * k) for k in range(1, groups)]
    far_kv = [swap(block, 1) for block in near_kv]
    picked = (groups * norm_pad, tokens)
    rows = 2 * ext + 3 * split_rows(picked[0], channels)
    queries, early, pick_own = run(
        lambda *refs: query_kernel(
            *refs, order=order, rows=norm_rows, padded=norm_pad, scale=scale
        ),
        [((tokens, heads * key_size), BF), ((rows, channels), BF), (picked, BF)],
        [normed, wq, early],
        flops=4 * tokens * width * heads * key_size,
        name="queries",
        after=near_kv[1:],
    )
    early = held(early, *far_kv)
    length = devices * tokens
    masks = [2 * k for k in range(groups)] + [2 * k + 1 for k in range(groups)]
    half_block = (groups, 5 * tokens // 4, key_size)
    slots = 2 if length <= 2048 else 1
    attended, query_cot, keep_a, send_a, keep_b, send_b = run(
        lambda *refs: attend_kernel(
            *refs,
            blocks=devices,
            masks=[
                [masks.index(m) for m in ordered(way)] for way in (bits, [1, 0] + bits[2:])
            ],
            heads=heads,
            key_size=key_size,
            value_size=value_size,
            scale=scale,
        ),
        [((tokens, heads * value_size), BF), ((tokens, heads * key_size), BF)]
        + [(half_block, F32), (half_block, BF)] * 2,
        [queries, cotangent] + near_kv + far_kv,
        [
            pltpu.VMEM((length, key_size), BF),
            pltpu.VMEM((length, value_size), BF),
            pltpu.VMEM((key_size, length), BF),
            pltpu.VMEM((value_size, length), BF),
            pltpu.VMEM((heads * tokens, key_size), BF),
            pltpu.VMEM((heads * tokens, value_size), BF),
            pltpu.VMEM((length, heads * tokens), BF),
            pltpu.VMEM((length, heads * tokens), BF),
            pltpu.VMEM((slots, length, 2 * tokens), F32),
            pltpu.VMEM((slots, length, 2 * tokens), F32),
        ],
        flops=6 * tokens * heads * length * (key_size + value_size),
        name="attend",
    )
    in_a, in_b = swap(send_a, 1), swap(send_b, 2)
    early_blocks = quad(early, send_a)
    conv_pick, norm_pick = run(
        lambda *refs: select_kernel(*refs, order=order, rows=conv_rows, padded=conv_pad),
        [((groups * conv_pad, 8 * tokens), BF), ((groups * norm_pad, 4 * tokens), BF)],
        [pick_own] + early_blocks,
        [pltpu.VMEM((ext, channels), F32), pltpu.VMEM((ext, channels), F32)],
        flops=2 * groups * conv_pad * taps * channels * 8 * tokens,
        name="select",
    )
    fourth = (groups // 2,) + half_block[1:]
    keep_a, send_a, keep_b, send_b = run(
        fold_two_kernel,
        [(fourth, F32), (fourth, BF)] * 2,
        [keep_a, in_a, keep_b, in_b],
        name="kv_cot_fold",
        after=[conv_pick],
    )
    in_a, in_b = swap(send_a, 2), swap(send_b, 1)
    block = (groups // 4, 5 * tokens // 2, key_size)
    keep, send = run(
        merge_kernel,
        [(block, F32), (block, BF)],
        [keep_a, in_a, keep_b, in_b],
        name="kv_cot_merge",
    )
    (normed_cot,) = run(
        query_cot_kernel,
        [((tokens, width), F32)],
        [query_cot, wq],
        flops=2 * tokens * width * heads * key_size,
        name="query_part",
    )
    query_cot = held(query_cot, keep)
    query_near, query_core = swap(query_cot, 1), swap(query_cot, 0, 1)
    kv_cot = halved(keep, send, bits[2:], "kv_cot_fold")
    first, second, *edge = run(
        middle_kernel,
        [
            ((tokens + 16, width // 2), BF),
            ((2 * tokens, width // 2), BF),
        ]
        + [((16, width), BF)] * (len(bits) > 3),
        kv_cot + [normed_cot, pooled, gain, wk, wv],
        flops=2 * tokens * width * (key_size + value_size),
        name="conv_cot",
    )
    near_first, near_second = swap(first, 1), swap(second, 1)
    query_last = swap(held(query_near, first), 0, 1)
    query_half = (groups // 2, norm_pad, heads * key_size)
    query_keep, query_send = run(
        query_grad_kernel,
        [(query_half, F32), (query_half, BF)],
        [norm_pick, query_cot, query_core, query_near, query_last],
        [pltpu.VMEM((4 * tokens, heads * key_size), BF)],
        flops=2 * groups * norm_pad * 4 * tokens * heads * key_size,
        name="query_grad",
    )
    query_parts = halved(query_keep, query_send, bits[1:], "query_fold")
    core_first, core_second = swap(first, 0, 1), swap(second, 0, 1)
    split = width // 2
    side = side_rows(norm_rows, key_size, split) + side_rows(norm_rows, value_size, split)
    above, below = round_up(conv_rows + 8, 16), round_up(conv_rows + side, 16)
    count = groups // 4
    last_first = swap(held(near_first, query_keep), 0, 1)
    near_keep, far_keep, near_send, far_send = run(
        lambda *refs: conv_first_kernel(*refs, conv_rows=conv_rows, conv_pad=conv_pad),
        [((count, above, split), t) for t in (F32, F32, BF, BF)],
        [held(conv_pick, query_parts[0]), first, core_first, near_first, last_first],
        [pltpu.VMEM((8 * tokens, split), BF), pltpu.VMEM((above, split), F32)],
        flops=groups * conv_pad * 8 * tokens * width,
        name="conv_grad_first",
    )
    far_in, near_in = swap(far_send, 2), swap(held(near_send, query_parts[1]), 2)
    last_second = swap(held(near_second, near_keep), 0, 1)
    near_keep_second, far_keep_second, near_send_second, far_send_second = run(
        lambda *refs: conv_second_kernel(
            *refs,
            conv_rows=conv_rows,
            conv_pad=conv_pad,
            norm_rows=norm_rows,
            norm_pad=norm_pad,
            key_size=key_size,
            value_size=value_size,
        ),
        [
            ((count, below, split), F32),
            ((count, below, split), F32),
            ((count, below, split), BF),
            ((count, below, split), BF),
        ],
        [conv_pick, norm_pick, second, core_second, near_second, last_second],
        [
            pltpu.VMEM((8 * tokens, split), BF),
            pltpu.VMEM((4 * tokens, split), BF),
            pltpu.VMEM((below, split), F32),
        ],
        flops=groups * conv_pad * 8 * tokens * width,
        name="conv_grad_second",
    )
    far_in_second, near_in_second = swap(far_send_second, 2), swap(near_send_second, 2)
    (far_sum,) = run(
        send_on_kernel,
        [((count, above, split), BF)],
        [far_keep, far_in],
        name="conv_send_on",
    )
    far_last = swap(far_sum, 4)
    (far_sum,) = run(
        send_on_kernel,
        [((count, below, split), BF)],
        [far_keep_second, far_in_second],
        name="conv_send_on",
    )
    edges = [far_in, far_last]
    if len(bits) > 3:
        came = lax.ppermute(edge[0], "seq", crossing)
        rows = jnp.concatenate([came[:1, :split], came[:1, split:], came[1:2, :split], came[1:2, split:]])
        edges = [jnp.pad(rows, ((above - 4, 0), (0, 0)))[None]] * 2
    (input_grad,) = run(
        input_kernel,
        [((positions, channels), BF)],
        [held(x, far_sum), first, second, near_first, near_second] + edges + [conv_weight],
        [
            pltpu.VMEM((tokens + 16, width), F32),
            pltpu.VMEM((channels // LANES, positions, LANES), F32),
        ],
        flops=20 * positions * taps * channels * width,
        name="input_grad",
    )
    (first_sum,) = run(
        first_sum_kernel,
        [((count, above, split), F32)],
        [held(near_keep, input_grad), near_in, far_last],
        flops=5 * 10**9,
        name="conv_first_sum",
    )
    conv_parts = [first_sum, near_keep_second, near_in_second, swap(far_sum, 4)]
    chunk = (count, above + below, split)
    if len(bits) > 3:
        keep = run(combine_kernel, [(chunk, F32)], conv_parts, name="conv_combine")[0]
        half = (count // 2,) + chunk[1:]
        keep, send = run(fold_kernel, [(half, F32), (half, BF)], [keep], name="conv_fold")
        conv_parts = halved(keep, send, bits[3:], "conv_fold")
    conv_grad, query_grad, key_grad, value_grad, gain_grad = run(
        lambda *refs: final_kernel(*refs, conv_parts=len(conv_parts), above=above),
        [
            ((conv_rows, width), F32),
            ((norm_rows, heads * key_size), F32),
            ((norm_rows, key_size), F32),
            ((norm_rows, value_size), F32),
            ((1, norm_rows), F32),
        ],
        conv_parts + query_parts,
        [pltpu.VMEM((1,) + chunk[1:], F32)],
        name="final_sum",
    )
    return (
        attended[None],
        input_grad[None],
        conv_grad,
        query_grad,
        key_grad,
        value_grad,
        gain_grad.reshape(norm_rows),
    )


def solution(mesh):
    placed = (
        P(("groups", "dp"), "seq", None),
        P(),
        P(),
        P(),
        P(),
        P(),
        P(("groups", "dp"), "seq", None),
    )
    return jax.shard_map(
        on_device,
        mesh=mesh,
        in_specs=placed,
        out_specs=(
            P(("groups", "dp"), "seq", None),
            P(("groups", "dp"), "seq", None),
            P(("groups", "seq", "dp"), None),
            P(("groups", "seq", "dp"), None),
            P(("groups", "seq", "dp"), None),
            P(("groups", "seq", "dp"), None),
            P(("groups", "seq", "dp")),
        ),
        check_vma=False,
    )
```

```python
import functools
import math

import jax
import jax.numpy as jnp
from jax import lax
from jax.experimental import pallas as pl
from jax.experimental.pallas import tpu as pltpu
from jax.sharding import PartitionSpec as P

BF = jnp.bfloat16
F32 = jnp.float32
ROOT = math.sqrt(2.0 / math.pi)
EPS = 1e-06
LANES = 128
VMEM_BYTES = 40 * 2**20


def dot(a, b):
    return lax.dot_general(a, b, (((1,), (0,)), ((), ())), preferred_element_type=F32)


def dot_t(a, b):
    return lax.dot_general(a, b, (((1,), (1,)), ((), ())), preferred_element_type=F32)


def run(body, outs, args, scratch=(), flops=0, name=None, after=()):
    size = sum(math.prod(a.shape) * a.dtype.itemsize for a in args)
    size += sum(math.prod(s) * jnp.dtype(t).itemsize for s, t in outs)
    vmem = pl.BlockSpec(memory_space=pltpu.VMEM)
    rest = pl.BlockSpec(memory_space=pl.ANY)
    count, skip = len(args), len(args) + len(after)

    def whole(*refs):
        body(*refs[:count], *refs[skip:])

    return pl.pallas_call(
        whole,
        out_shape=[jax.ShapeDtypeStruct(s, t) for s, t in outs],
        in_specs=[vmem] * count + [rest] * len(after),
        out_specs=[vmem] * len(outs),
        scratch_shapes=list(scratch),
        compiler_params=pltpu.CompilerParams(vmem_limit_bytes=VMEM_BYTES),
        cost_estimate=pl.CostEstimate(flops=flops, bytes_accessed=size, transcendentals=0),
        name=name,
    )(*args, *after)


def gelu(v):
    return v * (0.5 * (1.0 + jnp.tanh(ROOT * (v + 0.044715 * (v * v * v)))))


def gelu_slope(v):
    tangent = jnp.tanh(ROOT * (v + 0.044715 * v * v * v))
    return 0.5 * (1.0 + tangent) + 0.5 * v * (1.0 - tangent * tangent) * ROOT * (
        1.0 + 3.0 * 0.044715 * v * v
    )


def round_up(value, step):
    return -(-value // step) * step


def pack_kv(keys, values):
    tokens, size = keys.shape
    rest = values[:, size:]
    half = tokens // 2
    tail = jnp.concatenate([rest[:half], rest[half:]], axis=1)
    return jnp.concatenate([keys, values[:, :size], tail], axis=0)


def unpack_values(packed, tokens, size):
    tail = packed[2 * tokens :]
    width = tail.shape[1] // 2
    rest = jnp.concatenate([tail[:, :width], tail[:, width:]], axis=0)
    return jnp.concatenate([packed[tokens : 2 * tokens], rest], axis=1)


def put(ref, start, rows):
    for c in range(ref.shape[0]):
        ref[c, start : start + rows.shape[0]] = rows[:, c * LANES : (c + 1) * LANES]


def every_second(ref, start, count):
    parts = [ref[c, pl.ds(start, count, stride=2)] for c in range(ref.shape[0])]
    return jnp.concatenate(parts, axis=1)


def open_kernel(x, pad, ends):
    positions, channels = x.shape
    ends[:16] = x[:16]
    ends[16:] = x[positions - 16 :]
    put(pad, 0, jnp.zeros((8, channels), F32))
    put(pad, 8, gelu(x[...].astype(F32)).astype(BF).astype(F32))
    put(pad, 8 + positions, jnp.zeros((pad.shape[1] - 8 - positions, channels), F32))


def front_kernel(ready, pair, across, weight, gain, wk, wv, kv_out, early, normed_out, pooled_out, pad):
    tokens = pooled_out.shape[0]
    ext = early.shape[0] // 2
    even = lax.axis_index("seq") % 2 == 0
    pair_wide, across_wide = pair[...].astype(F32), across[...].astype(F32)
    before = jnp.where(even, across_wide[16:], pair_wide[16:])[14:]
    after = jnp.where(even, pair_wide[:16], across_wide[:16])[:2]
    pad[...] = ready[...]
    put(pad, 6, gelu(before).astype(BF).astype(F32))
    put(pad, 8 + 2 * tokens, gelu(after).astype(BF).astype(F32))
    pieces = [every_second(pad, 6 + u, tokens).astype(BF) for u in range(6)]
    total = None
    for tap in range(5):
        rows = jnp.concatenate([pieces[tap], pieces[tap + 1]], axis=0)
        term = dot(rows, weight[tap])
        total = term if total is None else total + term
    pooled = 0.5 * (total[:tokens] + total[tokens:])
    inv = lax.rsqrt(jnp.mean(pooled * pooled, axis=-1, keepdims=True) + EPS)
    normed = (pooled * inv * gain[...]).astype(BF)
    pooled_out[...] = pooled
    normed_out[...] = normed
    kv_out[...] = pack_kv(dot(normed, wk[...]), dot_t(normed, wv[...])).astype(BF)
    early[0:ext] = every_second(pad, 6, ext).astype(BF)
    early[ext : 2 * ext] = every_second(pad, 7, ext).astype(BF)


def ordered(bits):
    masks = [0]
    for bit in reversed(bits):
        masks = masks + [mask | (1 << bit) for mask in masks]
    return masks


def split_rows(rows, columns):
    return round_up(-(-rows * LANES // columns), 16)


def query_kernel(normed, wq, early, out, message, own, *, order, rows, padded, scale):
    width = normed.shape[1]
    value = normed[...]
    out[...] = (dot(value, wq[...]) * scale).astype(BF)
    at, channels = early.shape
    message[:at] = early[...]
    count = len(order) * padded
    step = split_rows(count, channels)
    for i in range(4):
        block_of = place(i)
        pick = [chosen(rows, padded, width, block_of(k)) for k in order]
        part = dot_t(jnp.concatenate(pick, axis=0), value).astype(BF)
        if i == 0:
            own[...] = part
            continue
        for c in range(channels // LANES):
            piece = part[c * step : min((c + 1) * step, count)]
            message[at : at + piece.shape[0], c * LANES : (c + 1) * LANES] = piece
        at += step


def by_eight(rows):
    return rows.reshape(rows.shape[0] // 8, 8, rows.shape[1])


def attend_kernel(*refs, blocks, masks, heads, key_size, value_size, scale):
    q, cot = refs[:2]
    parts = refs[2 : 2 + blocks]
    att, dq, keep_a, send_a, keep_b, send_b = refs[2 + blocks : 8 + blocks]
    ks, vs, kt, vt, qs, cs, weights, score_cots, scores, prob_cots = refs[8 + blocks :]
    tokens = q.shape[0]
    half = tokens // 2
    wide = value_size - key_size
    for i, part in enumerate(parts):
        at = i * tokens
        ks[at : at + tokens] = part[:tokens]
        vs[at : at + tokens, :key_size] = part[tokens : 2 * tokens]
        vs[at : at + half, key_size:] = part[2 * tokens :, :wide]
        vs[at + half : at + tokens, key_size:] = part[2 * tokens :, wide:]
        kt[:, at : at + tokens] = ks[at : at + tokens].astype(F32).T.astype(BF)
        vt[:, at : at + tokens] = vs[at : at + tokens].astype(F32).T.astype(BF)
    for pair in range(heads // 2):
        ql, cl = 2 * pair * key_size, 2 * pair * value_size
        rows = slice(2 * pair * tokens, 2 * (pair + 1) * tokens)
        both = cot[:, cl : cl + 2 * value_size]
        qs[rows] = jnp.concatenate(
            [q[:, ql : ql + key_size], q[:, ql + key_size : ql + 2 * key_size]], axis=0
        )
        cs[rows] = jnp.concatenate([both[:, :value_size], both[:, value_size:]], axis=0)
        slot = pair % scores.shape[0]
        parts_of = [slice(i * tokens, (i + 1) * tokens) for i in range(blocks)]
        scores[slot] = dot_t(ks[...], qs[rows])
        prob_cots[slot] = dot_t(vs[...], cs[rows])
        top = functools.reduce(jnp.maximum, [by_eight(scores[slot, at]).max(0) for at in parts_of])
        top = jnp.max(top, axis=0, keepdims=True)
        sums = 0.0
        for at in parts_of:
            raised = jnp.exp(scores[slot, at] - top)
            sums = sums + by_eight(raised).sum(0)
            scores[slot, at] = raised
        inverse = 1.0 / jnp.sum(sums, axis=0, keepdims=True)
        for at in parts_of:
            weights[at, rows] = (scores[slot, at] * inverse).astype(BF)
        out_t = dot(vt[...], weights[:, rows]).astype(BF).astype(F32)
        delta = jnp.sum(cs[rows].astype(F32).T * out_t, axis=0, keepdims=True)
        for at in parts_of:
            probs = scores[slot, at] * inverse
            score_cots[at, rows] = (probs * (prob_cots[slot, at] - delta)).astype(BF)
        dq_t = dot(kt[...], score_cots[:, rows]) * scale
        out_rows = jnp.concatenate([out_t[:, :tokens].T, out_t[:, tokens:].T], axis=1)
        att[:, cl : cl + 2 * value_size] = out_rows.astype(BF)
        dq_rows = jnp.concatenate([dq_t[:, :tokens].T, dq_t[:, tokens:].T], axis=1)
        dq[:, ql : ql + 2 * key_size] = dq_rows.astype(BF)
    key_cots, value_cots = dot(score_cots[...], qs[...]), dot(weights[...], cs[...])
    edge = keep_a.shape[1]
    count = blocks // 2
    for i in range(blocks):
        at = slice(i * tokens, (i + 1) * tokens)
        packed = pack_kv(key_cots[at], value_cots[at])
        for order, keep, send, part in (
            (masks[0], keep_a, send_a, packed[:edge]),
            (masks[1], keep_b, send_b, packed[edge:]),
        ):
            k = order.index(i)
            if k < count:
                keep[k] = part
            else:
                send[k - count] = part.astype(BF)


def total_of(parts):
    total = parts[0][...]
    for part in parts[1:]:
        total = total + part[...].astype(F32)
    return total


def fold_kernel(*refs):
    keep, send = refs[-2:]
    total = total_of(refs[:-2])
    keep[...] = total[: keep.shape[0]]
    send[...] = total[keep.shape[0] :].astype(BF)


def fold_two_kernel(*refs):
    fold_kernel(refs[0], refs[1], refs[4], refs[5])
    fold_kernel(refs[2], refs[3], refs[6], refs[7])


def merge_kernel(keep_a, in_a, keep_b, in_b, keep, send):
    total = jnp.concatenate([total_of((keep_a, in_a)), total_of((keep_b, in_b))], axis=1)
    keep[...] = total[: keep.shape[0]]
    send[...] = total[keep.shape[0] :].astype(BF)


def send_on_kernel(keep, came, out):
    out[...] = (keep[...] + came[...].astype(F32)).astype(BF)


def query_cot_kernel(dq, wq, out):
    out[...] = dot_t(dq[...], wq[...])


def middle_kernel(own, came, part, pooled_in, gain_in, wk, wv, first, second, *edges):
    size = own.shape[2]
    tokens, width = pooled_in.shape
    total = (own[0] + came[0].astype(F32)).astype(BF).astype(F32)
    key_cot = total[:tokens]
    value_cot = unpack_values(total, tokens, size)
    normed_cot = part[...] + dot_t(key_cot.astype(BF), wk[...])
    normed_cot = normed_cot + dot(value_cot.astype(BF), wv[...])
    pooled, gain = pooled_in[...], gain_in[...]
    inv = lax.rsqrt(jnp.mean(pooled * pooled, axis=-1, keepdims=True) + EPS)
    gain_term = jnp.sum(normed_cot * pooled * inv, axis=0, keepdims=True)
    gained = gain * normed_cot
    pooled_cot = inv * gained - pooled * (inv * inv * inv) * (
        jnp.sum(gained * pooled, axis=-1, keepdims=True) / width
    )
    conv_cot = 0.5 * pooled_cot
    high = gain_term.astype(BF).astype(F32)
    low = gain_term - high
    row = lax.broadcasted_iota(jnp.int32, (16, width), 0)
    split = width // 2
    lines = (high[:, :split], low[:, :split], high[:, split:], low[:, split:])
    lines += (conv_cot[:1, split:], conv_cot[tokens - 1 :, split:])
    gains = jnp.zeros((16, split), F32)
    for i, line in enumerate(lines):
        gains = jnp.where(row[:, :split] == i, line, gains)
    fill = split - size - value_cot.shape[1]
    side = jnp.concatenate([key_cot, value_cot, jnp.zeros((tokens, fill), F32)], axis=1)
    first[:tokens] = conv_cot[:, :split].astype(BF)
    first[tokens:] = gains.astype(BF)
    second[:tokens] = conv_cot[:, split:].astype(BF)
    second[tokens:] = side.astype(BF)
    for edge in edges:
        ends = jnp.where(row == 0, conv_cot[:1], jnp.where(row == 1, conv_cot[tokens - 1 :], 0.0))
        edge[...] = ends.astype(BF)


def place(other=0):
    seq, dp = lax.axis_index("seq"), lax.axis_index("dp") ^ (other % 2)
    high, low = seq // 2, (seq % 2) ^ (other // 2)
    return lambda k: ((high ^ k) * 2 + low) * 2 + dp


def chosen(rows, padded, columns, block):
    row = lax.broadcasted_iota(jnp.int32, (padded, columns), 0)
    column = lax.broadcasted_iota(jnp.int32, (padded, columns), 1)
    hit = (column == row + block * rows) & (row < rows)
    return jnp.where(hit, 1.0, 0.0).astype(BF)


def select_kernel(*refs, order, rows, padded):
    own, blocks = refs[0], refs[1:5]
    out, norm_out, even, odd = refs[5:]
    ext, channels = even.shape
    tokens = own.shape[1]
    count = own.shape[0]
    step = split_rows(count, channels)
    norm_out[:, :tokens] = own[...]
    for i in range(1, 4):
        at = 2 * ext + (i - 1) * step
        for c in range(channels // LANES):
            end = min((c + 1) * step, count)
            piece = blocks[i][at : at + end - c * step, c * LANES : (c + 1) * LANES]
            norm_out[c * step : end, i * tokens : (i + 1) * tokens] = piece
    block_of = place()
    pick = jnp.concatenate(
        [chosen(rows, padded, 5 * channels, block_of(k)) for k in order], axis=0
    )
    for i, block in enumerate(blocks):
        even[...] = block[:ext].astype(F32)
        odd[...] = block[ext : 2 * ext].astype(F32)
        pieces = []
        for shift in range(3):
            pieces += [even[shift : shift + tokens].astype(BF), odd[shift : shift + tokens].astype(BF)]
        shifted = jnp.concatenate(
            [jnp.concatenate(pieces[:5], axis=1), jnp.concatenate(pieces[1:], axis=1)], axis=0
        )
        out[:, 2 * i * tokens : 2 * (i + 1) * tokens] = dot_t(pick, shifted).astype(BF)


def query_grad_kernel(pick, first, second, third, fourth, keep, send, right):
    tokens = first.shape[0]
    for i, block in enumerate((first, second, third, fourth)):
        right[i * tokens : (i + 1) * tokens] = block[...]
    count, pad = keep.shape[:2]
    for k in range(2 * count):
        term = dot(pick[k * pad : (k + 1) * pad], right[...])
        if k < count:
            keep[k] = term
        else:
            send[k - count] = term.astype(BF)


def side_rows(norm_rows, size, width):
    return norm_rows * size // width


def put_side(stage, at, part, rows):
    pieces = [part[i : i + rows] for i in range(0, part.shape[0], rows)]
    stage[at : at + rows] = jnp.concatenate(pieces, axis=1)


def get_side(packed, part, rows):
    size = part.shape[1]
    for i in range(part.shape[0] // rows):
        part[i * rows : (i + 1) * rows] = packed[:, i * size : (i + 1) * size]


def stack_cots(blocks, right, tokens):
    for i, block in enumerate(blocks):
        piece = block[:tokens]
        right[2 * i * tokens : (2 * i + 1) * tokens] = piece
        right[(2 * i + 1) * tokens : (2 * i + 2) * tokens] = piece


def conv_first_kernel(*refs, conv_rows, conv_pad):
    pick, blocks, outs, right, stage = refs[0], refs[1:5], refs[5:9], refs[9], refs[10]
    tokens = right.shape[0] // 8
    stack_cots(blocks, right, tokens)
    stage[...] = jnp.zeros(stage.shape, F32)
    for half in range(2):
        gain = None
        for block in blocks:
            lines = block[tokens : tokens + 16].astype(F32)[2 * half : 2 * half + 2]
            term = lines[0:1] + lines[1:2]
            gain = term if gain is None else gain + term
        high = gain.astype(BF).astype(F32)
        at = conv_rows + 2 * half
        stage[at : at + 1] = high
        stage[at + 1 : at + 2] = gain - high
    count, above = outs[0].shape[:2]
    even = lax.axis_index("seq") % 2 == 0
    own, pair = blocks[0], blocks[2]
    tops = [b[0:16].astype(F32)[0:1] for b in (own, pair)]
    bottoms = [b[tokens - 16 : tokens].astype(F32)[15:16] for b in (own, pair)]
    rests = [b[tokens : tokens + 16].astype(F32)[4:6] for b in (own, pair)]
    for k in range(4 * count):
        conv = dot(pick[k * conv_pad : (k + 1) * conv_pad], right[...])
        stage[:conv_rows] = conv[:conv_rows]
        if k == 3 * count:
            stage[above - 4 : above - 3] = jnp.where(even, tops[0], tops[1])
            stage[above - 3 : above - 2] = jnp.where(even, rests[0][0:1], rests[1][0:1])
            stage[above - 2 : above - 1] = jnp.where(even, bottoms[1], bottoms[0])
            stage[above - 1 : above] = jnp.where(even, rests[1][1:2], rests[0][1:2])
        out = outs[k // count]
        out[k % count] = stage[...].astype(out.dtype)


def conv_second_kernel(*refs, conv_rows, conv_pad, norm_rows, norm_pad, key_size, value_size):
    pick, norm_pick, blocks, first_send = refs[0], refs[1], refs[2:6], refs[6]
    near_keep, far_keep, near_send, far_send, right, side, stage = refs[7:]
    tokens, width = right.shape[0] // 8, right.shape[1]
    stack_cots(blocks, right, tokens)
    for i, block in enumerate(blocks):
        side[i * tokens : (i + 1) * tokens] = block[tokens:]
    key_rows = side_rows(norm_rows, key_size, width)
    value_rows = side_rows(norm_rows, value_size, width)
    stage[...] = jnp.zeros(stage.shape, F32)
    count, above = first_send.shape[:2]
    near_send[:, :above] = first_send[...]
    for k in range(4 * count):
        conv = dot(pick[k * conv_pad : (k + 1) * conv_pad], right[...])
        stage[:conv_rows] = conv[:conv_rows]
        both = dot(norm_pick[k * norm_pad : (k + 1) * norm_pad], side[...])
        put_side(stage, conv_rows, both[:norm_rows, :key_size], key_rows)
        value = both[:norm_rows, key_size : key_size + value_size]
        put_side(stage, conv_rows + key_rows, value, value_rows)
        if k < 2 * count:
            (near_keep, far_keep)[k // count][k % count] = stage[...]
        elif k < 3 * count:
            near_send[k % count, above:] = stage[...].astype(BF)
        else:
            far_send[k % count] = stage[...].astype(BF)


def first_sum_kernel(keep, near, far, out):
    above = keep.shape[1]
    out[...] = keep[...] + near[:, :above].astype(F32) + far[...].astype(F32)


def combine_kernel(first, second, near, far, out):
    above = first.shape[1]
    out[:, :above] = first[...]
    out[:, above:] = second[...] + near[:, above:].astype(F32) + far[...].astype(F32)


def final_kernel(*refs, conv_parts, above):
    conv, query, key, value, gain, stage = refs[-6:]
    rows, width = conv.shape
    split = width // 2
    count = key.shape[0]
    if conv_parts == 4:
        combine_kernel(*refs[:4], stage)
    else:
        stage[...] = total_of(refs[:conv_parts])
    query[...] = total_of(refs[conv_parts:-6])[0, : query.shape[0]]
    conv[:, :split] = stage[0, :rows]
    conv[:, split:] = stage[0, above : above + rows]
    at = above + rows
    for part in (key, value):
        step = side_rows(count, part.shape[1], split)
        get_side(stage[0, at : at + step], part, step)
        at += step
    lines = stage[0, rows : rows + 4]
    line = jnp.concatenate([lines[0:1] + lines[1:2], lines[2:3] + lines[3:4]], axis=1)
    line = jnp.broadcast_to(line, (8, width))
    start = place()(0) * count
    gain[...] = pltpu.roll(line, lax.rem(width - start, width), 1)[:1, :count]


def input_kernel(*refs):
    x, first, second, pair_first, pair_second, one, three, weight, out, ext, mixed = refs
    tokens = x.shape[0] // 2
    seq, devices = lax.axis_index("seq"), lax.axis_size("seq")
    low, high = seq % 2, seq // 2
    split = first.shape[1]
    above = one.shape[1]
    one_rows = one[0, above - 16 :].astype(F32)[12:]
    three_rows = three[0, above - 16 :].astype(F32)[12:]
    heads = jnp.where(high % 2 == 0, one_rows[:2], three_rows[:2])
    tails = jnp.where(high % 2 == 0, three_rows[2:], one_rows[2:])
    heads = jnp.where(seq == devices - 1, 0.0, heads)
    tails = jnp.where(seq == 0, 0.0, tails)
    for half, own, pair in ((0, first, pair_first), (1, second, pair_second)):
        lanes = slice(half * split, (half + 1) * split)
        top = pair[0:16].astype(F32)[0:1]
        bottom = pair[tokens - 16 : tokens].astype(F32)[15:16]
        ext[8 : 8 + tokens, lanes] = own[:tokens].astype(F32)
        ext[7:8, lanes] = jnp.where(low == 0, tails[half : half + 1], bottom)
        ext[8 + tokens : 9 + tokens, lanes] = jnp.where(low == 0, top, heads[half : half + 1])
    back = ext[7 : 7 + tokens].astype(BF)
    here = ext[8 : 8 + tokens].astype(BF)
    ahead = ext[9 : 9 + tokens].astype(BF)
    evens = (ahead, here, here, back, back)
    odds = (ahead, ahead, here, here, back)
    total = None
    for tap in range(5):
        term = dot_t(jnp.concatenate([evens[tap], odds[tap]], axis=0), weight[tap])
        total = term if total is None else total + term
    for c in range(mixed.shape[0]):
        lanes = slice(c * LANES, (c + 1) * LANES)
        mixed[c, pl.ds(0, tokens, stride=2)] = total[:tokens, lanes]
        mixed[c, pl.ds(1, tokens, stride=2)] = total[tokens:, lanes]
        out[:, lanes] = (mixed[c] * gelu_slope(x[:, lanes].astype(F32))).astype(BF)


def on_device(x, conv_weight, norm_gain, wq, wk, wv, cotangent):
    devices = lax.axis_size("seq")
    both_axes = ("seq", "dp")
    x, cotangent = x[0], cotangent[0]
    positions, channels = x.shape
    tokens = positions // 2
    taps, _, width = conv_weight.shape
    key_size, value_size = wk.shape[1], wv.shape[1]
    heads = cotangent.shape[1] // value_size
    scale = key_size ** (-0.5)
    groups = devices // 2
    owners = devices * 2
    conv_rows, norm_rows = taps * channels // owners, width // owners
    conv_pad, norm_pad = round_up(conv_rows, 16), round_up(norm_rows, 16)
    ext = tokens + 16
    gain = norm_gain.reshape(1, width)

    def swap(value, seq_bits, dp_bit=0):
        mask = 2 * seq_bits + dp_bit
        return lax.ppermute(value, both_axes, [(i, i ^ mask) for i in range(owners)])

    def held(value, *until):
        return lax.optimization_barrier((value,) + until)[0]

    def quad(value, *until):
        core = swap(value, 0, 1)
        near = swap(value, 1)
        return [value, core, near, swap(held(near, *until), 0, 1)]

    def fold(parts, name):
        shape = (parts[0].shape[0] // 2,) + parts[0].shape[1:]
        return run(fold_kernel, [(shape, F32), (shape, BF)], parts, name=name)

    def halved(keep, send, bits, name):
        for bit in bits[:-1]:
            keep, send = fold([keep, swap(send, 1 << bit)], name)
        return [keep, swap(send, 1 << bits[-1])]

    bits = list(range(devices.bit_length() - 1))
    order = [mask // 2 for mask in ordered(bits[1:])]
    crossing = [(i, i + 1) for i in range(1, devices - 1, 2)]
    crossing = crossing + [(j, i) for i, j in crossing]
    pad_shape = (channels // LANES, 8 + 2 * ext + 8, LANES)
    ready, ends = run(
        open_kernel,
        [(pad_shape, F32), ((32, channels), BF)],
        [x],
        flops=4 * 10**9,
        name="gelu",
    )
    pair, across = swap(ends, 1), lax.ppermute(ends, "seq", crossing)
    wv = wv.T
    kv, early, normed, pooled = run(
        front_kernel,
        [
            ((5 * tokens // 2, key_size), BF),
            ((2 * ext, channels), BF),
            ((tokens, width), BF),
            ((tokens, width), F32),
        ],
        [ready, pair, across, conv_weight, gain, wk, wv],
        [pltpu.VMEM(pad_shape, F32)],
        flops=2 * positions * taps * channels * width,
        name="front",
    )
    near_kv = [kv] + [swap(kv, 2 * k) for k in range(1, groups)]
    far_kv = [swap(block, 1) for block in near_kv]
    picked = (groups * norm_pad, tokens)
    rows = 2 * ext + 3 * split_rows(picked[0], channels)
    queries, early, pick_own = run(
        lambda *refs: query_kernel(
            *refs, order=order, rows=norm_rows, padded=norm_pad, scale=scale
        ),
        [((tokens, heads * key_size), BF), ((rows, channels), BF), (picked, BF)],
        [normed, wq, early],
        flops=4 * tokens * width * heads * key_size,
        name="queries",
        after=near_kv[1:],
    )
    early = held(early, *far_kv)
    length = devices * tokens
    masks = [2 * k for k in range(groups)] + [2 * k + 1 for k in range(groups)]
    half_block = (groups, 5 * tokens // 4, key_size)
    slots = 2 if length <= 2048 else 1
    attended, query_cot, keep_a, send_a, keep_b, send_b = run(
        lambda *refs: attend_kernel(
            *refs,
            blocks=devices,
            masks=[
                [masks.index(m) for m in ordered(way)] for way in (bits, [1, 0] + bits[2:])
            ],
            heads=heads,
            key_size=key_size,
            value_size=value_size,
            scale=scale,
        ),
        [((tokens, heads * value_size), BF), ((tokens, heads * key_size), BF)]
        + [(half_block, F32), (half_block, BF)] * 2,
        [queries, cotangent] + near_kv + far_kv,
        [
            pltpu.VMEM((length, key_size), BF),
            pltpu.VMEM((length, value_size), BF),
            pltpu.VMEM((key_size, length), BF),
            pltpu.VMEM((value_size, length), BF),
            pltpu.VMEM((heads * tokens, key_size), BF),
            pltpu.VMEM((heads * tokens, value_size), BF),
            pltpu.VMEM((length, heads * tokens), BF),
            pltpu.VMEM((length, heads * tokens), BF),
            pltpu.VMEM((slots, length, 2 * tokens), F32),
            pltpu.VMEM((slots, length, 2 * tokens), F32),
        ],
        flops=6 * tokens * heads * length * (key_size + value_size),
        name="attend",
    )
    in_a, in_b = swap(send_a, 1), swap(send_b, 2)
    early_blocks = quad(early, send_a)
    conv_pick, norm_pick = run(
        lambda *refs: select_kernel(*refs, order=order, rows=conv_rows, padded=conv_pad),
        [((groups * conv_pad, 8 * tokens), BF), ((groups * norm_pad, 4 * tokens), BF)],
        [pick_own] + early_blocks,
        [pltpu.VMEM((ext, channels), F32), pltpu.VMEM((ext, channels), F32)],
        flops=2 * groups * conv_pad * taps * channels * 8 * tokens,
        name="select",
    )
    fourth = (groups // 2,) + half_block[1:]
    keep_a, send_a, keep_b, send_b = run(
        fold_two_kernel,
        [(fourth, F32), (fourth, BF)] * 2,
        [keep_a, in_a, keep_b, in_b],
        name="kv_cot_fold",
        after=[conv_pick],
    )
    in_a, in_b = swap(send_a, 2), swap(send_b, 1)
    block = (groups // 4, 5 * tokens // 2, key_size)
    keep, send = run(
        merge_kernel,
        [(block, F32), (block, BF)],
        [keep_a, in_a, keep_b, in_b],
        name="kv_cot_merge",
    )
    (normed_cot,) = run(
        query_cot_kernel,
        [((tokens, width), F32)],
        [query_cot, wq],
        flops=2 * tokens * width * heads * key_size,
        name="query_part",
    )
    query_cot = held(query_cot, keep)
    query_near, query_core = swap(query_cot, 1), swap(query_cot, 0, 1)
    kv_cot = halved(keep, send, bits[2:], "kv_cot_fold")
    first, second, *edge = run(
        middle_kernel,
        [
            ((tokens + 16, width // 2), BF),
            ((2 * tokens, width // 2), BF),
        ]
        + [((16, width), BF)] * (len(bits) > 3),
        kv_cot + [normed_cot, pooled, gain, wk, wv],
        flops=2 * tokens * width * (key_size + value_size),
        name="conv_cot",
    )
    near_first, near_second = swap(first, 1), swap(second, 1)
    query_last = swap(held(query_near, first), 0, 1)
    query_half = (groups // 2, norm_pad, heads * key_size)
    query_keep, query_send = run(
        query_grad_kernel,
        [(query_half, F32), (query_half, BF)],
        [norm_pick, query_cot, query_core, query_near, query_last],
        [pltpu.VMEM((4 * tokens, heads * key_size), BF)],
        flops=2 * groups * norm_pad * 4 * tokens * heads * key_size,
        name="query_grad",
    )
    query_parts = halved(query_keep, query_send, bits[1:], "query_fold")
    core_first, core_second = swap(first, 0, 1), swap(second, 0, 1)
    split = width // 2
    side = side_rows(norm_rows, key_size, split) + side_rows(norm_rows, value_size, split)
    above, below = round_up(conv_rows + 8, 16), round_up(conv_rows + side, 16)
    count = groups // 4
    last_first = swap(held(near_first, query_keep), 0, 1)
    near_keep, far_keep, near_send, far_send = run(
        lambda *refs: conv_first_kernel(*refs, conv_rows=conv_rows, conv_pad=conv_pad),
        [((count, above, split), t) for t in (F32, F32, BF, BF)],
        [conv_pick, first, core_first, near_first, last_first],
        [pltpu.VMEM((8 * tokens, split), BF), pltpu.VMEM((above, split), F32)],
        flops=groups * conv_pad * 8 * tokens * width,
        name="conv_grad_first",
    )
    far_in = swap(far_send, 2)
    last_second = swap(held(near_second, near_keep, query_parts[0]), 0, 1)
    near_keep_second, far_keep_second, near_send, far_send = run(
        lambda *refs: conv_second_kernel(
            *refs,
            conv_rows=conv_rows,
            conv_pad=conv_pad,
            norm_rows=norm_rows,
            norm_pad=norm_pad,
            key_size=key_size,
            value_size=value_size,
        ),
        [
            ((count, below, split), F32),
            ((count, below, split), F32),
            ((count, above + below, split), BF),
            ((count, below, split), BF),
        ],
        [conv_pick, norm_pick, second, core_second, near_second, last_second, near_send],
        [
            pltpu.VMEM((8 * tokens, split), BF),
            pltpu.VMEM((4 * tokens, split), BF),
            pltpu.VMEM((below, split), F32),
        ],
        flops=groups * conv_pad * 8 * tokens * width,
        name="conv_grad_second",
    )
    far_in_second = swap(far_send, 2)
    near_in = swap(near_send, 2)
    (far_sum,) = run(
        send_on_kernel,
        [((count, above, split), BF)],
        [far_keep, far_in],
        name="conv_send_on",
    )
    far_last = swap(far_sum, 4)
    (far_sum,) = run(
        send_on_kernel,
        [((count, below, split), BF)],
        [far_keep_second, far_in_second],
        name="conv_send_on",
    )
    edges = [far_in, far_last]
    if len(bits) > 3:
        came = lax.ppermute(edge[0], "seq", crossing)
        rows = jnp.concatenate([came[:1, :split], came[:1, split:], came[1:2, :split], came[1:2, split:]])
        edges = [jnp.pad(rows, ((above - 4, 0), (0, 0)))[None]] * 2
    (input_grad,) = run(
        input_kernel,
        [((positions, channels), BF)],
        [held(x, far_sum, query_parts[1]), first, second, near_first, near_second] + edges + [conv_weight],
        [
            pltpu.VMEM((tokens + 16, width), F32),
            pltpu.VMEM((channels // LANES, positions, LANES), F32),
        ],
        flops=20 * positions * taps * channels * width,
        name="input_grad",
    )
    (first_sum,) = run(
        first_sum_kernel,
        [((count, above, split), F32)],
        [near_keep, near_in, far_last],
        flops=5 * 10**9,
        name="conv_first_sum",
    )
    conv_parts = [first_sum, near_keep_second, near_in, swap(far_sum, 4)]
    chunk = (count, above + below, split)
    if len(bits) > 3:
        keep = run(combine_kernel, [(chunk, F32)], conv_parts, name="conv_combine")[0]
        half = (count // 2,) + chunk[1:]
        keep, send = run(fold_kernel, [(half, F32), (half, BF)], [keep], name="conv_fold")
        conv_parts = halved(keep, send, bits[3:], "conv_fold")
    conv_grad, query_grad, key_grad, value_grad, gain_grad = run(
        lambda *refs: final_kernel(*refs, conv_parts=len(conv_parts), above=above),
        [
            ((conv_rows, width), F32),
            ((norm_rows, heads * key_size), F32),
            ((norm_rows, key_size), F32),
            ((norm_rows, value_size), F32),
            ((1, norm_rows), F32),
        ],
        conv_parts + query_parts,
        [pltpu.VMEM((1,) + chunk[1:], F32)],
        name="final_sum",
    )
    return (
        attended[None],
        input_grad[None],
        conv_grad,
        query_grad,
        key_grad,
        value_grad,
        gain_grad.reshape(norm_rows),
    )


def solution(mesh):
    placed = (
        P(("groups", "dp"), "seq", None),
        P(),
        P(),
        P(),
        P(),
        P(),
        P(("groups", "dp"), "seq", None),
    )
    return jax.shard_map(
        on_device,
        mesh=mesh,
        in_specs=placed,
        out_specs=(
            P(("groups", "dp"), "seq", None),
            P(("groups", "dp"), "seq", None),
            P(("groups", "seq", "dp"), None),
            P(("groups", "seq", "dp"), None),
            P(("groups", "seq", "dp"), None),
            P(("groups", "seq", "dp"), None),
            P(("groups", "seq", "dp")),
        ),
        check_vma=False,
    )
```

```python
import functools
import math

import jax
import jax.numpy as jnp
from jax import lax
from jax.experimental import pallas as pl
from jax.experimental.pallas import tpu as pltpu
from jax.sharding import PartitionSpec as P

BF = jnp.bfloat16
F32 = jnp.float32
ROOT = math.sqrt(2.0 / math.pi)
EPS = 1e-06
LANES = 128
VMEM_BYTES = 40 * 2**20


def dot(a, b):
    return lax.dot_general(a, b, (((1,), (0,)), ((), ())), preferred_element_type=F32)


def dot_t(a, b):
    return lax.dot_general(a, b, (((1,), (1,)), ((), ())), preferred_element_type=F32)


def run(body, outs, args, scratch=(), flops=0, name=None, after=()):
    size = sum(math.prod(a.shape) * a.dtype.itemsize for a in args)
    size += sum(math.prod(s) * jnp.dtype(t).itemsize for s, t in outs)
    vmem = pl.BlockSpec(memory_space=pltpu.VMEM)
    rest = pl.BlockSpec(memory_space=pl.ANY)
    count, skip = len(args), len(args) + len(after)

    def whole(*refs):
        body(*refs[:count], *refs[skip:])

    return pl.pallas_call(
        whole,
        out_shape=[jax.ShapeDtypeStruct(s, t) for s, t in outs],
        in_specs=[vmem] * count + [rest] * len(after),
        out_specs=[vmem] * len(outs),
        scratch_shapes=list(scratch),
        compiler_params=pltpu.CompilerParams(vmem_limit_bytes=VMEM_BYTES),
        cost_estimate=pl.CostEstimate(flops=flops, bytes_accessed=size, transcendentals=0),
        name=name,
    )(*args, *after)


def gelu(v):
    return v * (0.5 * (1.0 + jnp.tanh(ROOT * (v + 0.044715 * (v * v * v)))))


def gelu_slope(v):
    tangent = jnp.tanh(ROOT * (v + 0.044715 * v * v * v))
    return 0.5 * (1.0 + tangent) + 0.5 * v * (1.0 - tangent * tangent) * ROOT * (
        1.0 + 3.0 * 0.044715 * v * v
    )


def round_up(value, step):
    return -(-value // step) * step


def pack_kv(keys, values):
    tokens, size = keys.shape
    rest = values[:, size:]
    half = tokens // 2
    tail = jnp.concatenate([rest[:half], rest[half:]], axis=1)
    return jnp.concatenate([keys, values[:, :size], tail], axis=0)


def unpack_values(packed, tokens, size):
    tail = packed[2 * tokens :]
    width = tail.shape[1] // 2
    rest = jnp.concatenate([tail[:, :width], tail[:, width:]], axis=0)
    return jnp.concatenate([packed[tokens : 2 * tokens], rest], axis=1)


def put(ref, start, rows):
    for c in range(ref.shape[0]):
        ref[c, start : start + rows.shape[0]] = rows[:, c * LANES : (c + 1) * LANES]


def every_second(ref, start, count):
    parts = [ref[c, pl.ds(start, count, stride=2)] for c in range(ref.shape[0])]
    return jnp.concatenate(parts, axis=1)


def open_kernel(x, pad, ends):
    positions, channels = x.shape
    ends[:16] = x[:16]
    ends[16:] = x[positions - 16 :]
    put(pad, 0, jnp.zeros((8, channels), F32))
    put(pad, 8, gelu(x[...].astype(F32)).astype(BF).astype(F32))
    put(pad, 8 + positions, jnp.zeros((pad.shape[1] - 8 - positions, channels), F32))


def front_kernel(ready, pair, across, weight, gain, wk, wv, kv_out, early, normed_out, pooled_out, pad):
    tokens = pooled_out.shape[0]
    ext = early.shape[0] // 2
    even = lax.axis_index("seq") % 2 == 0
    pair_wide, across_wide = pair[...].astype(F32), across[...].astype(F32)
    before = jnp.where(even, across_wide[16:], pair_wide[16:])[14:]
    after = jnp.where(even, pair_wide[:16], across_wide[:16])[:2]
    pad[...] = ready[...]
    put(pad, 6, gelu(before).astype(BF).astype(F32))
    put(pad, 8 + 2 * tokens, gelu(after).astype(BF).astype(F32))
    pieces = [every_second(pad, 6 + u, tokens).astype(BF) for u in range(6)]
    total = None
    for tap in range(5):
        rows = jnp.concatenate([pieces[tap], pieces[tap + 1]], axis=0)
        term = dot(rows, weight[tap])
        total = term if total is None else total + term
    pooled = 0.5 * (total[:tokens] + total[tokens:])
    inv = lax.rsqrt(jnp.mean(pooled * pooled, axis=-1, keepdims=True) + EPS)
    normed = (pooled * inv * gain[...]).astype(BF)
    pooled_out[...] = pooled
    normed_out[...] = normed
    kv_out[...] = pack_kv(dot(normed, wk[...]), dot_t(normed, wv[...])).astype(BF)
    early[0:ext] = every_second(pad, 6, ext).astype(BF)
    early[ext : 2 * ext] = every_second(pad, 7, ext).astype(BF)


def ordered(bits):
    masks = [0]
    for bit in reversed(bits):
        masks = masks + [mask | (1 << bit) for mask in masks]
    return masks


def split_rows(rows, columns):
    return round_up(-(-rows * LANES // columns), 16)


def query_kernel(normed, wq, early, out, near, core, own, *, order, rows, padded, scale):
    width = normed.shape[1]
    value = normed[...]
    out[...] = (dot(value, wq[...]) * scale).astype(BF)
    ext, channels = early.shape
    near[:ext] = early[...]
    core[:ext] = early[...]
    count = len(order) * padded
    step = split_rows(count, channels)
    for i in range(4):
        block_of = place(i)
        pick = [chosen(rows, padded, width, block_of(k)) for k in order]
        part = dot_t(jnp.concatenate(pick, axis=0), value).astype(BF)
        if i == 0:
            own[...] = part
            continue
        message, at = ((core, ext), (near, ext), (near, ext + step))[i - 1]
        for c in range(channels // LANES):
            piece = part[c * step : min((c + 1) * step, count)]
            message[at : at + piece.shape[0], c * LANES : (c + 1) * LANES] = piece


def by_eight(rows):
    return rows.reshape(rows.shape[0] // 8, 8, rows.shape[1])


def attend_kernel(*refs, blocks, masks, heads, key_size, value_size, scale):
    q, cot = refs[:2]
    parts = refs[2 : 2 + blocks]
    att, dq, keep_a, send_a, keep_b, send_b = refs[2 + blocks : 8 + blocks]
    ks, vs, kt, vt, qs, cs, weights, score_cots, scores, prob_cots = refs[8 + blocks :]
    tokens = q.shape[0]
    half = tokens // 2
    wide = value_size - key_size
    for i, part in enumerate(parts):
        at = i * tokens
        ks[at : at + tokens] = part[:tokens]
        vs[at : at + tokens, :key_size] = part[tokens : 2 * tokens]
        vs[at : at + half, key_size:] = part[2 * tokens :, :wide]
        vs[at + half : at + tokens, key_size:] = part[2 * tokens :, wide:]
        kt[:, at : at + tokens] = ks[at : at + tokens].astype(F32).T.astype(BF)
        vt[:, at : at + tokens] = vs[at : at + tokens].astype(F32).T.astype(BF)
    for pair in range(heads // 2):
        ql, cl = 2 * pair * key_size, 2 * pair * value_size
        rows = slice(2 * pair * tokens, 2 * (pair + 1) * tokens)
        both = cot[:, cl : cl + 2 * value_size]
        qs[rows] = jnp.concatenate(
            [q[:, ql : ql + key_size], q[:, ql + key_size : ql + 2 * key_size]], axis=0
        )
        cs[rows] = jnp.concatenate([both[:, :value_size], both[:, value_size:]], axis=0)
        slot = pair % scores.shape[0]
        parts_of = [slice(i * tokens, (i + 1) * tokens) for i in range(blocks)]
        scores[slot] = dot_t(ks[...], qs[rows])
        prob_cots[slot] = dot_t(vs[...], cs[rows])
        top = functools.reduce(jnp.maximum, [by_eight(scores[slot, at]).max(0) for at in parts_of])
        top = jnp.max(top, axis=0, keepdims=True)
        sums = 0.0
        for at in parts_of:
            raised = jnp.exp(scores[slot, at] - top)
            sums = sums + by_eight(raised).sum(0)
            scores[slot, at] = raised
        inverse = 1.0 / jnp.sum(sums, axis=0, keepdims=True)
        for at in parts_of:
            weights[at, rows] = (scores[slot, at] * inverse).astype(BF)
        out_t = dot(vt[...], weights[:, rows]).astype(BF).astype(F32)
        delta = jnp.sum(cs[rows].astype(F32).T * out_t, axis=0, keepdims=True)
        for at in parts_of:
            probs = scores[slot, at] * inverse
            score_cots[at, rows] = (probs * (prob_cots[slot, at] - delta)).astype(BF)
        dq_t = dot(kt[...], score_cots[:, rows]) * scale
        out_rows = jnp.concatenate([out_t[:, :tokens].T, out_t[:, tokens:].T], axis=1)
        att[:, cl : cl + 2 * value_size] = out_rows.astype(BF)
        dq_rows = jnp.concatenate([dq_t[:, :tokens].T, dq_t[:, tokens:].T], axis=1)
        dq[:, ql : ql + 2 * key_size] = dq_rows.astype(BF)
    key_cots, value_cots = dot(score_cots[...], qs[...]), dot(weights[...], cs[...])
    edge = keep_a.shape[1]
    count = blocks // 2
    for i in range(blocks):
        at = slice(i * tokens, (i + 1) * tokens)
        packed = pack_kv(key_cots[at], value_cots[at])
        for order, keep, send, part in (
            (masks[0], keep_a, send_a, packed[:edge]),
            (masks[1], keep_b, send_b, packed[edge:]),
        ):
            k = order.index(i)
            if k < count:
                keep[k] = part
            else:
                send[k - count] = part.astype(BF)


def total_of(parts):
    total = parts[0][...]
    for part in parts[1:]:
        total = total + part[...].astype(F32)
    return total


def fold_kernel(*refs):
    keep, send = refs[-2:]
    total = total_of(refs[:-2])
    keep[...] = total[: keep.shape[0]]
    send[...] = total[keep.shape[0] :].astype(BF)


def fold_two_kernel(*refs):
    fold_kernel(refs[0], refs[1], refs[4], refs[5])
    fold_kernel(refs[2], refs[3], refs[6], refs[7])


def merge_kernel(keep_a, in_a, keep_b, in_b, keep, send):
    total = jnp.concatenate([total_of((keep_a, in_a)), total_of((keep_b, in_b))], axis=1)
    keep[...] = total[: keep.shape[0]]
    send[...] = total[keep.shape[0] :].astype(BF)


def send_on_kernel(keep, came, out):
    out[...] = (keep[...] + came[...].astype(F32)).astype(BF)


def query_cot_kernel(dq, wq, out):
    out[...] = dot_t(dq[...], wq[...])


def middle_kernel(own, came, part, pooled_in, gain_in, wk, wv, first, second, *edges):
    size = own.shape[2]
    tokens, width = pooled_in.shape
    total = (own[0] + came[0].astype(F32)).astype(BF).astype(F32)
    key_cot = total[:tokens]
    value_cot = unpack_values(total, tokens, size)
    normed_cot = part[...] + dot_t(key_cot.astype(BF), wk[...])
    normed_cot = normed_cot + dot(value_cot.astype(BF), wv[...])
    pooled, gain = pooled_in[...], gain_in[...]
    inv = lax.rsqrt(jnp.mean(pooled * pooled, axis=-1, keepdims=True) + EPS)
    gain_term = jnp.sum(normed_cot * pooled * inv, axis=0, keepdims=True)
    gained = gain * normed_cot
    pooled_cot = inv * gained - pooled * (inv * inv * inv) * (
        jnp.sum(gained * pooled, axis=-1, keepdims=True) / width
    )
    conv_cot = 0.5 * pooled_cot
    high = gain_term.astype(BF).astype(F32)
    low = gain_term - high
    row = lax.broadcasted_iota(jnp.int32, (16, width), 0)
    split = width // 2
    lines = (high[:, :split], low[:, :split], high[:, split:], low[:, split:])
    lines += (conv_cot[:1, split:], conv_cot[tokens - 1 :, split:])
    gains = jnp.zeros((16, split), F32)
    for i, line in enumerate(lines):
        gains = jnp.where(row[:, :split] == i, line, gains)
    fill = split - size - value_cot.shape[1]
    side = jnp.concatenate([key_cot, value_cot, jnp.zeros((tokens, fill), F32)], axis=1)
    first[:tokens] = conv_cot[:, :split].astype(BF)
    first[tokens:] = gains.astype(BF)
    second[:tokens] = conv_cot[:, split:].astype(BF)
    second[tokens:] = side.astype(BF)
    for edge in edges:
        ends = jnp.where(row == 0, conv_cot[:1], jnp.where(row == 1, conv_cot[tokens - 1 :], 0.0))
        edge[...] = ends.astype(BF)


def place(other=0):
    seq, dp = lax.axis_index("seq"), lax.axis_index("dp") ^ (other % 2)
    high, low = seq // 2, (seq % 2) ^ (other // 2)
    return lambda k: ((high ^ k) * 2 + low) * 2 + dp


def chosen(rows, padded, columns, block):
    row = lax.broadcasted_iota(jnp.int32, (padded, columns), 0)
    column = lax.broadcasted_iota(jnp.int32, (padded, columns), 1)
    hit = (column == row + block * rows) & (row < rows)
    return jnp.where(hit, 1.0, 0.0).astype(BF)


def select_kernel(*refs, order, rows, padded):
    own, blocks = refs[0], refs[1:5]
    out, norm_out, even, odd = refs[5:]
    ext, channels = even.shape
    tokens = own.shape[1]
    count = own.shape[0]
    step = split_rows(count, channels)
    norm_out[:, :tokens] = own[...]
    for i in range(1, 4):
        at = 2 * ext + (i // 3) * step
        for c in range(channels // LANES):
            end = min((c + 1) * step, count)
            piece = blocks[i][at : at + end - c * step, c * LANES : (c + 1) * LANES]
            norm_out[c * step : end, i * tokens : (i + 1) * tokens] = piece
    block_of = place()
    pick = jnp.concatenate(
        [chosen(rows, padded, 5 * channels, block_of(k)) for k in order], axis=0
    )
    for i, block in enumerate(blocks):
        even[...] = block[:ext].astype(F32)
        odd[...] = block[ext : 2 * ext].astype(F32)
        pieces = []
        for shift in range(3):
            pieces += [even[shift : shift + tokens].astype(BF), odd[shift : shift + tokens].astype(BF)]
        shifted = jnp.concatenate(
            [jnp.concatenate(pieces[:5], axis=1), jnp.concatenate(pieces[1:], axis=1)], axis=0
        )
        out[:, 2 * i * tokens : 2 * (i + 1) * tokens] = dot_t(pick, shifted).astype(BF)


def query_grad_kernel(pick, first, second, third, fourth, keep, send, right):
    tokens = first.shape[0]
    for i, block in enumerate((first, second, third, fourth)):
        right[i * tokens : (i + 1) * tokens] = block[...]
    count, pad = keep.shape[:2]
    for k in range(2 * count):
        term = dot(pick[k * pad : (k + 1) * pad], right[...])
        if k < count:
            keep[k] = term
        else:
            send[k - count] = term.astype(BF)


def side_rows(norm_rows, size, width):
    return norm_rows * size // width


def put_side(stage, at, part, rows):
    pieces = [part[i : i + rows] for i in range(0, part.shape[0], rows)]
    stage[at : at + rows] = jnp.concatenate(pieces, axis=1)


def get_side(packed, part, rows):
    size = part.shape[1]
    for i in range(part.shape[0] // rows):
        part[i * rows : (i + 1) * rows] = packed[:, i * size : (i + 1) * size]


def stack_cots(blocks, right, tokens):
    for i, block in enumerate(blocks):
        piece = block[:tokens]
        right[2 * i * tokens : (2 * i + 1) * tokens] = piece
        right[(2 * i + 1) * tokens : (2 * i + 2) * tokens] = piece


def conv_first_kernel(*refs, conv_rows, conv_pad):
    pick, blocks, outs, right, stage = refs[0], refs[1:5], refs[5:9], refs[9], refs[10]
    tokens = right.shape[0] // 8
    stack_cots(blocks, right, tokens)
    stage[...] = jnp.zeros(stage.shape, F32)
    for half in range(2):
        gain = None
        for block in blocks:
            lines = block[tokens : tokens + 16].astype(F32)[2 * half : 2 * half + 2]
            term = lines[0:1] + lines[1:2]
            gain = term if gain is None else gain + term
        high = gain.astype(BF).astype(F32)
        at = conv_rows + 2 * half
        stage[at : at + 1] = high
        stage[at + 1 : at + 2] = gain - high
    count, above = outs[0].shape[:2]
    even = lax.axis_index("seq") % 2 == 0
    own, pair = blocks[0], blocks[2]
    tops = [b[0:16].astype(F32)[0:1] for b in (own, pair)]
    bottoms = [b[tokens - 16 : tokens].astype(F32)[15:16] for b in (own, pair)]
    rests = [b[tokens : tokens + 16].astype(F32)[4:6] for b in (own, pair)]
    for k in range(4 * count):
        conv = dot(pick[k * conv_pad : (k + 1) * conv_pad], right[...])
        stage[:conv_rows] = conv[:conv_rows]
        if k == 3 * count:
            stage[above - 4 : above - 3] = jnp.where(even, tops[0], tops[1])
            stage[above - 3 : above - 2] = jnp.where(even, rests[0][0:1], rests[1][0:1])
            stage[above - 2 : above - 1] = jnp.where(even, bottoms[1], bottoms[0])
            stage[above - 1 : above] = jnp.where(even, rests[1][1:2], rests[0][1:2])
        out = outs[k // count]
        out[k % count] = stage[...].astype(out.dtype)


def conv_second_kernel(*refs, conv_rows, conv_pad, norm_rows, norm_pad, key_size, value_size):
    pick, norm_pick, blocks, first_send = refs[0], refs[1], refs[2:6], refs[6]
    near_keep, far_keep, near_send, far_send, right, side, stage = refs[7:]
    tokens, width = right.shape[0] // 8, right.shape[1]
    stack_cots(blocks, right, tokens)
    for i, block in enumerate(blocks):
        side[i * tokens : (i + 1) * tokens] = block[tokens:]
    key_rows = side_rows(norm_rows, key_size, width)
    value_rows = side_rows(norm_rows, value_size, width)
    stage[...] = jnp.zeros(stage.shape, F32)
    count, above = first_send.shape[:2]
    near_send[:, :above] = first_send[...]
    for k in range(4 * count):
        conv = dot(pick[k * conv_pad : (k + 1) * conv_pad], right[...])
        stage[:conv_rows] = conv[:conv_rows]
        both = dot(norm_pick[k * norm_pad : (k + 1) * norm_pad], side[...])
        put_side(stage, conv_rows, both[:norm_rows, :key_size], key_rows)
        value = both[:norm_rows, key_size : key_size + value_size]
        put_side(stage, conv_rows + key_rows, value, value_rows)
        if k < 2 * count:
            (near_keep, far_keep)[k // count][k % count] = stage[...]
        elif k < 3 * count:
            near_send[k % count, above:] = stage[...].astype(BF)
        else:
            far_send[k % count] = stage[...].astype(BF)


def first_sum_kernel(keep, near, far, out):
    above = keep.shape[1]
    out[...] = keep[...] + near[:, :above].astype(F32) + far[...].astype(F32)


def combine_kernel(first, second, near, far, out):
    above = first.shape[1]
    out[:, :above] = first[...]
    out[:, above:] = second[...] + near[:, above:].astype(F32) + far[...].astype(F32)


def final_kernel(*refs, conv_parts, above):
    conv, query, key, value, gain, stage = refs[-6:]
    rows, width = conv.shape
    split = width // 2
    count = key.shape[0]
    if conv_parts == 4:
        combine_kernel(*refs[:4], stage)
    else:
        stage[...] = total_of(refs[:conv_parts])
    query[...] = total_of(refs[conv_parts:-6])[0, : query.shape[0]]
    conv[:, :split] = stage[0, :rows]
    conv[:, split:] = stage[0, above : above + rows]
    at = above + rows
    for part in (key, value):
        step = side_rows(count, part.shape[1], split)
        get_side(stage[0, at : at + step], part, step)
        at += step
    lines = stage[0, rows : rows + 4]
    line = jnp.concatenate([lines[0:1] + lines[1:2], lines[2:3] + lines[3:4]], axis=1)
    line = jnp.broadcast_to(line, (8, width))
    start = place()(0) * count
    gain[...] = pltpu.roll(line, lax.rem(width - start, width), 1)[:1, :count]


def input_kernel(*refs):
    x, first, second, pair_first, pair_second, one, three, weight, out, ext, mixed = refs
    tokens = x.shape[0] // 2
    seq, devices = lax.axis_index("seq"), lax.axis_size("seq")
    low, high = seq % 2, seq // 2
    split = first.shape[1]
    above = one.shape[1]
    one_rows = one[0, above - 16 :].astype(F32)[12:]
    three_rows = three[0, above - 16 :].astype(F32)[12:]
    heads = jnp.where(high % 2 == 0, one_rows[:2], three_rows[:2])
    tails = jnp.where(high % 2 == 0, three_rows[2:], one_rows[2:])
    heads = jnp.where(seq == devices - 1, 0.0, heads)
    tails = jnp.where(seq == 0, 0.0, tails)
    for half, own, pair in ((0, first, pair_first), (1, second, pair_second)):
        lanes = slice(half * split, (half + 1) * split)
        top = pair[0:16].astype(F32)[0:1]
        bottom = pair[tokens - 16 : tokens].astype(F32)[15:16]
        ext[8 : 8 + tokens, lanes] = own[:tokens].astype(F32)
        ext[7:8, lanes] = jnp.where(low == 0, tails[half : half + 1], bottom)
        ext[8 + tokens : 9 + tokens, lanes] = jnp.where(low == 0, top, heads[half : half + 1])
    back = ext[7 : 7 + tokens].astype(BF)
    here = ext[8 : 8 + tokens].astype(BF)
    ahead = ext[9 : 9 + tokens].astype(BF)
    evens = (ahead, here, here, back, back)
    odds = (ahead, ahead, here, here, back)
    total = None
    for tap in range(5):
        term = dot_t(jnp.concatenate([evens[tap], odds[tap]], axis=0), weight[tap])
        total = term if total is None else total + term
    for c in range(mixed.shape[0]):
        lanes = slice(c * LANES, (c + 1) * LANES)
        mixed[c, pl.ds(0, tokens, stride=2)] = total[:tokens, lanes]
        mixed[c, pl.ds(1, tokens, stride=2)] = total[tokens:, lanes]
        out[:, lanes] = (mixed[c] * gelu_slope(x[:, lanes].astype(F32))).astype(BF)


def on_device(x, conv_weight, norm_gain, wq, wk, wv, cotangent):
    devices = lax.axis_size("seq")
    both_axes = ("seq", "dp")
    x, cotangent = x[0], cotangent[0]
    positions, channels = x.shape
    tokens = positions // 2
    taps, _, width = conv_weight.shape
    key_size, value_size = wk.shape[1], wv.shape[1]
    heads = cotangent.shape[1] // value_size
    scale = key_size ** (-0.5)
    groups = devices // 2
    owners = devices * 2
    conv_rows, norm_rows = taps * channels // owners, width // owners
    conv_pad, norm_pad = round_up(conv_rows, 16), round_up(norm_rows, 16)
    ext = tokens + 16
    gain = norm_gain.reshape(1, width)

    def swap(value, seq_bits, dp_bit=0):
        mask = 2 * seq_bits + dp_bit
        return lax.ppermute(value, both_axes, [(i, i ^ mask) for i in range(owners)])

    def held(value, *until):
        return lax.optimization_barrier((value,) + until)[0]

    def quad(value, *until):
        core = swap(value, 0, 1)
        near = swap(value, 1)
        return [value, core, near, swap(held(near, *until), 0, 1)]

    def fold(parts, name):
        shape = (parts[0].shape[0] // 2,) + parts[0].shape[1:]
        return run(fold_kernel, [(shape, F32), (shape, BF)], parts, name=name)

    def halved(keep, send, bits, name):
        for bit in bits[:-1]:
            keep, send = fold([keep, swap(send, 1 << bit)], name)
        return [keep, swap(send, 1 << bits[-1])]

    bits = list(range(devices.bit_length() - 1))
    order = [mask // 2 for mask in ordered(bits[1:])]
    crossing = [(i, i + 1) for i in range(1, devices - 1, 2)]
    crossing = crossing + [(j, i) for i, j in crossing]
    pad_shape = (channels // LANES, 8 + 2 * ext + 8, LANES)
    ready, ends = run(
        open_kernel,
        [(pad_shape, F32), ((32, channels), BF)],
        [x],
        flops=4 * 10**9,
        name="gelu",
    )
    pair, across = swap(ends, 1), lax.ppermute(ends, "seq", crossing)
    wv = wv.T
    kv, early, normed, pooled = run(
        front_kernel,
        [
            ((5 * tokens // 2, key_size), BF),
            ((2 * ext, channels), BF),
            ((tokens, width), BF),
            ((tokens, width), F32),
        ],
        [ready, pair, across, conv_weight, gain, wk, wv],
        [pltpu.VMEM(pad_shape, F32)],
        flops=2 * positions * taps * channels * width,
        name="front",
    )
    parts = [0, *range(2, groups), 1]
    near_kv = [swap(kv, 2 * k) if k else kv for k in parts]
    far_kv = [swap(block, 1) for block in near_kv]
    picked = (groups * norm_pad, tokens)
    rows = split_rows(picked[0], channels)
    queries, to_near, to_core, pick_own = run(
        lambda *refs: query_kernel(
            *refs, order=order, rows=norm_rows, padded=norm_pad, scale=scale
        ),
        [
            ((tokens, heads * key_size), BF),
            ((2 * ext + 2 * rows, channels), BF),
            ((2 * ext + rows, channels), BF),
            (picked, BF),
        ],
        [normed, wq, early],
        flops=4 * tokens * width * heads * key_size,
        name="queries",
        after=near_kv[1:],
    )
    to_near, to_core = held(to_near, *far_kv), held(to_core, *far_kv)
    length = devices * tokens
    masks = [2 * k for k in parts] + [2 * k + 1 for k in parts]
    half_block = (groups, 5 * tokens // 4, key_size)
    slots = 2 if length <= 2048 else 1
    attended, query_cot, keep_a, send_a, keep_b, send_b = run(
        lambda *refs: attend_kernel(
            *refs,
            blocks=devices,
            masks=[
                [masks.index(m) for m in ordered(way)] for way in (bits, [1, 0] + bits[2:])
            ],
            heads=heads,
            key_size=key_size,
            value_size=value_size,
            scale=scale,
        ),
        [((tokens, heads * value_size), BF), ((tokens, heads * key_size), BF)]
        + [(half_block, F32), (half_block, BF)] * 2,
        [queries, cotangent] + near_kv + far_kv,
        [
            pltpu.VMEM((length, key_size), BF),
            pltpu.VMEM((length, value_size), BF),
            pltpu.VMEM((key_size, length), BF),
            pltpu.VMEM((value_size, length), BF),
            pltpu.VMEM((heads * tokens, key_size), BF),
            pltpu.VMEM((heads * tokens, value_size), BF),
            pltpu.VMEM((length, heads * tokens), BF),
            pltpu.VMEM((length, heads * tokens), BF),
            pltpu.VMEM((slots, length, 2 * tokens), F32),
            pltpu.VMEM((slots, length, 2 * tokens), F32),
        ],
        flops=6 * tokens * heads * length * (key_size + value_size),
        name="attend",
    )
    in_a, in_b = swap(send_a, 1), swap(send_b, 2)
    early_near = swap(to_near, 1)
    early_blocks = [early, swap(to_core, 0, 1), early_near, swap(held(early_near, send_a), 0, 1)]
    conv_pick, norm_pick = run(
        lambda *refs: select_kernel(*refs, order=order, rows=conv_rows, padded=conv_pad),
        [((groups * conv_pad, 8 * tokens), BF), ((groups * norm_pad, 4 * tokens), BF)],
        [pick_own] + early_blocks,
        [pltpu.VMEM((ext, channels), F32), pltpu.VMEM((ext, channels), F32)],
        flops=2 * groups * conv_pad * taps * channels * 8 * tokens,
        name="select",
    )
    fourth = (groups // 2,) + half_block[1:]
    keep_a, send_a, keep_b, send_b = run(
        fold_two_kernel,
        [(fourth, F32), (fourth, BF)] * 2,
        [keep_a, in_a, keep_b, in_b],
        name="kv_cot_fold",
        after=[conv_pick],
    )
    in_a, in_b = swap(send_a, 2), swap(send_b, 1)
    block = (groups // 4, 5 * tokens // 2, key_size)
    keep, send = run(
        merge_kernel,
        [(block, F32), (block, BF)],
        [keep_a, in_a, keep_b, in_b],
        name="kv_cot_merge",
    )
    (normed_cot,) = run(
        query_cot_kernel,
        [((tokens, width), F32)],
        [query_cot, wq],
        flops=2 * tokens * width * heads * key_size,
        name="query_part",
    )
    query_cot = held(query_cot, keep)
    query_near, query_core = swap(query_cot, 1), swap(query_cot, 0, 1)
    kv_cot = halved(keep, send, bits[2:], "kv_cot_fold")
    first, second, *edge = run(
        middle_kernel,
        [
            ((tokens + 16, width // 2), BF),
            ((2 * tokens, width // 2), BF),
        ]
        + [((16, width), BF)] * (len(bits) > 3),
        kv_cot + [normed_cot, pooled, gain, wk, wv],
        flops=2 * tokens * width * (key_size + value_size),
        name="conv_cot",
    )
    near_first, near_second = swap(first, 1), swap(second, 1)
    query_last = swap(held(query_near, first), 0, 1)
    query_half = (groups // 2, norm_pad, heads * key_size)
    query_keep, query_send = run(
        query_grad_kernel,
        [(query_half, F32), (query_half, BF)],
        [norm_pick, query_cot, query_core, query_near, query_last],
        [pltpu.VMEM((4 * tokens, heads * key_size), BF)],
        flops=2 * groups * norm_pad * 4 * tokens * heads * key_size,
        name="query_grad",
    )
    query_parts = halved(query_keep, query_send, bits[1:], "query_fold")
    core_first, core_second = swap(first, 0, 1), swap(second, 0, 1)
    split = width // 2
    side = side_rows(norm_rows, key_size, split) + side_rows(norm_rows, value_size, split)
    above, below = round_up(conv_rows + 8, 16), round_up(conv_rows + side, 16)
    count = groups // 4
    last_first = swap(held(near_first, query_keep), 0, 1)
    near_keep, far_keep, near_send, far_send = run(
        lambda *refs: conv_first_kernel(*refs, conv_rows=conv_rows, conv_pad=conv_pad),
        [((count, above, split), t) for t in (F32, F32, BF, BF)],
        [conv_pick, first, core_first, near_first, last_first],
        [pltpu.VMEM((8 * tokens, split), BF), pltpu.VMEM((above, split), F32)],
        flops=groups * conv_pad * 8 * tokens * width,
        name="conv_grad_first",
    )
    far_in = swap(far_send, 2)
    last_second = swap(held(near_second, near_keep, query_parts[0]), 0, 1)
    near_keep_second, far_keep_second, near_send, far_send = run(
        lambda *refs: conv_second_kernel(
            *refs,
            conv_rows=conv_rows,
            conv_pad=conv_pad,
            norm_rows=norm_rows,
            norm_pad=norm_pad,
            key_size=key_size,
            value_size=value_size,
        ),
        [
            ((count, below, split), F32),
            ((count, below, split), F32),
            ((count, above + below, split), BF),
            ((count, below, split), BF),
        ],
        [conv_pick, norm_pick, second, core_second, near_second, last_second, near_send],
        [
            pltpu.VMEM((8 * tokens, split), BF),
            pltpu.VMEM((4 * tokens, split), BF),
            pltpu.VMEM((below, split), F32),
        ],
        flops=groups * conv_pad * 8 * tokens * width,
        name="conv_grad_second",
    )
    far_in_second = swap(far_send, 2)
    near_in = swap(near_send, 2)
    (far_sum,) = run(
        send_on_kernel,
        [((count, above, split), BF)],
        [far_keep, far_in],
        name="conv_send_on",
    )
    far_last = swap(far_sum, 4)
    (far_sum,) = run(
        send_on_kernel,
        [((count, below, split), BF)],
        [far_keep_second, far_in_second],
        name="conv_send_on",
    )
    edges = [far_in, far_last]
    if len(bits) > 3:
        came = lax.ppermute(edge[0], "seq", crossing)
        rows = jnp.concatenate([came[:1, :split], came[:1, split:], came[1:2, :split], came[1:2, split:]])
        edges = [jnp.pad(rows, ((above - 4, 0), (0, 0)))[None]] * 2
    (input_grad,) = run(
        input_kernel,
        [((positions, channels), BF)],
        [held(x, far_sum, query_parts[1]), first, second, near_first, near_second] + edges + [conv_weight],
        [
            pltpu.VMEM((tokens + 16, width), F32),
            pltpu.VMEM((channels // LANES, positions, LANES), F32),
        ],
        flops=20 * positions * taps * channels * width,
        name="input_grad",
    )
    (first_sum,) = run(
        first_sum_kernel,
        [((count, above, split), F32)],
        [near_keep, near_in, far_last],
        flops=5 * 10**9,
        name="conv_first_sum",
    )
    conv_parts = [first_sum, near_keep_second, near_in, swap(far_sum, 4)]
    chunk = (count, above + below, split)
    if len(bits) > 3:
        keep = run(combine_kernel, [(chunk, F32)], conv_parts, name="conv_combine")[0]
        half = (count // 2,) + chunk[1:]
        keep, send = run(fold_kernel, [(half, F32), (half, BF)], [keep], name="conv_fold")
        conv_parts = halved(keep, send, bits[3:], "conv_fold")
    conv_grad, query_grad, key_grad, value_grad, gain_grad = run(
        lambda *refs: final_kernel(*refs, conv_parts=len(conv_parts), above=above),
        [
            ((conv_rows, width), F32),
            ((norm_rows, heads * key_size), F32),
            ((norm_rows, key_size), F32),
            ((norm_rows, value_size), F32),
            ((1, norm_rows), F32),
        ],
        conv_parts + query_parts,
        [pltpu.VMEM((1,) + chunk[1:], F32)],
        name="final_sum",
    )
    return (
        attended[None],
        input_grad[None],
        conv_grad,
        query_grad,
        key_grad,
        value_grad,
        gain_grad.reshape(norm_rows),
    )


def solution(mesh):
    placed = (
        P(("groups", "dp"), "seq", None),
        P(),
        P(),
        P(),
        P(),
        P(),
        P(("groups", "dp"), "seq", None),
    )
    return jax.shard_map(
        on_device,
        mesh=mesh,
        in_specs=placed,
        out_specs=(
            P(("groups", "dp"), "seq", None),
            P(("groups", "dp"), "seq", None),
            P(("groups", "seq", "dp"), None),
            P(("groups", "seq", "dp"), None),
            P(("groups", "seq", "dp"), None),
            P(("groups", "seq", "dp"), None),
            P(("groups", "seq", "dp")),
        ),
        check_vma=False,
    )
```

```python
import functools
import math

import jax
import jax.numpy as jnp
from jax import lax
from jax.experimental import pallas as pl
from jax.experimental.pallas import tpu as pltpu
from jax.sharding import PartitionSpec as P

BF = jnp.bfloat16
F32 = jnp.float32
ROOT = math.sqrt(2.0 / math.pi)
EPS = 1e-06
LANES = 128
VMEM_BYTES = 40 * 2**20


def dot(a, b):
    return lax.dot_general(a, b, (((1,), (0,)), ((), ())), preferred_element_type=F32)


def dot_t(a, b):
    return lax.dot_general(a, b, (((1,), (1,)), ((), ())), preferred_element_type=F32)


def run(body, outs, args, scratch=(), flops=0, name=None, after=()):
    size = sum(math.prod(a.shape) * a.dtype.itemsize for a in args)
    size += sum(math.prod(s) * jnp.dtype(t).itemsize for s, t in outs)
    vmem = pl.BlockSpec(memory_space=pltpu.VMEM)
    rest = pl.BlockSpec(memory_space=pl.ANY)
    count, skip = len(args), len(args) + len(after)

    def whole(*refs):
        body(*refs[:count], *refs[skip:])

    return pl.pallas_call(
        whole,
        out_shape=[jax.ShapeDtypeStruct(s, t) for s, t in outs],
        in_specs=[vmem] * count + [rest] * len(after),
        out_specs=[vmem] * len(outs),
        scratch_shapes=list(scratch),
        compiler_params=pltpu.CompilerParams(vmem_limit_bytes=VMEM_BYTES),
        cost_estimate=pl.CostEstimate(flops=flops, bytes_accessed=size, transcendentals=0),
        name=name,
    )(*args, *after)


def gelu(v):
    return v * (0.5 * (1.0 + jnp.tanh(ROOT * (v + 0.044715 * (v * v * v)))))


def gelu_slope(v):
    tangent = jnp.tanh(ROOT * (v + 0.044715 * v * v * v))
    return 0.5 * (1.0 + tangent) + 0.5 * v * (1.0 - tangent * tangent) * ROOT * (
        1.0 + 3.0 * 0.044715 * v * v
    )


def round_up(value, step):
    return -(-value // step) * step


def pack_kv(keys, values):
    tokens, size = keys.shape
    rest = values[:, size:]
    half = tokens // 2
    tail = jnp.concatenate([rest[:half], rest[half:]], axis=1)
    return jnp.concatenate([keys, values[:, :size], tail], axis=0)


def unpack_values(packed, tokens, size):
    tail = packed[2 * tokens :]
    width = tail.shape[1] // 2
    rest = jnp.concatenate([tail[:, :width], tail[:, width:]], axis=0)
    return jnp.concatenate([packed[tokens : 2 * tokens], rest], axis=1)


def put(ref, start, rows):
    for c in range(ref.shape[0]):
        ref[c, start : start + rows.shape[0]] = rows[:, c * LANES : (c + 1) * LANES]


def every_second(ref, start, count):
    parts = [ref[c, pl.ds(start, count, stride=2)] for c in range(ref.shape[0])]
    return jnp.concatenate(parts, axis=1)


def open_kernel(x, pad, ends):
    positions, channels = x.shape
    ends[:16] = x[:16]
    ends[16:] = x[positions - 16 :]
    put(pad, 0, jnp.zeros((8, channels), F32))
    put(pad, 8, gelu(x[...].astype(F32)).astype(BF).astype(F32))
    put(pad, 8 + positions, jnp.zeros((pad.shape[1] - 8 - positions, channels), F32))


def front_kernel(ready, pair, across, weight, gain, wk, wv, kv_out, early, normed_out, pooled_out, pad):
    tokens = pooled_out.shape[0]
    ext = early.shape[0] // 2
    even = lax.axis_index("seq") % 2 == 0
    pair_wide, across_wide = pair[...].astype(F32), across[...].astype(F32)
    before = jnp.where(even, across_wide[16:], pair_wide[16:])[14:]
    after = jnp.where(even, pair_wide[:16], across_wide[:16])[:2]
    pad[...] = ready[...]
    put(pad, 6, gelu(before).astype(BF).astype(F32))
    put(pad, 8 + 2 * tokens, gelu(after).astype(BF).astype(F32))
    pieces = [every_second(pad, 6 + u, tokens).astype(BF) for u in range(6)]
    total = None
    for tap in range(5):
        rows = jnp.concatenate([pieces[tap], pieces[tap + 1]], axis=0)
        term = dot(rows, weight[tap])
        total = term if total is None else total + term
    pooled = 0.5 * (total[:tokens] + total[tokens:])
    inv = lax.rsqrt(jnp.mean(pooled * pooled, axis=-1, keepdims=True) + EPS)
    normed = (pooled * inv * gain[...]).astype(BF)
    pooled_out[...] = pooled
    normed_out[...] = normed
    kv_out[...] = pack_kv(dot(normed, wk[...]), dot_t(normed, wv[...])).astype(BF)
    early[0:ext] = every_second(pad, 6, ext).astype(BF)
    early[ext : 2 * ext] = every_second(pad, 7, ext).astype(BF)


def ordered(bits):
    masks = [0]
    for bit in reversed(bits):
        masks = masks + [mask | (1 << bit) for mask in masks]
    return masks


def split_rows(rows, columns):
    return round_up(-(-rows * LANES // columns), 16)


def query_kernel(normed, wq, early, out, near, core, own, *, order, rows, padded, scale):
    width = normed.shape[1]
    value = normed[...]
    out[...] = (dot(value, wq[...]) * scale).astype(BF)
    ext, channels = early.shape
    near[:ext] = early[...]
    core[:ext] = early[...]
    count = len(order) * padded
    step = split_rows(count, channels)
    for i in range(4):
        block_of = place(i)
        pick = [chosen(rows, padded, width, block_of(k)) for k in order]
        part = dot_t(jnp.concatenate(pick, axis=0), value).astype(BF)
        if i == 0:
            own[...] = part
            continue
        message, at = ((core, ext), (near, ext), (near, ext + step))[i - 1]
        for c in range(channels // LANES):
            piece = part[c * step : min((c + 1) * step, count)]
            message[at : at + piece.shape[0], c * LANES : (c + 1) * LANES] = piece


def by_eight(rows):
    return rows.reshape(rows.shape[0] // 8, 8, rows.shape[1])


def attend_kernel(*refs, blocks, masks, heads, key_size, value_size, scale):
    q, cot = refs[:2]
    parts = refs[2 : 2 + blocks]
    att, dq, keep_a, send_a, keep_b, send_b = refs[2 + blocks : 8 + blocks]
    ks, vs, kt, vt, qs, cs, weights, score_cots, scores, prob_cots = refs[8 + blocks :]
    tokens = q.shape[0]
    half = tokens // 2
    wide = value_size - key_size
    for i, part in enumerate(parts):
        at = i * tokens
        ks[at : at + tokens] = part[:tokens]
        vs[at : at + tokens, :key_size] = part[tokens : 2 * tokens]
        vs[at : at + half, key_size:] = part[2 * tokens :, :wide]
        vs[at + half : at + tokens, key_size:] = part[2 * tokens :, wide:]
        kt[:, at : at + tokens] = ks[at : at + tokens].astype(F32).T.astype(BF)
        vt[:, at : at + tokens] = vs[at : at + tokens].astype(F32).T.astype(BF)
    for pair in range(heads // 2):
        ql, cl = 2 * pair * key_size, 2 * pair * value_size
        rows = slice(2 * pair * tokens, 2 * (pair + 1) * tokens)
        both = cot[:, cl : cl + 2 * value_size]
        qs[rows] = jnp.concatenate(
            [q[:, ql : ql + key_size], q[:, ql + key_size : ql + 2 * key_size]], axis=0
        )
        cs[rows] = jnp.concatenate([both[:, :value_size], both[:, value_size:]], axis=0)
        slot = pair % scores.shape[0]
        parts_of = [slice(i * tokens, (i + 1) * tokens) for i in range(blocks)]
        scores[slot] = dot_t(ks[...], qs[rows])
        prob_cots[slot] = dot_t(vs[...], cs[rows])
        top = functools.reduce(jnp.maximum, [by_eight(scores[slot, at]).max(0) for at in parts_of])
        top = jnp.max(top, axis=0, keepdims=True)
        sums = 0.0
        for at in parts_of:
            raised = jnp.exp(scores[slot, at] - top)
            sums = sums + by_eight(raised).sum(0)
            scores[slot, at] = raised
        inverse = 1.0 / jnp.sum(sums, axis=0, keepdims=True)
        for at in parts_of:
            weights[at, rows] = (scores[slot, at] * inverse).astype(BF)
        out_t = dot(vt[...], weights[:, rows]).astype(BF).astype(F32)
        delta = jnp.sum(cs[rows].astype(F32).T * out_t, axis=0, keepdims=True)
        for at in parts_of:
            probs = scores[slot, at] * inverse
            score_cots[at, rows] = (probs * (prob_cots[slot, at] - delta)).astype(BF)
        dq_t = dot(kt[...], score_cots[:, rows]) * scale
        out_rows = jnp.concatenate([out_t[:, :tokens].T, out_t[:, tokens:].T], axis=1)
        att[:, cl : cl + 2 * value_size] = out_rows.astype(BF)
        dq_rows = jnp.concatenate([dq_t[:, :tokens].T, dq_t[:, tokens:].T], axis=1)
        dq[:, ql : ql + 2 * key_size] = dq_rows.astype(BF)
    key_cots, value_cots = dot(score_cots[...], qs[...]), dot(weights[...], cs[...])
    edge = keep_a.shape[1]
    count = blocks // 2
    for i in range(blocks):
        at = slice(i * tokens, (i + 1) * tokens)
        packed = pack_kv(key_cots[at], value_cots[at])
        for order, keep, send, part in (
            (masks[0], keep_a, send_a, packed[:edge]),
            (masks[1], keep_b, send_b, packed[edge:]),
        ):
            k = order.index(i)
            if k < count:
                keep[k] = part
            else:
                send[k - count] = part.astype(BF)


def total_of(parts):
    total = parts[0][...]
    for part in parts[1:]:
        total = total + part[...].astype(F32)
    return total


def fold_kernel(*refs):
    keep, send = refs[-2:]
    total = total_of(refs[:-2])
    keep[...] = total[: keep.shape[0]]
    send[...] = total[keep.shape[0] :].astype(BF)


def fold_two_kernel(*refs):
    fold_kernel(refs[0], refs[1], refs[4], refs[5])
    fold_kernel(refs[2], refs[3], refs[6], refs[7])


def merge_kernel(keep_a, in_a, keep_b, in_b, keep, send):
    total = jnp.concatenate([total_of((keep_a, in_a)), total_of((keep_b, in_b))], axis=1)
    keep[...] = total[: keep.shape[0]]
    send[...] = total[keep.shape[0] :].astype(BF)


def send_on_kernel(keep, came, out):
    out[...] = (keep[...] + came[...].astype(F32)).astype(BF)


def query_cot_kernel(dq, wq, out):
    out[...] = dot_t(dq[...], wq[...])


def middle_kernel(own, came, part, pooled_in, gain_in, wk, wv, first, second, *edges):
    size = own.shape[2]
    tokens, width = pooled_in.shape
    total = (own[0] + came[0].astype(F32)).astype(BF).astype(F32)
    key_cot = total[:tokens]
    value_cot = unpack_values(total, tokens, size)
    normed_cot = part[...] + dot_t(key_cot.astype(BF), wk[...])
    normed_cot = normed_cot + dot(value_cot.astype(BF), wv[...])
    pooled, gain = pooled_in[...], gain_in[...]
    inv = lax.rsqrt(jnp.mean(pooled * pooled, axis=-1, keepdims=True) + EPS)
    gain_term = jnp.sum(normed_cot * pooled * inv, axis=0, keepdims=True)
    gained = gain * normed_cot
    pooled_cot = inv * gained - pooled * (inv * inv * inv) * (
        jnp.sum(gained * pooled, axis=-1, keepdims=True) / width
    )
    conv_cot = 0.5 * pooled_cot
    high = gain_term.astype(BF).astype(F32)
    low = gain_term - high
    row = lax.broadcasted_iota(jnp.int32, (16, width), 0)
    split = width // 2
    lines = (high[:, :split], low[:, :split], high[:, split:], low[:, split:])
    lines += (conv_cot[:1, split:], conv_cot[tokens - 1 :, split:])
    gains = jnp.zeros((16, split), F32)
    for i, line in enumerate(lines):
        gains = jnp.where(row[:, :split] == i, line, gains)
    fill = split - size - value_cot.shape[1]
    side = jnp.concatenate([key_cot, value_cot, jnp.zeros((tokens, fill), F32)], axis=1)
    first[:tokens] = conv_cot[:, :split].astype(BF)
    first[tokens:] = gains.astype(BF)
    second[:tokens] = conv_cot[:, split:].astype(BF)
    second[tokens:] = side.astype(BF)
    for edge in edges:
        ends = jnp.where(row == 0, conv_cot[:1], jnp.where(row == 1, conv_cot[tokens - 1 :], 0.0))
        edge[...] = ends.astype(BF)


def place(other=0):
    seq, dp = lax.axis_index("seq"), lax.axis_index("dp") ^ (other % 2)
    high, low = seq // 2, (seq % 2) ^ (other // 2)
    return lambda k: ((high ^ k) * 2 + low) * 2 + dp


def chosen(rows, padded, columns, block):
    row = lax.broadcasted_iota(jnp.int32, (padded, columns), 0)
    column = lax.broadcasted_iota(jnp.int32, (padded, columns), 1)
    hit = (column == row + block * rows) & (row < rows)
    return jnp.where(hit, 1.0, 0.0).astype(BF)


def select_kernel(*refs, order, rows, padded):
    own, blocks = refs[0], refs[1:5]
    out, norm_out, even, odd = refs[5:]
    ext, channels = even.shape
    tokens = own.shape[1]
    count = own.shape[0]
    step = split_rows(count, channels)
    norm_out[:, :tokens] = own[...]
    for i in range(1, 4):
        at = 2 * ext + (i // 3) * step
        for c in range(channels // LANES):
            end = min((c + 1) * step, count)
            piece = blocks[i][at : at + end - c * step, c * LANES : (c + 1) * LANES]
            norm_out[c * step : end, i * tokens : (i + 1) * tokens] = piece
    block_of = place()
    pick = jnp.concatenate(
        [chosen(rows, padded, 5 * channels, block_of(k)) for k in order], axis=0
    )
    for i, block in enumerate(blocks):
        even[...] = block[:ext].astype(F32)
        odd[...] = block[ext : 2 * ext].astype(F32)
        pieces = []
        for shift in range(3):
            pieces += [even[shift : shift + tokens].astype(BF), odd[shift : shift + tokens].astype(BF)]
        shifted = jnp.concatenate(
            [jnp.concatenate(pieces[:5], axis=1), jnp.concatenate(pieces[1:], axis=1)], axis=0
        )
        out[:, 2 * i * tokens : 2 * (i + 1) * tokens] = dot_t(pick, shifted).astype(BF)


def query_grad_kernel(pick, first, second, third, fourth, keep, send, right):
    tokens = first.shape[0]
    for i, block in enumerate((first, second, third, fourth)):
        right[i * tokens : (i + 1) * tokens] = block[...]
    count, pad = keep.shape[:2]
    for k in range(2 * count):
        term = dot(pick[k * pad : (k + 1) * pad], right[...])
        if k < count:
            keep[k] = term
        else:
            send[k - count] = term.astype(BF)


def side_rows(norm_rows, size, width):
    return norm_rows * size // width


def put_side(stage, at, part, rows):
    pieces = [part[i : i + rows] for i in range(0, part.shape[0], rows)]
    stage[at : at + rows] = jnp.concatenate(pieces, axis=1)


def get_side(packed, part, rows):
    size = part.shape[1]
    for i in range(part.shape[0] // rows):
        part[i * rows : (i + 1) * rows] = packed[:, i * size : (i + 1) * size]


def stack_cots(blocks, right, tokens):
    for i, block in enumerate(blocks):
        piece = block[:tokens]
        right[2 * i * tokens : (2 * i + 1) * tokens] = piece
        right[(2 * i + 1) * tokens : (2 * i + 2) * tokens] = piece


def conv_first_kernel(*refs, conv_rows, conv_pad):
    pick, blocks, outs, right, stage = refs[0], refs[1:5], refs[5:9], refs[9], refs[10]
    tokens = right.shape[0] // 8
    stack_cots(blocks, right, tokens)
    stage[...] = jnp.zeros(stage.shape, F32)
    for half in range(2):
        gain = None
        for block in blocks:
            lines = block[tokens : tokens + 16].astype(F32)[2 * half : 2 * half + 2]
            term = lines[0:1] + lines[1:2]
            gain = term if gain is None else gain + term
        high = gain.astype(BF).astype(F32)
        at = conv_rows + 2 * half
        stage[at : at + 1] = high
        stage[at + 1 : at + 2] = gain - high
    count, above = outs[0].shape[:2]
    even = lax.axis_index("seq") % 2 == 0
    own, pair = blocks[0], blocks[2]
    tops = [b[0:16].astype(F32)[0:1] for b in (own, pair)]
    bottoms = [b[tokens - 16 : tokens].astype(F32)[15:16] for b in (own, pair)]
    rests = [b[tokens : tokens + 16].astype(F32)[4:6] for b in (own, pair)]
    for k in range(4 * count):
        conv = dot(pick[k * conv_pad : (k + 1) * conv_pad], right[...])
        stage[:conv_rows] = conv[:conv_rows]
        if k == 3 * count:
            stage[above - 4 : above - 3] = jnp.where(even, tops[0], tops[1])
            stage[above - 3 : above - 2] = jnp.where(even, rests[0][0:1], rests[1][0:1])
            stage[above - 2 : above - 1] = jnp.where(even, bottoms[1], bottoms[0])
            stage[above - 1 : above] = jnp.where(even, rests[1][1:2], rests[0][1:2])
        out = outs[k // count]
        out[k % count] = stage[...].astype(out.dtype)


def conv_second_kernel(*refs, conv_rows, conv_pad, norm_rows, norm_pad, key_size, value_size):
    pick, norm_pick, blocks, first_send = refs[0], refs[1], refs[2:6], refs[6]
    near_keep, far_keep, near_send, far_send, right, side, stage = refs[7:]
    tokens, width = right.shape[0] // 8, right.shape[1]
    stack_cots(blocks, right, tokens)
    for i, block in enumerate(blocks):
        side[i * tokens : (i + 1) * tokens] = block[tokens:]
    key_rows = side_rows(norm_rows, key_size, width)
    value_rows = side_rows(norm_rows, value_size, width)
    stage[...] = jnp.zeros(stage.shape, F32)
    count, above = first_send.shape[:2]
    near_send[:, :above] = first_send[...]
    for k in range(4 * count):
        conv = dot(pick[k * conv_pad : (k + 1) * conv_pad], right[...])
        stage[:conv_rows] = conv[:conv_rows]
        both = dot(norm_pick[k * norm_pad : (k + 1) * norm_pad], side[...])
        put_side(stage, conv_rows, both[:norm_rows, :key_size], key_rows)
        value = both[:norm_rows, key_size : key_size + value_size]
        put_side(stage, conv_rows + key_rows, value, value_rows)
        if k < 2 * count:
            (near_keep, far_keep)[k // count][k % count] = stage[...]
        elif k < 3 * count:
            near_send[k % count, above:] = stage[...].astype(BF)
        else:
            far_send[k % count] = stage[...].astype(BF)


def first_sum_kernel(keep, near, far, out):
    above = keep.shape[1]
    out[...] = keep[...] + near[:, :above].astype(F32) + far[...].astype(F32)


def combine_kernel(first, second, near, far, out):
    above = first.shape[1]
    out[:, :above] = first[...]
    out[:, above:] = second[...] + near[:, above:].astype(F32) + far[...].astype(F32)


def final_kernel(*refs, conv_parts, above):
    conv, query, key, value, gain, stage = refs[-6:]
    rows, width = conv.shape
    split = width // 2
    count = key.shape[0]
    if conv_parts == 4:
        combine_kernel(*refs[:4], stage)
    else:
        stage[...] = total_of(refs[:conv_parts])
    query[...] = total_of(refs[conv_parts:-6])[0, : query.shape[0]]
    conv[:, :split] = stage[0, :rows]
    conv[:, split:] = stage[0, above : above + rows]
    at = above + rows
    for part in (key, value):
        step = side_rows(count, part.shape[1], split)
        get_side(stage[0, at : at + step], part, step)
        at += step
    lines = stage[0, rows : rows + 4]
    line = jnp.concatenate([lines[0:1] + lines[1:2], lines[2:3] + lines[3:4]], axis=1)
    line = jnp.broadcast_to(line, (8, width))
    start = place()(0) * count
    gain[...] = pltpu.roll(line, lax.rem(width - start, width), 1)[:1, :count]


def input_kernel(*refs):
    x, first, second, pair_first, pair_second, one, three, weight, out, ext, mixed = refs
    tokens = x.shape[0] // 2
    seq, devices = lax.axis_index("seq"), lax.axis_size("seq")
    low, high = seq % 2, seq // 2
    split = first.shape[1]
    above = one.shape[1]
    one_rows = one[0, above - 16 :].astype(F32)[12:]
    three_rows = three[0, above - 16 :].astype(F32)[12:]
    heads = jnp.where(high % 2 == 0, one_rows[:2], three_rows[:2])
    tails = jnp.where(high % 2 == 0, three_rows[2:], one_rows[2:])
    heads = jnp.where(seq == devices - 1, 0.0, heads)
    tails = jnp.where(seq == 0, 0.0, tails)
    for half, own, pair in ((0, first, pair_first), (1, second, pair_second)):
        lanes = slice(half * split, (half + 1) * split)
        top = pair[0:16].astype(F32)[0:1]
        bottom = pair[tokens - 16 : tokens].astype(F32)[15:16]
        ext[8 : 8 + tokens, lanes] = own[:tokens].astype(F32)
        ext[7:8, lanes] = jnp.where(low == 0, tails[half : half + 1], bottom)
        ext[8 + tokens : 9 + tokens, lanes] = jnp.where(low == 0, top, heads[half : half + 1])
    back = ext[7 : 7 + tokens].astype(BF)
    here = ext[8 : 8 + tokens].astype(BF)
    ahead = ext[9 : 9 + tokens].astype(BF)
    evens = (ahead, here, here, back, back)
    odds = (ahead, ahead, here, here, back)
    total = None
    for tap in range(5):
        term = dot_t(jnp.concatenate([evens[tap], odds[tap]], axis=0), weight[tap])
        total = term if total is None else total + term
    for c in range(mixed.shape[0]):
        lanes = slice(c * LANES, (c + 1) * LANES)
        mixed[c, pl.ds(0, tokens, stride=2)] = total[:tokens, lanes]
        mixed[c, pl.ds(1, tokens, stride=2)] = total[tokens:, lanes]
        out[:, lanes] = (mixed[c] * gelu_slope(x[:, lanes].astype(F32))).astype(BF)


def on_device(x, conv_weight, norm_gain, wq, wk, wv, cotangent):
    devices = lax.axis_size("seq")
    both_axes = ("seq", "dp")
    x, cotangent = x[0], cotangent[0]
    positions, channels = x.shape
    tokens = positions // 2
    taps, _, width = conv_weight.shape
    key_size, value_size = wk.shape[1], wv.shape[1]
    heads = cotangent.shape[1] // value_size
    scale = key_size ** (-0.5)
    groups = devices // 2
    owners = devices * 2
    conv_rows, norm_rows = taps * channels // owners, width // owners
    conv_pad, norm_pad = round_up(conv_rows, 16), round_up(norm_rows, 16)
    ext = tokens + 16
    gain = norm_gain.reshape(1, width)

    def swap(value, seq_bits, dp_bit=0):
        mask = 2 * seq_bits + dp_bit
        return lax.ppermute(value, both_axes, [(i, i ^ mask) for i in range(owners)])

    def held(value, *until):
        return lax.optimization_barrier((value,) + until)[0]

    def quad(value, *until):
        core = swap(value, 0, 1)
        near = swap(value, 1)
        return [value, core, near, swap(held(near, *until), 0, 1)]

    def fold(parts, name, flops=0):
        shape = (parts[0].shape[0] // 2,) + parts[0].shape[1:]
        return run(fold_kernel, [(shape, F32), (shape, BF)], parts, flops=flops, name=name)

    def halved(keep, send, bits, name, flops=0):
        for bit in bits[:-1]:
            keep, send = fold([keep, swap(send, 1 << bit)], name, flops)
        return [keep, swap(send, 1 << bits[-1])]

    bits = list(range(devices.bit_length() - 1))
    order = [mask // 2 for mask in ordered(bits[1:])]
    crossing = [(i, i + 1) for i in range(1, devices - 1, 2)]
    crossing = crossing + [(j, i) for i, j in crossing]
    pad_shape = (channels // LANES, 8 + 2 * ext + 8, LANES)
    ready, ends = run(
        open_kernel,
        [(pad_shape, F32), ((32, channels), BF)],
        [x],
        flops=4 * 10**9,
        name="gelu",
    )
    pair, across = swap(ends, 1), lax.ppermute(ends, "seq", crossing)
    wv = wv.T
    kv, early, normed, pooled = run(
        front_kernel,
        [
            ((5 * tokens // 2, key_size), BF),
            ((2 * ext, channels), BF),
            ((tokens, width), BF),
            ((tokens, width), F32),
        ],
        [ready, pair, across, conv_weight, gain, wk, wv],
        [pltpu.VMEM(pad_shape, F32)],
        flops=2 * positions * taps * channels * width,
        name="front",
    )
    parts = [0, *range(2, groups), 1]
    near_kv = [swap(kv, 2 * k) if k else kv for k in parts]
    far_kv = [swap(block, 1) for block in near_kv]
    picked = (groups * norm_pad, tokens)
    rows = split_rows(picked[0], channels)
    queries, to_near, to_core, pick_own = run(
        lambda *refs: query_kernel(
            *refs, order=order, rows=norm_rows, padded=norm_pad, scale=scale
        ),
        [
            ((tokens, heads * key_size), BF),
            ((2 * ext + 2 * rows, channels), BF),
            ((2 * ext + rows, channels), BF),
            (picked, BF),
        ],
        [normed, wq, early],
        flops=4 * tokens * width * heads * key_size,
        name="queries",
        after=near_kv[1:],
    )
    to_near, to_core = held(to_near, *far_kv), held(to_core, *far_kv)
    length = devices * tokens
    masks = [2 * k for k in parts] + [2 * k + 1 for k in parts]
    half_block = (groups, 5 * tokens // 4, key_size)
    slots = 2 if length <= 2048 else 1
    attended, query_cot, keep_a, send_a, keep_b, send_b = run(
        lambda *refs: attend_kernel(
            *refs,
            blocks=devices,
            masks=[
                [masks.index(m) for m in ordered(way)] for way in (bits, [1, 0] + bits[2:])
            ],
            heads=heads,
            key_size=key_size,
            value_size=value_size,
            scale=scale,
        ),
        [((tokens, heads * value_size), BF), ((tokens, heads * key_size), BF)]
        + [(half_block, F32), (half_block, BF)] * 2,
        [queries, cotangent] + near_kv + far_kv,
        [
            pltpu.VMEM((length, key_size), BF),
            pltpu.VMEM((length, value_size), BF),
            pltpu.VMEM((key_size, length), BF),
            pltpu.VMEM((value_size, length), BF),
            pltpu.VMEM((heads * tokens, key_size), BF),
            pltpu.VMEM((heads * tokens, value_size), BF),
            pltpu.VMEM((length, heads * tokens), BF),
            pltpu.VMEM((length, heads * tokens), BF),
            pltpu.VMEM((slots, length, 2 * tokens), F32),
            pltpu.VMEM((slots, length, 2 * tokens), F32),
        ],
        flops=6 * tokens * heads * length * (key_size + value_size),
        name="attend",
    )
    in_a, in_b = swap(send_a, 1), swap(send_b, 2)
    early_near = swap(to_near, 1)
    early_blocks = [early, swap(to_core, 0, 1), early_near, swap(held(early_near, send_a), 0, 1)]
    conv_pick, norm_pick = run(
        lambda *refs: select_kernel(*refs, order=order, rows=conv_rows, padded=conv_pad),
        [((groups * conv_pad, 8 * tokens), BF), ((groups * norm_pad, 4 * tokens), BF)],
        [pick_own] + early_blocks,
        [pltpu.VMEM((ext, channels), F32), pltpu.VMEM((ext, channels), F32)],
        flops=2 * groups * conv_pad * taps * channels * 8 * tokens,
        name="select",
    )
    fourth = (groups // 2,) + half_block[1:]
    keep_a, send_a, keep_b, send_b = run(
        fold_two_kernel,
        [(fourth, F32), (fourth, BF)] * 2,
        [keep_a, in_a, keep_b, in_b],
        name="kv_cot_fold",
        after=[conv_pick],
    )
    in_a, in_b = swap(send_a, 2), swap(send_b, 1)
    block = (groups // 4, 5 * tokens // 2, key_size)
    keep, send = run(
        merge_kernel,
        [(block, F32), (block, BF)],
        [keep_a, in_a, keep_b, in_b],
        name="kv_cot_merge",
    )
    (normed_cot,) = run(
        query_cot_kernel,
        [((tokens, width), F32)],
        [query_cot, wq],
        flops=2 * tokens * width * heads * key_size,
        name="query_part",
    )
    query_cot = held(query_cot, keep)
    query_near, query_core = swap(query_cot, 1), swap(query_cot, 0, 1)
    kv_cot = halved(keep, send, bits[2:], "kv_cot_fold")
    first, second, *edge = run(
        middle_kernel,
        [
            ((tokens + 16, width // 2), BF),
            ((2 * tokens, width // 2), BF),
        ]
        + [((16, width), BF)] * (len(bits) > 3),
        kv_cot + [normed_cot, pooled, gain, wk, wv],
        flops=2 * tokens * width * (key_size + value_size),
        name="conv_cot",
    )
    near_first, near_second = swap(first, 1), swap(second, 1)
    query_last = swap(held(query_near, first), 0, 1)
    query_half = (groups // 2, norm_pad, heads * key_size)
    query_keep, query_send = run(
        query_grad_kernel,
        [(query_half, F32), (query_half, BF)],
        [norm_pick, query_cot, query_core, query_near, query_last],
        [pltpu.VMEM((4 * tokens, heads * key_size), BF)],
        flops=2 * groups * norm_pad * 4 * tokens * heads * key_size,
        name="query_grad",
    )
    query_parts = halved(query_keep, query_send, bits[1:], "query_fold", 5 * 10**9)
    core_first, core_second = swap(first, 0, 1), swap(second, 0, 1)
    split = width // 2
    side = side_rows(norm_rows, key_size, split) + side_rows(norm_rows, value_size, split)
    above, below = round_up(conv_rows + 8, 16), round_up(conv_rows + side, 16)
    count = groups // 4
    last_first = swap(held(near_first, query_keep), 0, 1)
    near_keep, far_keep, near_send, far_send = run(
        lambda *refs: conv_first_kernel(*refs, conv_rows=conv_rows, conv_pad=conv_pad),
        [((count, above, split), t) for t in (F32, F32, BF, BF)],
        [conv_pick, first, core_first, near_first, last_first],
        [pltpu.VMEM((8 * tokens, split), BF), pltpu.VMEM((above, split), F32)],
        flops=groups * conv_pad * 8 * tokens * width,
        name="conv_grad_first",
    )
    far_in = swap(far_send, 2)
    last_second = swap(held(near_second, near_keep), 0, 1)
    near_keep_second, far_keep_second, near_send, far_send = run(
        lambda *refs: conv_second_kernel(
            *refs,
            conv_rows=conv_rows,
            conv_pad=conv_pad,
            norm_rows=norm_rows,
            norm_pad=norm_pad,
            key_size=key_size,
            value_size=value_size,
        ),
        [
            ((count, below, split), F32),
            ((count, below, split), F32),
            ((count, above + below, split), BF),
            ((count, below, split), BF),
        ],
        [held(conv_pick, query_parts[0]), norm_pick, second, core_second, near_second, last_second, near_send],
        [
            pltpu.VMEM((8 * tokens, split), BF),
            pltpu.VMEM((4 * tokens, split), BF),
            pltpu.VMEM((below, split), F32),
        ],
        flops=groups * conv_pad * 8 * tokens * width,
        name="conv_grad_second",
    )
    far_in_second = swap(far_send, 2)
    near_in = swap(near_send, 2)
    (far_sum,) = run(
        send_on_kernel,
        [((count, above, split), BF)],
        [far_keep, far_in],
        name="conv_send_on",
    )
    far_last = swap(far_sum, 4)
    (far_sum,) = run(
        send_on_kernel,
        [((count, below, split), BF)],
        [far_keep_second, far_in_second],
        name="conv_send_on",
    )
    edges = [far_in, far_last]
    if len(bits) > 3:
        came = lax.ppermute(edge[0], "seq", crossing)
        rows = jnp.concatenate([came[:1, :split], came[:1, split:], came[1:2, :split], came[1:2, split:]])
        edges = [jnp.pad(rows, ((above - 4, 0), (0, 0)))[None]] * 2
    (input_grad,) = run(
        input_kernel,
        [((positions, channels), BF)],
        [held(x, far_sum, query_parts[1]), first, second, near_first, near_second] + edges + [conv_weight],
        [
            pltpu.VMEM((tokens + 16, width), F32),
            pltpu.VMEM((channels // LANES, positions, LANES), F32),
        ],
        flops=20 * positions * taps * channels * width,
        name="input_grad",
    )
    (first_sum,) = run(
        first_sum_kernel,
        [((count, above, split), F32)],
        [near_keep, near_in, far_last],
        flops=5 * 10**9,
        name="conv_first_sum",
    )
    conv_parts = [first_sum, near_keep_second, near_in, swap(far_sum, 4)]
    chunk = (count, above + below, split)
    if len(bits) > 3:
        keep = run(combine_kernel, [(chunk, F32)], conv_parts, name="conv_combine")[0]
        half = (count // 2,) + chunk[1:]
        keep, send = run(fold_kernel, [(half, F32), (half, BF)], [keep], name="conv_fold")
        conv_parts = halved(keep, send, bits[3:], "conv_fold")
    conv_grad, query_grad, key_grad, value_grad, gain_grad = run(
        lambda *refs: final_kernel(*refs, conv_parts=len(conv_parts), above=above),
        [
            ((conv_rows, width), F32),
            ((norm_rows, heads * key_size), F32),
            ((norm_rows, key_size), F32),
            ((norm_rows, value_size), F32),
            ((1, norm_rows), F32),
        ],
        conv_parts + query_parts,
        [pltpu.VMEM((1,) + chunk[1:], F32)],
        name="final_sum",
    )
    return (
        attended[None],
        input_grad[None],
        conv_grad,
        query_grad,
        key_grad,
        value_grad,
        gain_grad.reshape(norm_rows),
    )


def solution(mesh):
    placed = (
        P(("groups", "dp"), "seq", None),
        P(),
        P(),
        P(),
        P(),
        P(),
        P(("groups", "dp"), "seq", None),
    )
    return jax.shard_map(
        on_device,
        mesh=mesh,
        in_specs=placed,
        out_specs=(
            P(("groups", "dp"), "seq", None),
            P(("groups", "dp"), "seq", None),
            P(("groups", "seq", "dp"), None),
            P(("groups", "seq", "dp"), None),
            P(("groups", "seq", "dp"), None),
            P(("groups", "seq", "dp"), None),
            P(("groups", "seq", "dp")),
        ),
        check_vma=False,
    )
```

```python
import functools
import math

import jax
import jax.numpy as jnp
from jax import lax
from jax.experimental import pallas as pl
from jax.experimental.pallas import tpu as pltpu
from jax.sharding import PartitionSpec as P

BF = jnp.bfloat16
F32 = jnp.float32
ROOT = math.sqrt(2.0 / math.pi)
EPS = 1e-06
LANES = 128
VMEM_BYTES = 40 * 2**20


def dot(a, b):
    return lax.dot_general(a, b, (((1,), (0,)), ((), ())), preferred_element_type=F32)


def dot_t(a, b):
    return lax.dot_general(a, b, (((1,), (1,)), ((), ())), preferred_element_type=F32)


def run(body, outs, args, scratch=(), flops=0, name=None, after=()):
    size = sum(math.prod(a.shape) * a.dtype.itemsize for a in args)
    size += sum(math.prod(s) * jnp.dtype(t).itemsize for s, t in outs)
    vmem = pl.BlockSpec(memory_space=pltpu.VMEM)
    rest = pl.BlockSpec(memory_space=pl.ANY)
    count, skip = len(args), len(args) + len(after)

    def whole(*refs):
        body(*refs[:count], *refs[skip:])

    return pl.pallas_call(
        whole,
        out_shape=[jax.ShapeDtypeStruct(s, t) for s, t in outs],
        in_specs=[vmem] * count + [rest] * len(after),
        out_specs=[vmem] * len(outs),
        scratch_shapes=list(scratch),
        compiler_params=pltpu.CompilerParams(vmem_limit_bytes=VMEM_BYTES),
        cost_estimate=pl.CostEstimate(flops=flops, bytes_accessed=size, transcendentals=0),
        name=name,
    )(*args, *after)


def gelu(v):
    return v * (0.5 * (1.0 + jnp.tanh(ROOT * (v + 0.044715 * (v * v * v)))))


def gelu_slope(v):
    tangent = jnp.tanh(ROOT * (v + 0.044715 * v * v * v))
    return 0.5 * (1.0 + tangent) + 0.5 * v * (1.0 - tangent * tangent) * ROOT * (
        1.0 + 3.0 * 0.044715 * v * v
    )


def round_up(value, step):
    return -(-value // step) * step


def pack_kv(keys, values):
    tokens, size = keys.shape
    rest = values[:, size:]
    half = tokens // 2
    tail = jnp.concatenate([rest[:half], rest[half:]], axis=1)
    return jnp.concatenate([keys, values[:, :size], tail], axis=0)


def unpack_values(packed, tokens, size):
    tail = packed[2 * tokens :]
    width = tail.shape[1] // 2
    rest = jnp.concatenate([tail[:, :width], tail[:, width:]], axis=0)
    return jnp.concatenate([packed[tokens : 2 * tokens], rest], axis=1)


def put(ref, start, rows):
    for c in range(ref.shape[0]):
        ref[c, start : start + rows.shape[0]] = rows[:, c * LANES : (c + 1) * LANES]


def every_second(ref, start, count):
    parts = [ref[c, pl.ds(start, count, stride=2)] for c in range(ref.shape[0])]
    return jnp.concatenate(parts, axis=1)


def open_kernel(x, pad, ends):
    positions, channels = x.shape
    ends[:16] = x[:16]
    ends[16:] = x[positions - 16 :]
    put(pad, 0, jnp.zeros((8, channels), F32))
    put(pad, 8, gelu(x[...].astype(F32)).astype(BF).astype(F32))
    put(pad, 8 + positions, jnp.zeros((pad.shape[1] - 8 - positions, channels), F32))


def front_kernel(ready, pair, across, weight, gain, wk, wv, kv_out, early, normed_out, pooled_out, pad):
    tokens = pooled_out.shape[0]
    ext = early.shape[0] // 2
    even = lax.axis_index("seq") % 2 == 0
    pair_wide, across_wide = pair[...].astype(F32), across[...].astype(F32)
    before = jnp.where(even, across_wide[16:], pair_wide[16:])[14:]
    after = jnp.where(even, pair_wide[:16], across_wide[:16])[:2]
    pad[...] = ready[...]
    put(pad, 6, gelu(before).astype(BF).astype(F32))
    put(pad, 8 + 2 * tokens, gelu(after).astype(BF).astype(F32))
    pieces = [every_second(pad, 6 + u, tokens).astype(BF) for u in range(6)]
    total = None
    for tap in range(5):
        rows = jnp.concatenate([pieces[tap], pieces[tap + 1]], axis=0)
        term = dot(rows, weight[tap])
        total = term if total is None else total + term
    pooled = 0.5 * (total[:tokens] + total[tokens:])
    inv = lax.rsqrt(jnp.mean(pooled * pooled, axis=-1, keepdims=True) + EPS)
    normed = (pooled * inv * gain[...]).astype(BF)
    pooled_out[...] = pooled
    normed_out[...] = normed
    kv_out[...] = pack_kv(dot(normed, wk[...]), dot_t(normed, wv[...])).astype(BF)
    early[0:ext] = every_second(pad, 6, ext).astype(BF)
    early[ext : 2 * ext] = every_second(pad, 7, ext).astype(BF)


def ordered(bits):
    masks = [0]
    for bit in reversed(bits):
        masks = masks + [mask | (1 << bit) for mask in masks]
    return masks


def split_rows(rows, columns):
    return round_up(-(-rows * LANES // columns), 16)


def query_kernel(normed, wq, early, out, near, core, own, *, order, rows, padded, scale):
    width = normed.shape[1]
    value = normed[...]
    out[...] = (dot(value, wq[...]) * scale).astype(BF)
    ext, channels = early.shape
    near[:ext] = early[...]
    core[:ext] = early[...]
    count = len(order) * padded
    step = split_rows(count, channels)
    for i in range(4):
        block_of = place(i)
        pick = [chosen(rows, padded, width, block_of(k)) for k in order]
        part = dot_t(jnp.concatenate(pick, axis=0), value).astype(BF)
        if i == 0:
            own[...] = part
            continue
        message, at = ((core, ext), (near, ext), (near, ext + step))[i - 1]
        for c in range(channels // LANES):
            piece = part[c * step : min((c + 1) * step, count)]
            message[at : at + piece.shape[0], c * LANES : (c + 1) * LANES] = piece


def by_eight(rows):
    return rows.reshape(rows.shape[0] // 8, 8, rows.shape[1])


def attend_kernel(*refs, blocks, masks, heads, key_size, value_size, scale):
    q, cot = refs[:2]
    parts = refs[2 : 2 + blocks]
    att, dq, keep_a, send_a, keep_b, send_b = refs[2 + blocks : 8 + blocks]
    ks, vs, kt, vt, qs, cs, weights, score_cots, scores, prob_cots = refs[8 + blocks :]
    tokens = q.shape[0]
    half = tokens // 2
    wide = value_size - key_size
    for i, part in enumerate(parts):
        at = i * tokens
        ks[at : at + tokens] = part[:tokens]
        vs[at : at + tokens, :key_size] = part[tokens : 2 * tokens]
        vs[at : at + half, key_size:] = part[2 * tokens :, :wide]
        vs[at + half : at + tokens, key_size:] = part[2 * tokens :, wide:]
        kt[:, at : at + tokens] = ks[at : at + tokens].astype(F32).T.astype(BF)
        vt[:, at : at + tokens] = vs[at : at + tokens].astype(F32).T.astype(BF)
    for pair in range(heads // 2):
        ql, cl = 2 * pair * key_size, 2 * pair * value_size
        rows = slice(2 * pair * tokens, 2 * (pair + 1) * tokens)
        both = cot[:, cl : cl + 2 * value_size]
        qs[rows] = jnp.concatenate(
            [q[:, ql : ql + key_size], q[:, ql + key_size : ql + 2 * key_size]], axis=0
        )
        cs[rows] = jnp.concatenate([both[:, :value_size], both[:, value_size:]], axis=0)
        slot = pair % scores.shape[0]
        parts_of = [slice(i * tokens, (i + 1) * tokens) for i in range(blocks)]
        scores[slot] = dot_t(ks[...], qs[rows])
        prob_cots[slot] = dot_t(vs[...], cs[rows])
        top = functools.reduce(jnp.maximum, [by_eight(scores[slot, at]).max(0) for at in parts_of])
        top = jnp.max(top, axis=0, keepdims=True)
        sums = 0.0
        for at in parts_of:
            raised = jnp.exp(scores[slot, at] - top)
            sums = sums + by_eight(raised).sum(0)
            scores[slot, at] = raised
        inverse = 1.0 / jnp.sum(sums, axis=0, keepdims=True)
        for at in parts_of:
            weights[at, rows] = (scores[slot, at] * inverse).astype(BF)
        out_t = dot(vt[...], weights[:, rows]).astype(BF).astype(F32)
        delta = jnp.sum(cs[rows].astype(F32).T * out_t, axis=0, keepdims=True)
        for at in parts_of:
            probs = scores[slot, at] * inverse
            score_cots[at, rows] = (probs * (prob_cots[slot, at] - delta)).astype(BF)
        dq_t = dot(kt[...], score_cots[:, rows]) * scale
        out_rows = jnp.concatenate([out_t[:, :tokens].T, out_t[:, tokens:].T], axis=1)
        att[:, cl : cl + 2 * value_size] = out_rows.astype(BF)
        dq_rows = jnp.concatenate([dq_t[:, :tokens].T, dq_t[:, tokens:].T], axis=1)
        dq[:, ql : ql + 2 * key_size] = dq_rows.astype(BF)
    key_cots, value_cots = dot(score_cots[...], qs[...]), dot(weights[...], cs[...])
    edge = keep_a.shape[1]
    count = blocks // 2
    for i in range(blocks):
        at = slice(i * tokens, (i + 1) * tokens)
        packed = pack_kv(key_cots[at], value_cots[at])
        for order, keep, send, part in (
            (masks[0], keep_a, send_a, packed[:edge]),
            (masks[1], keep_b, send_b, packed[edge:]),
        ):
            k = order.index(i)
            if k < count:
                keep[k] = part
            else:
                send[k - count] = part.astype(BF)


def total_of(parts):
    total = parts[0][...]
    for part in parts[1:]:
        total = total + part[...].astype(F32)
    return total


def fold_kernel(*refs):
    keep, send = refs[-2:]
    total = total_of(refs[:-2])
    keep[...] = total[: keep.shape[0]]
    send[...] = total[keep.shape[0] :].astype(BF)


def share_kernel(keep_a, in_a, keep_b, in_b, *outs, masks_a, masks_b):
    left = left_masks(masks_a, masks_b)
    total_a, total_b = total_of((keep_a, in_a)), total_of((keep_b, in_b))
    for out, mask in zip(outs, left):
        parts = []
        if mask in masks_a:
            parts.append(total_a[masks_a.index(mask)])
        if mask in masks_b:
            parts.append(total_b[masks_b.index(mask)])
        out[...] = jnp.concatenate(parts, axis=0).astype(out.dtype)


def left_masks(masks_a, masks_b):
    return sorted(set(masks_a) | set(masks_b))


def send_on_kernel(keep, came, out):
    out[...] = (keep[...] + came[...].astype(F32)).astype(BF)


def query_cot_kernel(dq, wq, out):
    out[...] = dot_t(dq[...], wq[...])


def middle_kernel(*refs, masks_a, masks_b):
    left = left_masks(masks_a, masks_b)
    part, pooled_in, gain_in, wk, wv, first, second, *edges = refs[len(left) :]
    size = refs[0].shape[1]
    tokens, width = pooled_in.shape
    half = refs[0].shape[0] // 2
    top, bottom = refs[0][:half], refs[0][half:]
    for came, mask in zip(refs[1:], left[1:]):
        came = came[...].astype(F32)
        top = top + came[:half] if mask in masks_a else top
        bottom = bottom + came[-half:] if mask in masks_b else bottom
    total = jnp.concatenate([top, bottom], axis=0).astype(BF).astype(F32)
    key_cot = total[:tokens]
    value_cot = unpack_values(total, tokens, size)
    normed_cot = part[...] + dot_t(key_cot.astype(BF), wk[...])
    normed_cot = normed_cot + dot(value_cot.astype(BF), wv[...])
    pooled, gain = pooled_in[...], gain_in[...]
    inv = lax.rsqrt(jnp.mean(pooled * pooled, axis=-1, keepdims=True) + EPS)
    gain_term = jnp.sum(normed_cot * pooled * inv, axis=0, keepdims=True)
    gained = gain * normed_cot
    pooled_cot = inv * gained - pooled * (inv * inv * inv) * (
        jnp.sum(gained * pooled, axis=-1, keepdims=True) / width
    )
    conv_cot = 0.5 * pooled_cot
    high = gain_term.astype(BF).astype(F32)
    low = gain_term - high
    row = lax.broadcasted_iota(jnp.int32, (16, width), 0)
    split = width // 2
    lines = (high[:, :split], low[:, :split], high[:, split:], low[:, split:])
    lines += (conv_cot[:1, split:], conv_cot[tokens - 1 :, split:])
    gains = jnp.zeros((16, split), F32)
    for i, line in enumerate(lines):
        gains = jnp.where(row[:, :split] == i, line, gains)
    fill = split - size - value_cot.shape[1]
    side = jnp.concatenate([key_cot, value_cot, jnp.zeros((tokens, fill), F32)], axis=1)
    first[:tokens] = conv_cot[:, :split].astype(BF)
    first[tokens:] = gains.astype(BF)
    second[:tokens] = conv_cot[:, split:].astype(BF)
    second[tokens:] = side.astype(BF)
    for edge in edges:
        ends = jnp.where(row == 0, conv_cot[:1], jnp.where(row == 1, conv_cot[tokens - 1 :], 0.0))
        edge[...] = ends.astype(BF)


def place(other=0):
    seq, dp = lax.axis_index("seq"), lax.axis_index("dp") ^ (other % 2)
    high, low = seq // 2, (seq % 2) ^ (other // 2)
    return lambda k: ((high ^ k) * 2 + low) * 2 + dp


def chosen(rows, padded, columns, block):
    row = lax.broadcasted_iota(jnp.int32, (padded, columns), 0)
    column = lax.broadcasted_iota(jnp.int32, (padded, columns), 1)
    hit = (column == row + block * rows) & (row < rows)
    return jnp.where(hit, 1.0, 0.0).astype(BF)


def select_kernel(*refs, order, rows, padded):
    own, blocks = refs[0], refs[1:5]
    out, norm_out, even, odd = refs[5:]
    ext, channels = even.shape
    tokens = own.shape[1]
    count = own.shape[0]
    step = split_rows(count, channels)
    norm_out[:, :tokens] = own[...]
    for i in range(1, 4):
        at = 2 * ext + (i // 3) * step
        for c in range(channels // LANES):
            end = min((c + 1) * step, count)
            piece = blocks[i][at : at + end - c * step, c * LANES : (c + 1) * LANES]
            norm_out[c * step : end, i * tokens : (i + 1) * tokens] = piece
    block_of = place()
    pick = jnp.concatenate(
        [chosen(rows, padded, 5 * channels, block_of(k)) for k in order], axis=0
    )
    for i, block in enumerate(blocks):
        even[...] = block[:ext].astype(F32)
        odd[...] = block[ext : 2 * ext].astype(F32)
        pieces = []
        for shift in range(3):
            pieces += [even[shift : shift + tokens].astype(BF), odd[shift : shift + tokens].astype(BF)]
        shifted = jnp.concatenate(
            [jnp.concatenate(pieces[:5], axis=1), jnp.concatenate(pieces[1:], axis=1)], axis=0
        )
        out[:, 2 * i * tokens : 2 * (i + 1) * tokens] = dot_t(pick, shifted).astype(BF)


def query_grad_kernel(pick, first, second, third, fourth, keep, send, right):
    tokens = first.shape[0]
    for i, block in enumerate((first, second, third, fourth)):
        right[i * tokens : (i + 1) * tokens] = block[...]
    count, pad = keep.shape[:2]
    for k in range(2 * count):
        term = dot(pick[k * pad : (k + 1) * pad], right[...])
        if k < count:
            keep[k] = term
        else:
            send[k - count] = term.astype(BF)


def side_rows(norm_rows, size, width):
    return norm_rows * size // width


def put_side(stage, at, part, rows):
    pieces = [part[i : i + rows] for i in range(0, part.shape[0], rows)]
    stage[at : at + rows] = jnp.concatenate(pieces, axis=1)


def get_side(packed, part, rows):
    size = part.shape[1]
    for i in range(part.shape[0] // rows):
        part[i * rows : (i + 1) * rows] = packed[:, i * size : (i + 1) * size]


def stack_cots(blocks, right, tokens):
    for i, block in enumerate(blocks):
        piece = block[:tokens]
        right[2 * i * tokens : (2 * i + 1) * tokens] = piece
        right[(2 * i + 1) * tokens : (2 * i + 2) * tokens] = piece


def conv_first_kernel(*refs, conv_rows, conv_pad):
    pick, blocks, outs, right, stage = refs[0], refs[1:5], refs[5:9], refs[9], refs[10]
    tokens = right.shape[0] // 8
    stack_cots(blocks, right, tokens)
    stage[...] = jnp.zeros(stage.shape, F32)
    for half in range(2):
        gain = None
        for block in blocks:
            lines = block[tokens : tokens + 16].astype(F32)[2 * half : 2 * half + 2]
            term = lines[0:1] + lines[1:2]
            gain = term if gain is None else gain + term
        high = gain.astype(BF).astype(F32)
        at = conv_rows + 2 * half
        stage[at : at + 1] = high
        stage[at + 1 : at + 2] = gain - high
    count, above = outs[0].shape[:2]
    even = lax.axis_index("seq") % 2 == 0
    own, pair = blocks[0], blocks[2]
    tops = [b[0:16].astype(F32)[0:1] for b in (own, pair)]
    bottoms = [b[tokens - 16 : tokens].astype(F32)[15:16] for b in (own, pair)]
    rests = [b[tokens : tokens + 16].astype(F32)[4:6] for b in (own, pair)]
    for k in range(4 * count):
        conv = dot(pick[k * conv_pad : (k + 1) * conv_pad], right[...])
        stage[:conv_rows] = conv[:conv_rows]
        if k == 3 * count:
            stage[above - 4 : above - 3] = jnp.where(even, tops[0], tops[1])
            stage[above - 3 : above - 2] = jnp.where(even, rests[0][0:1], rests[1][0:1])
            stage[above - 2 : above - 1] = jnp.where(even, bottoms[1], bottoms[0])
            stage[above - 1 : above] = jnp.where(even, rests[1][1:2], rests[0][1:2])
        out = outs[k // count]
        out[k % count] = stage[...].astype(out.dtype)


def conv_second_kernel(*refs, conv_rows, conv_pad, norm_rows, norm_pad, key_size, value_size):
    pick, norm_pick, blocks, first_send = refs[0], refs[1], refs[2:6], refs[6]
    near_keep, far_keep, near_send, far_send, right, side, stage = refs[7:]
    tokens, width = right.shape[0] // 8, right.shape[1]
    stack_cots(blocks, right, tokens)
    for i, block in enumerate(blocks):
        side[i * tokens : (i + 1) * tokens] = block[tokens:]
    key_rows = side_rows(norm_rows, key_size, width)
    value_rows = side_rows(norm_rows, value_size, width)
    stage[...] = jnp.zeros(stage.shape, F32)
    count, above = first_send.shape[:2]
    near_send[:, :above] = first_send[...]
    for k in range(4 * count):
        conv = dot(pick[k * conv_pad : (k + 1) * conv_pad], right[...])
        stage[:conv_rows] = conv[:conv_rows]
        both = dot(norm_pick[k * norm_pad : (k + 1) * norm_pad], side[...])
        put_side(stage, conv_rows, both[:norm_rows, :key_size], key_rows)
        value = both[:norm_rows, key_size : key_size + value_size]
        put_side(stage, conv_rows + key_rows, value, value_rows)
        if k < 2 * count:
            (near_keep, far_keep)[k // count][k % count] = stage[...]
        elif k < 3 * count:
            near_send[k % count, above:] = stage[...].astype(BF)
        else:
            far_send[k % count] = stage[...].astype(BF)


def first_sum_kernel(keep, near, far, out):
    above = keep.shape[1]
    out[...] = keep[...] + near[:, :above].astype(F32) + far[...].astype(F32)


def combine_kernel(first, second, near, far, out):
    above = first.shape[1]
    out[:, :above] = first[...]
    out[:, above:] = second[...] + near[:, above:].astype(F32) + far[...].astype(F32)


def final_kernel(*refs, conv_parts, above):
    conv, query, key, value, gain, stage = refs[-6:]
    rows, width = conv.shape
    split = width // 2
    count = key.shape[0]
    if conv_parts == 4:
        combine_kernel(*refs[:4], stage)
    else:
        stage[...] = total_of(refs[:conv_parts])
    query[...] = total_of(refs[conv_parts:-6])[0, : query.shape[0]]
    conv[:, :split] = stage[0, :rows]
    conv[:, split:] = stage[0, above : above + rows]
    at = above + rows
    for part in (key, value):
        step = side_rows(count, part.shape[1], split)
        get_side(stage[0, at : at + step], part, step)
        at += step
    lines = stage[0, rows : rows + 4]
    line = jnp.concatenate([lines[0:1] + lines[1:2], lines[2:3] + lines[3:4]], axis=1)
    line = jnp.broadcast_to(line, (8, width))
    start = place()(0) * count
    gain[...] = pltpu.roll(line, lax.rem(width - start, width), 1)[:1, :count]


def input_kernel(*refs):
    x, first, second, pair_first, pair_second, one, three, weight, out, ext, mixed = refs
    tokens = x.shape[0] // 2
    seq, devices = lax.axis_index("seq"), lax.axis_size("seq")
    low, high = seq % 2, seq // 2
    split = first.shape[1]
    above = one.shape[1]
    one_rows = one[0, above - 16 :].astype(F32)[12:]
    three_rows = three[0, above - 16 :].astype(F32)[12:]
    heads = jnp.where(high % 2 == 0, one_rows[:2], three_rows[:2])
    tails = jnp.where(high % 2 == 0, three_rows[2:], one_rows[2:])
    heads = jnp.where(seq == devices - 1, 0.0, heads)
    tails = jnp.where(seq == 0, 0.0, tails)
    for half, own, pair in ((0, first, pair_first), (1, second, pair_second)):
        lanes = slice(half * split, (half + 1) * split)
        top = pair[0:16].astype(F32)[0:1]
        bottom = pair[tokens - 16 : tokens].astype(F32)[15:16]
        ext[8 : 8 + tokens, lanes] = own[:tokens].astype(F32)
        ext[7:8, lanes] = jnp.where(low == 0, tails[half : half + 1], bottom)
        ext[8 + tokens : 9 + tokens, lanes] = jnp.where(low == 0, top, heads[half : half + 1])
    back = ext[7 : 7 + tokens].astype(BF)
    here = ext[8 : 8 + tokens].astype(BF)
    ahead = ext[9 : 9 + tokens].astype(BF)
    evens = (ahead, here, here, back, back)
    odds = (ahead, ahead, here, here, back)
    total = None
    for tap in range(5):
        term = dot_t(jnp.concatenate([evens[tap], odds[tap]], axis=0), weight[tap])
        total = term if total is None else total + term
    for c in range(mixed.shape[0]):
        lanes = slice(c * LANES, (c + 1) * LANES)
        mixed[c, pl.ds(0, tokens, stride=2)] = total[:tokens, lanes]
        mixed[c, pl.ds(1, tokens, stride=2)] = total[tokens:, lanes]
        out[:, lanes] = (mixed[c] * gelu_slope(x[:, lanes].astype(F32))).astype(BF)


def on_device(x, conv_weight, norm_gain, wq, wk, wv, cotangent):
    devices = lax.axis_size("seq")
    both_axes = ("seq", "dp")
    x, cotangent = x[0], cotangent[0]
    positions, channels = x.shape
    tokens = positions // 2
    taps, _, width = conv_weight.shape
    key_size, value_size = wk.shape[1], wv.shape[1]
    heads = cotangent.shape[1] // value_size
    scale = key_size ** (-0.5)
    groups = devices // 2
    owners = devices * 2
    conv_rows, norm_rows = taps * channels // owners, width // owners
    conv_pad, norm_pad = round_up(conv_rows, 16), round_up(norm_rows, 16)
    ext = tokens + 16
    gain = norm_gain.reshape(1, width)

    def swap(value, seq_bits, dp_bit=0):
        mask = 2 * seq_bits + dp_bit
        return lax.ppermute(value, both_axes, [(i, i ^ mask) for i in range(owners)])

    def held(value, *until):
        return lax.optimization_barrier((value,) + until)[0]

    def quad(value, *until):
        core = swap(value, 0, 1)
        near = swap(value, 1)
        return [value, core, near, swap(held(near, *until), 0, 1)]

    def fold(parts, name, flops=0):
        shape = (parts[0].shape[0] // 2,) + parts[0].shape[1:]
        return run(fold_kernel, [(shape, F32), (shape, BF)], parts, flops=flops, name=name)

    def halved(keep, send, bits, name, flops=0):
        for bit in bits[:-1]:
            keep, send = fold([keep, swap(send, 1 << bit)], name, flops)
        return [keep, swap(send, 1 << bits[-1])]

    bits = list(range(devices.bit_length() - 1))
    order = [mask // 2 for mask in ordered(bits[1:])]
    crossing = [(i, i + 1) for i in range(1, devices - 1, 2)]
    crossing = crossing + [(j, i) for i, j in crossing]
    pad_shape = (channels // LANES, 8 + 2 * ext + 8, LANES)
    ready, ends = run(
        open_kernel,
        [(pad_shape, F32), ((32, channels), BF)],
        [x],
        flops=4 * 10**9,
        name="gelu",
    )
    pair, across = swap(ends, 1), lax.ppermute(ends, "seq", crossing)
    wv = wv.T
    kv, early, normed, pooled = run(
        front_kernel,
        [
            ((5 * tokens // 2, key_size), BF),
            ((2 * ext, channels), BF),
            ((tokens, width), BF),
            ((tokens, width), F32),
        ],
        [ready, pair, across, conv_weight, gain, wk, wv],
        [pltpu.VMEM(pad_shape, F32)],
        flops=2 * positions * taps * channels * width,
        name="front",
    )
    parts = [0, *range(2, groups), 1]
    near_kv = [swap(kv, 2 * k) if k else kv for k in parts]
    far_kv = [swap(block, 1) for block in near_kv]
    picked = (groups * norm_pad, tokens)
    rows = split_rows(picked[0], channels)
    queries, to_near, to_core, pick_own = run(
        lambda *refs: query_kernel(
            *refs, order=order, rows=norm_rows, padded=norm_pad, scale=scale
        ),
        [
            ((tokens, heads * key_size), BF),
            ((2 * ext + 2 * rows, channels), BF),
            ((2 * ext + rows, channels), BF),
            (picked, BF),
        ],
        [normed, wq, early],
        flops=4 * tokens * width * heads * key_size,
        name="queries",
        after=near_kv[1:],
    )
    to_near, to_core = held(to_near, *far_kv), held(to_core, *far_kv)
    length = devices * tokens
    masks = [2 * k for k in parts] + [2 * k + 1 for k in parts]
    half_block = (groups, 5 * tokens // 4, key_size)
    slots = 2 if length <= 2048 else 1
    attended, query_cot, keep_a, send_a, keep_b, send_b = run(
        lambda *refs: attend_kernel(
            *refs,
            blocks=devices,
            masks=[
                [masks.index(m) for m in ordered(way)] for way in (bits, [1, 0] + bits[2:])
            ],
            heads=heads,
            key_size=key_size,
            value_size=value_size,
            scale=scale,
        ),
        [((tokens, heads * value_size), BF), ((tokens, heads * key_size), BF)]
        + [(half_block, F32), (half_block, BF)] * 2,
        [queries, cotangent] + near_kv + far_kv,
        [
            pltpu.VMEM((length, key_size), BF),
            pltpu.VMEM((length, value_size), BF),
            pltpu.VMEM((key_size, length), BF),
            pltpu.VMEM((value_size, length), BF),
            pltpu.VMEM((heads * tokens, key_size), BF),
            pltpu.VMEM((heads * tokens, value_size), BF),
            pltpu.VMEM((length, heads * tokens), BF),
            pltpu.VMEM((length, heads * tokens), BF),
            pltpu.VMEM((slots, length, 2 * tokens), F32),
            pltpu.VMEM((slots, length, 2 * tokens), F32),
        ],
        flops=6 * tokens * heads * length * (key_size + value_size),
        name="attend",
    )
    in_a, in_b = swap(send_a, 1), swap(send_b, 2)
    early_near = swap(to_near, 1)
    early_blocks = [early, swap(to_core, 0, 1), early_near, swap(held(early_near, send_a), 0, 1)]
    conv_pick, norm_pick = run(
        lambda *refs: select_kernel(*refs, order=order, rows=conv_rows, padded=conv_pad),
        [((groups * conv_pad, 8 * tokens), BF), ((groups * norm_pad, 4 * tokens), BF)],
        [pick_own] + early_blocks,
        [pltpu.VMEM((ext, channels), F32), pltpu.VMEM((ext, channels), F32)],
        flops=2 * groups * conv_pad * taps * channels * 8 * tokens,
        name="select",
    )
    ways = dict(masks_a=ordered(bits[1:]), masks_b=ordered([0] + bits[2:]))
    left = left_masks(**ways)
    both = [(mask in ways["masks_a"]) + (mask in ways["masks_b"]) for mask in left]
    sums = run(
        lambda *refs: share_kernel(*refs, **ways),
        [
            ((half_block[1] * n, key_size), F32 if mask == 0 else BF)
            for mask, n in zip(left, both)
        ],
        [keep_a, in_a, keep_b, in_b],
        name="kv_cot_share",
        after=[conv_pick],
    )
    query_cot = held(query_cot, sums[0])
    query_near, query_core = swap(query_cot, 1), swap(query_cot, 0, 1)
    kv_cot = [sums[0]] + [swap(part, mask) for part, mask in zip(sums[1:], left[1:])]
    (normed_cot,) = run(
        query_cot_kernel,
        [((tokens, width), F32)],
        [query_cot, wq],
        flops=2 * tokens * width * heads * key_size,
        name="query_part",
    )
    first, second, *edge = run(
        lambda *refs: middle_kernel(*refs, **ways),
        [
            ((tokens + 16, width // 2), BF),
            ((2 * tokens, width // 2), BF),
        ]
        + [((16, width), BF)] * (len(bits) > 3),
        kv_cot + [normed_cot, pooled, gain, wk, wv],
        flops=2 * tokens * width * (key_size + value_size),
        name="conv_cot",
    )
    near_first, near_second = swap(first, 1), swap(second, 1)
    query_last = swap(held(query_near, first), 0, 1)
    query_half = (groups // 2, norm_pad, heads * key_size)
    query_keep, query_send = run(
        query_grad_kernel,
        [(query_half, F32), (query_half, BF)],
        [norm_pick, query_cot, query_core, query_near, query_last],
        [pltpu.VMEM((4 * tokens, heads * key_size), BF)],
        flops=2 * groups * norm_pad * 4 * tokens * heads * key_size,
        name="query_grad",
    )
    query_parts = halved(query_keep, query_send, bits[1:], "query_fold", 5 * 10**9)
    core_first, core_second = swap(first, 0, 1), swap(second, 0, 1)
    split = width // 2
    side = side_rows(norm_rows, key_size, split) + side_rows(norm_rows, value_size, split)
    above, below = round_up(conv_rows + 8, 16), round_up(conv_rows + side, 16)
    count = groups // 4
    last_first = swap(held(near_first, query_keep), 0, 1)
    near_keep, far_keep, near_send, far_send = run(
        lambda *refs: conv_first_kernel(*refs, conv_rows=conv_rows, conv_pad=conv_pad),
        [((count, above, split), t) for t in (F32, F32, BF, BF)],
        [conv_pick, first, core_first, near_first, last_first],
        [pltpu.VMEM((8 * tokens, split), BF), pltpu.VMEM((above, split), F32)],
        flops=groups * conv_pad * 8 * tokens * width,
        name="conv_grad_first",
    )
    far_in = swap(far_send, 2)
    last_second = swap(held(near_second, near_keep), 0, 1)
    near_keep_second, far_keep_second, near_send, far_send = run(
        lambda *refs: conv_second_kernel(
            *refs,
            conv_rows=conv_rows,
            conv_pad=conv_pad,
            norm_rows=norm_rows,
            norm_pad=norm_pad,
            key_size=key_size,
            value_size=value_size,
        ),
        [
            ((count, below, split), F32),
            ((count, below, split), F32),
            ((count, above + below, split), BF),
            ((count, below, split), BF),
        ],
        [held(conv_pick, query_parts[0]), norm_pick, second, core_second, near_second, last_second, near_send],
        [
            pltpu.VMEM((8 * tokens, split), BF),
            pltpu.VMEM((4 * tokens, split), BF),
            pltpu.VMEM((below, split), F32),
        ],
        flops=groups * conv_pad * 8 * tokens * width,
        name="conv_grad_second",
    )
    far_in_second = swap(far_send, 2)
    near_in = swap(near_send, 2)
    (far_sum,) = run(
        send_on_kernel,
        [((count, above, split), BF)],
        [far_keep, far_in],
        name="conv_send_on",
    )
    far_last = swap(far_sum, 4)
    (far_sum,) = run(
        send_on_kernel,
        [((count, below, split), BF)],
        [far_keep_second, far_in_second],
        name="conv_send_on",
    )
    edges = [far_in, far_last]
    if len(bits) > 3:
        came = lax.ppermute(edge[0], "seq", crossing)
        rows = jnp.concatenate([came[:1, :split], came[:1, split:], came[1:2, :split], came[1:2, split:]])
        edges = [jnp.pad(rows, ((above - 4, 0), (0, 0)))[None]] * 2
    (input_grad,) = run(
        input_kernel,
        [((positions, channels), BF)],
        [held(x, far_sum, query_parts[1]), first, second, near_first, near_second] + edges + [conv_weight],
        [
            pltpu.VMEM((tokens + 16, width), F32),
            pltpu.VMEM((channels // LANES, positions, LANES), F32),
        ],
        flops=20 * positions * taps * channels * width,
        name="input_grad",
    )
    (first_sum,) = run(
        first_sum_kernel,
        [((count, above, split), F32)],
        [near_keep, near_in, far_last],
        flops=5 * 10**9,
        name="conv_first_sum",
    )
    conv_parts = [first_sum, near_keep_second, near_in, swap(far_sum, 4)]
    chunk = (count, above + below, split)
    if len(bits) > 3:
        keep = run(combine_kernel, [(chunk, F32)], conv_parts, name="conv_combine")[0]
        half = (count // 2,) + chunk[1:]
        keep, send = run(fold_kernel, [(half, F32), (half, BF)], [keep], name="conv_fold")
        conv_parts = halved(keep, send, bits[3:], "conv_fold")
    conv_grad, query_grad, key_grad, value_grad, gain_grad = run(
        lambda *refs: final_kernel(*refs, conv_parts=len(conv_parts), above=above),
        [
            ((conv_rows, width), F32),
            ((norm_rows, heads * key_size), F32),
            ((norm_rows, key_size), F32),
            ((norm_rows, value_size), F32),
            ((1, norm_rows), F32),
        ],
        conv_parts + query_parts,
        [pltpu.VMEM((1,) + chunk[1:], F32)],
        name="final_sum",
    )
    return (
        attended[None],
        input_grad[None],
        conv_grad,
        query_grad,
        key_grad,
        value_grad,
        gain_grad.reshape(norm_rows),
    )


def solution(mesh):
    placed = (
        P(("groups", "dp"), "seq", None),
        P(),
        P(),
        P(),
        P(),
        P(),
        P(("groups", "dp"), "seq", None),
    )
    return jax.shard_map(
        on_device,
        mesh=mesh,
        in_specs=placed,
        out_specs=(
            P(("groups", "dp"), "seq", None),
            P(("groups", "dp"), "seq", None),
            P(("groups", "seq", "dp"), None),
            P(("groups", "seq", "dp"), None),
            P(("groups", "seq", "dp"), None),
            P(("groups", "seq", "dp"), None),
            P(("groups", "seq", "dp")),
        ),
        check_vma=False,
    )
```

```python
import functools
import math

import jax
import jax.numpy as jnp
from jax import lax
from jax.experimental import pallas as pl
from jax.experimental.pallas import tpu as pltpu
from jax.sharding import PartitionSpec as P

BF = jnp.bfloat16
F32 = jnp.float32
ROOT = math.sqrt(2.0 / math.pi)
EPS = 1e-06
LANES = 128
VMEM_BYTES = 40 * 2**20


def dot(a, b):
    return lax.dot_general(a, b, (((1,), (0,)), ((), ())), preferred_element_type=F32)


def dot_t(a, b):
    return lax.dot_general(a, b, (((1,), (1,)), ((), ())), preferred_element_type=F32)


def run(body, outs, args, scratch=(), flops=0, name=None, after=()):
    size = sum(math.prod(a.shape) * a.dtype.itemsize for a in args)
    size += sum(math.prod(s) * jnp.dtype(t).itemsize for s, t in outs)
    vmem = pl.BlockSpec(memory_space=pltpu.VMEM)
    rest = pl.BlockSpec(memory_space=pl.ANY)
    count, skip = len(args), len(args) + len(after)

    def whole(*refs):
        body(*refs[:count], *refs[skip:])

    return pl.pallas_call(
        whole,
        out_shape=[jax.ShapeDtypeStruct(s, t) for s, t in outs],
        in_specs=[vmem] * count + [rest] * len(after),
        out_specs=[vmem] * len(outs),
        scratch_shapes=list(scratch),
        compiler_params=pltpu.CompilerParams(vmem_limit_bytes=VMEM_BYTES),
        cost_estimate=pl.CostEstimate(flops=flops, bytes_accessed=size, transcendentals=0),
        name=name,
    )(*args, *after)


def gelu(v):
    return v * (0.5 * (1.0 + jnp.tanh(ROOT * (v + 0.044715 * (v * v * v)))))


def gelu_slope(v):
    tangent = jnp.tanh(ROOT * (v + 0.044715 * v * v * v))
    return 0.5 * (1.0 + tangent) + 0.5 * v * (1.0 - tangent * tangent) * ROOT * (
        1.0 + 3.0 * 0.044715 * v * v
    )


def round_up(value, step):
    return -(-value // step) * step


def pack_kv(keys, values):
    tokens, size = keys.shape
    rest = values[:, size:]
    half = tokens // 2
    tail = jnp.concatenate([rest[:half], rest[half:]], axis=1)
    return jnp.concatenate([keys, values[:, :size], tail], axis=0)


def unpack_values(packed, tokens, size):
    tail = packed[2 * tokens :]
    width = tail.shape[1] // 2
    rest = jnp.concatenate([tail[:, :width], tail[:, width:]], axis=0)
    return jnp.concatenate([packed[tokens : 2 * tokens], rest], axis=1)


def put(ref, start, rows):
    for c in range(ref.shape[0]):
        ref[c, start : start + rows.shape[0]] = rows[:, c * LANES : (c + 1) * LANES]


def every_second(ref, start, count):
    parts = [ref[c, pl.ds(start, count, stride=2)] for c in range(ref.shape[0])]
    return jnp.concatenate(parts, axis=1)


def open_kernel(x, pad, ends):
    positions, channels = x.shape
    ends[:16] = x[:16]
    ends[16:] = x[positions - 16 :]
    put(pad, 0, jnp.zeros((8, channels), F32))
    put(pad, 8, gelu(x[...].astype(F32)).astype(BF).astype(F32))
    put(pad, 8 + positions, jnp.zeros((pad.shape[1] - 8 - positions, channels), F32))


def front_kernel(ready, pair, across, weight, gain, wk, wv, kv_out, early, normed_out, pooled_out, pad):
    tokens = pooled_out.shape[0]
    ext = early.shape[0] // 2
    even = lax.axis_index("seq") % 2 == 0
    pair_wide, across_wide = pair[...].astype(F32), across[...].astype(F32)
    before = jnp.where(even, across_wide[16:], pair_wide[16:])[14:]
    after = jnp.where(even, pair_wide[:16], across_wide[:16])[:2]
    pad[...] = ready[...]
    put(pad, 6, gelu(before).astype(BF).astype(F32))
    put(pad, 8 + 2 * tokens, gelu(after).astype(BF).astype(F32))
    pieces = [every_second(pad, 6 + u, tokens).astype(BF) for u in range(6)]
    total = None
    for tap in range(5):
        rows = jnp.concatenate([pieces[tap], pieces[tap + 1]], axis=0)
        term = dot(rows, weight[tap])
        total = term if total is None else total + term
    pooled = 0.5 * (total[:tokens] + total[tokens:])
    inv = lax.rsqrt(jnp.mean(pooled * pooled, axis=-1, keepdims=True) + EPS)
    normed = (pooled * inv * gain[...]).astype(BF)
    pooled_out[...] = pooled
    normed_out[...] = normed
    kv_out[...] = pack_kv(dot(normed, wk[...]), dot_t(normed, wv[...])).astype(BF)
    early[0:ext] = every_second(pad, 6, ext).astype(BF)
    early[ext : 2 * ext] = every_second(pad, 7, ext).astype(BF)


def ordered(bits):
    masks = [0]
    for bit in reversed(bits):
        masks = masks + [mask | (1 << bit) for mask in masks]
    return masks


def split_rows(rows, columns):
    return round_up(-(-rows * LANES // columns), 16)


def query_kernel(normed, wq, early, out, near, core, own, *, order, rows, padded, scale):
    width = normed.shape[1]
    value = normed[...]
    out[...] = (dot(value, wq[...]) * scale).astype(BF)
    ext, channels = early.shape
    near[:ext] = early[...]
    core[:ext] = early[...]
    count = len(order) * padded
    step = split_rows(count, channels)
    for i in range(4):
        block_of = place(i)
        pick = [chosen(rows, padded, width, block_of(k)) for k in order]
        part = dot_t(jnp.concatenate(pick, axis=0), value).astype(BF)
        if i == 0:
            own[...] = part
            continue
        message, at = ((core, ext), (near, ext), (near, ext + step))[i - 1]
        for c in range(channels // LANES):
            piece = part[c * step : min((c + 1) * step, count)]
            message[at : at + piece.shape[0], c * LANES : (c + 1) * LANES] = piece


def by_eight(rows):
    return rows.reshape(rows.shape[0] // 8, 8, rows.shape[1])


def attend_kernel(*refs, blocks, masks, heads, key_size, value_size, scale):
    q, cot = refs[:2]
    parts = refs[2 : 2 + blocks]
    att, dq, keep_a, send_a, keep_b, send_b = refs[2 + blocks : 8 + blocks]
    ks, vs, kt, vt, qs, cs, weights, score_cots, scores, prob_cots = refs[8 + blocks :]
    tokens = q.shape[0]
    half = tokens // 2
    wide = value_size - key_size
    for i, part in enumerate(parts):
        at = i * tokens
        ks[at : at + tokens] = part[:tokens]
        vs[at : at + tokens, :key_size] = part[tokens : 2 * tokens]
        vs[at : at + half, key_size:] = part[2 * tokens :, :wide]
        vs[at + half : at + tokens, key_size:] = part[2 * tokens :, wide:]
        kt[:, at : at + tokens] = ks[at : at + tokens].astype(F32).T.astype(BF)
        vt[:, at : at + tokens] = vs[at : at + tokens].astype(F32).T.astype(BF)
    slots = scores.shape[0]
    parts_of = [slice(i * tokens, (i + 1) * tokens) for i in range(blocks)]

    def products(pair):
        ql, cl = 2 * pair * key_size, 2 * pair * value_size
        rows = slice(2 * pair * tokens, 2 * (pair + 1) * tokens)
        both = cot[:, cl : cl + 2 * value_size]
        qs[rows] = jnp.concatenate(
            [q[:, ql : ql + key_size], q[:, ql + key_size : ql + 2 * key_size]], axis=0
        )
        cs[rows] = jnp.concatenate([both[:, :value_size], both[:, value_size:]], axis=0)
        scores[pair % slots] = dot_t(ks[...], qs[rows])
        prob_cots[pair % slots] = dot_t(vs[...], cs[rows])

    products(0)
    for pair in range(heads // 2):
        ql, cl = 2 * pair * key_size, 2 * pair * value_size
        rows = slice(2 * pair * tokens, 2 * (pair + 1) * tokens)
        slot = pair % slots
        if slots > 1 and pair + 1 < heads // 2:
            products(pair + 1)
        top = functools.reduce(jnp.maximum, [by_eight(scores[slot, at]).max(0) for at in parts_of])
        top = jnp.max(top, axis=0, keepdims=True)
        sums = 0.0
        for at in parts_of:
            raised = jnp.exp(scores[slot, at] - top)
            sums = sums + by_eight(raised).sum(0)
            scores[slot, at] = raised
        inverse = 1.0 / jnp.sum(sums, axis=0, keepdims=True)
        for at in parts_of:
            weights[at, rows] = (scores[slot, at] * inverse).astype(BF)
        out_t = dot(vt[...], weights[:, rows]).astype(BF).astype(F32)
        delta = jnp.sum(cs[rows].astype(F32).T * out_t, axis=0, keepdims=True)
        for at in parts_of:
            probs = scores[slot, at] * inverse
            score_cots[at, rows] = (probs * (prob_cots[slot, at] - delta)).astype(BF)
        if slots == 1 and pair + 1 < heads // 2:
            products(pair + 1)
        dq_t = dot(kt[...], score_cots[:, rows]) * scale
        out_rows = jnp.concatenate([out_t[:, :tokens].T, out_t[:, tokens:].T], axis=1)
        att[:, cl : cl + 2 * value_size] = out_rows.astype(BF)
        dq_rows = jnp.concatenate([dq_t[:, :tokens].T, dq_t[:, tokens:].T], axis=1)
        dq[:, ql : ql + 2 * key_size] = dq_rows.astype(BF)
    key_cots, value_cots = dot(score_cots[...], qs[...]), dot(weights[...], cs[...])
    edge = keep_a.shape[1]
    count = blocks // 2
    for i in range(blocks):
        at = slice(i * tokens, (i + 1) * tokens)
        packed = pack_kv(key_cots[at], value_cots[at])
        for order, keep, send, part in (
            (masks[0], keep_a, send_a, packed[:edge]),
            (masks[1], keep_b, send_b, packed[edge:]),
        ):
            k = order.index(i)
            if k < count:
                keep[k] = part
            else:
                send[k - count] = part.astype(BF)


def total_of(parts):
    total = parts[0][...]
    for part in parts[1:]:
        total = total + part[...].astype(F32)
    return total


def fold_kernel(*refs):
    keep, send = refs[-2:]
    total = total_of(refs[:-2])
    keep[...] = total[: keep.shape[0]]
    send[...] = total[keep.shape[0] :].astype(BF)


def fold_two_kernel(*refs):
    fold_kernel(refs[0], refs[1], refs[4], refs[5])
    fold_kernel(refs[2], refs[3], refs[6], refs[7])


def merge_kernel(keep_a, in_a, keep_b, in_b, keep, send):
    total = jnp.concatenate([total_of((keep_a, in_a)), total_of((keep_b, in_b))], axis=1)
    keep[...] = total[: keep.shape[0]]
    send[...] = total[keep.shape[0] :].astype(BF)


def send_on_kernel(keep, came, out):
    out[...] = (keep[...] + came[...].astype(F32)).astype(BF)


def query_cot_kernel(dq, wq, out):
    out[...] = dot_t(dq[...], wq[...])


def middle_kernel(own, came, part, pooled_in, gain_in, wk, wv, first, second, *edges):
    size = own.shape[2]
    tokens, width = pooled_in.shape
    total = (own[0] + came[0].astype(F32)).astype(BF).astype(F32)
    key_cot = total[:tokens]
    value_cot = unpack_values(total, tokens, size)
    normed_cot = part[...] + dot_t(key_cot.astype(BF), wk[...])
    normed_cot = normed_cot + dot(value_cot.astype(BF), wv[...])
    pooled, gain = pooled_in[...], gain_in[...]
    inv = lax.rsqrt(jnp.mean(pooled * pooled, axis=-1, keepdims=True) + EPS)
    gain_term = jnp.sum(normed_cot * pooled * inv, axis=0, keepdims=True)
    gained = gain * normed_cot
    pooled_cot = inv * gained - pooled * (inv * inv * inv) * (
        jnp.sum(gained * pooled, axis=-1, keepdims=True) / width
    )
    conv_cot = 0.5 * pooled_cot
    high = gain_term.astype(BF).astype(F32)
    low = gain_term - high
    row = lax.broadcasted_iota(jnp.int32, (16, width), 0)
    split = width // 2
    lines = (high[:, :split], low[:, :split], high[:, split:], low[:, split:])
    lines += (conv_cot[:1, split:], conv_cot[tokens - 1 :, split:])
    gains = jnp.zeros((16, split), F32)
    for i, line in enumerate(lines):
        gains = jnp.where(row[:, :split] == i, line, gains)
    fill = split - size - value_cot.shape[1]
    side = jnp.concatenate([key_cot, value_cot, jnp.zeros((tokens, fill), F32)], axis=1)
    first[:tokens] = conv_cot[:, :split].astype(BF)
    first[tokens:] = gains.astype(BF)
    second[:tokens] = conv_cot[:, split:].astype(BF)
    second[tokens:] = side.astype(BF)
    for edge in edges:
        ends = jnp.where(row == 0, conv_cot[:1], jnp.where(row == 1, conv_cot[tokens - 1 :], 0.0))
        edge[...] = ends.astype(BF)


def place(other=0):
    seq, dp = lax.axis_index("seq"), lax.axis_index("dp") ^ (other % 2)
    high, low = seq // 2, (seq % 2) ^ (other // 2)
    return lambda k: ((high ^ k) * 2 + low) * 2 + dp


def chosen(rows, padded, columns, block):
    row = lax.broadcasted_iota(jnp.int32, (padded, columns), 0)
    column = lax.broadcasted_iota(jnp.int32, (padded, columns), 1)
    hit = (column == row + block * rows) & (row < rows)
    return jnp.where(hit, 1.0, 0.0).astype(BF)


def select_kernel(*refs, order, rows, padded):
    own, blocks = refs[0], refs[1:5]
    out, norm_out, even, odd = refs[5:]
    ext, channels = even.shape
    tokens = own.shape[1]
    count = own.shape[0]
    step = split_rows(count, channels)
    norm_out[:, :tokens] = own[...]
    for i in range(1, 4):
        at = 2 * ext + (i // 3) * step
        for c in range(channels // LANES):
            end = min((c + 1) * step, count)
            piece = blocks[i][at : at + end - c * step, c * LANES : (c + 1) * LANES]
            norm_out[c * step : end, i * tokens : (i + 1) * tokens] = piece
    block_of = place()
    pick = jnp.concatenate(
        [chosen(rows, padded, 5 * channels, block_of(k)) for k in order], axis=0
    )
    for i, block in enumerate(blocks):
        even[...] = block[:ext].astype(F32)
        odd[...] = block[ext : 2 * ext].astype(F32)
        pieces = []
        for shift in range(3):
            pieces += [even[shift : shift + tokens].astype(BF), odd[shift : shift + tokens].astype(BF)]
        shifted = jnp.concatenate(
            [jnp.concatenate(pieces[:5], axis=1), jnp.concatenate(pieces[1:], axis=1)], axis=0
        )
        out[:, 2 * i * tokens : 2 * (i + 1) * tokens] = dot_t(pick, shifted).astype(BF)


def query_grad_kernel(pick, first, second, third, fourth, keep, send, right):
    tokens = first.shape[0]
    for i, block in enumerate((first, second, third, fourth)):
        right[i * tokens : (i + 1) * tokens] = block[...]
    count, pad = keep.shape[:2]
    for k in range(2 * count):
        term = dot(pick[k * pad : (k + 1) * pad], right[...])
        if k < count:
            keep[k] = term
        else:
            send[k - count] = term.astype(BF)


def side_rows(norm_rows, size, width):
    return norm_rows * size // width


def put_side(stage, at, part, rows):
    pieces = [part[i : i + rows] for i in range(0, part.shape[0], rows)]
    stage[at : at + rows] = jnp.concatenate(pieces, axis=1)


def get_side(packed, part, rows):
    size = part.shape[1]
    for i in range(part.shape[0] // rows):
        part[i * rows : (i + 1) * rows] = packed[:, i * size : (i + 1) * size]


def stack_cots(blocks, right, tokens):
    for i, block in enumerate(blocks):
        piece = block[:tokens]
        right[2 * i * tokens : (2 * i + 1) * tokens] = piece
        right[(2 * i + 1) * tokens : (2 * i + 2) * tokens] = piece


def conv_first_kernel(*refs, conv_rows, conv_pad):
    pick, blocks, outs, right, stage = refs[0], refs[1:5], refs[5:9], refs[9], refs[10]
    tokens = right.shape[0] // 8
    stack_cots(blocks, right, tokens)
    stage[...] = jnp.zeros(stage.shape, F32)
    for half in range(2):
        gain = None
        for block in blocks:
            lines = block[tokens : tokens + 16].astype(F32)[2 * half : 2 * half + 2]
            term = lines[0:1] + lines[1:2]
            gain = term if gain is None else gain + term
        high = gain.astype(BF).astype(F32)
        at = conv_rows + 2 * half
        stage[at : at + 1] = high
        stage[at + 1 : at + 2] = gain - high
    count, above = outs[0].shape[:2]
    even = lax.axis_index("seq") % 2 == 0
    own, pair = blocks[0], blocks[2]
    tops = [b[0:16].astype(F32)[0:1] for b in (own, pair)]
    bottoms = [b[tokens - 16 : tokens].astype(F32)[15:16] for b in (own, pair)]
    rests = [b[tokens : tokens + 16].astype(F32)[4:6] for b in (own, pair)]
    for k in range(4 * count):
        conv = dot(pick[k * conv_pad : (k + 1) * conv_pad], right[...])
        stage[:conv_rows] = conv[:conv_rows]
        if k == 3 * count:
            stage[above - 4 : above - 3] = jnp.where(even, tops[0], tops[1])
            stage[above - 3 : above - 2] = jnp.where(even, rests[0][0:1], rests[1][0:1])
            stage[above - 2 : above - 1] = jnp.where(even, bottoms[1], bottoms[0])
            stage[above - 1 : above] = jnp.where(even, rests[1][1:2], rests[0][1:2])
        out = outs[k // count]
        out[k % count] = stage[...].astype(out.dtype)


def conv_second_kernel(*refs, conv_rows, conv_pad, norm_rows, norm_pad, key_size, value_size):
    pick, norm_pick, blocks, first_send = refs[0], refs[1], refs[2:6], refs[6]
    near_keep, far_keep, near_send, far_send, right, side, stage = refs[7:]
    tokens, width = right.shape[0] // 8, right.shape[1]
    stack_cots(blocks, right, tokens)
    for i, block in enumerate(blocks):
        side[i * tokens : (i + 1) * tokens] = block[tokens:]
    key_rows = side_rows(norm_rows, key_size, width)
    value_rows = side_rows(norm_rows, value_size, width)
    stage[...] = jnp.zeros(stage.shape, F32)
    count, above = first_send.shape[:2]
    near_send[:, :above] = first_send[...]
    for k in range(4 * count):
        conv = dot(pick[k * conv_pad : (k + 1) * conv_pad], right[...])
        stage[:conv_rows] = conv[:conv_rows]
        both = dot(norm_pick[k * norm_pad : (k + 1) * norm_pad], side[...])
        put_side(stage, conv_rows, both[:norm_rows, :key_size], key_rows)
        value = both[:norm_rows, key_size : key_size + value_size]
        put_side(stage, conv_rows + key_rows, value, value_rows)
        if k < 2 * count:
            (near_keep, far_keep)[k // count][k % count] = stage[...]
        elif k < 3 * count:
            near_send[k % count, above:] = stage[...].astype(BF)
        else:
            far_send[k % count] = stage[...].astype(BF)


def first_sum_kernel(keep, near, far, out):
    above = keep.shape[1]
    out[...] = keep[...] + near[:, :above].astype(F32) + far[...].astype(F32)


def combine_kernel(first, second, near, far, out):
    above = first.shape[1]
    out[:, :above] = first[...]
    out[:, above:] = second[...] + near[:, above:].astype(F32) + far[...].astype(F32)


def final_kernel(*refs, conv_parts, above):
    conv, query, key, value, gain, stage = refs[-6:]
    rows, width = conv.shape
    split = width // 2
    count = key.shape[0]
    if conv_parts == 4:
        combine_kernel(*refs[:4], stage)
    else:
        stage[...] = total_of(refs[:conv_parts])
    query[...] = total_of(refs[conv_parts:-6])[0, : query.shape[0]]
    conv[:, :split] = stage[0, :rows]
    conv[:, split:] = stage[0, above : above + rows]
    at = above + rows
    for part in (key, value):
        step = side_rows(count, part.shape[1], split)
        get_side(stage[0, at : at + step], part, step)
        at += step
    lines = stage[0, rows : rows + 4]
    line = jnp.concatenate([lines[0:1] + lines[1:2], lines[2:3] + lines[3:4]], axis=1)
    line = jnp.broadcast_to(line, (8, width))
    start = place()(0) * count
    gain[...] = pltpu.roll(line, lax.rem(width - start, width), 1)[:1, :count]


def input_kernel(*refs):
    x, first, second, pair_first, pair_second, one, three, weight, out, ext, mixed = refs
    tokens = x.shape[0] // 2
    seq, devices = lax.axis_index("seq"), lax.axis_size("seq")
    low, high = seq % 2, seq // 2
    split = first.shape[1]
    above = one.shape[1]
    one_rows = one[0, above - 16 :].astype(F32)[12:]
    three_rows = three[0, above - 16 :].astype(F32)[12:]
    heads = jnp.where(high % 2 == 0, one_rows[:2], three_rows[:2])
    tails = jnp.where(high % 2 == 0, three_rows[2:], one_rows[2:])
    heads = jnp.where(seq == devices - 1, 0.0, heads)
    tails = jnp.where(seq == 0, 0.0, tails)
    for half, own, pair in ((0, first, pair_first), (1, second, pair_second)):
        lanes = slice(half * split, (half + 1) * split)
        top = pair[0:16].astype(F32)[0:1]
        bottom = pair[tokens - 16 : tokens].astype(F32)[15:16]
        ext[8 : 8 + tokens, lanes] = own[:tokens].astype(F32)
        ext[7:8, lanes] = jnp.where(low == 0, tails[half : half + 1], bottom)
        ext[8 + tokens : 9 + tokens, lanes] = jnp.where(low == 0, top, heads[half : half + 1])
    back = ext[7 : 7 + tokens].astype(BF)
    here = ext[8 : 8 + tokens].astype(BF)
    ahead = ext[9 : 9 + tokens].astype(BF)
    evens = (ahead, here, here, back, back)
    odds = (ahead, ahead, here, here, back)
    total = None
    for tap in range(5):
        term = dot_t(jnp.concatenate([evens[tap], odds[tap]], axis=0), weight[tap])
        total = term if total is None else total + term
    for c in range(mixed.shape[0]):
        lanes = slice(c * LANES, (c + 1) * LANES)
        mixed[c, pl.ds(0, tokens, stride=2)] = total[:tokens, lanes]
        mixed[c, pl.ds(1, tokens, stride=2)] = total[tokens:, lanes]
        out[:, lanes] = (mixed[c] * gelu_slope(x[:, lanes].astype(F32))).astype(BF)


def on_device(x, conv_weight, norm_gain, wq, wk, wv, cotangent):
    devices = lax.axis_size("seq")
    both_axes = ("seq", "dp")
    x, cotangent = x[0], cotangent[0]
    positions, channels = x.shape
    tokens = positions // 2
    taps, _, width = conv_weight.shape
    key_size, value_size = wk.shape[1], wv.shape[1]
    heads = cotangent.shape[1] // value_size
    scale = key_size ** (-0.5)
    groups = devices // 2
    owners = devices * 2
    conv_rows, norm_rows = taps * channels // owners, width // owners
    conv_pad, norm_pad = round_up(conv_rows, 16), round_up(norm_rows, 16)
    ext = tokens + 16
    gain = norm_gain.reshape(1, width)

    def swap(value, seq_bits, dp_bit=0):
        mask = 2 * seq_bits + dp_bit
        return lax.ppermute(value, both_axes, [(i, i ^ mask) for i in range(owners)])

    def held(value, *until):
        return lax.optimization_barrier((value,) + until)[0]

    def quad(value, *until):
        core = swap(value, 0, 1)
        near = swap(value, 1)
        return [value, core, near, swap(held(near, *until), 0, 1)]

    def fold(parts, name):
        shape = (parts[0].shape[0] // 2,) + parts[0].shape[1:]
        return run(fold_kernel, [(shape, F32), (shape, BF)], parts, name=name)

    def halved(keep, send, bits, name):
        for bit in bits[:-1]:
            keep, send = fold([keep, swap(send, 1 << bit)], name)
        return [keep, swap(send, 1 << bits[-1])]

    bits = list(range(devices.bit_length() - 1))
    order = [mask // 2 for mask in ordered(bits[1:])]
    crossing = [(i, i + 1) for i in range(1, devices - 1, 2)]
    crossing = crossing + [(j, i) for i, j in crossing]
    pad_shape = (channels // LANES, 8 + 2 * ext + 8, LANES)
    ready, ends = run(
        open_kernel,
        [(pad_shape, F32), ((32, channels), BF)],
        [x],
        flops=4 * 10**9,
        name="gelu",
    )
    pair, across = swap(ends, 1), lax.ppermute(ends, "seq", crossing)
    wv = wv.T
    kv, early, normed, pooled = run(
        front_kernel,
        [
            ((5 * tokens // 2, key_size), BF),
            ((2 * ext, channels), BF),
            ((tokens, width), BF),
            ((tokens, width), F32),
        ],
        [ready, pair, across, conv_weight, gain, wk, wv],
        [pltpu.VMEM(pad_shape, F32)],
        flops=2 * positions * taps * channels * width,
        name="front",
    )
    parts = [0, *range(2, groups), 1]
    near_kv = [swap(kv, 2 * k) if k else kv for k in parts]
    far_kv = [swap(block, 1) for block in near_kv]
    picked = (groups * norm_pad, tokens)
    rows = split_rows(picked[0], channels)
    queries, to_near, to_core, pick_own = run(
        lambda *refs: query_kernel(
            *refs, order=order, rows=norm_rows, padded=norm_pad, scale=scale
        ),
        [
            ((tokens, heads * key_size), BF),
            ((2 * ext + 2 * rows, channels), BF),
            ((2 * ext + rows, channels), BF),
            (picked, BF),
        ],
        [normed, wq, early],
        flops=4 * tokens * width * heads * key_size,
        name="queries",
        after=near_kv[1:],
    )
    to_near, to_core = held(to_near, *far_kv), held(to_core, *far_kv)
    length = devices * tokens
    masks = [2 * k for k in parts] + [2 * k + 1 for k in parts]
    half_block = (groups, 5 * tokens // 4, key_size)
    slots = 2 if length <= 2048 else 1
    attended, query_cot, keep_a, send_a, keep_b, send_b = run(
        lambda *refs: attend_kernel(
            *refs,
            blocks=devices,
            masks=[
                [masks.index(m) for m in ordered(way)] for way in (bits, [1, 0] + bits[2:])
            ],
            heads=heads,
            key_size=key_size,
            value_size=value_size,
            scale=scale,
        ),
        [((tokens, heads * value_size), BF), ((tokens, heads * key_size), BF)]
        + [(half_block, F32), (half_block, BF)] * 2,
        [queries, cotangent] + near_kv + far_kv,
        [
            pltpu.VMEM((length, key_size), BF),
            pltpu.VMEM((length, value_size), BF),
            pltpu.VMEM((key_size, length), BF),
            pltpu.VMEM((value_size, length), BF),
            pltpu.VMEM((heads * tokens, key_size), BF),
            pltpu.VMEM((heads * tokens, value_size), BF),
            pltpu.VMEM((length, heads * tokens), BF),
            pltpu.VMEM((length, heads * tokens), BF),
            pltpu.VMEM((slots, length, 2 * tokens), F32),
            pltpu.VMEM((slots, length, 2 * tokens), F32),
        ],
        flops=6 * tokens * heads * length * (key_size + value_size),
        name="attend",
    )
    in_a, in_b = swap(send_a, 1), swap(send_b, 2)
    early_near = swap(to_near, 1)
    early_blocks = [early, swap(to_core, 0, 1), early_near, swap(held(early_near, send_a), 0, 1)]
    conv_pick, norm_pick = run(
        lambda *refs: select_kernel(*refs, order=order, rows=conv_rows, padded=conv_pad),
        [((groups * conv_pad, 8 * tokens), BF), ((groups * norm_pad, 4 * tokens), BF)],
        [pick_own] + early_blocks,
        [pltpu.VMEM((ext, channels), F32), pltpu.VMEM((ext, channels), F32)],
        flops=2 * groups * conv_pad * taps * channels * 8 * tokens,
        name="select",
    )
    fourth = (groups // 2,) + half_block[1:]
    keep_a, send_a, keep_b, send_b = run(
        fold_two_kernel,
        [(fourth, F32), (fourth, BF)] * 2,
        [keep_a, in_a, keep_b, in_b],
        name="kv_cot_fold",
        after=[conv_pick],
    )
    in_a, in_b = swap(send_a, 2), swap(send_b, 1)
    block = (groups // 4, 5 * tokens // 2, key_size)
    keep, send = run(
        merge_kernel,
        [(block, F32), (block, BF)],
        [keep_a, in_a, keep_b, in_b],
        name="kv_cot_merge",
    )
    (normed_cot,) = run(
        query_cot_kernel,
        [((tokens, width), F32)],
        [query_cot, wq],
        flops=2 * tokens * width * heads * key_size,
        name="query_part",
    )
    query_cot = held(query_cot, keep)
    query_near, query_core = swap(query_cot, 1), swap(query_cot, 0, 1)
    kv_cot = halved(keep, send, bits[2:], "kv_cot_fold")
    first, second, *edge = run(
        middle_kernel,
        [
            ((tokens + 16, width // 2), BF),
            ((2 * tokens, width // 2), BF),
        ]
        + [((16, width), BF)] * (len(bits) > 3),
        kv_cot + [normed_cot, pooled, gain, wk, wv],
        flops=2 * tokens * width * (key_size + value_size),
        name="conv_cot",
    )
    near_first, near_second = swap(first, 1), swap(second, 1)
    query_last = swap(held(query_near, first), 0, 1)
    query_half = (groups // 2, norm_pad, heads * key_size)
    query_keep, query_send = run(
        query_grad_kernel,
        [(query_half, F32), (query_half, BF)],
        [norm_pick, query_cot, query_core, query_near, query_last],
        [pltpu.VMEM((4 * tokens, heads * key_size), BF)],
        flops=2 * groups * norm_pad * 4 * tokens * heads * key_size,
        name="query_grad",
    )
    query_parts = halved(query_keep, query_send, bits[1:], "query_fold")
    core_first, core_second = swap(first, 0, 1), swap(second, 0, 1)
    split = width // 2
    side = side_rows(norm_rows, key_size, split) + side_rows(norm_rows, value_size, split)
    above, below = round_up(conv_rows + 8, 16), round_up(conv_rows + side, 16)
    count = groups // 4
    last_first = swap(held(near_first, query_keep), 0, 1)
    near_keep, far_keep, near_send, far_send = run(
        lambda *refs: conv_first_kernel(*refs, conv_rows=conv_rows, conv_pad=conv_pad),
        [((count, above, split), t) for t in (F32, F32, BF, BF)],
        [conv_pick, first, core_first, near_first, last_first],
        [pltpu.VMEM((8 * tokens, split), BF), pltpu.VMEM((above, split), F32)],
        flops=groups * conv_pad * 8 * tokens * width,
        name="conv_grad_first",
    )
    far_in = swap(far_send, 2)
    last_second = swap(held(near_second, near_keep, query_parts[0]), 0, 1)
    near_keep_second, far_keep_second, near_send, far_send = run(
        lambda *refs: conv_second_kernel(
            *refs,
            conv_rows=conv_rows,
            conv_pad=conv_pad,
            norm_rows=norm_rows,
            norm_pad=norm_pad,
            key_size=key_size,
            value_size=value_size,
        ),
        [
            ((count, below, split), F32),
            ((count, below, split), F32),
            ((count, above + below, split), BF),
            ((count, below, split), BF),
        ],
        [conv_pick, norm_pick, second, core_second, near_second, last_second, near_send],
        [
            pltpu.VMEM((8 * tokens, split), BF),
            pltpu.VMEM((4 * tokens, split), BF),
            pltpu.VMEM((below, split), F32),
        ],
        flops=groups * conv_pad * 8 * tokens * width,
        name="conv_grad_second",
    )
    far_in_second = swap(far_send, 2)
    near_in = swap(near_send, 2)
    (far_sum,) = run(
        send_on_kernel,
        [((count, above, split), BF)],
        [far_keep, far_in],
        name="conv_send_on",
    )
    far_last = swap(far_sum, 4)
    (far_sum,) = run(
        send_on_kernel,
        [((count, below, split), BF)],
        [far_keep_second, far_in_second],
        name="conv_send_on",
    )
    edges = [far_in, far_last]
    if len(bits) > 3:
        came = lax.ppermute(edge[0], "seq", crossing)
        rows = jnp.concatenate([came[:1, :split], came[:1, split:], came[1:2, :split], came[1:2, split:]])
        edges = [jnp.pad(rows, ((above - 4, 0), (0, 0)))[None]] * 2
    (input_grad,) = run(
        input_kernel,
        [((positions, channels), BF)],
        [held(x, far_sum, query_parts[1]), first, second, near_first, near_second] + edges + [conv_weight],
        [
            pltpu.VMEM((tokens + 16, width), F32),
            pltpu.VMEM((channels // LANES, positions, LANES), F32),
        ],
        flops=20 * positions * taps * channels * width,
        name="input_grad",
    )
    (first_sum,) = run(
        first_sum_kernel,
        [((count, above, split), F32)],
        [near_keep, near_in, far_last],
        flops=5 * 10**9,
        name="conv_first_sum",
    )
    conv_parts = [first_sum, near_keep_second, near_in, swap(far_sum, 4)]
    chunk = (count, above + below, split)
    if len(bits) > 3:
        keep = run(combine_kernel, [(chunk, F32)], conv_parts, name="conv_combine")[0]
        half = (count // 2,) + chunk[1:]
        keep, send = run(fold_kernel, [(half, F32), (half, BF)], [keep], name="conv_fold")
        conv_parts = halved(keep, send, bits[3:], "conv_fold")
    conv_grad, query_grad, key_grad, value_grad, gain_grad = run(
        lambda *refs: final_kernel(*refs, conv_parts=len(conv_parts), above=above),
        [
            ((conv_rows, width), F32),
            ((norm_rows, heads * key_size), F32),
            ((norm_rows, key_size), F32),
            ((norm_rows, value_size), F32),
            ((1, norm_rows), F32),
        ],
        conv_parts + query_parts,
        [pltpu.VMEM((1,) + chunk[1:], F32)],
        name="final_sum",
    )
    return (
        attended[None],
        input_grad[None],
        conv_grad,
        query_grad,
        key_grad,
        value_grad,
        gain_grad.reshape(norm_rows),
    )


def solution(mesh):
    placed = (
        P(("groups", "dp"), "seq", None),
        P(),
        P(),
        P(),
        P(),
        P(),
        P(("groups", "dp"), "seq", None),
    )
    return jax.shard_map(
        on_device,
        mesh=mesh,
        in_specs=placed,
        out_specs=(
            P(("groups", "dp"), "seq", None),
            P(("groups", "dp"), "seq", None),
            P(("groups", "seq", "dp"), None),
            P(("groups", "seq", "dp"), None),
            P(("groups", "seq", "dp"), None),
            P(("groups", "seq", "dp"), None),
            P(("groups", "seq", "dp")),
        ),
        check_vma=False,
    )
```

```python
import functools
import math

import jax
import jax.numpy as jnp
from jax import lax
from jax.experimental import pallas as pl
from jax.experimental.pallas import tpu as pltpu
from jax.sharding import PartitionSpec as P

BF = jnp.bfloat16
F32 = jnp.float32
ROOT = math.sqrt(2.0 / math.pi)
EPS = 1e-06
LANES = 128
VMEM_BYTES = 40 * 2**20


def dot(a, b):
    return lax.dot_general(a, b, (((1,), (0,)), ((), ())), preferred_element_type=F32)


def dot_t(a, b):
    return lax.dot_general(a, b, (((1,), (1,)), ((), ())), preferred_element_type=F32)


def run(body, outs, args, scratch=(), flops=0, name=None, after=()):
    size = sum(math.prod(a.shape) * a.dtype.itemsize for a in args)
    size += sum(math.prod(s) * jnp.dtype(t).itemsize for s, t in outs)
    vmem = pl.BlockSpec(memory_space=pltpu.VMEM)
    rest = pl.BlockSpec(memory_space=pl.ANY)
    count, skip = len(args), len(args) + len(after)

    def whole(*refs):
        body(*refs[:count], *refs[skip:])

    return pl.pallas_call(
        whole,
        out_shape=[jax.ShapeDtypeStruct(s, t) for s, t in outs],
        in_specs=[vmem] * count + [rest] * len(after),
        out_specs=[vmem] * len(outs),
        scratch_shapes=list(scratch),
        compiler_params=pltpu.CompilerParams(vmem_limit_bytes=VMEM_BYTES),
        cost_estimate=pl.CostEstimate(flops=flops, bytes_accessed=size, transcendentals=0),
        name=name,
    )(*args, *after)


def gelu(v):
    return v * (0.5 * (1.0 + jnp.tanh(ROOT * (v + 0.044715 * (v * v * v)))))


def gelu_slope(v):
    tangent = jnp.tanh(ROOT * (v + 0.044715 * v * v * v))
    return 0.5 * (1.0 + tangent) + 0.5 * v * (1.0 - tangent * tangent) * ROOT * (
        1.0 + 3.0 * 0.044715 * v * v
    )


def round_up(value, step):
    return -(-value // step) * step


def pack_kv(keys, values):
    tokens, size = keys.shape
    rest = values[:, size:]
    half = tokens // 2
    tail = jnp.concatenate([rest[:half], rest[half:]], axis=1)
    return jnp.concatenate([keys, values[:, :size], tail], axis=0)


def unpack_values(packed, tokens, size):
    tail = packed[2 * tokens :]
    width = tail.shape[1] // 2
    rest = jnp.concatenate([tail[:, :width], tail[:, width:]], axis=0)
    return jnp.concatenate([packed[tokens : 2 * tokens], rest], axis=1)


def put(ref, start, rows):
    for c in range(ref.shape[0]):
        ref[c, start : start + rows.shape[0]] = rows[:, c * LANES : (c + 1) * LANES]


def every_second(ref, start, count):
    parts = [ref[c, pl.ds(start, count, stride=2)] for c in range(ref.shape[0])]
    return jnp.concatenate(parts, axis=1)


def open_kernel(x, pad, ends):
    positions, channels = x.shape
    ends[:16] = x[:16]
    ends[16:] = x[positions - 16 :]
    put(pad, 0, jnp.zeros((8, channels), F32))
    put(pad, 8, gelu(x[...].astype(F32)).astype(BF).astype(F32))
    put(pad, 8 + positions, jnp.zeros((pad.shape[1] - 8 - positions, channels), F32))


def front_kernel(ready, pair, across, weight, gain, wk, wv, kv_out, early, normed_out, pooled_out, pad):
    tokens = pooled_out.shape[0]
    ext = early.shape[0] // 2
    even = lax.axis_index("seq") % 2 == 0
    pair_wide, across_wide = pair[...].astype(F32), across[...].astype(F32)
    before = jnp.where(even, across_wide[16:], pair_wide[16:])[14:]
    after = jnp.where(even, pair_wide[:16], across_wide[:16])[:2]
    pad[...] = ready[...]
    put(pad, 6, gelu(before).astype(BF).astype(F32))
    put(pad, 8 + 2 * tokens, gelu(after).astype(BF).astype(F32))
    pieces = [every_second(pad, 6 + u, tokens).astype(BF) for u in range(6)]
    total = None
    for tap in range(5):
        rows = jnp.concatenate([pieces[tap], pieces[tap + 1]], axis=0)
        term = dot(rows, weight[tap])
        total = term if total is None else total + term
    pooled = 0.5 * (total[:tokens] + total[tokens:])
    inv = lax.rsqrt(jnp.mean(pooled * pooled, axis=-1, keepdims=True) + EPS)
    normed = (pooled * inv * gain[...]).astype(BF)
    pooled_out[...] = pooled
    normed_out[...] = normed
    kv_out[...] = pack_kv(dot(normed, wk[...]), dot_t(normed, wv[...])).astype(BF)
    early[0:ext] = every_second(pad, 6, ext).astype(BF)
    early[ext : 2 * ext] = every_second(pad, 7, ext).astype(BF)


def ordered(bits):
    masks = [0]
    for bit in reversed(bits):
        masks = masks + [mask | (1 << bit) for mask in masks]
    return masks


def split_rows(rows, columns):
    return round_up(-(-rows * LANES // columns), 16)


def query_kernel(normed, wq, early, out, near, core, own, *, order, rows, padded, scale):
    width = normed.shape[1]
    value = normed[...]
    out[...] = (dot(value, wq[...]) * scale).astype(BF)
    ext, channels = early.shape
    near[:ext] = early[...]
    core[:ext] = early[...]
    count = len(order) * padded
    step = split_rows(count, channels)
    for i in range(4):
        block_of = place(i)
        pick = [chosen(rows, padded, width, block_of(k)) for k in order]
        part = dot_t(jnp.concatenate(pick, axis=0), value).astype(BF)
        if i == 0:
            own[...] = part
            continue
        message, at = ((core, ext), (near, ext), (near, ext + step))[i - 1]
        for c in range(channels // LANES):
            piece = part[c * step : min((c + 1) * step, count)]
            message[at : at + piece.shape[0], c * LANES : (c + 1) * LANES] = piece


def by_eight(rows):
    return rows.reshape(rows.shape[0] // 8, 8, rows.shape[1])


def attend_kernel(*refs, blocks, masks, heads, key_size, value_size, scale):
    q, cot = refs[:2]
    parts = refs[2 : 2 + blocks]
    att, dq, keep_a, send_a, keep_b, send_b = refs[2 + blocks : 8 + blocks]
    ks, vs, kt, vt, qs, cs, weights, score_cots, scores, prob_cots = refs[8 + blocks :]
    tokens = q.shape[0]
    half = tokens // 2
    wide = value_size - key_size
    for i, part in enumerate(parts):
        at = i * tokens
        ks[at : at + tokens] = part[:tokens]
        vs[at : at + tokens, :key_size] = part[tokens : 2 * tokens]
        vs[at : at + half, key_size:] = part[2 * tokens :, :wide]
        vs[at + half : at + tokens, key_size:] = part[2 * tokens :, wide:]
        kt[:, at : at + tokens] = ks[at : at + tokens].astype(F32).T.astype(BF)
        vt[:, at : at + tokens] = vs[at : at + tokens].astype(F32).T.astype(BF)
    slots = scores.shape[0]
    parts_of = [slice(i * tokens, (i + 1) * tokens) for i in range(blocks)]

    def products(pair):
        ql, cl = 2 * pair * key_size, 2 * pair * value_size
        rows = slice(2 * pair * tokens, 2 * (pair + 1) * tokens)
        both = cot[:, cl : cl + 2 * value_size]
        qs[rows] = jnp.concatenate(
            [q[:, ql : ql + key_size], q[:, ql + key_size : ql + 2 * key_size]], axis=0
        )
        cs[rows] = jnp.concatenate([both[:, :value_size], both[:, value_size:]], axis=0)
        scores[pair % slots] = dot_t(ks[...], qs[rows])
        prob_cots[pair % slots] = dot_t(vs[...], cs[rows])

    products(0)
    for pair in range(heads // 2):
        ql, cl = 2 * pair * key_size, 2 * pair * value_size
        rows = slice(2 * pair * tokens, 2 * (pair + 1) * tokens)
        slot = pair % slots
        if slots > 1 and pair + 1 < heads // 2:
            products(pair + 1)
        top = functools.reduce(jnp.maximum, [by_eight(scores[slot, at]).max(0) for at in parts_of])
        top = jnp.max(top, axis=0, keepdims=True)
        sums = 0.0
        for at in parts_of:
            raised = jnp.exp(scores[slot, at] - top)
            sums = sums + by_eight(raised).sum(0)
            scores[slot, at] = raised
        inverse = 1.0 / jnp.sum(sums, axis=0, keepdims=True)
        for at in parts_of:
            weights[at, rows] = (scores[slot, at] * inverse).astype(BF)
        out_t = dot(vt[...], weights[:, rows]).astype(BF).astype(F32)
        delta = jnp.sum(cs[rows].astype(F32).T * out_t, axis=0, keepdims=True)
        for at in parts_of:
            probs = scores[slot, at] * inverse
            score_cots[at, rows] = (probs * (prob_cots[slot, at] - delta)).astype(BF)
        if slots == 1 and pair + 1 < heads // 2:
            products(pair + 1)
        dq_t = dot(kt[...], score_cots[:, rows]) * scale
        out_rows = jnp.concatenate([out_t[:, :tokens].T, out_t[:, tokens:].T], axis=1)
        att[:, cl : cl + 2 * value_size] = out_rows.astype(BF)
        dq_rows = jnp.concatenate([dq_t[:, :tokens].T, dq_t[:, tokens:].T], axis=1)
        dq[:, ql : ql + 2 * key_size] = dq_rows.astype(BF)
    key_cots, value_cots = dot(score_cots[...], qs[...]), dot(weights[...], cs[...])
    edge = keep_a.shape[1]
    count = blocks // 2
    for i in range(blocks):
        at = slice(i * tokens, (i + 1) * tokens)
        packed = pack_kv(key_cots[at], value_cots[at])
        for order, keep, send, part in (
            (masks[0], keep_a, send_a, packed[:edge]),
            (masks[1], keep_b, send_b, packed[edge:]),
        ):
            k = order.index(i)
            if k < count:
                keep[k] = part
            else:
                send[k - count] = part.astype(BF)


def total_of(parts):
    total = parts[0][...]
    for part in parts[1:]:
        total = total + part[...].astype(F32)
    return total


def fold_kernel(*refs):
    keep, send = refs[-2:]
    total = total_of(refs[:-2])
    keep[...] = total[: keep.shape[0]]
    send[...] = total[keep.shape[0] :].astype(BF)


def fold_two_kernel(*refs):
    fold_kernel(refs[0], refs[1], refs[4], refs[5])
    fold_kernel(refs[2], refs[3], refs[6], refs[7])


def merge_kernel(keep_a, in_a, keep_b, in_b, keep, send):
    total = jnp.concatenate([total_of((keep_a, in_a)), total_of((keep_b, in_b))], axis=1)
    keep[...] = total[: keep.shape[0]]
    send[...] = total[keep.shape[0] :].astype(BF)


def send_on_kernel(keep, came, out):
    out[...] = (keep[...] + came[...].astype(F32)).astype(BF)


def query_cot_kernel(dq, wq, out):
    out[...] = dot_t(dq[...], wq[...])


def middle_kernel(own, came, part, pooled_in, gain_in, wk, wv, first, second, *edges):
    size = own.shape[2]
    tokens, width = pooled_in.shape
    total = (own[0] + came[0].astype(F32)).astype(BF).astype(F32)
    key_cot = total[:tokens]
    value_cot = unpack_values(total, tokens, size)
    normed_cot = part[...] + dot_t(key_cot.astype(BF), wk[...])
    normed_cot = normed_cot + dot(value_cot.astype(BF), wv[...])
    pooled, gain = pooled_in[...], gain_in[...]
    inv = lax.rsqrt(jnp.mean(pooled * pooled, axis=-1, keepdims=True) + EPS)
    gain_term = jnp.sum(normed_cot * pooled * inv, axis=0, keepdims=True)
    gained = gain * normed_cot
    pooled_cot = inv * gained - pooled * (inv * inv * inv) * (
        jnp.sum(gained * pooled, axis=-1, keepdims=True) / width
    )
    conv_cot = 0.5 * pooled_cot
    high = gain_term.astype(BF).astype(F32)
    low = gain_term - high
    row = lax.broadcasted_iota(jnp.int32, (16, width), 0)
    split = width // 2
    lines = (high[:, :split], low[:, :split], high[:, split:], low[:, split:])
    lines += (conv_cot[:1, split:], conv_cot[tokens - 1 :, split:])
    gains = jnp.zeros((16, split), F32)
    for i, line in enumerate(lines):
        gains = jnp.where(row[:, :split] == i, line, gains)
    fill = split - size - value_cot.shape[1]
    side = jnp.concatenate([key_cot, value_cot, jnp.zeros((tokens, fill), F32)], axis=1)
    first[:tokens] = conv_cot[:, :split].astype(BF)
    first[tokens:] = gains.astype(BF)
    second[:tokens] = conv_cot[:, split:].astype(BF)
    second[tokens:] = side.astype(BF)
    for edge in edges:
        ends = jnp.where(row == 0, conv_cot[:1], jnp.where(row == 1, conv_cot[tokens - 1 :], 0.0))
        edge[...] = ends.astype(BF)


def place(other=0):
    seq, dp = lax.axis_index("seq"), lax.axis_index("dp") ^ (other % 2)
    high, low = seq // 2, (seq % 2) ^ (other // 2)
    return lambda k: ((high ^ k) * 2 + low) * 2 + dp


def chosen(rows, padded, columns, block):
    row = lax.broadcasted_iota(jnp.int32, (padded, columns), 0)
    column = lax.broadcasted_iota(jnp.int32, (padded, columns), 1)
    hit = (column == row + block * rows) & (row < rows)
    return jnp.where(hit, 1.0, 0.0).astype(BF)


def select_kernel(*refs, order, rows, padded):
    own, blocks = refs[0], refs[1:5]
    out, norm_out, even, odd = refs[5:]
    ext, channels = even.shape
    tokens = own.shape[1]
    count = own.shape[0]
    step = split_rows(count, channels)
    norm_out[:, :tokens] = own[...]
    for i in range(1, 4):
        at = 2 * ext + (i // 3) * step
        for c in range(channels // LANES):
            end = min((c + 1) * step, count)
            piece = blocks[i][at : at + end - c * step, c * LANES : (c + 1) * LANES]
            norm_out[c * step : end, i * tokens : (i + 1) * tokens] = piece
    block_of = place()
    pick = jnp.concatenate(
        [chosen(rows, padded, 5 * channels, block_of(k)) for k in order], axis=0
    )
    for i, block in enumerate(blocks):
        even[...] = block[:ext].astype(F32)
        odd[...] = block[ext : 2 * ext].astype(F32)
        pieces = []
        for shift in range(3):
            pieces += [even[shift : shift + tokens].astype(BF), odd[shift : shift + tokens].astype(BF)]
        shifted = jnp.concatenate(
            [jnp.concatenate(pieces[:5], axis=1), jnp.concatenate(pieces[1:], axis=1)], axis=0
        )
        out[:, 2 * i * tokens : 2 * (i + 1) * tokens] = dot_t(pick, shifted).astype(BF)


def query_grad_kernel(pick, first, second, third, fourth, keep, send, right):
    tokens = first.shape[0]
    for i, block in enumerate((first, second, third, fourth)):
        right[i * tokens : (i + 1) * tokens] = block[...]
    count, pad = keep.shape[:2]
    for k in range(2 * count):
        term = dot(pick[k * pad : (k + 1) * pad], right[...])
        if k < count:
            keep[k] = term
        else:
            send[k - count] = term.astype(BF)


def side_rows(norm_rows, size, width):
    return norm_rows * size // width


def put_side(stage, at, part, rows):
    pieces = [part[i : i + rows] for i in range(0, part.shape[0], rows)]
    stage[at : at + rows] = jnp.concatenate(pieces, axis=1)


def get_side(packed, part, rows):
    size = part.shape[1]
    for i in range(part.shape[0] // rows):
        part[i * rows : (i + 1) * rows] = packed[:, i * size : (i + 1) * size]


def stack_cots(blocks, right, tokens):
    for i, block in enumerate(blocks):
        piece = block[:tokens]
        right[2 * i * tokens : (2 * i + 1) * tokens] = piece
        right[(2 * i + 1) * tokens : (2 * i + 2) * tokens] = piece


def conv_first_kernel(*refs, conv_rows, conv_pad):
    pick, blocks, outs, right, stage = refs[0], refs[1:5], refs[5:9], refs[9], refs[10]
    tokens = right.shape[0] // 8
    stack_cots(blocks, right, tokens)
    stage[...] = jnp.zeros(stage.shape, F32)
    for half in range(2):
        gain = None
        for block in blocks:
            lines = block[tokens : tokens + 16].astype(F32)[2 * half : 2 * half + 2]
            term = lines[0:1] + lines[1:2]
            gain = term if gain is None else gain + term
        high = gain.astype(BF).astype(F32)
        at = conv_rows + 2 * half
        stage[at : at + 1] = high
        stage[at + 1 : at + 2] = gain - high
    count, above = outs[0].shape[:2]
    even = lax.axis_index("seq") % 2 == 0
    own, pair = blocks[0], blocks[2]
    tops = [b[0:16].astype(F32)[0:1] for b in (own, pair)]
    bottoms = [b[tokens - 16 : tokens].astype(F32)[15:16] for b in (own, pair)]
    rests = [b[tokens : tokens + 16].astype(F32)[4:6] for b in (own, pair)]
    for k in range(4 * count):
        conv = dot(pick[k * conv_pad : (k + 1) * conv_pad], right[...])
        stage[:conv_rows] = conv[:conv_rows]
        if k == 3 * count:
            stage[above - 4 : above - 3] = jnp.where(even, tops[0], tops[1])
            stage[above - 3 : above - 2] = jnp.where(even, rests[0][0:1], rests[1][0:1])
            stage[above - 2 : above - 1] = jnp.where(even, bottoms[1], bottoms[0])
            stage[above - 1 : above] = jnp.where(even, rests[1][1:2], rests[0][1:2])
        out = outs[k // count]
        out[k % count] = stage[...].astype(out.dtype)


def conv_second_kernel(*refs, conv_rows, conv_pad, norm_rows, norm_pad, key_size, value_size):
    pick, norm_pick, blocks, first_send = refs[0], refs[1], refs[2:6], refs[6]
    near_keep, far_keep, near_send, far_send, right, side, stage = refs[7:]
    tokens, width = right.shape[0] // 8, right.shape[1]
    stack_cots(blocks, right, tokens)
    for i, block in enumerate(blocks):
        side[i * tokens : (i + 1) * tokens] = block[tokens:]
    key_rows = side_rows(norm_rows, key_size, width)
    value_rows = side_rows(norm_rows, value_size, width)
    stage[...] = jnp.zeros(stage.shape, F32)
    count, above = first_send.shape[:2]
    near_send[:, :above] = first_send[...]
    for k in range(4 * count):
        conv = dot(pick[k * conv_pad : (k + 1) * conv_pad], right[...])
        stage[:conv_rows] = conv[:conv_rows]
        both = dot(norm_pick[k * norm_pad : (k + 1) * norm_pad], side[...])
        put_side(stage, conv_rows, both[:norm_rows, :key_size], key_rows)
        value = both[:norm_rows, key_size : key_size + value_size]
        put_side(stage, conv_rows + key_rows, value, value_rows)
        if k < 2 * count:
            (near_keep, far_keep)[k // count][k % count] = stage[...]
        elif k < 3 * count:
            near_send[k % count, above:] = stage[...].astype(BF)
        else:
            far_send[k % count] = stage[...].astype(BF)


def first_sum_kernel(keep, near, far, out):
    above = keep.shape[1]
    out[...] = keep[...] + near[:, :above].astype(F32) + far[...].astype(F32)


def combine_kernel(first, second, near, far, out):
    above = first.shape[1]
    out[:, :above] = first[...]
    out[:, above:] = second[...] + near[:, above:].astype(F32) + far[...].astype(F32)


def final_kernel(*refs, conv_parts, above):
    conv, query, key, value, gain, stage = refs[-6:]
    rows, width = conv.shape
    split = width // 2
    count = key.shape[0]
    if conv_parts == 4:
        combine_kernel(*refs[:4], stage)
    else:
        stage[...] = total_of(refs[:conv_parts])
    query[...] = total_of(refs[conv_parts:-6])[0, : query.shape[0]]
    conv[:, :split] = stage[0, :rows]
    conv[:, split:] = stage[0, above : above + rows]
    at = above + rows
    for part in (key, value):
        step = side_rows(count, part.shape[1], split)
        get_side(stage[0, at : at + step], part, step)
        at += step
    lines = stage[0, rows : rows + 4]
    line = jnp.concatenate([lines[0:1] + lines[1:2], lines[2:3] + lines[3:4]], axis=1)
    line = jnp.broadcast_to(line, (8, width))
    start = place()(0) * count
    gain[...] = pltpu.roll(line, lax.rem(width - start, width), 1)[:1, :count]


def input_kernel(*refs):
    x, first, second, pair_first, pair_second, one, three, weight, out, ext, mixed = refs
    tokens = x.shape[0] // 2
    seq, devices = lax.axis_index("seq"), lax.axis_size("seq")
    low, high = seq % 2, seq // 2
    split = first.shape[1]
    above = one.shape[1]
    one_rows = one[0, above - 16 :].astype(F32)[12:]
    three_rows = three[0, above - 16 :].astype(F32)[12:]
    heads = jnp.where(high % 2 == 0, one_rows[:2], three_rows[:2])
    tails = jnp.where(high % 2 == 0, three_rows[2:], one_rows[2:])
    heads = jnp.where(seq == devices - 1, 0.0, heads)
    tails = jnp.where(seq == 0, 0.0, tails)
    for half, own, pair in ((0, first, pair_first), (1, second, pair_second)):
        lanes = slice(half * split, (half + 1) * split)
        top = pair[0:16].astype(F32)[0:1]
        bottom = pair[tokens - 16 : tokens].astype(F32)[15:16]
        ext[8 : 8 + tokens, lanes] = own[:tokens].astype(F32)
        ext[7:8, lanes] = jnp.where(low == 0, tails[half : half + 1], bottom)
        ext[8 + tokens : 9 + tokens, lanes] = jnp.where(low == 0, top, heads[half : half + 1])
    back = ext[7 : 7 + tokens].astype(BF)
    here = ext[8 : 8 + tokens].astype(BF)
    ahead = ext[9 : 9 + tokens].astype(BF)
    evens = (ahead, here, here, back, back)
    odds = (ahead, ahead, here, here, back)
    total = None
    for tap in range(5):
        term = dot_t(jnp.concatenate([evens[tap], odds[tap]], axis=0), weight[tap])
        total = term if total is None else total + term
    for c in range(mixed.shape[0]):
        lanes = slice(c * LANES, (c + 1) * LANES)
        mixed[c, pl.ds(0, tokens, stride=2)] = total[:tokens, lanes]
        mixed[c, pl.ds(1, tokens, stride=2)] = total[tokens:, lanes]
        out[:, lanes] = (mixed[c] * gelu_slope(x[:, lanes].astype(F32))).astype(BF)


def on_device(x, conv_weight, norm_gain, wq, wk, wv, cotangent):
    devices = lax.axis_size("seq")
    both_axes = ("seq", "dp")
    x, cotangent = x[0], cotangent[0]
    positions, channels = x.shape
    tokens = positions // 2
    taps, _, width = conv_weight.shape
    key_size, value_size = wk.shape[1], wv.shape[1]
    heads = cotangent.shape[1] // value_size
    scale = key_size ** (-0.5)
    groups = devices // 2
    owners = devices * 2
    conv_rows, norm_rows = taps * channels // owners, width // owners
    conv_pad, norm_pad = round_up(conv_rows, 16), round_up(norm_rows, 16)
    ext = tokens + 16
    gain = norm_gain.reshape(1, width)

    def swap(value, seq_bits, dp_bit=0):
        mask = 2 * seq_bits + dp_bit
        return lax.ppermute(value, both_axes, [(i, i ^ mask) for i in range(owners)])

    def held(value, *until):
        return lax.optimization_barrier((value,) + until)[0]

    def quad(value, *until):
        core = swap(value, 0, 1)
        near = swap(value, 1)
        return [value, core, near, swap(held(near, *until), 0, 1)]

    def fold(parts, name):
        shape = (parts[0].shape[0] // 2,) + parts[0].shape[1:]
        return run(fold_kernel, [(shape, F32), (shape, BF)], parts, name=name)

    def halved(keep, send, bits, name):
        for bit in bits[:-1]:
            keep, send = fold([keep, swap(send, 1 << bit)], name)
        return [keep, swap(send, 1 << bits[-1])]

    bits = list(range(devices.bit_length() - 1))
    order = [mask // 2 for mask in ordered(bits[1:])]
    crossing = [(i, i + 1) for i in range(1, devices - 1, 2)]
    crossing = crossing + [(j, i) for i, j in crossing]
    pad_shape = (channels // LANES, 8 + 2 * ext + 8, LANES)
    ready, ends = run(
        open_kernel,
        [(pad_shape, F32), ((32, channels), BF)],
        [x],
        flops=4 * 10**9,
        name="gelu",
    )
    pair, across = swap(ends, 1), lax.ppermute(ends, "seq", crossing)
    wv = wv.T
    kv, early, normed, pooled = run(
        front_kernel,
        [
            ((5 * tokens // 2, key_size), BF),
            ((2 * ext, channels), BF),
            ((tokens, width), BF),
            ((tokens, width), F32),
        ],
        [ready, pair, across, conv_weight, gain, wk, wv],
        [pltpu.VMEM(pad_shape, F32)],
        flops=2 * positions * taps * channels * width,
        name="front",
    )
    parts = [0, *range(2, groups), 1]
    near_kv = [swap(kv, 2 * k) if k else kv for k in parts]
    far_kv = [swap(block, 1) for block in near_kv]
    picked = (groups * norm_pad, tokens)
    rows = split_rows(picked[0], channels)
    queries, to_near, to_core, pick_own = run(
        lambda *refs: query_kernel(
            *refs, order=order, rows=norm_rows, padded=norm_pad, scale=scale
        ),
        [
            ((tokens, heads * key_size), BF),
            ((2 * ext + 2 * rows, channels), BF),
            ((2 * ext + rows, channels), BF),
            (picked, BF),
        ],
        [normed, wq, early],
        flops=4 * tokens * width * heads * key_size,
        name="queries",
        after=near_kv[1:],
    )
    to_near, to_core = held(to_near, *far_kv), held(to_core, *far_kv)
    length = devices * tokens
    masks = [2 * k for k in parts] + [2 * k + 1 for k in parts]
    half_block = (groups, 5 * tokens // 4, key_size)
    slots = 2 if length <= 2048 else 1
    attended, query_cot, keep_a, send_a, keep_b, send_b = run(
        lambda *refs: attend_kernel(
            *refs,
            blocks=devices,
            masks=[
                [masks.index(m) for m in ordered(way)] for way in (bits, [1, 0] + bits[2:])
            ],
            heads=heads,
            key_size=key_size,
            value_size=value_size,
            scale=scale,
        ),
        [((tokens, heads * value_size), BF), ((tokens, heads * key_size), BF)]
        + [(half_block, F32), (half_block, BF)] * 2,
        [queries, cotangent] + near_kv + far_kv,
        [
            pltpu.VMEM((length, key_size), BF),
            pltpu.VMEM((length, value_size), BF),
            pltpu.VMEM((key_size, length), BF),
            pltpu.VMEM((value_size, length), BF),
            pltpu.VMEM((heads * tokens, key_size), BF),
            pltpu.VMEM((heads * tokens, value_size), BF),
            pltpu.VMEM((length, heads * tokens), BF),
            pltpu.VMEM((length, heads * tokens), BF),
            pltpu.VMEM((slots, length, 2 * tokens), F32),
            pltpu.VMEM((slots, length, 2 * tokens), F32),
        ],
        flops=6 * tokens * heads * length * (key_size + value_size),
        name="attend",
    )
    in_a, in_b = swap(send_a, 1), swap(send_b, 2)
    early_near = swap(to_near, 1)
    (normed_cot,) = run(
        query_cot_kernel,
        [((tokens, width), F32)],
        [query_cot, wq],
        flops=2 * tokens * width * heads * key_size,
        name="query_part",
    )
    fourth = (groups // 2,) + half_block[1:]
    keep_a, send_a, keep_b, send_b = run(
        fold_two_kernel,
        [(fourth, F32), (fourth, BF)] * 2,
        [keep_a, in_a, keep_b, in_b],
        name="kv_cot_fold",
        after=[normed_cot],
    )
    early_core, early_last = swap(held(to_core, keep_a), 0, 1), swap(held(early_near, keep_a), 0, 1)
    early_blocks = [early, early_core, early_near, early_last]
    in_a, in_b = swap(send_a, 2), swap(send_b, 1)
    block = (groups // 4, 5 * tokens // 2, key_size)
    keep, send = run(
        merge_kernel,
        [(block, F32), (block, BF)],
        [keep_a, in_a, keep_b, in_b],
        name="kv_cot_merge",
    )
    conv_pick, norm_pick = run(
        lambda *refs: select_kernel(*refs, order=order, rows=conv_rows, padded=conv_pad),
        [((groups * conv_pad, 8 * tokens), BF), ((groups * norm_pad, 4 * tokens), BF)],
        [held(pick_own, keep)] + early_blocks,
        [pltpu.VMEM((ext, channels), F32), pltpu.VMEM((ext, channels), F32)],
        flops=2 * groups * conv_pad * taps * channels * 8 * tokens,
        name="select",
    )
    query_cot = held(query_cot, keep)
    query_near, query_core = swap(query_cot, 1), swap(query_cot, 0, 1)
    kv_cot = halved(keep, send, bits[2:], "kv_cot_fold")
    first, second, *edge = run(
        middle_kernel,
        [
            ((tokens + 16, width // 2), BF),
            ((2 * tokens, width // 2), BF),
        ]
        + [((16, width), BF)] * (len(bits) > 3),
        kv_cot + [normed_cot, held(pooled, conv_pick), gain, wk, wv],
        flops=2 * tokens * width * (key_size + value_size),
        name="conv_cot",
    )
    near_first, near_second = swap(first, 1), swap(second, 1)
    query_last = swap(held(query_near, first), 0, 1)
    query_half = (groups // 2, norm_pad, heads * key_size)
    query_keep, query_send = run(
        query_grad_kernel,
        [(query_half, F32), (query_half, BF)],
        [norm_pick, query_cot, query_core, query_near, query_last],
        [pltpu.VMEM((4 * tokens, heads * key_size), BF)],
        flops=2 * groups * norm_pad * 4 * tokens * heads * key_size,
        name="query_grad",
    )
    query_parts = halved(query_keep, query_send, bits[1:], "query_fold")
    core_first, core_second = swap(first, 0, 1), swap(second, 0, 1)
    split = width // 2
    side = side_rows(norm_rows, key_size, split) + side_rows(norm_rows, value_size, split)
    above, below = round_up(conv_rows + 8, 16), round_up(conv_rows + side, 16)
    count = groups // 4
    last_first = swap(held(near_first, query_keep), 0, 1)
    near_keep, far_keep, near_send, far_send = run(
        lambda *refs: conv_first_kernel(*refs, conv_rows=conv_rows, conv_pad=conv_pad),
        [((count, above, split), t) for t in (F32, F32, BF, BF)],
        [conv_pick, first, core_first, near_first, last_first],
        [pltpu.VMEM((8 * tokens, split), BF), pltpu.VMEM((above, split), F32)],
        flops=groups * conv_pad * 8 * tokens * width,
        name="conv_grad_first",
    )
    far_in = swap(far_send, 2)
    last_second = swap(held(near_second, near_keep, query_parts[0]), 0, 1)
    near_keep_second, far_keep_second, near_send, far_send = run(
        lambda *refs: conv_second_kernel(
            *refs,
            conv_rows=conv_rows,
            conv_pad=conv_pad,
            norm_rows=norm_rows,
            norm_pad=norm_pad,
            key_size=key_size,
            value_size=value_size,
        ),
        [
            ((count, below, split), F32),
            ((count, below, split), F32),
            ((count, above + below, split), BF),
            ((count, below, split), BF),
        ],
        [conv_pick, norm_pick, second, core_second, near_second, last_second, near_send],
        [
            pltpu.VMEM((8 * tokens, split), BF),
            pltpu.VMEM((4 * tokens, split), BF),
            pltpu.VMEM((below, split), F32),
        ],
        flops=groups * conv_pad * 8 * tokens * width,
        name="conv_grad_second",
    )
    far_in_second = swap(far_send, 2)
    near_in = swap(near_send, 2)
    (far_sum,) = run(
        send_on_kernel,
        [((count, above, split), BF)],
        [far_keep, far_in],
        name="conv_send_on",
    )
    far_last = swap(far_sum, 4)
    (far_sum,) = run(
        send_on_kernel,
        [((count, below, split), BF)],
        [far_keep_second, far_in_second],
        name="conv_send_on",
    )
    edges = [far_in, far_last]
    if len(bits) > 3:
        came = lax.ppermute(edge[0], "seq", crossing)
        rows = jnp.concatenate([came[:1, :split], came[:1, split:], came[1:2, :split], came[1:2, split:]])
        edges = [jnp.pad(rows, ((above - 4, 0), (0, 0)))[None]] * 2
    (input_grad,) = run(
        input_kernel,
        [((positions, channels), BF)],
        [held(x, far_sum, query_parts[1]), first, second, near_first, near_second] + edges + [conv_weight],
        [
            pltpu.VMEM((tokens + 16, width), F32),
            pltpu.VMEM((channels // LANES, positions, LANES), F32),
        ],
        flops=20 * positions * taps * channels * width,
        name="input_grad",
    )
    (first_sum,) = run(
        first_sum_kernel,
        [((count, above, split), F32)],
        [near_keep, near_in, far_last],
        flops=5 * 10**9,
        name="conv_first_sum",
    )
    conv_parts = [first_sum, near_keep_second, near_in, swap(far_sum, 4)]
    chunk = (count, above + below, split)
    if len(bits) > 3:
        keep = run(combine_kernel, [(chunk, F32)], conv_parts, name="conv_combine")[0]
        half = (count // 2,) + chunk[1:]
        keep, send = run(fold_kernel, [(half, F32), (half, BF)], [keep], name="conv_fold")
        conv_parts = halved(keep, send, bits[3:], "conv_fold")
    conv_grad, query_grad, key_grad, value_grad, gain_grad = run(
        lambda *refs: final_kernel(*refs, conv_parts=len(conv_parts), above=above),
        [
            ((conv_rows, width), F32),
            ((norm_rows, heads * key_size), F32),
            ((norm_rows, key_size), F32),
            ((norm_rows, value_size), F32),
            ((1, norm_rows), F32),
        ],
        conv_parts + query_parts,
        [pltpu.VMEM((1,) + chunk[1:], F32)],
        name="final_sum",
    )
    return (
        attended[None],
        input_grad[None],
        conv_grad,
        query_grad,
        key_grad,
        value_grad,
        gain_grad.reshape(norm_rows),
    )


def solution(mesh):
    placed = (
        P(("groups", "dp"), "seq", None),
        P(),
        P(),
        P(),
        P(),
        P(),
        P(("groups", "dp"), "seq", None),
    )
    return jax.shard_map(
        on_device,
        mesh=mesh,
        in_specs=placed,
        out_specs=(
            P(("groups", "dp"), "seq", None),
            P(("groups", "dp"), "seq", None),
            P(("groups", "seq", "dp"), None),
            P(("groups", "seq", "dp"), None),
            P(("groups", "seq", "dp"), None),
            P(("groups", "seq", "dp"), None),
            P(("groups", "seq", "dp")),
        ),
        check_vma=False,
    )
```

```python
import functools
import math

import jax
import jax.numpy as jnp
from jax import lax
from jax.experimental import pallas as pl
from jax.experimental.pallas import tpu as pltpu
from jax.sharding import PartitionSpec as P

BF = jnp.bfloat16
F32 = jnp.float32
ROOT = math.sqrt(2.0 / math.pi)
EPS = 1e-06
LANES = 128
VMEM_BYTES = 40 * 2**20


def dot(a, b):
    return lax.dot_general(a, b, (((1,), (0,)), ((), ())), preferred_element_type=F32)


def dot_t(a, b):
    return lax.dot_general(a, b, (((1,), (1,)), ((), ())), preferred_element_type=F32)


def run(body, outs, args, scratch=(), flops=0, name=None, after=()):
    size = sum(math.prod(a.shape) * a.dtype.itemsize for a in args)
    size += sum(math.prod(s) * jnp.dtype(t).itemsize for s, t in outs)
    vmem = pl.BlockSpec(memory_space=pltpu.VMEM)
    rest = pl.BlockSpec(memory_space=pl.ANY)
    count, skip = len(args), len(args) + len(after)

    def whole(*refs):
        body(*refs[:count], *refs[skip:])

    return pl.pallas_call(
        whole,
        out_shape=[jax.ShapeDtypeStruct(s, t) for s, t in outs],
        in_specs=[vmem] * count + [rest] * len(after),
        out_specs=[vmem] * len(outs),
        scratch_shapes=list(scratch),
        compiler_params=pltpu.CompilerParams(vmem_limit_bytes=VMEM_BYTES),
        cost_estimate=pl.CostEstimate(flops=flops, bytes_accessed=size, transcendentals=0),
        name=name,
    )(*args, *after)


def gelu(v):
    return v * (0.5 * (1.0 + jnp.tanh(ROOT * (v + 0.044715 * (v * v * v)))))


def gelu_slope(v):
    tangent = jnp.tanh(ROOT * (v + 0.044715 * v * v * v))
    return 0.5 * (1.0 + tangent) + 0.5 * v * (1.0 - tangent * tangent) * ROOT * (
        1.0 + 3.0 * 0.044715 * v * v
    )


def round_up(value, step):
    return -(-value // step) * step


def pack_kv(keys, values):
    tokens, size = keys.shape
    rest = values[:, size:]
    half = tokens // 2
    tail = jnp.concatenate([rest[:half], rest[half:]], axis=1)
    return jnp.concatenate([keys, values[:, :size], tail], axis=0)


def unpack_values(packed, tokens, size):
    tail = packed[2 * tokens :]
    width = tail.shape[1] // 2
    rest = jnp.concatenate([tail[:, :width], tail[:, width:]], axis=0)
    return jnp.concatenate([packed[tokens : 2 * tokens], rest], axis=1)


def put(ref, start, rows):
    for c in range(ref.shape[0]):
        ref[c, start : start + rows.shape[0]] = rows[:, c * LANES : (c + 1) * LANES]


def every_second(ref, start, count):
    parts = [ref[c, pl.ds(start, count, stride=2)] for c in range(ref.shape[0])]
    return jnp.concatenate(parts, axis=1)


def open_kernel(x, pad, ends):
    positions, channels = x.shape
    ends[:16] = x[:16]
    ends[16:] = x[positions - 16 :]
    put(pad, 0, jnp.zeros((8, channels), F32))
    put(pad, 8, gelu(x[...].astype(F32)).astype(BF).astype(F32))
    put(pad, 8 + positions, jnp.zeros((pad.shape[1] - 8 - positions, channels), F32))


def front_kernel(ready, pair, across, weight, gain, wk, wv, kv_out, early, normed_out, pooled_out, pad):
    tokens = pooled_out.shape[0]
    ext = early.shape[0] // 2
    even = lax.axis_index("seq") % 2 == 0
    pair_wide, across_wide = pair[...].astype(F32), across[...].astype(F32)
    before = jnp.where(even, across_wide[16:], pair_wide[16:])[14:]
    after = jnp.where(even, pair_wide[:16], across_wide[:16])[:2]
    pad[...] = ready[...]
    put(pad, 6, gelu(before).astype(BF).astype(F32))
    put(pad, 8 + 2 * tokens, gelu(after).astype(BF).astype(F32))
    pieces = [every_second(pad, 6 + u, tokens).astype(BF) for u in range(6)]
    total = None
    for tap in range(5):
        rows = jnp.concatenate([pieces[tap], pieces[tap + 1]], axis=0)
        term = dot(rows, weight[tap])
        total = term if total is None else total + term
    pooled = 0.5 * (total[:tokens] + total[tokens:])
    inv = lax.rsqrt(jnp.mean(pooled * pooled, axis=-1, keepdims=True) + EPS)
    normed = (pooled * inv * gain[...]).astype(BF)
    pooled_out[...] = pooled
    normed_out[...] = normed
    kv_out[...] = pack_kv(dot(normed, wk[...]), dot_t(normed, wv[...])).astype(BF)
    early[0:ext] = every_second(pad, 6, ext).astype(BF)
    early[ext : 2 * ext] = every_second(pad, 7, ext).astype(BF)


def ordered(bits):
    masks = [0]
    for bit in reversed(bits):
        masks = masks + [mask | (1 << bit) for mask in masks]
    return masks


def split_rows(rows, columns):
    return round_up(-(-rows * LANES // columns), 16)


def query_kernel(normed, wq, early, out, near, core, own, *, order, rows, padded, scale):
    width = normed.shape[1]
    value = normed[...]
    out[...] = (dot(value, wq[...]) * scale).astype(BF)
    ext, channels = early.shape
    near[:ext] = early[...]
    core[:ext] = early[...]
    count = len(order) * padded
    step = split_rows(count, channels)
    for i in range(4):
        block_of = place(i)
        pick = [chosen(rows, padded, width, block_of(k)) for k in order]
        part = dot_t(jnp.concatenate(pick, axis=0), value).astype(BF)
        if i == 0:
            own[...] = part
            continue
        message, at = ((core, ext), (near, ext), (near, ext + step))[i - 1]
        for c in range(channels // LANES):
            piece = part[c * step : min((c + 1) * step, count)]
            message[at : at + piece.shape[0], c * LANES : (c + 1) * LANES] = piece


def by_eight(rows):
    return rows.reshape(rows.shape[0] // 8, 8, rows.shape[1])


def attend_kernel(*refs, blocks, masks, heads, key_size, value_size, scale):
    q, cot = refs[:2]
    parts = refs[2 : 2 + blocks]
    att, dq, keep_a, send_a, keep_b, send_b = refs[2 + blocks : 8 + blocks]
    ks, vs, kt, vt, qs, cs, weights, score_cots, scores, prob_cots = refs[8 + blocks :]
    tokens = q.shape[0]
    half = tokens // 2
    wide = value_size - key_size
    for i, part in enumerate(parts):
        at = i * tokens
        ks[at : at + tokens] = part[:tokens]
        vs[at : at + tokens, :key_size] = part[tokens : 2 * tokens]
        vs[at : at + half, key_size:] = part[2 * tokens :, :wide]
        vs[at + half : at + tokens, key_size:] = part[2 * tokens :, wide:]
        kt[:, at : at + tokens] = ks[at : at + tokens].astype(F32).T.astype(BF)
        vt[:, at : at + tokens] = vs[at : at + tokens].astype(F32).T.astype(BF)
    slots = scores.shape[0]
    parts_of = [slice(i * tokens, (i + 1) * tokens) for i in range(blocks)]

    def products(pair):
        ql, cl = 2 * pair * key_size, 2 * pair * value_size
        rows = slice(2 * pair * tokens, 2 * (pair + 1) * tokens)
        both = cot[:, cl : cl + 2 * value_size]
        qs[rows] = jnp.concatenate(
            [q[:, ql : ql + key_size], q[:, ql + key_size : ql + 2 * key_size]], axis=0
        )
        cs[rows] = jnp.concatenate([both[:, :value_size], both[:, value_size:]], axis=0)
        scores[pair % slots] = dot_t(ks[...], qs[rows])
        prob_cots[pair % slots] = dot_t(vs[...], cs[rows])

    products(0)
    for pair in range(heads // 2):
        ql, cl = 2 * pair * key_size, 2 * pair * value_size
        rows = slice(2 * pair * tokens, 2 * (pair + 1) * tokens)
        slot = pair % slots
        if slots > 1 and pair + 1 < heads // 2:
            products(pair + 1)
        top = functools.reduce(jnp.maximum, [by_eight(scores[slot, at]).max(0) for at in parts_of])
        top = jnp.max(top, axis=0, keepdims=True)
        sums = 0.0
        for at in parts_of:
            raised = jnp.exp(scores[slot, at] - top)
            sums = sums + by_eight(raised).sum(0)
            scores[slot, at] = raised
        inverse = 1.0 / jnp.sum(sums, axis=0, keepdims=True)
        for at in parts_of:
            weights[at, rows] = (scores[slot, at] * inverse).astype(BF)
        out_t = dot(vt[...], weights[:, rows]).astype(BF).astype(F32)
        delta = jnp.sum(cs[rows].astype(F32).T * out_t, axis=0, keepdims=True)
        for at in parts_of:
            probs = scores[slot, at] * inverse
            score_cots[at, rows] = (probs * (prob_cots[slot, at] - delta)).astype(BF)
        if slots == 1 and pair + 1 < heads // 2:
            products(pair + 1)
        dq_t = dot(kt[...], score_cots[:, rows]) * scale
        out_rows = jnp.concatenate([out_t[:, :tokens].T, out_t[:, tokens:].T], axis=1)
        att[:, cl : cl + 2 * value_size] = out_rows.astype(BF)
        dq_rows = jnp.concatenate([dq_t[:, :tokens].T, dq_t[:, tokens:].T], axis=1)
        dq[:, ql : ql + 2 * key_size] = dq_rows.astype(BF)
    key_cots, value_cots = dot(score_cots[...], qs[...]), dot(weights[...], cs[...])
    edge = keep_a.shape[1]
    count = blocks // 2
    for i in range(blocks):
        at = slice(i * tokens, (i + 1) * tokens)
        packed = pack_kv(key_cots[at], value_cots[at])
        for order, keep, send, part in (
            (masks[0], keep_a, send_a, packed[:edge]),
            (masks[1], keep_b, send_b, packed[edge:]),
        ):
            k = order.index(i)
            if k < count:
                keep[k] = part
            else:
                send[k - count] = part.astype(BF)


def total_of(parts):
    total = parts[0][...]
    for part in parts[1:]:
        total = total + part[...].astype(F32)
    return total


def fold_kernel(*refs):
    keep, send = refs[-2:]
    total = total_of(refs[:-2])
    keep[...] = total[: keep.shape[0]]
    send[...] = total[keep.shape[0] :].astype(BF)


def fold_two_kernel(*refs):
    fold_kernel(refs[0], refs[1], refs[4], refs[5])
    fold_kernel(refs[2], refs[3], refs[6], refs[7])


def merge_kernel(keep_a, in_a, keep_b, in_b, keep, send):
    total = jnp.concatenate([total_of((keep_a, in_a)), total_of((keep_b, in_b))], axis=1)
    keep[...] = total[: keep.shape[0]]
    send[...] = total[keep.shape[0] :].astype(BF)


def send_on_kernel(keep, came, out):
    out[...] = (keep[...] + came[...].astype(F32)).astype(BF)


def query_cot_kernel(dq, wq, out):
    out[...] = dot_t(dq[...], wq[...])


def middle_kernel(own, came, part, pooled_in, gain_in, wk, wv, first, second, *edges):
    size = own.shape[2]
    tokens, width = pooled_in.shape
    total = (own[0] + came[0].astype(F32)).astype(BF).astype(F32)
    key_cot = total[:tokens]
    value_cot = unpack_values(total, tokens, size)
    normed_cot = part[...] + dot_t(key_cot.astype(BF), wk[...])
    normed_cot = normed_cot + dot(value_cot.astype(BF), wv[...])
    pooled, gain = pooled_in[...], gain_in[...]
    inv = lax.rsqrt(jnp.mean(pooled * pooled, axis=-1, keepdims=True) + EPS)
    gain_term = jnp.sum(normed_cot * pooled * inv, axis=0, keepdims=True)
    gained = gain * normed_cot
    pooled_cot = inv * gained - pooled * (inv * inv * inv) * (
        jnp.sum(gained * pooled, axis=-1, keepdims=True) / width
    )
    conv_cot = 0.5 * pooled_cot
    high = gain_term.astype(BF).astype(F32)
    low = gain_term - high
    row = lax.broadcasted_iota(jnp.int32, (16, width), 0)
    split = width // 2
    lines = (high[:, :split], low[:, :split], high[:, split:], low[:, split:])
    lines += (conv_cot[:1, split:], conv_cot[tokens - 1 :, split:])
    gains = jnp.zeros((16, split), F32)
    for i, line in enumerate(lines):
        gains = jnp.where(row[:, :split] == i, line, gains)
    fill = split - size - value_cot.shape[1]
    side = jnp.concatenate([key_cot, value_cot, jnp.zeros((tokens, fill), F32)], axis=1)
    first[:tokens] = conv_cot[:, :split].astype(BF)
    first[tokens:] = gains.astype(BF)
    second[:tokens] = conv_cot[:, split:].astype(BF)
    second[tokens:] = side.astype(BF)
    for edge in edges:
        ends = jnp.where(row == 0, conv_cot[:1], jnp.where(row == 1, conv_cot[tokens - 1 :], 0.0))
        edge[...] = ends.astype(BF)


def place(other=0):
    seq, dp = lax.axis_index("seq"), lax.axis_index("dp") ^ (other % 2)
    high, low = seq // 2, (seq % 2) ^ (other // 2)
    return lambda k: ((high ^ k) * 2 + low) * 2 + dp


def chosen(rows, padded, columns, block):
    row = lax.broadcasted_iota(jnp.int32, (padded, columns), 0)
    column = lax.broadcasted_iota(jnp.int32, (padded, columns), 1)
    hit = (column == row + block * rows) & (row < rows)
    return jnp.where(hit, 1.0, 0.0).astype(BF)


def select_kernel(*refs, order, rows, padded):
    own, blocks = refs[0], refs[1:5]
    out, norm_out, even, odd = refs[5:]
    ext, channels = even.shape
    tokens = own.shape[1]
    count = own.shape[0]
    step = split_rows(count, channels)
    norm_out[:, :tokens] = own[...]
    for i in range(1, 4):
        at = 2 * ext + (i // 3) * step
        for c in range(channels // LANES):
            end = min((c + 1) * step, count)
            piece = blocks[i][at : at + end - c * step, c * LANES : (c + 1) * LANES]
            norm_out[c * step : end, i * tokens : (i + 1) * tokens] = piece
    block_of = place()
    pick = jnp.concatenate(
        [chosen(rows, padded, 5 * channels, block_of(k)) for k in order], axis=0
    )
    for i, block in enumerate(blocks):
        even[...] = block[:ext].astype(F32)
        odd[...] = block[ext : 2 * ext].astype(F32)
        pieces = []
        for shift in range(3):
            pieces += [even[shift : shift + tokens].astype(BF), odd[shift : shift + tokens].astype(BF)]
        shifted = jnp.concatenate(
            [jnp.concatenate(pieces[:5], axis=1), jnp.concatenate(pieces[1:], axis=1)], axis=0
        )
        out[:, 2 * i * tokens : 2 * (i + 1) * tokens] = dot_t(pick, shifted).astype(BF)


def query_grad_kernel(pick, first, second, third, fourth, keep, send, right):
    tokens = first.shape[0]
    for i, block in enumerate((first, second, third, fourth)):
        right[i * tokens : (i + 1) * tokens] = block[...]
    count, pad = keep.shape[:2]
    for k in range(2 * count):
        term = dot(pick[k * pad : (k + 1) * pad], right[...])
        if k < count:
            keep[k] = term
        else:
            send[k - count] = term.astype(BF)


def side_rows(norm_rows, size, width):
    return norm_rows * size // width


def put_side(stage, at, part, rows):
    pieces = [part[i : i + rows] for i in range(0, part.shape[0], rows)]
    stage[at : at + rows] = jnp.concatenate(pieces, axis=1)


def get_side(packed, part, rows):
    size = part.shape[1]
    for i in range(part.shape[0] // rows):
        part[i * rows : (i + 1) * rows] = packed[:, i * size : (i + 1) * size]


def stack_cots(blocks, right, tokens):
    for i, block in enumerate(blocks):
        piece = block[:tokens]
        right[2 * i * tokens : (2 * i + 1) * tokens] = piece
        right[(2 * i + 1) * tokens : (2 * i + 2) * tokens] = piece


def conv_first_kernel(*refs, conv_rows, conv_pad):
    pick, blocks, outs, right, stage = refs[0], refs[1:5], refs[5:9], refs[9], refs[10]
    tokens = right.shape[0] // 8
    stack_cots(blocks, right, tokens)
    stage[...] = jnp.zeros(stage.shape, F32)
    for half in range(2):
        gain = None
        for block in blocks:
            lines = block[tokens : tokens + 16].astype(F32)[2 * half : 2 * half + 2]
            term = lines[0:1] + lines[1:2]
            gain = term if gain is None else gain + term
        high = gain.astype(BF).astype(F32)
        at = conv_rows + 2 * half
        stage[at : at + 1] = high
        stage[at + 1 : at + 2] = gain - high
    count, above = outs[0].shape[:2]
    even = lax.axis_index("seq") % 2 == 0
    own, pair = blocks[0], blocks[2]
    tops = [b[0:16].astype(F32)[0:1] for b in (own, pair)]
    bottoms = [b[tokens - 16 : tokens].astype(F32)[15:16] for b in (own, pair)]
    rests = [b[tokens : tokens + 16].astype(F32)[4:6] for b in (own, pair)]
    for k in range(4 * count):
        conv = dot(pick[k * conv_pad : (k + 1) * conv_pad], right[...])
        stage[:conv_rows] = conv[:conv_rows]
        if k == 3 * count:
            stage[above - 4 : above - 3] = jnp.where(even, tops[0], tops[1])
            stage[above - 3 : above - 2] = jnp.where(even, rests[0][0:1], rests[1][0:1])
            stage[above - 2 : above - 1] = jnp.where(even, bottoms[1], bottoms[0])
            stage[above - 1 : above] = jnp.where(even, rests[1][1:2], rests[0][1:2])
        out = outs[k // count]
        out[k % count] = stage[...].astype(out.dtype)


def conv_second_kernel(*refs, conv_rows, conv_pad, norm_rows, norm_pad, key_size, value_size):
    pick, norm_pick, blocks, first_send = refs[0], refs[1], refs[2:6], refs[6]
    near_keep, far_keep, near_send, far_send, right, side, stage = refs[7:]
    tokens, width = right.shape[0] // 8, right.shape[1]
    stack_cots(blocks, right, tokens)
    for i, block in enumerate(blocks):
        side[i * tokens : (i + 1) * tokens] = block[tokens:]
    key_rows = side_rows(norm_rows, key_size, width)
    value_rows = side_rows(norm_rows, value_size, width)
    stage[...] = jnp.zeros(stage.shape, F32)
    count, above = first_send.shape[:2]
    near_send[:, :above] = first_send[...]
    for k in range(4 * count):
        conv = dot(pick[k * conv_pad : (k + 1) * conv_pad], right[...])
        stage[:conv_rows] = conv[:conv_rows]
        both = dot(norm_pick[k * norm_pad : (k + 1) * norm_pad], side[...])
        put_side(stage, conv_rows, both[:norm_rows, :key_size], key_rows)
        value = both[:norm_rows, key_size : key_size + value_size]
        put_side(stage, conv_rows + key_rows, value, value_rows)
        if k < 2 * count:
            (near_keep, far_keep)[k // count][k % count] = stage[...]
        elif k < 3 * count:
            near_send[k % count, above:] = stage[...].astype(BF)
        else:
            far_send[k % count] = stage[...].astype(BF)


def first_sum_kernel(keep, near, far, out):
    above = keep.shape[1]
    out[...] = keep[...] + near[:, :above].astype(F32) + far[...].astype(F32)


def combine_kernel(first, second, near, far, out):
    above = first.shape[1]
    out[:, :above] = first[...]
    out[:, above:] = second[...] + near[:, above:].astype(F32) + far[...].astype(F32)


def final_kernel(*refs, conv_parts, above):
    conv, query, key, value, gain, stage = refs[-6:]
    rows, width = conv.shape
    split = width // 2
    count = key.shape[0]
    if conv_parts == 4:
        combine_kernel(*refs[:4], stage)
    else:
        stage[...] = total_of(refs[:conv_parts])
    query[...] = total_of(refs[conv_parts:-6])[0, : query.shape[0]]
    conv[:, :split] = stage[0, :rows]
    conv[:, split:] = stage[0, above : above + rows]
    at = above + rows
    for part in (key, value):
        step = side_rows(count, part.shape[1], split)
        get_side(stage[0, at : at + step], part, step)
        at += step
    lines = stage[0, rows : rows + 4]
    line = jnp.concatenate([lines[0:1] + lines[1:2], lines[2:3] + lines[3:4]], axis=1)
    line = jnp.broadcast_to(line, (8, width))
    start = place()(0) * count
    gain[...] = pltpu.roll(line, lax.rem(width - start, width), 1)[:1, :count]


def input_kernel(*refs):
    x, first, second, pair_first, pair_second, one, three, weight, out, ext, mixed = refs
    tokens = x.shape[0] // 2
    seq, devices = lax.axis_index("seq"), lax.axis_size("seq")
    low, high = seq % 2, seq // 2
    split = first.shape[1]
    above = one.shape[1]
    one_rows = one[0, above - 16 :].astype(F32)[12:]
    three_rows = three[0, above - 16 :].astype(F32)[12:]
    heads = jnp.where(high % 2 == 0, one_rows[:2], three_rows[:2])
    tails = jnp.where(high % 2 == 0, three_rows[2:], one_rows[2:])
    heads = jnp.where(seq == devices - 1, 0.0, heads)
    tails = jnp.where(seq == 0, 0.0, tails)
    for half, own, pair in ((0, first, pair_first), (1, second, pair_second)):
        lanes = slice(half * split, (half + 1) * split)
        top = pair[0:16].astype(F32)[0:1]
        bottom = pair[tokens - 16 : tokens].astype(F32)[15:16]
        ext[8 : 8 + tokens, lanes] = own[:tokens].astype(F32)
        ext[7:8, lanes] = jnp.where(low == 0, tails[half : half + 1], bottom)
        ext[8 + tokens : 9 + tokens, lanes] = jnp.where(low == 0, top, heads[half : half + 1])
    back = ext[7 : 7 + tokens].astype(BF)
    here = ext[8 : 8 + tokens].astype(BF)
    ahead = ext[9 : 9 + tokens].astype(BF)
    evens = (ahead, here, here, back, back)
    odds = (ahead, ahead, here, here, back)
    total = None
    for tap in range(5):
        term = dot_t(jnp.concatenate([evens[tap], odds[tap]], axis=0), weight[tap])
        total = term if total is None else total + term
    for c in range(mixed.shape[0]):
        lanes = slice(c * LANES, (c + 1) * LANES)
        mixed[c, pl.ds(0, tokens, stride=2)] = total[:tokens, lanes]
        mixed[c, pl.ds(1, tokens, stride=2)] = total[tokens:, lanes]
        out[:, lanes] = (mixed[c] * gelu_slope(x[:, lanes].astype(F32))).astype(BF)


def on_device(x, conv_weight, norm_gain, wq, wk, wv, cotangent):
    devices = lax.axis_size("seq")
    both_axes = ("seq", "dp")
    x, cotangent = x[0], cotangent[0]
    positions, channels = x.shape
    tokens = positions // 2
    taps, _, width = conv_weight.shape
    key_size, value_size = wk.shape[1], wv.shape[1]
    heads = cotangent.shape[1] // value_size
    scale = key_size ** (-0.5)
    groups = devices // 2
    owners = devices * 2
    conv_rows, norm_rows = taps * channels // owners, width // owners
    conv_pad, norm_pad = round_up(conv_rows, 16), round_up(norm_rows, 16)
    ext = tokens + 16
    gain = norm_gain.reshape(1, width)

    def swap(value, seq_bits, dp_bit=0):
        mask = 2 * seq_bits + dp_bit
        return lax.ppermute(value, both_axes, [(i, i ^ mask) for i in range(owners)])

    def held(value, *until):
        return lax.optimization_barrier((value,) + until)[0]

    def quad(value, *until):
        core = swap(value, 0, 1)
        near = swap(value, 1)
        return [value, core, near, swap(held(near, *until), 0, 1)]

    def fold(parts, name):
        shape = (parts[0].shape[0] // 2,) + parts[0].shape[1:]
        return run(fold_kernel, [(shape, F32), (shape, BF)], parts, name=name)

    def halved(keep, send, bits, name):
        for bit in bits[:-1]:
            keep, send = fold([keep, swap(send, 1 << bit)], name)
        return [keep, swap(send, 1 << bits[-1])]

    bits = list(range(devices.bit_length() - 1))
    order = [mask // 2 for mask in ordered(bits[1:])]
    crossing = [(i, i + 1) for i in range(1, devices - 1, 2)]
    crossing = crossing + [(j, i) for i, j in crossing]
    pad_shape = (channels // LANES, 8 + 2 * ext + 8, LANES)
    ready, ends = run(
        open_kernel,
        [(pad_shape, F32), ((32, channels), BF)],
        [x],
        flops=4 * 10**9,
        name="gelu",
    )
    pair, across = swap(ends, 1), lax.ppermute(ends, "seq", crossing)
    wv = wv.T
    kv, early, normed, pooled = run(
        front_kernel,
        [
            ((5 * tokens // 2, key_size), BF),
            ((2 * ext, channels), BF),
            ((tokens, width), BF),
            ((tokens, width), F32),
        ],
        [ready, pair, across, conv_weight, gain, wk, wv],
        [pltpu.VMEM(pad_shape, F32)],
        flops=2 * positions * taps * channels * width,
        name="front",
    )
    parts = [0, *range(2, groups), 1]
    near_kv = [swap(kv, 2 * k) if k else kv for k in parts]
    far_kv = [swap(block, 1) for block in near_kv]
    picked = (groups * norm_pad, tokens)
    rows = split_rows(picked[0], channels)
    queries, to_near, to_core, pick_own = run(
        lambda *refs: query_kernel(
            *refs, order=order, rows=norm_rows, padded=norm_pad, scale=scale
        ),
        [
            ((tokens, heads * key_size), BF),
            ((2 * ext + 2 * rows, channels), BF),
            ((2 * ext + rows, channels), BF),
            (picked, BF),
        ],
        [normed, wq, early],
        flops=4 * tokens * width * heads * key_size,
        name="queries",
        after=near_kv[1:],
    )
    to_near, to_core = held(to_near, *far_kv), held(to_core, *far_kv)
    length = devices * tokens
    masks = [2 * k for k in parts] + [2 * k + 1 for k in parts]
    half_block = (groups, 5 * tokens // 4, key_size)
    slots = 2 if length <= 2048 else 1
    attended, query_cot, keep_a, send_a, keep_b, send_b = run(
        lambda *refs: attend_kernel(
            *refs,
            blocks=devices,
            masks=[
                [masks.index(m) for m in ordered(way)] for way in (bits, [1, 0] + bits[2:])
            ],
            heads=heads,
            key_size=key_size,
            value_size=value_size,
            scale=scale,
        ),
        [((tokens, heads * value_size), BF), ((tokens, heads * key_size), BF)]
        + [(half_block, F32), (half_block, BF)] * 2,
        [queries, cotangent] + near_kv + far_kv,
        [
            pltpu.VMEM((length, key_size), BF),
            pltpu.VMEM((length, value_size), BF),
            pltpu.VMEM((key_size, length), BF),
            pltpu.VMEM((value_size, length), BF),
            pltpu.VMEM((heads * tokens, key_size), BF),
            pltpu.VMEM((heads * tokens, value_size), BF),
            pltpu.VMEM((length, heads * tokens), BF),
            pltpu.VMEM((length, heads * tokens), BF),
            pltpu.VMEM((slots, length, 2 * tokens), F32),
            pltpu.VMEM((slots, length, 2 * tokens), F32),
        ],
        flops=6 * tokens * heads * length * (key_size + value_size),
        name="attend",
    )
    in_a, in_b = swap(send_a, 1), swap(send_b, 2)
    early_near = swap(to_near, 1)
    (normed_cot,) = run(
        query_cot_kernel,
        [((tokens, width), F32)],
        [query_cot, wq],
        flops=2 * tokens * width * heads * key_size,
        name="query_part",
    )
    fourth = (groups // 2,) + half_block[1:]
    keep_a, send_a, keep_b, send_b = run(
        fold_two_kernel,
        [(fourth, F32), (fourth, BF)] * 2,
        [keep_a, in_a, keep_b, in_b],
        name="kv_cot_fold",
        after=[normed_cot],
    )
    early_core, early_last = swap(held(to_core, keep_a), 0, 1), swap(held(early_near, keep_a), 0, 1)
    early_blocks = [early, early_core, early_near, early_last]
    in_a, in_b = swap(send_a, 2), swap(send_b, 1)
    block = (groups // 4, 5 * tokens // 2, key_size)
    keep, send = run(
        merge_kernel,
        [(block, F32), (block, BF)],
        [keep_a, in_a, keep_b, in_b],
        name="kv_cot_merge",
    )
    conv_pick, norm_pick = run(
        lambda *refs: select_kernel(*refs, order=order, rows=conv_rows, padded=conv_pad),
        [((groups * conv_pad, 8 * tokens), BF), ((groups * norm_pad, 4 * tokens), BF)],
        [held(pick_own, keep)] + early_blocks,
        [pltpu.VMEM((ext, channels), F32), pltpu.VMEM((ext, channels), F32)],
        flops=2 * groups * conv_pad * taps * channels * 8 * tokens,
        name="select",
    )
    query_cot = held(query_cot, keep)
    query_near, query_core = swap(query_cot, 1), swap(held(query_cot, conv_pick), 0, 1)
    kv_cot = halved(keep, send, bits[2:], "kv_cot_fold")
    first, second, *edge = run(
        middle_kernel,
        [
            ((tokens + 16, width // 2), BF),
            ((2 * tokens, width // 2), BF),
        ]
        + [((16, width), BF)] * (len(bits) > 3),
        kv_cot + [normed_cot, held(pooled, conv_pick), gain, wk, wv],
        flops=2 * tokens * width * (key_size + value_size),
        name="conv_cot",
    )
    near_first, near_second = swap(first, 1), swap(second, 1)
    query_last = swap(held(query_near, first), 0, 1)
    query_half = (groups // 2, norm_pad, heads * key_size)
    query_keep, query_send = run(
        query_grad_kernel,
        [(query_half, F32), (query_half, BF)],
        [norm_pick, query_cot, query_core, query_near, query_last],
        [pltpu.VMEM((4 * tokens, heads * key_size), BF)],
        flops=2 * groups * norm_pad * 4 * tokens * heads * key_size,
        name="query_grad",
    )
    query_parts = halved(query_keep, query_send, bits[1:], "query_fold")
    core_first, core_second = swap(first, 0, 1), swap(second, 0, 1)
    split = width // 2
    side = side_rows(norm_rows, key_size, split) + side_rows(norm_rows, value_size, split)
    above, below = round_up(conv_rows + 8, 16), round_up(conv_rows + side, 16)
    count = groups // 4
    last_first = swap(held(near_first, query_keep), 0, 1)
    near_keep, far_keep, near_send, far_send = run(
        lambda *refs: conv_first_kernel(*refs, conv_rows=conv_rows, conv_pad=conv_pad),
        [((count, above, split), t) for t in (F32, F32, BF, BF)],
        [conv_pick, first, core_first, near_first, last_first],
        [pltpu.VMEM((8 * tokens, split), BF), pltpu.VMEM((above, split), F32)],
        flops=groups * conv_pad * 8 * tokens * width,
        name="conv_grad_first",
    )
    far_in = swap(far_send, 2)
    last_second = swap(held(near_second, near_keep, query_parts[0]), 0, 1)
    near_keep_second, far_keep_second, near_send, far_send = run(
        lambda *refs: conv_second_kernel(
            *refs,
            conv_rows=conv_rows,
            conv_pad=conv_pad,
            norm_rows=norm_rows,
            norm_pad=norm_pad,
            key_size=key_size,
            value_size=value_size,
        ),
        [
            ((count, below, split), F32),
            ((count, below, split), F32),
            ((count, above + below, split), BF),
            ((count, below, split), BF),
        ],
        [conv_pick, norm_pick, second, core_second, near_second, last_second, near_send],
        [
            pltpu.VMEM((8 * tokens, split), BF),
            pltpu.VMEM((4 * tokens, split), BF),
            pltpu.VMEM((below, split), F32),
        ],
        flops=groups * conv_pad * 8 * tokens * width,
        name="conv_grad_second",
    )
    far_in_second = swap(far_send, 2)
    near_in = swap(near_send, 2)
    (far_sum,) = run(
        send_on_kernel,
        [((count, above, split), BF)],
        [far_keep, far_in],
        name="conv_send_on",
    )
    far_last = swap(far_sum, 4)
    (far_sum,) = run(
        send_on_kernel,
        [((count, below, split), BF)],
        [far_keep_second, far_in_second],
        name="conv_send_on",
    )
    edges = [far_in, far_last]
    if len(bits) > 3:
        came = lax.ppermute(edge[0], "seq", crossing)
        rows = jnp.concatenate([came[:1, :split], came[:1, split:], came[1:2, :split], came[1:2, split:]])
        edges = [jnp.pad(rows, ((above - 4, 0), (0, 0)))[None]] * 2
    (input_grad,) = run(
        input_kernel,
        [((positions, channels), BF)],
        [held(x, far_sum, query_parts[1]), first, second, near_first, near_second] + edges + [conv_weight],
        [
            pltpu.VMEM((tokens + 16, width), F32),
            pltpu.VMEM((channels // LANES, positions, LANES), F32),
        ],
        flops=20 * positions * taps * channels * width,
        name="input_grad",
    )
    (first_sum,) = run(
        first_sum_kernel,
        [((count, above, split), F32)],
        [near_keep, near_in, far_last],
        flops=5 * 10**9,
        name="conv_first_sum",
    )
    conv_parts = [first_sum, near_keep_second, near_in, swap(far_sum, 4)]
    chunk = (count, above + below, split)
    if len(bits) > 3:
        keep = run(combine_kernel, [(chunk, F32)], conv_parts, name="conv_combine")[0]
        half = (count // 2,) + chunk[1:]
        keep, send = run(fold_kernel, [(half, F32), (half, BF)], [keep], name="conv_fold")
        conv_parts = halved(keep, send, bits[3:], "conv_fold")
    conv_grad, query_grad, key_grad, value_grad, gain_grad = run(
        lambda *refs: final_kernel(*refs, conv_parts=len(conv_parts), above=above),
        [
            ((conv_rows, width), F32),
            ((norm_rows, heads * key_size), F32),
            ((norm_rows, key_size), F32),
            ((norm_rows, value_size), F32),
            ((1, norm_rows), F32),
        ],
        conv_parts + query_parts,
        [pltpu.VMEM((1,) + chunk[1:], F32)],
        name="final_sum",
    )
    return (
        attended[None],
        input_grad[None],
        conv_grad,
        query_grad,
        key_grad,
        value_grad,
        gain_grad.reshape(norm_rows),
    )


def solution(mesh):
    placed = (
        P(("groups", "dp"), "seq", None),
        P(),
        P(),
        P(),
        P(),
        P(),
        P(("groups", "dp"), "seq", None),
    )
    return jax.shard_map(
        on_device,
        mesh=mesh,
        in_specs=placed,
        out_specs=(
            P(("groups", "dp"), "seq", None),
            P(("groups", "dp"), "seq", None),
            P(("groups", "seq", "dp"), None),
            P(("groups", "seq", "dp"), None),
            P(("groups", "seq", "dp"), None),
            P(("groups", "seq", "dp"), None),
            P(("groups", "seq", "dp")),
        ),
        check_vma=False,
    )
```
